32 devices in a mesh: br: 2 (over x), rows: 16 (over z, y, core).
Axes of the slice: x: 2, y: 2, z: 4, core: 2. Of those that a mesh axis runs over, the one named last changes fastest.
Arguments:
- tile_embed: bfloat16 [16, 512, 768], P('rows', 'br'), may hold values from -6 to 6
- slide_lengths: int32 [16], replicated, may hold values from 1 to 2048, 8192 in all
- head_offsets: int32 [5, 16], replicated, may hold values from 0 to 15, as said below
- pre_gain: float32 [1, 768], replicated, may hold values from 0.25 to 1.75
- pre_shift: float32 [1, 768], replicated, may hold values from -4 to 4
- qkv_weight: bfloat16 [768, 2304], replicated, may hold values from -0.21875 to 0.21875
- query_bias: float32 [1, 768], replicated, may hold values from -6 to 6
- value_bias: float32 [1, 768], replicated, may hold values from -1.5 to 1.5
- out_weight: bfloat16 [768, 768], replicated, may hold values from -1.75 to 1.75
- out_bias: float32 [1, 768], replicated, may hold values from -4 to 4
- post_gain: float32 [1, 768], replicated, may hold values from 0.25 to 1.75
- post_shift: float32 [1, 768], replicated, may hold values from -4 to 4
- up_weight: bfloat16 [768, 3072], replicated, may hold values from -0.21875 to 0.21875
- up_bias: float32 [1, 3072], replicated, may hold values from -4 to 4
- down_weight: bfloat16 [3072, 768], replicated, may hold values from -0.109375 to 0.109375
- down_bias: float32 [1, 768], replicated, may hold values from -4 to 4
- out_grad: bfloat16 [16, 512, 768], P('rows', 'br'), may hold values from -6 to 6
Outputs:
- layer_out: bfloat16 [16, 512, 768], P('rows', 'br')
- tile_grad: bfloat16 [16, 512, 768], P('rows', 'br')
- pre_gain_grad: float32 [1, 768], P(None, ('br', 'rows'))
- pre_shift_grad: float32 [1, 768], P(None, ('br', 'rows'))
- qkv_weight_grad: float32 [768, 2304], P(None, ('br', 'rows'))
- query_bias_grad: float32 [1, 768], P(None, ('br', 'rows'))
- value_bias_grad: float32 [1, 768], P(None, ('br', 'rows'))
- out_weight_grad: float32 [768, 768], P(None, ('br', 'rows'))
- out_bias_grad: float32 [1, 768], P(None, ('br', 'rows'))
- post_gain_grad: float32 [1, 768], P(None, ('br', 'rows'))
- post_shift_grad: float32 [1, 768], P(None, ('br', 'rows'))
- up_weight_grad: float32 [768, 3072], P(None, ('br', 'rows'))
- up_bias_grad: float32 [1, 3072], P(None, ('br', 'rows'))
- down_weight_grad: float32 [3072, 768], P(None, ('br', 'rows'))
- down_bias_grad: float32 [1, 768], P(None, ('br', 'rows'))
The draws below stay inside these ranges and needn't reach their ends.
Inputs may be any that keep to these rules, and one draw needn't show every extreme that they name: `slide_lengths`: the slides' lengths add up to 8192. `head_offsets`: every entry of row b is smaller than 2 to the power b.
All inputs are finite; a program needn't handle non-finite values.
Results may differ from the reference program's by a relative error of at most 0.017.
Values may be sent and summed in bfloat16 or wider, within the bound.
No kernel may reach another device: no remote copies, remote signals or barrier semaphores. Data moves between devices by JAX's collectives and lax.ppermute only.
A program may use at most 192 MiB of HBM per device.

```python
import math
import jax
import jax.numpy as jnp
import numpy as np
from jax import lax

D = 768
HEADS = 16
HEAD_DIM = 48
FF = 3072
TOK_DEV = 512
SEG_BASE = 1024
BRANCHES = 5
TOKENS = 8192
DOC_MOST = 2048
SLIDES = 16
N_ROWS = 16


def draw_head_offsets(key, part):
    table = []
    for branch_level in range(BRANCHES):
        order = jax.random.permutation(jax.random.fold_in(key, branch_level + 11), HEADS)
        table.append((order % 2 ** branch_level).astype(jnp.int32))
    return jnp.stack(table)


def raised(values, rng, source, target, shards_of, factor):
    owner, partner = [(jnp.arange(values.shape[dim]) // (values.shape[dim] // shards_of)).reshape([-1 if axis == dim else 1 for axis in range(values.ndim)]) for dim in (source, target)]
    chosen = jax.random.permutation(rng, shards_of)[partner]
    strong = (owner == chosen) | (owner == (partner + shards_of // 2) % shards_of)
    return jnp.where(strong, factor * values, values)


def level_of(own_key, shape, cuts, least, high):
    level = 1.0
    for dim, parts in cuts:
        heights = jax.random.uniform(jax.random.fold_in(jax.random.fold_in(own_key, 6), dim), (parts,), jnp.float32, least / len(cuts), high / len(cuts))
        level = level * jnp.repeat(jnp.exp(heights), shape[dim] // parts).reshape((-1,) + (1,) * (len(shape) - 1 - dim))
    return level


def length_profile(count, total, most, slope):
    loads = [(1 << 20) // math.isqrt(standing ** slope) + 1 for standing in range(2, count + 1)]
    spare, holding = total - most - (count - 1), [1] * (count - 1)
    while spare > 0:
        candidates = [i for i in range(count - 1) if holding[i] < most]
        whole, left = sum([loads[i] for i in candidates]), spare
        for i in candidates:
            addition = min(most - holding[i], max(1, left * loads[i] // whole), spare)
            holding[i] = holding[i] + addition
            spare = spare - addition
    return np.array([most] + holding)


def uneven(stream_key, count, total, reach, lean):
    if count == 2:
        one = jax.random.randint(stream_key, (), max(1, total - reach), min(reach, total - 1) + 1)
        return jnp.stack([one, total - one])
    lengths = jnp.asarray(length_profile(count, total, reach, lean), jnp.int32)
    pairs = (count - 1) // 2
    giver, sink = lengths[1:1 + 2 * pairs:2], lengths[2:2 + 2 * pairs:2]
    slack = jnp.minimum(giver - 1, reach - sink)
    moved = jax.random.randint(jax.random.fold_in(stream_key, 1), (pairs,), 0, 1 << 20) % (slack + 1)
    lengths = lengths.at[1:1 + 2 * pairs:2].set(giver - moved).at[2:2 + 2 * pairs:2].set(sink + moved)
    return lengths[jax.random.permutation(jax.random.fold_in(stream_key, 2), count)]


def normal_values(stream_key, dims, scale, most, cuts=(), kind=jnp.bfloat16):
    values = scale * jax.random.normal(stream_key, dims, jnp.float32)
    if cuts:
        values = values * level_of(stream_key, dims, cuts, -0.22, 0.18)
    return jnp.clip(values, -most, most).astype(kind)


def noise_with(stream_key, shape, spread, most, shards, heavy, held_as=jnp.bfloat16):
    values = spread * jax.random.normal(stream_key, shape, jnp.float32)
    if shards:
        values = values * level_of(stream_key, shape, shards, -0.22, 0.18)
    return jnp.clip(raised(values, jax.random.fold_in(stream_key, 3), *heavy), -most, most).astype(held_as)


def setup_inputs(seed: int = 0) -> dict:
    arg_keys = jax.random.split(jax.random.key(seed), 18)
    tile_embed = normal_values(arg_keys[0], (N_ROWS, TOK_DEV, D), 1.0, 6.0, ((0, 16), (1, 2)))
    slide_lengths = uneven(arg_keys[1], SLIDES, TOKENS, DOC_MOST, 2).astype(jnp.int32)
    head_offsets = draw_head_offsets(jax.random.fold_in(arg_keys[17], 71), 0)
    pre_gain = jnp.clip(1.0 + 0.15 * jax.random.normal(arg_keys[3], (1, D), jnp.float32), 0.25, 1.75)
    pre_shift = normal_values(arg_keys[4], (1, D), 0.3, 4.0, (), jnp.float32)
    qkv_weight = normal_values(arg_keys[5], (D, 3 * D), D ** -0.5, 0.21875)
    query_bias = normal_values(arg_keys[6], (1, D), 0.5, 6.0, (), jnp.float32)
    value_bias = normal_values(arg_keys[7], (1, D), 0.1, 1.5, (), jnp.float32)
    out_weight = normal_values(arg_keys[8], (D, D), (D // 64) ** -0.5, 1.75)
    out_bias = normal_values(arg_keys[9], (1, D), 0.3, 4.0, (), jnp.float32)
    post_gain = jnp.clip(1.0 + 0.15 * jax.random.normal(arg_keys[10], (1, D), jnp.float32), 0.25, 1.75)
    post_shift = normal_values(arg_keys[11], (1, D), 0.3, 4.0, (), jnp.float32)
    up_weight = normal_values(arg_keys[12], (D, FF), D ** -0.5, 0.21875)
    up_bias = normal_values(arg_keys[13], (1, FF), 0.3, 4.0, (), jnp.float32)
    down_weight = normal_values(arg_keys[14], (FF, D), FF ** -0.5, 0.109375)
    down_bias = normal_values(arg_keys[15], (1, D), 0.3, 4.0, (), jnp.float32)
    out_grad = noise_with(arg_keys[16], (N_ROWS, TOK_DEV, D), 1.0, 6.0, ((0, 16), (1, 2)), (0, 2, 16, 2.0))
    return dict(tile_embed=tile_embed, slide_lengths=slide_lengths, head_offsets=head_offsets, pre_gain=pre_gain, pre_shift=pre_shift, qkv_weight=qkv_weight, query_bias=query_bias, value_bias=value_bias, out_weight=out_weight, out_bias=out_bias, post_gain=post_gain, post_shift=post_shift, up_weight=up_weight, up_bias=up_bias, down_weight=down_weight, down_bias=down_bias, out_grad=out_grad)


@jax.custom_vjp
def low(v):
    return lax.optimization_barrier(v.astype(jnp.bfloat16)).astype(jnp.float32)

@jax.custom_vjp
def low_back(v):
    return v

def low_keep(v):
    return (low(v), None)

def low_pass(kept, grad):
    return (grad,)

def back_keep(v):
    return (v, None)

def back_low(kept, grad):
    return (low(grad),)
low.defvjp(low_keep, low_pass)
low_back.defvjp(back_keep, back_low)
HIGH = lax.Precision.HIGHEST
EPS = 1e-05
NEG = -1e+30

def product(left_side, right_side):
    return jnp.dot(left_side, right_side, precision=HIGH, preferred_element_type=jnp.float32)

def layer_norm(values, norm_gain, norm_shift):
    row_mean = lax.optimization_barrier(jnp.mean(values, -1, keepdims=True))
    centred = values - row_mean
    scaled = centred * lax.rsqrt(lax.optimization_barrier(jnp.mean(centred * centred, -1, keepdims=True)) + EPS)
    return scaled * norm_gain + norm_shift

def slide_of(positions, starts):
    return lax.optimization_barrier(jnp.sum((positions[..., None] >= starts).astype(jnp.int32), -1))

def pick_heads(rows, dilation, offsets):
    row_count = rows.shape[0]
    shaped = rows.reshape(row_count // dilation, dilation, HEADS, HEAD_DIM)
    pick_index = jnp.broadcast_to(offsets[None, None, :, None], (row_count // dilation, 1, HEADS, HEAD_DIM))
    return jnp.take_along_axis(shaped, pick_index, axis=1)[:, 0]

def segment_attend(pieces):
    query_part, key_part, value_part, query_ids, key_ids = pieces
    scores = low_back(jnp.einsum('qhd,khd->hqk', query_part, key_part, precision=HIGH) * HEAD_DIM ** (-0.5))
    allowed = query_ids.T[:, :, None] == key_ids.T[:, None, :]
    row_top = lax.optimization_barrier(jnp.max(jnp.where(allowed, scores, NEG), -1, keepdims=True))
    row_total = lax.optimization_barrier(jnp.sum(jnp.exp(jnp.where(allowed, scores - row_top, NEG)), -1, keepdims=True))
    row_lse = row_top + jnp.log(row_total)
    attn_weights = jnp.exp(jnp.where(allowed, scores - row_lse, NEG))
    mixed_out = jnp.einsum('hqk,khd->qhd', low(attn_weights), value_part, precision=HIGH)
    return (low_back(mixed_out), row_lse[..., 0].T)

def reference(tile_embed, slide_lengths, head_offsets, pre_gain, pre_shift, qkv_weight, query_bias, value_bias, out_weight, out_bias, post_gain, post_shift, up_weight, up_bias, down_weight, down_bias, out_grad):
    starts = (jnp.cumsum(slide_lengths) - slide_lengths).astype(jnp.int32)
    row_ids = slide_of(jnp.arange(TOKENS, dtype=jnp.int32), starts)
    block_rows = min(TOKENS, 4096)
    block_count = TOKENS // block_rows

    def forward(tiles, gain_pre, shift_pre, weight_qkv, bias_query, bias_value, weight_out, bias_out, gain_post, shift_post, weight_up, bias_up, weight_down, bias_down):

        def pre_block(rows):
            normed = low(layer_norm(rows, gain_pre, shift_pre))
            bias_row = jnp.concatenate([bias_query, jnp.zeros_like(bias_query), bias_value], 1)
            return low(low_back(product(normed, weight_qkv) + bias_row))
        joined = lax.map(jax.checkpoint(pre_block), tiles.reshape(block_count, block_rows, D)).reshape(TOKENS, 3 * D)
        query_rows = joined[:, :D]
        key_side = joined[:, D:2 * D]
        value_side = joined[:, 2 * D:]
        branch_outs = []
        branch_lses = []
        for branch_level in range(BRANCHES):
            dilation = 2 ** branch_level
            seg_span = min(SEG_BASE * dilation, TOKENS)
            seg_count = TOKENS // seg_span
            seg_rows = seg_span // dilation
            offsets = head_offsets[branch_level]
            picked_q = pick_heads(query_rows, dilation, offsets).reshape(seg_count, seg_rows, HEADS, HEAD_DIM)
            picked_k = pick_heads(key_side, dilation, offsets).reshape(seg_count, seg_rows, HEADS, HEAD_DIM)
            picked_v = pick_heads(value_side, dilation, offsets).reshape(seg_count, seg_rows, HEADS, HEAD_DIM)
            id_index = jnp.broadcast_to(offsets[None, :], (TOKENS // dilation, HEADS))
            picked_ids = jnp.take_along_axis(row_ids.reshape(TOKENS // dilation, dilation), id_index, axis=1).reshape(seg_count, seg_rows, HEADS)
            mixed, lses = lax.map(jax.checkpoint(segment_attend), (picked_q, picked_k, picked_v, picked_ids, picked_ids))
            branch_outs.append(mixed.reshape(block_count, block_rows // dilation, HEADS, HEAD_DIM))
            branch_lses.append(lses.reshape(block_count, block_rows // dilation, HEADS))

        def post_block(pieces):
            rows, outs_block, lses_block = pieces
            full_outs = []
            full_lses = []
            for branch_level in range(BRANCHES):
                dilation = 2 ** branch_level
                chosen = jnp.arange(dilation, dtype=jnp.int32)[:, None] == head_offsets[branch_level][None, :]
                full_outs.append(jnp.where(chosen[None, :, :, None], outs_block[branch_level][:, None], 0.0).reshape(block_rows, HEADS, HEAD_DIM))
                full_lses.append(jnp.where(chosen[None], lses_block[branch_level][:, None], NEG).reshape(block_rows, HEADS))
            stacked = jnp.stack(full_lses)
            row_top = lax.optimization_barrier(jnp.max(stacked, 0))
            merged_lse = row_top + jnp.log(lax.optimization_barrier(jnp.sum(jnp.exp(stacked - row_top), 0)))
            shares = jnp.exp(stacked - merged_lse)
            attn = lax.optimization_barrier(jnp.sum(shares[..., None] * jnp.stack(full_outs), 0)).reshape(block_rows, D)
            attn_low = low(low_back(attn))
            projected = low_back(product(attn_low, weight_out))
            residual = rows + projected + bias_out
            lifted = low(layer_norm(residual, gain_post, shift_post))
            gate_in = low_back(product(lifted, weight_up) + bias_up)
            act_low = low(jax.nn.gelu(gate_in, approximate=False))
            return residual + product(act_low, weight_down) + bias_down
        result = lax.map(jax.checkpoint(post_block), (tiles.reshape(block_count, block_rows, D), tuple(branch_outs), tuple(branch_lses)))
        return result.reshape(TOKENS, D)
    primals = (tile_embed.reshape(TOKENS, D).astype(jnp.float32), pre_gain, pre_shift, qkv_weight.astype(jnp.float32), query_bias, value_bias, out_weight.astype(jnp.float32), out_bias, post_gain, post_shift, up_weight.astype(jnp.float32), up_bias, down_weight.astype(jnp.float32), down_bias)
    result, pull_back = jax.vjp(forward, *primals)
    grads = pull_back(out_grad.reshape(TOKENS, D).astype(jnp.float32))
    return (result.astype(jnp.bfloat16).reshape(N_ROWS, TOK_DEV, D), grads[0].astype(jnp.bfloat16).reshape(N_ROWS, TOK_DEV, D), grads[1], grads[2], grads[3], grads[4], grads[5], grads[6], grads[7], grads[8], grads[9], grads[10], grads[11], grads[12], grads[13])
```

```python
import functools
import math

import jax
import jax.numpy as jnp
from jax import lax
from jax.experimental import pallas as pl
from jax.experimental.pallas import tpu as pltpu
from jax.sharding import PartitionSpec as P

SEG_BASE = 1024
DOC_MOST = 2048
LANES = 128
BF = jnp.bfloat16
F32 = jnp.float32
NEG = -1e30
ONE_LANE = 48
ID_Q = 51
ID_K = 52


class Plan:
    def __init__(self, heads, head_size, branches, groups, members, tq, total):
        self.heads, self.size, self.groups, self.members, self.tq = heads, head_size, groups, members, tq
        self.blocks = groups * members
        self.tokens = self.blocks * tq
        self.total = total
        self.halo = min(DOC_MOST, self.tokens)
        self.factor = math.log2(math.e) * head_size**-0.5
        self.branches = []
        keys, sel = 0, 0
        for level in range(branches):
            rate = 2**level
            span = min(SEG_BASE * rate, total)
            near = span <= self.tokens
            extra = 0 if near else self.halo // rate
            segs = self.tokens // span if near else 1
            seg_q = self.tokens // rate // segs
            seg_k = seg_q + 2 * extra
            self.branches.append(
                dict(
                    level=level, rate=rate, span=span, near=near, extra=extra, segs=segs,
                    seg_q=seg_q, seg_k=seg_k, tile=min(256, seg_q), first=keys, sel=sel,
                )
            )
            keys += segs * seg_k
            sel += extra
        self.keys = keys
        self.sel = sel
        self.widest = max(b["seg_k"] for b in self.branches)

    def slot(self, block):
        return lax.rem(block, self.groups) * self.members + lax.div(block, self.groups)


def dot_nt(a, b):
    return lax.dot_general(a, b, (((1,), (1,)), ((), ())), preferred_element_type=F32)


def dot_tn(a, b):
    return lax.dot_general(a, b, (((0,), (0,)), ((), ())), preferred_element_type=F32)


def dot_nn(a, b):
    return lax.dot_general(a, b, (((1,), (0,)), ((), ())), preferred_element_type=F32)


def iota(shape, dim):
    return lax.broadcasted_iota(jnp.int32, shape, dim)


def placement(size, parts):
    shape = (parts * size + 16, parts * LANES)
    row, col = iota(shape, 0), iota(shape, 1)
    hit = col < 0
    for part in range(parts):
        hit |= (row >= part * size) & (row < (part + 1) * size) & (col == row - part * size + part * LANES)
    return row, col, hit


def ids_of(pos, starts, gate=None):
    found = jnp.zeros(pos.shape, jnp.int32)
    for start in starts:
        found += jnp.where(pos >= start, 1, 0)
    if gate is not None:
        found = jnp.where(gate, found, -1)
    return found.astype(F32)


def slide_starts(lens_ref):
    starts, at = [], jnp.int32(0)
    for i in range(lens_ref.shape[0]):
        starts.append(at)
        at = at + lens_ref[i]
    return starts


def branch_pos(plan, branch, base, off, first, count):
    start = base - branch["extra"] * branch["rate"] + off
    pos = start + branch["rate"] * (first + iota((1, count), 1))
    if branch["near"]:
        return pos, None
    shift = int(math.log2(branch["span"]))
    return pos, lax.shift_right_arithmetic(pos, shift) == lax.shift_right_arithmetic(base, shift)


def to_rows(plan, base, starts, x_ref, q_tm, k_tm, v_tm, extra_q=None):
    size, tq = plan.size, plan.tq
    row, col, hit = placement(size, 3)
    hit |= (row == 3 * size) & ((col == ID_Q) | (col == LANES + ID_K))
    place = jnp.where(hit, 1.0, 0.0).astype(BF)
    lane = iota((1, 3 * LANES), 1)
    in_k, in_v = lane - LANES, lane - 2 * LANES
    ones = jnp.where(
        ((in_k >= ONE_LANE) & (in_k < ONE_LANE + 3)) | ((in_v >= ONE_LANE) & (in_v < ONE_LANE + 3)), 1.0, 0.0
    )

    def block(n, carry):
        pos = base + n * tq + iota((1, tq), 1)
        ids = jnp.where(iota((16, tq), 0) == 0, ids_of(pos, starts), 0.0).astype(BF)
        full = jnp.concatenate([x_ref[plan.slot(n)], ids], 0)
        rows = dot_tn(full, place) + ones
        at = pl.ds(pl.multiple_of(n * tq, tq), tq)
        queries = rows[:, :LANES]
        if extra_q is not None:
            queries = queries + extra_q(n, at)
        q_tm[at, :] = queries
        k_tm[at, :] = rows[:, LANES : 2 * LANES]
        v_tm[at, :] = rows[:, 2 * LANES :]
        return carry

    lax.fori_loop(0, plan.blocks, block, 0)


def gather_keys(plan, base, offs, starts, halo_ref, k_tm, v_tm, kall, vall):
    size = plan.size
    if plan.sel:
        row, col, hit = placement(size, 2)
        hit |= (row == 2 * size) & (col == ID_K)
        place = jnp.where(hit, 1.0, 0.0).astype(BF)
        lane = iota((1, 2 * LANES), 1)
        in_v = lane - LANES
        ones = jnp.where(
            ((lane >= ONE_LANE) & (lane < ONE_LANE + 3)) | ((in_v >= ONE_LANE) & (in_v < ONE_LANE + 3)), 1.0, 0.0
        )
    for branch in plan.branches:
        rate, first, extra, off = branch["rate"], branch["first"], branch["extra"], offs[branch["level"]]
        count = plan.tokens // rate
        step = min(256, count)

        def chunk(i, carry, rate=rate, first=first, extra=extra, off=off, step=step):
            rows = pl.ds(off + i * step * rate, step, stride=rate) if rate > 1 else pl.ds(i * step, step)
            to = pl.ds(pl.multiple_of(first + extra + i * step, step), step)
            kall[to, :] = k_tm[rows, :].astype(BF)
            vall[to, :] = v_tm[rows, :].astype(BF)
            return carry

        lax.fori_loop(0, count // step, chunk, 0)
        if extra:
            for side in range(2):
                begin = side * (extra + count)
                pos, gate = branch_pos(plan, branch, base, off, begin, extra)
                ids = jnp.where(iota((16, extra), 0) == 0, ids_of(pos, starts, gate), 0.0).astype(BF)
                piece = halo_ref[side, :, branch["sel"] : branch["sel"] + extra]
                rows = dot_tn(jnp.concatenate([piece, ids], 0), place) + ones
                kall[first + begin : first + begin + extra, :] = rows[:, :LANES].astype(BF)
                vall[first + begin : first + begin + extra, :] = rows[:, LANES:].astype(BF)


def picked(branch, off, i):
    tile, rate = branch["tile"], branch["rate"]
    if rate == 1:
        return pl.ds(pl.multiple_of(i * tile, tile), tile)
    return pl.ds(off + i * tile * rate, tile, stride=rate)


def forward_kernel(plan, meta, lens, offsets, x_ref, halo_ref, o_ref, st_ref, q_tm, k_tm, v_tm, kall, vall, kid):
    base, head = meta[0], meta[1]
    starts = slide_starts(lens)
    offs = [offsets[b["level"], head] for b in plan.branches]
    to_rows(plan, base, starts, x_ref, q_tm, k_tm, v_tm)
    gather_keys(plan, base, offs, starts, halo_ref, k_tm, v_tm, kall, vall)
    factor = plan.factor
    for branch in plan.branches:
        off, first, wide, tile = offs[branch["level"]], branch["first"], branch["seg_k"], branch["tile"]
        total = branch["segs"] * wide
        pos, gate = branch_pos(plan, branch, base, off, 0, total)
        kid[:, first : first + total] = ids_of(pos, starts, gate)
        per = branch["seg_q"] // tile

        def attend(i, carry, branch=branch, off=off, first=first, wide=wide, tile=tile, per=per):
            rows = picked(branch, off, i)
            queries = q_tm[rows, :]
            at = pl.ds(pl.multiple_of(first + lax.div(i, per) * wide, 128), wide)
            scores = dot_nt(queries.astype(BF), kall[at, :])
            scores = jnp.where(queries[:, ID_Q : ID_Q + 1] == kid[:, at], scores, NEG)
            top = jnp.max(scores, 1, keepdims=True)
            weights = jnp.exp2((scores - top) * factor)
            mixed = dot_nn(weights.astype(BF), vall[at, :])
            lane = iota((tile, LANES), 1)
            if branch["level"]:
                old = st_ref[rows, :]
                old_top = old[:, ID_Q : ID_Q + 1]
                new_top = jnp.maximum(old_top, top)
                mixed = old * jnp.exp2((old_top - new_top) * factor) + mixed * jnp.exp2((top - new_top) * factor)
                top = new_top
            st_ref[rows, :] = jnp.where(lane == ID_Q, top, mixed)
            return carry

        lax.fori_loop(0, branch["segs"] * per, attend, 0)
    eye = jnp.where(iota((plan.size, LANES), 0) == iota((plan.size, LANES), 1), 1.0, 0.0).astype(BF)

    def finish(n, carry):
        at = pl.ds(pl.multiple_of(n * plan.tq, plan.tq), plan.tq)
        state = st_ref[at, :]
        weight = state[:, ONE_LANE : ONE_LANE + 1]
        top = state[:, ID_Q : ID_Q + 1]
        attn = state * (1.0 / weight)
        merged = top + jnp.log2(weight) * (1.0 / factor)
        lane = iota((plan.tq, LANES), 1)
        st_ref[at, :] = jnp.where(lane < plan.size, attn, jnp.where(lane == ONE_LANE, merged, 0.0))
        o_ref[plan.slot(n)] = dot_nt(eye, attn.astype(BF)).astype(BF)
        return carry

    lax.fori_loop(0, plan.blocks, finish, 0)


def split3(column, lane):
    high = column.astype(BF).astype(F32)
    rest = column - high
    mid = rest.astype(BF).astype(F32)
    low = rest - mid
    return jnp.where(
        lane == ONE_LANE, high, jnp.where(lane == ONE_LANE + 1, mid, jnp.where(lane == ONE_LANE + 2, low, 0.0))
    )


def backward_kernel(
    plan, meta, lens, offsets, x_ref, halo_ref, st_ref, do_ref, dx_ref, dh_ref,
    q_tm, k_tm, v_tm, do_tm, dq_tm, dk_tm, dv_tm, kall, vall, k_fm, qid, dk_acc, dv_acc,
):
    base, head = meta[0], meta[1]
    starts = slide_starts(lens)
    offs = [offsets[b["level"], head] for b in plan.branches]
    size, tq, factor = plan.size, plan.tq, plan.factor
    row, col, hit = placement(size, 1)
    place = jnp.where(hit, 1.0, 0.0).astype(BF)
    lane = iota((tq, LANES), 1)

    def extra_q(n, at):
        state = st_ref[at, :]
        grads = dot_tn(jnp.concatenate([do_ref[plan.slot(n)], jnp.zeros((16, tq), BF)], 0), place)
        dots = jnp.sum(jnp.where(lane < size, grads * state, 0.0), 1, keepdims=True)
        do_tm[at, :] = grads + split3(-dots, lane)
        return split3(-state[:, ONE_LANE : ONE_LANE + 1], lane)

    to_rows(plan, base, starts, x_ref, q_tm, k_tm, v_tm, extra_q)
    gather_keys(plan, base, offs, starts, halo_ref, k_tm, v_tm, kall, vall)
    eye = jnp.where(iota((LANES, LANES), 0) == iota((LANES, LANES), 1), 1.0, 0.0).astype(BF)
    eye_small = eye[:size]
    for branch in plan.branches:
        off, first, wide, tile = offs[branch["level"]], branch["first"], branch["seg_k"], branch["tile"]
        count = branch["segs"] * branch["seg_q"]
        per = branch["seg_q"] // tile
        extra, rate = branch["extra"], branch["rate"]
        pos, _ = branch_pos(plan, branch, base, off, extra, count)
        qid[:, :count] = ids_of(pos, starts)

        def segment(seg, carry, branch=branch, off=off, first=first, wide=wide, tile=tile, per=per):
            at = pl.ds(pl.multiple_of(first + seg * wide, 128), wide)
            k_fm[:, :wide] = dot_nt(eye, kall[at, :]).astype(BF)
            dk_acc[:wide, :] = jnp.zeros((wide, LANES), F32)
            dv_acc[:wide, :] = jnp.zeros((wide, LANES), F32)

            def one(j, carry):
                i = seg * per + j
                rows = picked(branch, off, i)
                queries = q_tm[rows, :].astype(BF)
                grads = do_tm[rows, :].astype(BF)
                keys = kall[at, :]
                linked = keys[:, ID_K : ID_K + 1].astype(F32) == qid[:, pl.ds(pl.multiple_of(i * tile, tile), tile)]
                probs = jnp.where(linked, jnp.exp2(dot_nt(keys, queries) * factor), 0.0)
                dv_acc[:wide, :] += dot_nn(probs.astype(BF), grads)
                moved = (probs * dot_nt(vall[at, :], grads)).astype(BF)
                dk_acc[:wide, :] += dot_nn(moved, queries)
                dq = dot_nn(k_fm[:, :wide], moved).T
                if branch["level"]:
                    dq = dq_tm[rows, :] + dq
                dq_tm[rows, :] = dq
                return carry

            lax.fori_loop(0, per, one, 0)
            step = min(256, branch["seg_q"])
            for c in range(branch["seg_q"] // step):
                begin = branch["extra"] + c * step
                if branch["rate"] == 1:
                    to = pl.ds(pl.multiple_of(seg * branch["seg_q"] + c * step, step), step)
                    dk_tm[to, :] = dk_acc[begin : begin + step, :]
                    dv_tm[to, :] = dv_acc[begin : begin + step, :]
                else:
                    to = pl.ds(off + (seg * branch["seg_q"] + c * step) * branch["rate"], step, stride=branch["rate"])
                    dk_tm[to, :] += dk_acc[begin : begin + step, :]
                    dv_tm[to, :] += dv_acc[begin : begin + step, :]
            return carry

        lax.fori_loop(0, branch["segs"], segment, 0)
        if extra:
            for side in range(2):
                begin = side * (extra + count)
                to = slice(branch["sel"], branch["sel"] + extra)
                dk = (dk_acc[begin : begin + extra, :] * size**-0.5).astype(BF)
                dh_ref[side, :size, to] = dot_nt(eye_small, dk).astype(BF)
                dh_ref[side, size:, to] = dot_nt(eye_small, dv_acc[begin : begin + extra, :].astype(BF)).astype(BF)

    def finish(n, carry):
        at = pl.ds(pl.multiple_of(n * tq, tq), tq)
        slot = plan.slot(n)
        dx_ref[slot, :size, :] = dot_nt(eye_small, (dq_tm[at, :] * size**-0.5).astype(BF)).astype(BF)
        dx_ref[slot, size : 2 * size, :] = dot_nt(eye_small, (dk_tm[at, :] * size**-0.5).astype(BF)).astype(BF)
        dx_ref[slot, 2 * size :, :] = dot_nt(eye_small, dv_tm[at, :].astype(BF)).astype(BF)
        return carry

    lax.fori_loop(0, plan.blocks, finish, 0)


SMEM = pl.BlockSpec(memory_space=pltpu.SMEM)
VMEM = pl.BlockSpec(memory_space=pltpu.VMEM)


def forward_call(plan, meta, lens, offsets, x, halo):
    rows = pltpu.VMEM((plan.tokens, LANES), F32)
    keys = pltpu.VMEM((plan.keys, LANES), BF)
    return pl.pallas_call(
        functools.partial(forward_kernel, plan),
        out_shape=(
            jax.ShapeDtypeStruct((plan.blocks, plan.size, plan.tq), BF),
            jax.ShapeDtypeStruct((plan.tokens, LANES), F32),
        ),
        in_specs=[SMEM] * 3 + [VMEM] * 2,
        out_specs=(VMEM, VMEM),
        scratch_shapes=[rows, rows, rows, keys, keys, pltpu.VMEM((1, plan.keys), F32)],
        compiler_params=pltpu.CompilerParams(vmem_limit_bytes=48 << 20),
        name="attend",
    )(meta, lens, offsets, x, halo)


def backward_call(plan, meta, lens, offsets, x, halo, state, do):
    rows = pltpu.VMEM((plan.tokens, LANES), F32)
    keys = pltpu.VMEM((plan.keys, LANES), BF)
    acc = pltpu.VMEM((plan.widest, LANES), F32)
    return pl.pallas_call(
        functools.partial(backward_kernel, plan),
        out_shape=(
            jax.ShapeDtypeStruct((plan.blocks, 3 * plan.size, plan.tq), BF),
            jax.ShapeDtypeStruct((2, 2 * plan.size, max(plan.sel, 128)), BF),
        ),
        in_specs=[SMEM] * 3 + [VMEM] * 4,
        out_specs=(VMEM, VMEM),
        scratch_shapes=[rows] * 7
        + [keys, keys, pltpu.VMEM((LANES, plan.widest), BF), pltpu.VMEM((1, plan.tokens), F32), acc, acc],
        compiler_params=pltpu.CompilerParams(vmem_limit_bytes=56 << 20),
        name="attend_back",
    )(meta, lens, offsets, x, halo, state, do)


EPS = 1e-05
ALL = ("br", "grp", "s2", "s1", "s0")
GROUP = ("br", "s2", "s1", "s0")


def layer_norm_rows(values, norm_gain, norm_shift):
    row_mean = jnp.mean(values, -1, keepdims=True)
    centred = values - row_mean
    inverse = lax.rsqrt(jnp.mean(centred * centred, -1, keepdims=True) + EPS)
    normed = centred * inverse
    return (normed * norm_gain + norm_shift, normed, inverse)


def norm_back(grad_out, normed, inverse, norm_gain):
    grad_norm = grad_out * norm_gain
    grad_in = inverse * (
        grad_norm
        - jnp.mean(grad_norm, -1, keepdims=True)
        - normed * jnp.mean(grad_norm * normed, -1, keepdims=True)
    )
    return (grad_in, jnp.sum(grad_out * normed, 0), jnp.sum(grad_out, 0))


def swap(values, axes):
    return lax.all_to_all(values, axes, 0, 0, tiled=True)


def scatter_sum(values, orders):
    sizes = {name: lax.axis_size(name) for name in ALL}
    left = list(ALL)
    rows, cols = values.shape[1:]
    for stage, axes in enumerate(orders):
        values = values.reshape([sizes[name] for name in left] + [rows, cols])
        rest = [name for name in left if name not in axes]
        order = [left.index(name) for name in list(axes) + rest]
        values = values.transpose(order + [len(left), len(left) + 1])
        count = math.prod(sizes[name] for name in axes)
        values = values.reshape((count, -1, rows, cols))
        if count > 1:
            values = swap(values, axes)
            values = jnp.sum(values.astype(F32), 0)
            if stage < len(orders) - 1:
                values = values.astype(BF)
        left = rest
    return values.reshape(rows, cols).astype(F32)


def halo_table(plan, offs, side):
    place = jnp.arange(plan.halo, dtype=jnp.int32)[:, None]
    columns = []
    for branch in plan.branches:
        if branch["extra"]:
            wanted = jnp.arange(branch["extra"], dtype=jnp.int32) * branch["rate"]
            columns.append(wanted + offs[branch["level"]])
    wanted = jnp.concatenate(columns)
    wanted = jnp.pad(wanted, (0, max(plan.sel, LANES) - plan.sel), constant_values=-1)
    return (place == wanted[None, :]).astype(BF)


def halo_tokens(plan, x, side):
    parts = x.reshape(plan.groups, plan.members, 3 * plan.size, plan.tq)[:, :, plan.size :]
    count = plan.halo // (plan.groups * plan.tq)
    parts = parts[:, plan.members - count :] if side == 0 else parts[:, :count]
    return parts.transpose(2, 1, 0, 3).reshape(2 * plan.size, plan.halo)


def to_neighbours(pieces, count):
    return jnp.stack(
        [
            lax.ppermute(pieces[0], "grp", [(i, i + 1) for i in range(count - 1)]),
            lax.ppermute(pieces[1], "grp", [(i + 1, i) for i in range(count - 1)]),
        ]
    )


def share_columns(weight_t, sums, width):
    groups, members = lax.axis_size("grp"), lax.axis_size(GROUP)
    devices = groups * members
    size = weight_t.shape[1]
    mine = lax.axis_index("grp")
    head = lax.axis_index(GROUP)
    unit = size // groups
    inner = members // lax.axis_size("br")
    if groups != 2:
        full = jnp.zeros((3, members) + weight_t.shape[1:], F32)
        full = lax.dynamic_update_slice(full, weight_t[:, None], (0, head, 0, 0))
        full_sums = lax.dynamic_update_slice(jnp.zeros((3, members, size), F32), sums[:, None], (0, head, 0))
        weight = lax.psum_scatter(full.reshape(3 * members * size, width), ALL, scatter_dimension=0, tiled=True)
        full_sums = full_sums.reshape(3, members * size)
        sums = lax.psum_scatter(full_sums, ALL, scatter_dimension=1, tiled=True)
        return weight, sums[0], sums[2]
    halves = weight_t.reshape(3, groups, unit, width)
    keep = lax.dynamic_index_in_dim(halves, mine, 1, False)
    give = lax.dynamic_index_in_dim(halves, 1 - mine, 1, False)
    pair = [(0, 1), (1, 0)]
    total = keep + lax.ppermute(give.astype(BF), "grp", pair).astype(F32)
    sums = sums.reshape(3, groups, unit)
    give_sums = jnp.pad(lax.dynamic_index_in_dim(sums, 1 - mine, 1, False), ((0, 5), (0, LANES - unit)))
    keep_sums = lax.dynamic_index_in_dim(sums, mine, 1, False)
    sums = keep_sums + lax.ppermute(give_sums, "grp", pair)[:3, :unit]
    place = {}
    for br in range(devices // groups // inner):
        for grp in range(groups):
            for sub in range(inner):
                place[(br * inner + sub) * groups + grp] = (br * groups + grp) * inner + sub
    here = lax.axis_index(ALL)
    pieces = []
    low = total.astype(BF)
    for slot in range(3):
        route, part_of = [], [0] * devices
        for owner in range(devices):
            part, which = divmod(3 * owner + slot, devices)
            route.append((place[which], owner))
            part_of[place[which]] = part
        part = jnp.array(part_of, jnp.int32)[here]
        pieces.append(lax.ppermute(lax.dynamic_index_in_dim(low, part, 0, False), ALL, route))
    weight = jnp.concatenate(pieces).astype(F32)
    sums = jnp.pad(sums, ((0, 5), (0, LANES - unit)))
    sums = lax.ppermute(sums, ALL, [(place[unit_index], unit_index) for unit_index in range(devices)])
    return weight, sums[0, :unit], sums[2, :unit]


def body(
    tile_embed,
    slide_lengths,
    head_offsets,
    pre_gain,
    pre_shift,
    qkv_weight,
    query_bias,
    value_bias,
    out_weight,
    out_bias,
    post_gain,
    post_shift,
    up_weight,
    up_bias,
    down_weight,
    down_bias,
    out_grad,
):
    width = qkv_weight.shape[0]
    hidden = up_weight.shape[1]
    heads = head_offsets.shape[1]
    size = width // heads
    tq = tile_embed.shape[1]
    br, groups = lax.axis_size("br"), lax.axis_size("grp")
    members = heads // br
    devices = heads * groups
    plan = Plan(heads, size, head_offsets.shape[0], br, members, tq, devices * tq)
    head = lax.axis_index(GROUP)
    base = lax.axis_index("grp") * plan.tokens
    meta = jnp.stack([base, head]).astype(jnp.int32)
    offs = lax.dynamic_index_in_dim(head_offsets, head, 1, False)

    tiles = tile_embed[0].astype(F32)
    pre_out, normed_pre, inverse_pre = layer_norm_rows(tiles, pre_gain, pre_shift)
    normed_low = pre_out.astype(BF)
    bias_col = jnp.concatenate([query_bias, jnp.zeros_like(query_bias), value_bias], 1).reshape(-1, 1)
    joined_t = (
        lax.dot_general(qkv_weight, normed_low, (((0,), (1,)), ((), ())), preferred_element_type=F32) + bias_col
    ).astype(BF)
    x = joined_t.reshape(3, heads, size, tq).transpose(1, 0, 2, 3).reshape(heads, 3 * size, tq)
    x = swap(x, GROUP)
    normed_all = lax.all_gather(normed_low, GROUP, axis=0, tiled=True)

    tables = [halo_table(plan, offs, side) for side in range(2)]
    chosen = [
        jnp.dot(halo_tokens(plan, x, side), tables[side], preferred_element_type=F32).astype(BF)
        for side in range(2)
    ]
    halo = to_neighbours(chosen, groups)
    mixed, state = forward_call(plan, meta, slide_lengths, head_offsets, x, halo)
    attn_t = swap(mixed, GROUP).reshape(width, tq)

    projected = lax.dot_general(attn_t, out_weight, (((0,), (0,)), ((), ())), preferred_element_type=F32)
    residual = tiles + projected + out_bias
    post_out, normed_post, inverse_post = layer_norm_rows(residual, post_gain, post_shift)
    lifted = post_out.astype(BF)
    gate_in = jnp.dot(lifted, up_weight, preferred_element_type=F32) + up_bias
    act_float, gelu_pull = jax.vjp(lambda v: jax.nn.gelu(v, approximate=False), gate_in)
    act_low = act_float.astype(BF)
    layer_out = (residual + jnp.dot(act_low, down_weight, preferred_element_type=F32) + down_bias).astype(BF)[None]
    grad_low = out_grad[0]
    grad_float = grad_low.astype(F32)
    act_grad = lax.dot_general(grad_low, down_weight, (((1,), (1,)), ((), ())), preferred_element_type=F32)
    gate_grad = gelu_pull(act_grad)[0].astype(BF)
    lifted_grad = lax.dot_general(gate_grad, up_weight, (((1,), (1,)), ((), ())), preferred_element_type=F32)
    norm_part, post_gain_sum, post_shift_sum = norm_back(lifted_grad, normed_post, inverse_post, post_gain)
    residual_grad = grad_float + norm_part
    proj_grad = residual_grad.astype(BF)
    attn_grad_t = lax.dot_general(
        out_weight, proj_grad, (((1,), (1,)), ((), ())), preferred_element_type=F32
    ).astype(BF)
    do = swap(attn_grad_t.reshape(heads, size, tq), GROUP)

    tokens = (((0,), (0,)), ((), ()))
    up_part = lax.dot_general(gate_grad, lifted, tokens, preferred_element_type=F32).astype(BF)
    down_part = lax.dot_general(grad_low, act_low, tokens, preferred_element_type=F32).astype(BF)
    out_part = lax.dot_general(proj_grad, attn_t, (((0,), (1,)), ((), ())), preferred_element_type=F32).astype(BF)
    vectors = [
        jnp.sum(gate_grad.astype(F32), 0).reshape(devices, -1),
        jnp.sum(grad_float, 0).reshape(devices, -1),
        jnp.sum(residual_grad, 0).reshape(devices, -1),
        post_gain_sum.reshape(devices, -1),
        post_shift_sum.reshape(devices, -1),
    ]
    ends = [0]
    for vector in vectors:
        ends.append(ends[-1] + vector.shape[1])
    small = jnp.concatenate(vectors, 1)
    small = jnp.pad(small[:, None, :], ((0, 0), (0, 7), (0, width - small.shape[1]))).astype(BF)
    misc = jnp.concatenate([out_part.reshape(devices, -1, width), small], 1)
    first, second = (("s0",), ("br", "s1"), ("grp", "s2")), (("s0",), ("grp", "s2"), ("br", "s1"))
    up_own = scatter_sum(up_part.reshape(devices, -1, width), first)
    down_own = scatter_sum(down_part.reshape(devices, -1, hidden), second)
    misc_own = scatter_sum(misc, first)
    unit = width // devices
    small_own = misc_own[unit]
    small_own = [small_own[None, ends[i] : ends[i + 1]] for i in range(len(vectors))]

    dx, dh = backward_call(plan, meta, slide_lengths, head_offsets, x, halo, state, do)
    back = to_neighbours([dh[1], dh[0]], groups)
    counts = plan.halo // (br * tq)
    dx_parts = dx.reshape(br, members, 3 * size, tq)
    adds = jnp.zeros((br, members, 2 * size, tq), F32)
    for side, (piece, table) in enumerate(zip([back[1], back[0]], tables)):
        spread = lax.dot_general(piece, table, (((1,), (1,)), ((), ())), preferred_element_type=F32)
        spread = spread.reshape(2 * size, counts, br, tq).transpose(2, 1, 0, 3)
        pads = (members - counts, 0) if side == 0 else (0, members - counts)
        adds = adds + jnp.pad(spread, ((0, 0), pads, (0, 0), (0, 0)))
    adds = jnp.pad(adds, ((0, 0), (0, 0), (size, 0), (0, 0)))
    dx = (dx_parts.astype(F32) + adds).astype(BF).reshape(heads, 3 * size, tq)
    joined_grad_t = swap(dx, GROUP).reshape(heads, 3, size, tq).transpose(1, 0, 2, 3).reshape(3 * width, tq)
    weight_t = jnp.einsum(
        "nct,ntd->cd", dx, normed_all.reshape(heads, tq, width), preferred_element_type=F32
    ).reshape(3, size, width)
    head_sums = jnp.sum(dx.astype(F32), (0, 2)).reshape(3, size)
    qkv_own, query_own, value_own = share_columns(weight_t, head_sums, width)
    normed_grad = lax.dot_general(joined_grad_t, qkv_weight, (((0,), (1,)), ((), ())), preferred_element_type=F32)
    tile_part, pre_gain_sum, pre_shift_sum = norm_back(normed_grad, normed_pre, inverse_pre, pre_gain)
    tile_grad = (residual_grad + tile_part).astype(BF)[None]
    last = jnp.stack([pre_gain_sum, pre_shift_sum]).reshape(2, devices, unit).transpose(1, 0, 2)
    last = jnp.pad(last, ((0, 0), (0, 6), (0, LANES - unit)))
    last = jnp.sum(swap(last, ALL).reshape(devices, 8, LANES), 0)
    return (
        layer_out,
        tile_grad,
        last[0:1, :unit],
        last[1:2, :unit],
        qkv_own.T,
        query_own[None],
        value_own[None],
        misc_own[:unit].T,
        small_own[2],
        small_own[3],
        small_own[4],
        up_own.T,
        small_own[0],
        down_own.T,
        small_own[1],
    )


def solution(mesh):
    br, rows = mesh.shape["br"], mesh.shape["rows"]

    def run(*args):
        members = args[2].shape[1] // br
        shape = (br, rows // members, members // 4, 2, 2)
        split = jax.sharding.Mesh(mesh.devices.reshape(shape), ALL)
        tokens = P(("grp", "s2", "s1", "s0"), "br", None)
        owned = P(None, ALL)
        return jax.shard_map(
            body,
            mesh=split,
            in_specs=(tokens,) + (P(),) * 15 + (tokens,),
            out_specs=(tokens, tokens) + (owned,) * 13,
            check_vma=False,
        )(*args)

    return run
```

```python
import functools
import math

import jax
import jax.numpy as jnp
from jax import lax
from jax.experimental import pallas as pl
from jax.experimental.pallas import tpu as pltpu
from jax.sharding import PartitionSpec as P

SEG_BASE = 1024
DOC_MOST = 2048
LANES = 128
BF = jnp.bfloat16
F32 = jnp.float32
NEG = -1e30
EPS = 1e-05
ALL = ("br", "grp", "s2", "s1", "s0")
GROUP = ("br", "s2", "s1", "s0")
ONE_LANE = 48
ID_Q = 51
ID_K = 52


class Plan:
    def __init__(self, heads, head_size, branches, groups, members, tq, total):
        self.heads, self.size, self.groups, self.members, self.tq = heads, head_size, groups, members, tq
        self.blocks = groups * members
        self.tokens = self.blocks * tq
        self.total = total
        self.halo = min(DOC_MOST, self.tokens)
        self.factor = math.log2(math.e) * head_size**-0.5
        self.branches = []
        keys, sel = 0, 0
        for level in range(branches):
            rate = 2**level
            span = min(SEG_BASE * rate, total)
            near = span <= self.tokens
            extra = 0 if near else self.halo // rate
            segs = self.tokens // span if near else 1
            seg_q = self.tokens // rate // segs
            seg_k = seg_q + 2 * extra
            self.branches.append(
                dict(
                    level=level, rate=rate, span=span, near=near, extra=extra, segs=segs,
                    seg_q=seg_q, seg_k=seg_k, tile=min(256, seg_q), first=keys, sel=sel,
                )
            )
            keys += segs * seg_k
            sel += extra
        self.keys = keys
        self.sel = sel
        self.widest = max(b["seg_k"] for b in self.branches)

    def slot(self, block):
        return lax.rem(block, self.groups) * self.members + lax.div(block, self.groups)


def dot_nt(a, b):
    return lax.dot_general(a, b, (((1,), (1,)), ((), ())), preferred_element_type=F32)


def dot_tn(a, b):
    return lax.dot_general(a, b, (((0,), (0,)), ((), ())), preferred_element_type=F32)


def dot_nn(a, b):
    return lax.dot_general(a, b, (((1,), (0,)), ((), ())), preferred_element_type=F32)


def iota(shape, dim):
    return lax.broadcasted_iota(jnp.int32, shape, dim)


def placement(size, parts):
    shape = (parts * size + 16, parts * LANES)
    row, col = iota(shape, 0), iota(shape, 1)
    hit = col < 0
    for part in range(parts):
        hit |= (row >= part * size) & (row < (part + 1) * size) & (col == row - part * size + part * LANES)
    return row, col, hit


def ids_of(pos, starts, gate=None):
    found = jnp.zeros(pos.shape, jnp.int32)
    for start in starts:
        found += jnp.where(pos >= start, 1, 0)
    if gate is not None:
        found = jnp.where(gate, found, -1)
    return found.astype(F32)


def slide_starts(lens_ref):
    starts, at = [], jnp.int32(0)
    for i in range(lens_ref.shape[0]):
        starts.append(at)
        at = at + lens_ref[i]
    return starts


def branch_pos(plan, branch, base, off, first, count):
    start = base - branch["extra"] * branch["rate"] + off
    pos = start + branch["rate"] * (first + iota((1, count), 1))
    if branch["near"]:
        return pos, None
    shift = int(math.log2(branch["span"]))
    return pos, lax.shift_right_arithmetic(pos, shift) == lax.shift_right_arithmetic(base, shift)


def to_rows(plan, base, starts, x_ref, q_tm, k_tm, v_tm, extra_q=None):
    size, tq = plan.size, plan.tq
    row, col, hit = placement(size, 3)
    hit |= (row == 3 * size) & ((col == ID_Q) | (col == LANES + ID_K))
    place = jnp.where(hit, 1.0, 0.0).astype(BF)
    lane = iota((1, 3 * LANES), 1)
    in_k, in_v = lane - LANES, lane - 2 * LANES
    ones = jnp.where(
        ((in_k >= ONE_LANE) & (in_k < ONE_LANE + 3)) | ((in_v >= ONE_LANE) & (in_v < ONE_LANE + 3)), 1.0, 0.0
    )

    def block(n, carry):
        pos = base + n * tq + iota((1, tq), 1)
        ids = jnp.where(iota((16, tq), 0) == 0, ids_of(pos, starts), 0.0).astype(BF)
        full = jnp.concatenate([x_ref[plan.slot(n)], ids], 0)
        rows = dot_tn(full, place) + ones
        at = pl.ds(pl.multiple_of(n * tq, tq), tq)
        queries = rows[:, :LANES]
        if extra_q is not None:
            queries = queries + extra_q(n, at)
        q_tm[at, :] = queries
        k_tm[at, :] = rows[:, LANES : 2 * LANES]
        v_tm[at, :] = rows[:, 2 * LANES :]
        return carry

    lax.fori_loop(0, plan.blocks, block, 0)


def gather_keys(plan, base, offs, starts, halo_ref, k_tm, v_tm, kall, vall):
    size = plan.size
    if plan.sel:
        row, col, hit = placement(size, 2)
        hit |= (row == 2 * size) & (col == ID_K)
        place = jnp.where(hit, 1.0, 0.0).astype(BF)
        lane = iota((1, 2 * LANES), 1)
        in_v = lane - LANES
        ones = jnp.where(
            ((lane >= ONE_LANE) & (lane < ONE_LANE + 3)) | ((in_v >= ONE_LANE) & (in_v < ONE_LANE + 3)), 1.0, 0.0
        )
    for branch in plan.branches:
        rate, first, extra, off = branch["rate"], branch["first"], branch["extra"], offs[branch["level"]]
        count = plan.tokens // rate
        step = min(256, count)

        def chunk(i, carry, rate=rate, first=first, extra=extra, off=off, step=step):
            rows = pl.ds(off + i * step * rate, step, stride=rate) if rate > 1 else pl.ds(i * step, step)
            to = pl.ds(pl.multiple_of(first + extra + i * step, step), step)
            kall[to, :] = k_tm[rows, :].astype(BF)
            vall[to, :] = v_tm[rows, :].astype(BF)
            return carry

        lax.fori_loop(0, count // step, chunk, 0)
        if extra:
            for side in range(2):
                begin = side * (extra + count)
                pos, gate = branch_pos(plan, branch, base, off, begin, extra)
                ids = jnp.where(iota((16, extra), 0) == 0, ids_of(pos, starts, gate), 0.0).astype(BF)
                piece = halo_ref[side, :, branch["sel"] : branch["sel"] + extra]
                rows = dot_tn(jnp.concatenate([piece, ids], 0), place) + ones
                kall[first + begin : first + begin + extra, :] = rows[:, :LANES].astype(BF)
                vall[first + begin : first + begin + extra, :] = rows[:, LANES:].astype(BF)


def picked(branch, off, i):
    tile, rate = branch["tile"], branch["rate"]
    if rate == 1:
        return pl.ds(pl.multiple_of(i * tile, tile), tile)
    return pl.ds(off + i * tile * rate, tile, stride=rate)


def forward_kernel(plan, meta, lens, offsets, x_ref, halo_ref, o_ref, st_ref, q_tm, k_tm, v_tm, kall, vall, kid):
    base, head = meta[0], meta[1]
    starts = slide_starts(lens)
    offs = [offsets[b["level"], head] for b in plan.branches]
    to_rows(plan, base, starts, x_ref, q_tm, k_tm, v_tm)
    gather_keys(plan, base, offs, starts, halo_ref, k_tm, v_tm, kall, vall)
    factor = plan.factor
    for branch in plan.branches:
        off, first, wide, tile = offs[branch["level"]], branch["first"], branch["seg_k"], branch["tile"]
        total = branch["segs"] * wide
        pos, gate = branch_pos(plan, branch, base, off, 0, total)
        kid[:, first : first + total] = ids_of(pos, starts, gate)
        per = branch["seg_q"] // tile

        def attend(i, carry, branch=branch, off=off, first=first, wide=wide, tile=tile, per=per):
            rows = picked(branch, off, i)
            queries = q_tm[rows, :]
            at = pl.ds(pl.multiple_of(first + lax.div(i, per) * wide, 128), wide)
            scores = dot_nt(queries.astype(BF), kall[at, :])
            scores = jnp.where(queries[:, ID_Q : ID_Q + 1] == kid[:, at], scores, NEG)
            top = jnp.max(scores, 1, keepdims=True)
            weights = jnp.exp2((scores - top) * factor)
            mixed = dot_nn(weights.astype(BF), vall[at, :])
            lane = iota((tile, LANES), 1)
            if branch["level"]:
                old = st_ref[rows, :]
                old_top = old[:, ID_Q : ID_Q + 1]
                new_top = jnp.maximum(old_top, top)
                mixed = old * jnp.exp2((old_top - new_top) * factor) + mixed * jnp.exp2((top - new_top) * factor)
                top = new_top
            st_ref[rows, :] = jnp.where(lane == ID_Q, top, mixed)
            return carry

        lax.fori_loop(0, branch["segs"] * per, attend, 0)
    eye = jnp.where(iota((plan.size, LANES), 0) == iota((plan.size, LANES), 1), 1.0, 0.0).astype(BF)

    def finish(n, carry):
        at = pl.ds(pl.multiple_of(n * plan.tq, plan.tq), plan.tq)
        state = st_ref[at, :]
        weight = state[:, ONE_LANE : ONE_LANE + 1]
        top = state[:, ID_Q : ID_Q + 1]
        attn = state * (1.0 / weight)
        merged = top + jnp.log2(weight) * (1.0 / factor)
        lane = iota((plan.tq, LANES), 1)
        st_ref[at, :] = jnp.where(lane < plan.size, attn, jnp.where(lane == ONE_LANE, merged, 0.0))
        o_ref[plan.slot(n)] = dot_nt(eye, attn.astype(BF)).astype(BF)
        return carry

    lax.fori_loop(0, plan.blocks, finish, 0)


def split3(column, lane):
    high = column.astype(BF).astype(F32)
    rest = column - high
    mid = rest.astype(BF).astype(F32)
    low = rest - mid
    return jnp.where(
        lane == ONE_LANE, high, jnp.where(lane == ONE_LANE + 1, mid, jnp.where(lane == ONE_LANE + 2, low, 0.0))
    )


def backward_kernel(
    plan, meta, lens, offsets, x_ref, halo_ref, st_ref, do_ref, dx_ref, dh_ref,
    q_tm, k_tm, v_tm, do_tm, dq_tm, dk_tm, dv_tm, kall, vall, k_fm, qid, dk_acc, dv_acc,
):
    base, head = meta[0], meta[1]
    starts = slide_starts(lens)
    offs = [offsets[b["level"], head] for b in plan.branches]
    size, tq, factor = plan.size, plan.tq, plan.factor
    row, col, hit = placement(size, 1)
    place = jnp.where(hit, 1.0, 0.0).astype(BF)
    lane = iota((tq, LANES), 1)

    def extra_q(n, at):
        state = st_ref[at, :]
        grads = dot_tn(jnp.concatenate([do_ref[plan.slot(n)], jnp.zeros((16, tq), BF)], 0), place)
        dots = jnp.sum(jnp.where(lane < size, grads * state, 0.0), 1, keepdims=True)
        do_tm[at, :] = grads + split3(-dots, lane)
        return split3(-state[:, ONE_LANE : ONE_LANE + 1], lane)

    to_rows(plan, base, starts, x_ref, q_tm, k_tm, v_tm, extra_q)
    gather_keys(plan, base, offs, starts, halo_ref, k_tm, v_tm, kall, vall)
    eye = jnp.where(iota((LANES, LANES), 0) == iota((LANES, LANES), 1), 1.0, 0.0).astype(BF)
    eye_small = eye[:size]
    for branch in plan.branches:
        off, first, wide, tile = offs[branch["level"]], branch["first"], branch["seg_k"], branch["tile"]
        count = branch["segs"] * branch["seg_q"]
        per = branch["seg_q"] // tile
        extra, rate = branch["extra"], branch["rate"]
        pos, _ = branch_pos(plan, branch, base, off, extra, count)
        qid[:, :count] = ids_of(pos, starts)

        def segment(seg, carry, branch=branch, off=off, first=first, wide=wide, tile=tile, per=per):
            at = pl.ds(pl.multiple_of(first + seg * wide, 128), wide)
            k_fm[:, :wide] = dot_nt(eye, kall[at, :]).astype(BF)
            dk_acc[:wide, :] = jnp.zeros((wide, LANES), F32)
            dv_acc[:wide, :] = jnp.zeros((wide, LANES), F32)

            def one(j, carry):
                i = seg * per + j
                rows = picked(branch, off, i)
                queries = q_tm[rows, :].astype(BF)
                grads = do_tm[rows, :].astype(BF)
                keys = kall[at, :]
                linked = keys[:, ID_K : ID_K + 1].astype(F32) == qid[:, pl.ds(pl.multiple_of(i * tile, tile), tile)]
                probs = jnp.where(linked, jnp.exp2(dot_nt(keys, queries) * factor), 0.0)
                dv_acc[:wide, :] += dot_nn(probs.astype(BF), grads)
                moved = (probs * dot_nt(vall[at, :], grads)).astype(BF)
                dk_acc[:wide, :] += dot_nn(moved, queries)
                dq = dot_nn(k_fm[:, :wide], moved).T
                if branch["level"]:
                    dq = dq_tm[rows, :] + dq
                dq_tm[rows, :] = dq
                return carry

            lax.fori_loop(0, per, one, 0)
            step = min(256, branch["seg_q"])
            for c in range(branch["seg_q"] // step):
                begin = branch["extra"] + c * step
                if branch["rate"] == 1:
                    to = pl.ds(pl.multiple_of(seg * branch["seg_q"] + c * step, step), step)
                    dk_tm[to, :] = dk_acc[begin : begin + step, :]
                    dv_tm[to, :] = dv_acc[begin : begin + step, :]
                else:
                    to = pl.ds(off + (seg * branch["seg_q"] + c * step) * branch["rate"], step, stride=branch["rate"])
                    dk_tm[to, :] += dk_acc[begin : begin + step, :]
                    dv_tm[to, :] += dv_acc[begin : begin + step, :]
            return carry

        lax.fori_loop(0, branch["segs"], segment, 0)
        if extra:
            for side in range(2):
                begin = side * (extra + count)
                to = slice(branch["sel"], branch["sel"] + extra)
                dk = (dk_acc[begin : begin + extra, :] * size**-0.5).astype(BF)
                dh_ref[side, :size, to] = dot_nt(eye_small, dk).astype(BF)
                dh_ref[side, size:, to] = dot_nt(eye_small, dv_acc[begin : begin + extra, :].astype(BF)).astype(BF)

    def finish(n, carry):
        at = pl.ds(pl.multiple_of(n * tq, tq), tq)
        slot = plan.slot(n)
        dx_ref[slot, :size, :] = dot_nt(eye_small, (dq_tm[at, :] * size**-0.5).astype(BF)).astype(BF)
        dx_ref[slot, size : 2 * size, :] = dot_nt(eye_small, (dk_tm[at, :] * size**-0.5).astype(BF)).astype(BF)
        dx_ref[slot, 2 * size :, :] = dot_nt(eye_small, dv_tm[at, :].astype(BF)).astype(BF)
        return carry

    lax.fori_loop(0, plan.blocks, finish, 0)


SMEM = pl.BlockSpec(memory_space=pltpu.SMEM)
VMEM = pl.BlockSpec(memory_space=pltpu.VMEM)


def forward_call(plan, meta, lens, offsets, x, halo):
    rows = pltpu.VMEM((plan.tokens, LANES), F32)
    keys = pltpu.VMEM((plan.keys, LANES), BF)
    return pl.pallas_call(
        functools.partial(forward_kernel, plan),
        out_shape=(
            jax.ShapeDtypeStruct((plan.blocks, plan.size, plan.tq), BF),
            jax.ShapeDtypeStruct((plan.tokens, LANES), F32),
        ),
        in_specs=[SMEM] * 3 + [VMEM] * 2,
        out_specs=(VMEM, VMEM),
        scratch_shapes=[rows, rows, rows, keys, keys, pltpu.VMEM((1, plan.keys), F32)],
        compiler_params=pltpu.CompilerParams(vmem_limit_bytes=48 << 20),
        cost_estimate=pl.CostEstimate(flops=30_000_000_000, bytes_accessed=4 << 20, transcendentals=0),
        name="attend",
    )(meta, lens, offsets, x, halo)


def backward_call(plan, meta, lens, offsets, x, halo, state, do):
    rows = pltpu.VMEM((plan.tokens, LANES), F32)
    keys = pltpu.VMEM((plan.keys, LANES), BF)
    acc = pltpu.VMEM((plan.widest, LANES), F32)
    return pl.pallas_call(
        functools.partial(backward_kernel, plan),
        out_shape=(
            jax.ShapeDtypeStruct((plan.blocks, 3 * plan.size, plan.tq), BF),
            jax.ShapeDtypeStruct((2, 2 * plan.size, max(plan.sel, 128)), BF),
        ),
        in_specs=[SMEM] * 3 + [VMEM] * 4,
        out_specs=(VMEM, VMEM),
        scratch_shapes=[rows] * 7
        + [keys, keys, pltpu.VMEM((LANES, plan.widest), BF), pltpu.VMEM((1, plan.tokens), F32), acc, acc],
        compiler_params=pltpu.CompilerParams(vmem_limit_bytes=56 << 20),
        cost_estimate=pl.CostEstimate(flops=45_000_000_000, bytes_accessed=4 << 20, transcendentals=0),
        name="attend_back",
    )(meta, lens, offsets, x, halo, state, do)


def near_rows(values, norm_gain, norm_shift):
    centred = values - jnp.mean(values, 1, keepdims=True)
    inverse = lax.rsqrt(jnp.mean(centred * centred, 1, keepdims=True) + EPS)
    normed = centred * inverse
    return normed * norm_gain + norm_shift, normed, inverse


def back_rows(grad_out, normed, inverse, norm_gain):
    grad_norm = grad_out * norm_gain
    return inverse * (
        grad_norm
        - jnp.mean(grad_norm, 1, keepdims=True)
        - normed * jnp.mean(grad_norm * normed, 1, keepdims=True)
    )


def own_columns(size, unit, core):
    row, col = iota((size, size), 0), iota((size, size), 1)
    half = size // 2
    other = row >= half
    place = jnp.where(other, row - half, row)
    whole = jnp.floor((place.astype(F32) + 0.5) * (1.0 / unit)).astype(jnp.int32)
    parity = jnp.where(other, 1 - core, core)
    return jnp.where(col == place + unit * (whole + parity), 1.0, 0.0).astype(BF)


def middle_kernel(
    unit_up, unit, core_ref, attn_ref, tiles_ref, out_w, out_b, gain, shift, up_w, up_b, down_w, down_b, g_ref,
    y_ref, res_ref, ag_ref, common_ref, mine_ref, theirs_ref, sums_ref, up_sum_ref,
    pick_up, normed_s, lifted_s, inverse_s, out_s, back_s,
):
    step, steps = pl.program_id(0), pl.num_programs(0)
    width = tiles_ref.shape[1]
    chunk = up_w.shape[1]
    half = chunk // 2
    core = core_ref[0]
    hidden_sel = steps * half

    @pl.when(step == 0)
    def _():
        pick_up[...] = own_columns(chunk, unit_up, core)
        residual = tiles_ref[...].astype(F32) + dot_tn(attn_ref[...], out_w[...]) + out_b[...]
        lifted, normed, inverse = near_rows(residual, gain[...], shift[...])
        low = lifted.astype(BF)
        lifted_s[...] = low
        normed_s[...] = normed
        inverse_s[...] = jnp.broadcast_to(inverse, inverse_s.shape)
        out_s[...] = residual + down_b[...]
        back_s[...] = jnp.zeros_like(back_s)
        common_ref[pl.ds(steps * chunk, width), :] = low.T
        pick = own_columns(width, unit, core)
        picked_g = dot_nt(pick, g_ref[...]).astype(BF)
        mine_ref[pl.ds(hidden_sel, width // 2), :] = picked_g[: width // 2]
        theirs_ref[pl.ds(hidden_sel, width // 2), :] = picked_g[width // 2 :]

    lifted = lifted_s[...]
    gate_in = dot_nn(lifted, up_w[...]) + up_b[...]
    cdf = 0.5 + 0.5 * lax.erf(gate_in * (0.5**0.5))
    act = (gate_in * cdf).astype(BF)
    slope = cdf + gate_in * (jnp.exp(-0.5 * gate_in * gate_in) * (1.0 / math.sqrt(2.0 * math.pi)))
    gate_grad = (dot_nt(g_ref[...], down_w[...]) * slope).astype(BF)
    out_s[...] += dot_nn(act, down_w[...])
    back_s[...] += dot_nt(gate_grad, up_w[...])
    up_sum_ref[...] = jnp.sum(gate_grad.astype(F32), 0, keepdims=True)
    common_ref[pl.ds(pl.multiple_of(step * chunk, chunk), chunk), :] = act.T
    picked_gate = dot_nt(pick_up[...], gate_grad).astype(BF)
    at = pl.ds(pl.multiple_of(step * half, half), half)
    mine_ref[at, :] = picked_gate[:half]
    theirs_ref[at, :] = picked_gate[half:]

    @pl.when(step == steps - 1)
    def _():
        y_ref[...] = out_s[...].astype(BF)
        grads = g_ref[...].astype(F32)
        lifted_grad = back_s[...]
        normed = normed_s[...]
        residual_grad = grads + back_rows(lifted_grad, normed, inverse_s[:, :1], gain[...])
        res_ref[...] = residual_grad
        low = residual_grad.astype(BF)
        ag_ref[...] = dot_nt(out_w[...], low).astype(BF)
        pick = own_columns(width, unit, core)
        picked_p = dot_nt(pick, low).astype(BF)
        at = pl.ds(hidden_sel + width // 2, width // 2)
        mine_ref[at, :] = picked_p[: width // 2]
        theirs_ref[at, :] = picked_p[width // 2 :]
        sums_ref[0:1, :] = jnp.sum(grads, 0, keepdims=True)
        sums_ref[1:2, :] = jnp.sum(residual_grad, 0, keepdims=True)
        sums_ref[2:3, :] = jnp.sum(lifted_grad * normed, 0, keepdims=True)
        sums_ref[3:4, :] = jnp.sum(lifted_grad, 0, keepdims=True)
        sums_ref[4:8, :] = jnp.zeros((4, width), F32)


def middle_call(devices, core, attn_t, tiles, out_w, out_b, gain, shift, up_w, up_b, down_w, down_b, g):
    tq, width = tiles.shape
    hidden = up_w.shape[1]
    steps = hidden // width
    whole = lambda *shape: pl.BlockSpec(shape, lambda j: (0,) * len(shape))
    vec = whole(1, width)
    sel = hidden // 2 + width
    return pl.pallas_call(
        functools.partial(middle_kernel, hidden // devices, width // devices),
        grid=(steps,),
        in_specs=[
            SMEM, whole(width, tq), whole(tq, width), whole(width, width), vec, vec, vec,
            pl.BlockSpec((width, width), lambda j: (0, j)), pl.BlockSpec((1, width), lambda j: (0, j)),
            pl.BlockSpec((width, width), lambda j: (j, 0)), vec, whole(tq, width),
        ],
        out_specs=(
            whole(tq, width), whole(tq, width), whole(width, tq), whole(hidden + width, tq), whole(sel, tq),
            whole(sel, tq), whole(8, width), pl.BlockSpec((1, width), lambda j: (0, j)),
        ),
        out_shape=(
            jax.ShapeDtypeStruct((tq, width), BF),
            jax.ShapeDtypeStruct((tq, width), F32),
            jax.ShapeDtypeStruct((width, tq), BF),
            jax.ShapeDtypeStruct((hidden + width, tq), BF),
            jax.ShapeDtypeStruct((sel, tq), BF),
            jax.ShapeDtypeStruct((sel, tq), BF),
            jax.ShapeDtypeStruct((8, width), F32),
            jax.ShapeDtypeStruct((1, hidden), F32),
        ),
        scratch_shapes=[
            pltpu.VMEM((width, width), BF), pltpu.VMEM((tq, width), F32), pltpu.VMEM((tq, width), BF),
            pltpu.VMEM((tq, LANES), F32), pltpu.VMEM((tq, width), F32), pltpu.VMEM((tq, width), F32),
        ],
        compiler_params=pltpu.CompilerParams(vmem_limit_bytes=48 << 20),
        cost_estimate=pl.CostEstimate(flops=14 * tq * width * hidden, bytes_accessed=20 << 20, transcendentals=0),
        name="middle",
    )(core, attn_t, tiles, out_w, out_b, gain, shift, up_w, up_b, down_w, down_b, g)


def weights_kernel(unit_up, unit, meta, attn_a, attn_b, common_a, common_b, sel_a, sel_b, first_ref, *rest):
    second_refs, held = rest[:4], rest[4]
    width = attn_a.shape[0]
    hidden = common_a.shape[0] - width
    chips = width // (2 * unit)

    def spot(chip):
        return (chip // 8) * 2 + chip % 2, chip // 2 % 4

    lifted = slice(hidden, hidden + width)
    group = width // (2 * unit_up)
    for step in range(hidden // width):
        rows = slice(step * width // 2, (step + 1) * width // 2)
        part = dot_nt(sel_a[rows, :], common_a[lifted, :]) + dot_nt(sel_b[rows, :], common_b[lifted, :])
        for i in range(group):
            plane, line = spot(step * group + i)
            first_ref[plane, line, :unit_up, :] = part[i * unit_up : (i + 1) * unit_up].astype(BF)
    rows_out = slice(hidden // 2 + width // 2, hidden // 2 + width)
    rows = slice(hidden // 2, hidden // 2 + width // 2)
    out = dot_nt(sel_a[rows_out, :], attn_a[...]) + dot_nt(sel_b[rows_out, :], attn_b[...])
    for step in range(hidden // width):
        cols = slice(step * width, (step + 1) * width)
        part = dot_nt(sel_a[rows, :], common_a[cols, :]) + dot_nt(sel_b[rows, :], common_b[cols, :])
        for chip in range(chips):
            plane, line = spot(chip)
            at = slice(chip * unit, (chip + 1) * unit)
            if step == 0:
                both = jnp.concatenate([out[at], part[at]], 0)
                first_ref[plane, line, unit_up:, :] = both.astype(BF)
            else:
                held[line, plane, :, (step - 1) * width : step * width] = part[at].astype(BF)
    line = meta[5]
    for k, ref in enumerate(second_refs):
        ref[...] = held[line ^ k]


def weights_call(devices, meta, attn_a, attn_b, common_a, common_b, sel_a, sel_b):
    width, tq = attn_a.shape
    hidden = common_a.shape[0] - width
    unit_up, unit = hidden // devices, width // devices
    piece = (4, unit, hidden - width)
    return pl.pallas_call(
        functools.partial(weights_kernel, unit_up, unit),
        in_specs=[SMEM] + [VMEM] * 6,
        out_specs=(VMEM,) * 5,
        out_shape=(jax.ShapeDtypeStruct((4, 4, unit_up + 2 * unit, width), BF),)
        + (jax.ShapeDtypeStruct(piece, BF),) * 4,
        scratch_shapes=[pltpu.VMEM((4,) + piece, BF)],
        compiler_params=pltpu.CompilerParams(vmem_limit_bytes=48 << 20),
        cost_estimate=pl.CostEstimate(flops=4 * tq * width * hidden, bytes_accessed=14 << 20, transcendentals=0),
        name="weights",
    )(meta, attn_a, attn_b, common_a, common_b, sel_a, sel_b)


def fold_kernel(meta, first_ref, own, got1, got2, got3, *outs):
    plane, line = meta[4], meta[5]
    for k in range(4):
        at = line ^ k
        total = first_ref[0, at].astype(F32)
        for i in range(1, 4):
            total += first_ref[i, at].astype(F32)
        outs[k][...] = total.astype(BF)
        at = plane ^ k
        total = own[at].astype(F32) + got1[at].astype(F32) + got2[at].astype(F32) + got3[at].astype(F32)
        outs[4 + k][...] = total.astype(BF)


def fold_call(meta, first, second):
    shapes = [jax.ShapeDtypeStruct(first.shape[2:], BF)] * 4 + [jax.ShapeDtypeStruct(second[0].shape[1:], BF)] * 4
    return pl.pallas_call(
        fold_kernel,
        in_specs=[SMEM] + [VMEM] * 5,
        out_specs=(VMEM,) * 8,
        out_shape=tuple(shapes),
        compiler_params=pltpu.CompilerParams(vmem_limit_bytes=48 << 20),
        name="fold",
    )(meta, first, *second)


def last_kernel(unit_up, unit, *refs):
    first, second, (up_ref, out_ref, down_ref) = refs[:4], refs[4:8], refs[8:]
    total = first[0][...].astype(F32)
    for ref in first[1:]:
        total += ref[...].astype(F32)
    up_ref[...] = total[:unit_up]
    out_ref[...] = total[unit_up : unit_up + unit]
    width = total.shape[1]
    down_ref[:, :width] = total[unit_up + unit :]
    total = second[0][...].astype(F32)
    for ref in second[1:]:
        total += ref[...].astype(F32)
    down_ref[:, width:] = total


def last_call(unit_up, unit, first, second):
    width = first[0].shape[1]
    hidden = width + second[0].shape[1]
    return pl.pallas_call(
        functools.partial(last_kernel, unit_up, unit),
        in_specs=[VMEM] * 8,
        out_specs=(VMEM,) * 3,
        out_shape=tuple(jax.ShapeDtypeStruct(s, F32) for s in ((unit_up, width), (unit, width), (unit, hidden))),
        compiler_params=pltpu.CompilerParams(vmem_limit_bytes=32 << 20),
        name="last",
    )(*first, *second)


def enter_kernel(tiles_ref, gain, shift, w_ref, query_b, value_b, x_ref, npre_ref, low_s):
    part = pl.program_id(0)

    @pl.when((part == 0) & (pl.program_id(1) == 0))
    def _():
        scaled, normed, _ = near_rows(tiles_ref[...].astype(F32), gain[...], shift[...])
        low_s[...] = scaled.astype(BF)
        npre_ref[...] = normed.astype(BF)

    bias = jnp.where(part == 0, query_b[...], jnp.where(part == 2, value_b[...], 0.0))
    joined = (dot_nn(low_s[...], w_ref[...]) + bias).astype(BF).T
    size = x_ref.shape[2]
    for i in range(x_ref.shape[0]):
        x_ref[i, 0] = joined[i * size : (i + 1) * size]


def enter_call(heads, tiles, gain, shift, weight, query_b, value_b):
    tq, width = tiles.shape
    size = width // heads
    half = width // 2
    whole = lambda *shape: pl.BlockSpec(shape, lambda i, j: (0,) * len(shape))
    vec = whole(1, width)
    bias = pl.BlockSpec((1, half), lambda i, j: (0, j))
    return pl.pallas_call(
        enter_kernel,
        grid=(3, 2),
        in_specs=[whole(tq, width), vec, vec, pl.BlockSpec((width, half), lambda i, j: (0, i * 2 + j)), bias, bias],
        out_specs=(pl.BlockSpec((heads // 2, 1, size, tq), lambda i, j: (j, i, 0, 0)), whole(tq, width)),
        out_shape=(jax.ShapeDtypeStruct((heads, 3, size, tq), BF), jax.ShapeDtypeStruct((tq, width), BF)),
        scratch_shapes=[pltpu.VMEM((tq, width), BF)],
        compiler_params=pltpu.CompilerParams(vmem_limit_bytes=32 << 20),
        name="enter",
    )(tiles, gain, shift, weight, query_b, value_b)


def leave_kernel(tiles_ref, gain, w_ref, jg_ref, res_ref, out_ref, acc):
    first = (pl.program_id(0) == 0) & (pl.program_id(1) == 0)

    @pl.when(first)
    def _():
        acc[...] = jnp.zeros_like(acc)

    heads, size = jg_ref.shape[0], jg_ref.shape[2]
    grads = jnp.concatenate([jg_ref[i, 0] for i in range(heads)], 0)
    acc[...] += dot_nt(grads.T, w_ref[...])

    @pl.when((pl.program_id(0) == 2) & (pl.program_id(1) == 1))
    def _():
        _, normed, inverse = near_rows(tiles_ref[...].astype(F32), gain[...], gain[...])
        out_ref[...] = (res_ref[...] + back_rows(acc[...], normed, inverse, gain[...])).astype(BF)


def leave_call(tiles, gain, weight, joined_grad, residual_grad):
    tq, width = tiles.shape
    heads, _, size, _ = joined_grad.shape
    half = width // 2
    whole = lambda *shape: pl.BlockSpec(shape, lambda i, j: (0,) * len(shape))
    return pl.pallas_call(
        leave_kernel,
        grid=(3, 2),
        in_specs=[
            whole(tq, width), whole(1, width), pl.BlockSpec((width, half), lambda i, j: (0, i * 2 + j)),
            pl.BlockSpec((heads // 2, 1, size, tq), lambda i, j: (j, i, 0, 0)), whole(tq, width),
        ],
        out_specs=whole(tq, width),
        out_shape=jax.ShapeDtypeStruct((tq, width), BF),
        scratch_shapes=[pltpu.VMEM((tq, width), F32)],
        compiler_params=pltpu.CompilerParams(vmem_limit_bytes=32 << 20),
        name="leave",
    )(tiles, gain, weight, joined_grad, residual_grad)


def halo_hits(plan, offs, first, dims):
    wide = max(plan.sel, LANES)
    shape = (plan.tq, wide)
    token, col = iota(shape, 0) + first, iota(shape, 1)
    hit = col < 0
    for branch in plan.branches:
        if branch["extra"]:
            at = col - branch["sel"]
            inside = (at >= 0) & (at < branch["extra"])
            hit |= inside & (token == at * branch["rate"] + offs[branch["level"]])
    return jnp.where(hit, 1.0, 0.0).astype(BF)


def halo_blocks(plan):
    count = plan.halo // plan.tq
    for i in range(count):
        yield 0, plan.blocks - count + i, i * plan.tq
        yield 1, i, i * plan.tq


def static_slot(plan, block):
    return block % plan.groups * plan.members + block // plan.groups


def select_kernel(plan, meta, offsets, x_ref, last_ref, first_ref):
    offs = [offsets[b["level"], meta[1]] for b in plan.branches]
    total = [jnp.zeros((2 * plan.size, max(plan.sel, LANES)), F32) for _ in range(2)]
    for side, block, first in halo_blocks(plan):
        hits = halo_hits(plan, offs, first, None)
        total[side] += dot_nn(x_ref[static_slot(plan, block), plan.size :, :], hits)
    last_ref[...] = total[0].astype(BF)
    first_ref[...] = total[1].astype(BF)


def select_call(plan, meta, offsets, x):
    shape = jax.ShapeDtypeStruct((2 * plan.size, max(plan.sel, LANES)), BF)
    return pl.pallas_call(
        functools.partial(select_kernel, plan),
        in_specs=[SMEM, SMEM, VMEM],
        out_specs=(VMEM, VMEM),
        out_shape=(shape, shape),
        compiler_params=pltpu.CompilerParams(vmem_limit_bytes=32 << 20),
        name="select",
    )(meta, offsets, x)


def spread_kernel(plan, meta, offsets, dx_ref, last_ref, first_ref, out_ref):
    offs = [offsets[b["level"], meta[1]] for b in plan.branches]
    adds = {}
    for side, block, first in halo_blocks(plan):
        adds.setdefault(block, []).append(((last_ref, first_ref)[side], first))
    for block in range(plan.blocks):
        slot = static_slot(plan, block)
        out_ref[slot, : plan.size, :] = dx_ref[slot, : plan.size, :]
        total = dx_ref[slot, plan.size :, :].astype(F32)
        for ref, first in adds.get(block, ()):
            total += dot_nt(ref[...], halo_hits(plan, offs, first, None))
        out_ref[slot, plan.size :, :] = total.astype(BF)


def spread_call(plan, meta, offsets, dx, last, first):
    return pl.pallas_call(
        functools.partial(spread_kernel, plan),
        in_specs=[SMEM, SMEM, VMEM, VMEM, VMEM],
        out_specs=VMEM,
        out_shape=jax.ShapeDtypeStruct(dx.shape, BF),
        compiler_params=pltpu.CompilerParams(vmem_limit_bytes=32 << 20),
        name="spread",
    )(meta, offsets, dx, last, first)


def to_owners(vector, owner, lane_of, devices):
    count = vector.shape[1]
    held = jnp.where(iota((devices, count), 0) == owner, vector, 0.0)
    hits = jnp.where(iota((count, LANES), 1) == lane_of, 1.0, 0.0)
    return lax.dot_general(
        held, hits, (((1,), (0,)), ((), ())), precision=lax.Precision.HIGHEST, preferred_element_type=F32
    )


def cut(index, unit):
    whole = jnp.floor((index.astype(F32) + 0.5) * (1.0 / unit)).astype(jnp.int32)
    return whole, index - whole * unit


def head_kernel(devices, meta, dx_ref, npre_ref, w_ref, gain, shift, sums_ref, up_ref, pair_ref, small_ref, acc, col_s, row_s):
    step, steps = pl.program_id(0), pl.num_programs(0)
    per = dx_ref.shape[0]
    tq = dx_ref.shape[2]
    rows = dx_ref.shape[1]
    size = rows // 3
    width = npre_ref.shape[1]

    @pl.when(step == 0)
    def _():
        acc[...] = jnp.zeros_like(acc)
        col_s[...] = jnp.zeros_like(col_s)
        row_s[...] = jnp.zeros_like(row_s)

    for i in range(per):
        grads = dx_ref[i]
        acc[...] += dot_nn(grads, npre_ref[i * tq : (i + 1) * tq, :])
        col_s[...] += jnp.broadcast_to(jnp.sum(grads.astype(F32), 1, keepdims=True), col_s.shape)
        row_s[...] += dot_nt(jnp.ones((8, tq), BF), grads)

    @pl.when(step == steps - 1)
    def _():
        grp, head = meta[2], meta[1]
        plain = acc[...]
        weight = plain * gain[...] + col_s[:, :1] * shift[...]
        for part in range(3):
            for half in range(2):
                at = part * size + half * (size // 2)
                pair_ref[lax.rem(half + grp, 2), part] = weight[at : at + size // 2].astype(BF)
        own = w_ref[...].astype(F32)
        gain_part = jnp.sum(own * plain, 0, keepdims=True)
        shift_part = jnp.sum(own * col_s[:, :1], 0, keepdims=True)
        unit = width // devices
        owner = cut(iota((1, width), 1), unit)[0]
        lane = cut(iota((width, 1), 0), unit)[1]
        small_ref[:, 0, :] = to_owners(gain_part, owner, lane, devices)
        small_ref[:, 1, :] = to_owners(shift_part, owner, lane, devices)
        held = jnp.zeros((devices, LANES), F32)
        for i in range(4):
            held += to_owners(sums_ref[i : i + 1, :], owner, lane + i * unit, devices)
        small_ref[:, 2, :] = held
        hidden = up_ref.shape[1]
        unit_up = hidden // devices
        held = jnp.zeros((devices, LANES), F32)
        for i in range(hidden // width):
            owner_up = cut(iota((1, width), 1) + i * width, unit_up)[0]
            lane_up = cut(iota((width, 1), 0) + i * width, unit_up)[1]
            held += to_owners(up_ref[:, i * width : (i + 1) * width], owner_up, lane_up, devices)
        small_ref[:, 3, :] = held
        line = row_s[0:1, :]
        for i, part in enumerate((0, 2)):
            index = iota((1, rows), 1) - part * size
            inside = (index >= 0) & (index < size)
            owner_h = jnp.where(inside, 2 * head + cut(index, size // 2)[0], -1)
            lane_h = cut(iota((rows, 1), 0), size // 2)[1]
            small_ref[:, 4 + i, :] = to_owners(line, owner_h, lane_h, devices)
        small_ref[:, 6, :] = jnp.zeros((devices, LANES), F32)
        small_ref[:, 7, :] = jnp.zeros((devices, LANES), F32)


def head_call(devices, meta, dx, npre_all, own_w, gain, shift, sums, up_sums):
    blocks, rows, tq = dx.shape
    width = npre_all.shape[1]
    per = 4
    whole = lambda *shape: pl.BlockSpec(shape, lambda i: (0,) * len(shape))
    return pl.pallas_call(
        functools.partial(head_kernel, devices),
        grid=(blocks // per,),
        in_specs=[
            SMEM, pl.BlockSpec((per, rows, tq), lambda i: (i, 0, 0)), pl.BlockSpec((per * tq, width), lambda i: (i, 0)),
            whole(rows, width), whole(1, width), whole(1, width), whole(8, width), whole(1, up_sums.shape[1]),
        ],
        out_specs=(whole(2, 3, rows // 6, width), whole(devices, 8, LANES)),
        out_shape=(
            jax.ShapeDtypeStruct((2, 3, rows // 6, width), BF),
            jax.ShapeDtypeStruct((devices, 8, LANES), F32),
        ),
        scratch_shapes=[
            pltpu.VMEM((rows, width), F32), pltpu.VMEM((rows, LANES), F32), pltpu.VMEM((8, rows), F32),
        ],
        compiler_params=pltpu.CompilerParams(vmem_limit_bytes=32 << 20),
        name="head",
    )(meta, dx, npre_all, own_w, gain, shift, sums, up_sums)


def layer_norm_rows(values, norm_gain, norm_shift):
    row_mean = jnp.mean(values, -1, keepdims=True)
    centred = values - row_mean
    inverse = lax.rsqrt(jnp.mean(centred * centred, -1, keepdims=True) + EPS)
    normed = centred * inverse
    return (normed * norm_gain + norm_shift, normed, inverse)


def norm_back(grad_out, normed, inverse, norm_gain):
    grad_norm = grad_out * norm_gain
    grad_in = inverse * (
        grad_norm
        - jnp.mean(grad_norm, -1, keepdims=True)
        - normed * jnp.mean(grad_norm * normed, -1, keepdims=True)
    )
    return (grad_in, jnp.sum(grad_out * normed, 0), jnp.sum(grad_out, 0))


def swap(values, axes):
    return lax.all_to_all(values, axes, 0, 0, tiled=True)


def scatter_sum(values, orders):
    sizes = {name: lax.axis_size(name) for name in ALL}
    left = list(ALL)
    rows, cols = values.shape[1:]
    for stage, axes in enumerate(orders):
        values = values.reshape([sizes[name] for name in left] + [rows, cols])
        rest = [name for name in left if name not in axes]
        order = [left.index(name) for name in list(axes) + rest]
        values = values.transpose(order + [len(left), len(left) + 1])
        count = math.prod(sizes[name] for name in axes)
        values = values.reshape((count, -1, rows, cols))
        if count > 1:
            values = swap(values, axes)
            values = jnp.sum(values.astype(F32), 0)
            if stage < len(orders) - 1:
                values = values.astype(BF)
        left = rest
    return values.reshape(rows, cols).astype(F32)


def halo_table(plan, offs, side):
    place = jnp.arange(plan.halo, dtype=jnp.int32)[:, None]
    columns = []
    for branch in plan.branches:
        if branch["extra"]:
            wanted = jnp.arange(branch["extra"], dtype=jnp.int32) * branch["rate"]
            columns.append(wanted + offs[branch["level"]])
    wanted = jnp.concatenate(columns)
    wanted = jnp.pad(wanted, (0, max(plan.sel, LANES) - plan.sel), constant_values=-1)
    return (place == wanted[None, :]).astype(BF)


def halo_tokens(plan, x, side):
    parts = x.reshape(plan.groups, plan.members, 3 * plan.size, plan.tq)[:, :, plan.size :]
    count = plan.halo // (plan.groups * plan.tq)
    parts = parts[:, plan.members - count :] if side == 0 else parts[:, :count]
    return parts.transpose(2, 1, 0, 3).reshape(2 * plan.size, plan.halo)


def to_neighbours(pieces, count):
    return jnp.stack(
        [
            lax.ppermute(pieces[0], "grp", [(i, i + 1) for i in range(count - 1)]),
            lax.ppermute(pieces[1], "grp", [(i + 1, i) for i in range(count - 1)]),
        ]
    )


def share_columns(weight_t, sums, width):
    members, size = lax.axis_size(GROUP), weight_t.shape[1]
    head = lax.axis_index(GROUP)
    full = jnp.zeros((3, members) + weight_t.shape[1:], F32)
    full = lax.dynamic_update_slice(full, weight_t[:, None], (0, head, 0, 0))
    full_sums = lax.dynamic_update_slice(jnp.zeros((3, members, size), F32), sums[:, None], (0, head, 0))
    weight = lax.psum_scatter(full.reshape(3 * members * size, width), ALL, scatter_dimension=0, tiled=True)
    sums = lax.psum_scatter(full_sums.reshape(3, members * size), ALL, scatter_dimension=1, tiled=True)
    return weight, sums[0], sums[2]


def body(
    tile_embed,
    slide_lengths,
    head_offsets,
    pre_gain,
    pre_shift,
    qkv_weight,
    query_bias,
    value_bias,
    out_weight,
    out_bias,
    post_gain,
    post_shift,
    up_weight,
    up_bias,
    down_weight,
    down_bias,
    out_grad,
):
    width = qkv_weight.shape[0]
    hidden = up_weight.shape[1]
    heads = head_offsets.shape[1]
    size = width // heads
    tq = tile_embed.shape[1]
    br, groups = lax.axis_size("br"), lax.axis_size("grp")
    members = heads // br
    devices = heads * groups
    plan = Plan(heads, size, head_offsets.shape[0], br, members, tq, devices * tq)
    head = lax.axis_index(GROUP)
    base = lax.axis_index("grp") * plan.tokens
    meta = jnp.stack([base, head]).astype(jnp.int32)
    offs = lax.dynamic_index_in_dim(head_offsets, head, 1, False)

    tiles = tile_embed[0].astype(F32)
    pre_out, normed_pre, inverse_pre = layer_norm_rows(tiles, pre_gain, pre_shift)
    normed_low = pre_out.astype(BF)
    bias_col = jnp.concatenate([query_bias, jnp.zeros_like(query_bias), value_bias], 1).reshape(-1, 1)
    joined_t = (
        lax.dot_general(qkv_weight, normed_low, (((0,), (1,)), ((), ())), preferred_element_type=F32) + bias_col
    ).astype(BF)
    x = joined_t.reshape(3, heads, size, tq).transpose(1, 0, 2, 3).reshape(heads, 3 * size, tq)
    x = swap(x, GROUP)
    normed_all = lax.all_gather(normed_low, GROUP, axis=0, tiled=True)

    tables = [halo_table(plan, offs, side) for side in range(2)]
    chosen = [
        jnp.dot(halo_tokens(plan, x, side), tables[side], preferred_element_type=F32).astype(BF)
        for side in range(2)
    ]
    halo = to_neighbours(chosen, groups)
    mixed, state = forward_call(plan, meta, slide_lengths, head_offsets, x, halo)
    attn_t = swap(mixed, GROUP).reshape(width, tq)

    projected = lax.dot_general(attn_t, out_weight, (((0,), (0,)), ((), ())), preferred_element_type=F32)
    residual = tiles + projected + out_bias
    post_out, normed_post, inverse_post = layer_norm_rows(residual, post_gain, post_shift)
    lifted = post_out.astype(BF)
    gate_in = jnp.dot(lifted, up_weight, preferred_element_type=F32) + up_bias
    act_float, gelu_pull = jax.vjp(lambda v: jax.nn.gelu(v, approximate=False), gate_in)
    act_low = act_float.astype(BF)
    layer_out = (residual + jnp.dot(act_low, down_weight, preferred_element_type=F32) + down_bias).astype(BF)[None]
    grad_low = out_grad[0]
    grad_float = grad_low.astype(F32)
    act_grad = lax.dot_general(grad_low, down_weight, (((1,), (1,)), ((), ())), preferred_element_type=F32)
    gate_grad = gelu_pull(act_grad)[0].astype(BF)
    lifted_grad = lax.dot_general(gate_grad, up_weight, (((1,), (1,)), ((), ())), preferred_element_type=F32)
    norm_part, post_gain_sum, post_shift_sum = norm_back(lifted_grad, normed_post, inverse_post, post_gain)
    residual_grad = grad_float + norm_part
    proj_grad = residual_grad.astype(BF)
    attn_grad_t = lax.dot_general(
        out_weight, proj_grad, (((1,), (1,)), ((), ())), preferred_element_type=F32
    ).astype(BF)
    do = swap(attn_grad_t.reshape(heads, size, tq), GROUP)

    tokens = (((0,), (0,)), ((), ()))
    up_part = lax.dot_general(gate_grad, lifted, tokens, preferred_element_type=F32).astype(BF)
    down_part = lax.dot_general(grad_low, act_low, tokens, preferred_element_type=F32).astype(BF)
    out_part = lax.dot_general(proj_grad, attn_t, (((0,), (1,)), ((), ())), preferred_element_type=F32).astype(BF)
    vectors = [
        jnp.sum(gate_grad.astype(F32), 0).reshape(devices, -1),
        jnp.sum(grad_float, 0).reshape(devices, -1),
        jnp.sum(residual_grad, 0).reshape(devices, -1),
        post_gain_sum.reshape(devices, -1),
        post_shift_sum.reshape(devices, -1),
    ]
    ends = [0]
    for vector in vectors:
        ends.append(ends[-1] + vector.shape[1])
    small = jnp.concatenate(vectors, 1)
    small = jnp.pad(small[:, None, :], ((0, 0), (0, 7), (0, width - small.shape[1]))).astype(BF)
    misc = jnp.concatenate([out_part.reshape(devices, -1, width), small], 1)
    first, second = (("s0",), ("br", "s1"), ("grp", "s2")), (("s0",), ("grp", "s2"), ("br", "s1"))
    up_own = scatter_sum(up_part.reshape(devices, -1, width), first)
    down_own = scatter_sum(down_part.reshape(devices, -1, hidden), second)
    misc_own = scatter_sum(misc, first)
    unit = width // devices
    small_own = misc_own[unit]
    small_own = [small_own[None, ends[i] : ends[i + 1]] for i in range(len(vectors))]

    dx, dh = backward_call(plan, meta, slide_lengths, head_offsets, x, halo, state, do)
    back = to_neighbours([dh[1], dh[0]], groups)
    counts = plan.halo // (br * tq)
    dx_parts = dx.reshape(br, members, 3 * size, tq)
    adds = jnp.zeros((br, members, 2 * size, tq), F32)
    for side, (piece, table) in enumerate(zip([back[1], back[0]], tables)):
        spread = lax.dot_general(piece, table, (((1,), (1,)), ((), ())), preferred_element_type=F32)
        spread = spread.reshape(2 * size, counts, br, tq).transpose(2, 1, 0, 3)
        pads = (members - counts, 0) if side == 0 else (0, members - counts)
        adds = adds + jnp.pad(spread, ((0, 0), pads, (0, 0), (0, 0)))
    adds = jnp.pad(adds, ((0, 0), (0, 0), (size, 0), (0, 0)))
    dx = (dx_parts.astype(F32) + adds).astype(BF).reshape(heads, 3 * size, tq)
    joined_grad_t = swap(dx, GROUP).reshape(heads, 3, size, tq).transpose(1, 0, 2, 3).reshape(3 * width, tq)
    weight_t = jnp.einsum(
        "nct,ntd->cd", dx, normed_all.reshape(heads, tq, width), preferred_element_type=F32
    ).reshape(3, size, width)
    head_sums = jnp.sum(dx.astype(F32), (0, 2)).reshape(3, size)
    qkv_own, query_own, value_own = share_columns(weight_t, head_sums, width)
    normed_grad = lax.dot_general(joined_grad_t, qkv_weight, (((0,), (1,)), ((), ())), preferred_element_type=F32)
    tile_part, pre_gain_sum, pre_shift_sum = norm_back(normed_grad, normed_pre, inverse_pre, pre_gain)
    tile_grad = (residual_grad + tile_part).astype(BF)[None]
    last = jnp.stack([pre_gain_sum, pre_shift_sum]).reshape(2, devices, unit).transpose(1, 0, 2)
    last = jnp.pad(last, ((0, 0), (0, 6), (0, LANES - unit)))
    last = jnp.sum(swap(last, ALL).reshape(devices, 8, LANES), 0)
    return (
        layer_out,
        tile_grad,
        last[0:1, :unit],
        last[1:2, :unit],
        qkv_own.T,
        query_own[None],
        value_own[None],
        misc_own[:unit].T,
        small_own[2],
        small_own[3],
        small_own[4],
        up_own.T,
        small_own[0],
        down_own.T,
        small_own[1],
    )


def across(pieces, axes):
    got = []
    for k in range(1, 4):
        got.append(lax.ppermute(pieces[k], axes, [(i, i ^ k) for i in range(4)]))
    return [pieces[0]] + got


def owner_places():
    sizes = [lax.axis_size(name) for name in ALL]
    inner = sizes[2] * sizes[3] * sizes[4]
    place = {}
    for br in range(sizes[0]):
        for grp in range(sizes[1]):
            for sub in range(inner):
                place[(br * inner + sub) * sizes[1] + grp] = (br * sizes[1] + grp) * inner + sub
    return place


def send_units(total):
    place = owner_places()
    devices = len(place)
    here = lax.axis_index(ALL)
    pieces = []
    for slot in range(3):
        route, part_of = [], [0] * devices
        for owner in range(devices):
            part, which = divmod(3 * owner + slot, devices)
            route.append((place[which], owner))
            part_of[place[which]] = part
        part = jnp.array(part_of, jnp.int32)[here]
        pieces.append(lax.ppermute(lax.dynamic_index_in_dim(total, part, 0, False), ALL, route))
    return jnp.concatenate(pieces).astype(F32)


def fast_body(
    tile_embed, slide_lengths, head_offsets, pre_gain, pre_shift, qkv_weight, query_bias, value_bias, out_weight,
    out_bias, post_gain, post_shift, up_weight, up_bias, down_weight, down_bias, out_grad,
):
    width = qkv_weight.shape[0]
    heads = head_offsets.shape[1]
    size = width // heads
    tq = tile_embed.shape[1]
    br, groups = lax.axis_size("br"), lax.axis_size("grp")
    members = heads // br
    devices = heads * groups
    plan = Plan(heads, size, head_offsets.shape[0], br, members, tq, devices * tq)
    head = lax.axis_index(GROUP)
    group = lax.axis_index("grp")
    core = lax.axis_index("s0")
    meta = [group * plan.tokens, head, group, core, lax.axis_index(("br", "s1")), lax.axis_index(("grp", "s2"))]
    meta = jnp.stack(meta).astype(jnp.int32)
    tiles = tile_embed[0]
    own_w = jnp.concatenate(
        [lax.dynamic_slice_in_dim(qkv_weight, part * width + head * size, size, 1) for part in range(3)], 1
    ).T
    pair = [(0, 1), (1, 0)]
    plane, line = ("br", "s1"), ("grp", "s2")

    x, npre = enter_call(heads, tiles, pre_gain, pre_shift, qkv_weight, query_bias, value_bias)
    x = swap(x.reshape(heads, 3 * size, tq), GROUP)
    last, first = select_call(plan, meta, head_offsets, x)
    halo = to_neighbours([last, first], groups)
    mixed, state = forward_call(plan, meta, slide_lengths, head_offsets, x, halo)
    attn_t = swap(mixed, GROUP).reshape(width, tq)
    npre_all = lax.all_gather(npre, GROUP, axis=0, tiled=True)
    attn_t, npre_all = lax.optimization_barrier((attn_t, npre_all))

    attn_b = lax.ppermute(attn_t, "s0", pair)
    layer_out, residual_grad, attn_grad_t, common, sel, sel_give, sums, up_sums = middle_call(
        devices, core[None].astype(jnp.int32), attn_t, tiles, out_weight, out_bias, post_gain, post_shift,
        up_weight, up_bias, down_weight, down_bias, out_grad[0],
    )
    do = swap(attn_grad_t.reshape(heads, size, tq), GROUP)
    common_b = lax.ppermute(common, "s0", pair)
    sel_b = lax.ppermute(sel_give, "s0", pair)
    first, *second = weights_call(devices, meta, attn_t, attn_b, common, common_b, sel, sel_b)
    do, first, *second = lax.optimization_barrier((do, first, *second))
    first = swap(first, plane)
    second = across(second, line)

    dx, dh = backward_call(plan, meta, slide_lengths, head_offsets, x, halo, state, do)
    dx, dh, first, *second = lax.optimization_barrier((dx, dh, first, *second))
    pieces = fold_call(meta, first, second)
    back = to_neighbours([dh[1], dh[0]], groups)
    dx = spread_call(plan, meta, head_offsets, dx, back[1], back[0])
    joined_grad = swap(dx, GROUP).reshape(heads, 3, size, tq)
    halves, small = head_call(devices, meta, dx, npre_all, own_w, pre_gain, pre_shift, sums, up_sums)
    joined_grad, small = lax.optimization_barrier((joined_grad, small))
    small = jnp.sum(swap(small, ALL), 0)
    total = (halves[0].astype(F32) + lax.ppermute(halves[1], "grp", pair).astype(F32)).astype(BF)
    qkv_own = send_units(total)
    first = across(pieces[:4], line)
    second = across(pieces[4:], plane)
    tile_grad = leave_call(tiles, pre_gain, qkv_weight, joined_grad, residual_grad)
    unit_up, unit = up_weight.shape[1] // devices, width // devices
    up_own, out_own, down_own = last_call(unit_up, unit, first, second)
    return (
        layer_out[None],
        tile_grad[None],
        small[0:1, :unit],
        small[1:2, :unit],
        qkv_own.T,
        small[4:5, :unit],
        small[5:6, :unit],
        out_own.T,
        small[2:3, unit : 2 * unit],
        small[2:3, 2 * unit : 3 * unit],
        small[2:3, 3 * unit : 4 * unit],
        up_own.T,
        small[3:4, :unit_up],
        down_own.T,
        small[2:3, :unit],
    )


def solution(mesh):
    br, rows = mesh.shape["br"], mesh.shape["rows"]

    def run(*args):
        members = args[2].shape[1] // br
        shape = (br, rows // members, members // 4, 2, 2)
        split = jax.sharding.Mesh(mesh.devices.reshape(shape), ALL)
        tokens = P(("grp", "s2", "s1", "s0"), "br", None)
        owned = P(None, ALL)
        return jax.shard_map(
            fast_body if shape == (2, 2, 2, 2, 2) else body,
            mesh=split,
            in_specs=(tokens,) + (P(),) * 15 + (tokens,),
            out_specs=(tokens, tokens) + (owned,) * 13,
            check_vma=False,
        )(*args)

    return run
```

```python
import functools
import math

import jax
import jax.numpy as jnp
from jax import lax
from jax.experimental import pallas as pl
from jax.experimental.pallas import tpu as pltpu
from jax.sharding import PartitionSpec as P

SEG_BASE = 1024
DOC_MOST = 2048
LANES = 128
BF = jnp.bfloat16
F32 = jnp.float32
NEG = -1e30
EPS = 1e-05
ALL = ("br", "grp", "s2", "s1", "s0")
GROUP = ("br", "s2", "s1", "s0")
FIRST_DOWN = 1
ONE_LANE = 48
ID_Q = 51
ID_K = 52


class Plan:
    def __init__(self, heads, head_size, branches, groups, members, tq, total):
        self.heads, self.size, self.groups, self.members, self.tq = heads, head_size, groups, members, tq
        self.blocks = groups * members
        self.paired = groups * members * tq * 2 == total
        self.tokens = self.blocks * tq
        self.total = total
        self.halo = min(DOC_MOST, self.tokens)
        self.factor = math.log2(math.e) * head_size**-0.5
        self.branches = []
        keys, sel = 0, 0
        for level in range(branches):
            rate = 2**level
            span = min(SEG_BASE * rate, total)
            near = span <= self.tokens
            extra = 0 if near else self.halo // rate
            segs = self.tokens // span if near else 1
            seg_q = self.tokens // rate // segs
            seg_k = seg_q + 2 * extra
            self.branches.append(
                dict(
                    level=level, rate=rate, span=span, near=near, extra=extra, segs=segs,
                    seg_q=seg_q, seg_k=seg_k, tile=min(1024, seg_q), first=keys, sel=sel,
                )
            )
            keys += segs * seg_k
            sel += extra
        self.sel = sel
        self.near = [b for b in self.branches if b["near"]]
        self.far = [b for b in self.branches if not b["near"]]
        self.near_keys = sum(b["segs"] * b["seg_k"] for b in self.near)
        self.far_keys, self.own = 0, 0
        for b in self.far:
            b["begin"], b["own"] = self.far_keys, self.own
            self.far_keys += b["seg_k"]
            self.own += b["seg_q"]
        self.widest = max(b["seg_k"] for b in self.branches)

    def slot(self, block):
        return lax.rem(block, self.groups) * self.members + lax.div(block, self.groups)


def dot_nt(a, b):
    return lax.dot_general(a, b, (((1,), (1,)), ((), ())), preferred_element_type=F32)


def dot_tn(a, b):
    return lax.dot_general(a, b, (((0,), (0,)), ((), ())), preferred_element_type=F32)


def dot_nn(a, b):
    return lax.dot_general(a, b, (((1,), (0,)), ((), ())), preferred_element_type=F32)


def iota(shape, dim):
    return lax.broadcasted_iota(jnp.int32, shape, dim)


def placement(size, parts):
    shape = (parts * size + 16, parts * LANES)
    row, col = iota(shape, 0), iota(shape, 1)
    hit = col < 0
    for part in range(parts):
        hit |= (row >= part * size) & (row < (part + 1) * size) & (col == row - part * size + part * LANES)
    return row, col, hit


def ids_of(pos, starts, gate=None):
    found = jnp.zeros(pos.shape, jnp.int32)
    for start in starts:
        found += jnp.where(pos >= start, 1, 0)
    if gate is not None:
        found = jnp.where(gate, found, -1)
    return found.astype(F32)


def slide_starts(lens_ref):
    starts, at = [], jnp.int32(0)
    for i in range(lens_ref.shape[0]):
        starts.append(at)
        at = at + lens_ref[i]
    return starts


def branch_pos(plan, branch, base, off, first, count):
    start = base - branch["extra"] * branch["rate"] + off
    pos = start + branch["rate"] * (first + iota((1, count), 1))
    if branch["near"]:
        return pos, None
    shift = int(math.log2(branch["span"]))
    return pos, lax.shift_right_arithmetic(pos, shift) == lax.shift_right_arithmetic(base, shift)


def to_rows(plan, base, starts, x_ref, q_tm, k_tm, v_tm, extra_q=None):
    size, tq = plan.size, plan.tq
    row, col, hit = placement(size, 3)
    hit |= (row == 3 * size) & ((col == ID_Q) | (col == LANES + ID_K))
    place = jnp.where(hit, 1.0, 0.0).astype(BF)
    lane = iota((1, 3 * LANES), 1)
    in_k, in_v = lane - LANES, lane - 2 * LANES
    ones = jnp.where(
        ((in_k >= ONE_LANE) & (in_k < ONE_LANE + 3)) | ((in_v >= ONE_LANE) & (in_v < ONE_LANE + 3)), 1.0, 0.0
    )

    def block(n, carry):
        pos = base + n * tq + iota((1, tq), 1)
        ids = jnp.where(iota((16, tq), 0) == 0, ids_of(pos, starts), 0.0).astype(BF)
        full = jnp.concatenate([x_ref[plan.slot(n)], ids], 0)
        rows = dot_tn(full, place) + ones
        at = pl.ds(pl.multiple_of(n * tq, tq), tq)
        queries = rows[:, :LANES]
        if extra_q is not None:
            queries = queries + extra_q(n, at)
        q_tm[at, :] = queries
        k_tm[at, :] = rows[:, LANES : 2 * LANES]
        v_tm[at, :] = rows[:, 2 * LANES :]
        if extra_q is not None:
            return carry
        squares = [jnp.square(full[i * size : (i + 1) * size].astype(F32)) for i in range(2)]
        return tuple(jnp.maximum(a, jnp.sum(b, 0, keepdims=True)) for a, b in zip(carry, squares))

    start = (jnp.zeros((1, tq), F32),) * 2 if extra_q is None else 0
    most = lax.fori_loop(0, plan.blocks, block, start, unroll=4)
    if extra_q is None:
        return jnp.sqrt(jnp.max(most[0], 1, keepdims=True) * jnp.max(most[1], 1, keepdims=True)) * 1.0001
    return None


def gather_near(plan, offs, k_tm, v_tm, kall, vall, branches):
    for branch in branches:
        rate, first, off = branch["rate"], branch["first"], offs[branch["level"]]
        count = plan.tokens // rate
        step = min(256, count)

        def chunk(i, carry, rate=rate, first=first, off=off, step=step):
            rows = pl.ds(off + i * step * rate, step, stride=rate) if rate > 1 else pl.ds(i * step, step)
            to = pl.ds(pl.multiple_of(first + i * step, step), step)
            kall[to, :] = k_tm[rows, :].astype(BF)
            vall[to, :] = v_tm[rows, :].astype(BF)
            return carry

        lax.fori_loop(0, count // step, chunk, 0, unroll=min(4, count // step))


def far_keys(plan, base, offs, starts, halos, k_far, v_far, kall, vall):
    size = plan.size
    row, col, hit = placement(size, 2)
    hit |= (row == 2 * size) & (col == ID_K)
    place = jnp.where(hit, 1.0, 0.0).astype(BF)
    lane = iota((1, 2 * LANES), 1)
    in_v = lane - LANES
    ones = jnp.where(
        ((lane >= ONE_LANE) & (lane < ONE_LANE + 3)) | ((in_v >= ONE_LANE) & (in_v < ONE_LANE + 3)), 1.0, 0.0
    )
    for branch in plan.far:
        extra, first, own, count = branch["extra"], branch["begin"], branch["own"], branch["seg_q"]
        kall[first + extra : first + extra + count, :] = k_far[own : own + count, :]
        vall[first + extra : first + extra + count, :] = v_far[own : own + count, :]
        for side, ref in enumerate((halos[0], halos[-1])):
            begin = side * (extra + count)
            pos, gate = branch_pos(plan, branch, base, offs[branch["level"]], begin, extra)
            ids = jnp.where(iota((16, extra), 0) == 0, ids_of(pos, starts, gate), 0.0).astype(BF)
            piece = ref[:, branch["sel"] : branch["sel"] + extra]
            rows = dot_tn(jnp.concatenate([piece, ids], 0), place) + ones
            kall[first + begin : first + begin + extra, :] = rows[:, :LANES].astype(BF)
            vall[first + begin : first + begin + extra, :] = rows[:, LANES:].astype(BF)


def picked(branch, off, i):
    tile, rate = branch["tile"], branch["rate"]
    if rate == 1:
        return pl.ds(pl.multiple_of(i * tile, tile), tile)
    return pl.ds(off + i * tile * rate, tile, stride=rate)


def pieces_of(wide, most):
    step = next(n for n in (most, 512, 256, 128) if wide % n == 0)
    return [(at, step) for at in range(0, wide, step)]


def split3(column, lane):
    high = column.astype(BF).astype(F32)
    rest = column - high
    mid = rest.astype(BF).astype(F32)
    low = rest - mid
    return jnp.where(
        lane == ONE_LANE, high, jnp.where(lane == ONE_LANE + 1, mid, jnp.where(lane == ONE_LANE + 2, low, 0.0))
    )


def near_kernel(plan, meta, lens, offsets, x_ref, st_ref, qf_ref, kf_ref, vf_ref, q_tm, k_tm, v_tm, kall, vall, kid):
    base, head = meta[0], meta[1]
    starts = slide_starts(lens)
    offs = [offsets[b["level"], head] for b in plan.branches]
    top = to_rows(plan, base, starts, x_ref, q_tm, k_tm, v_tm)
    gather_near(plan, offs, k_tm, v_tm, kall, vall, plan.near)
    for branch in plan.far:
        rows = pl.ds(offs[branch["level"]], branch["seg_q"], stride=branch["rate"])
        own = slice(branch["own"], branch["own"] + branch["seg_q"])
        for ref, source in ((qf_ref, q_tm), (kf_ref, k_tm), (vf_ref, v_tm)):
            ref[own, :] = source[rows, :].astype(BF)
    for branch in plan.near:
        first, total = branch["first"], branch["segs"] * branch["seg_k"]
        pos, gate = branch_pos(plan, branch, base, offs[branch["level"]], 0, total)
        kid[:, first : first + total] = ids_of(pos, starts, gate)
    factor = plan.factor
    lane = iota((1, LANES), 1)

    def scan(visit):
        for branch in plan.near:
            per = branch["seg_q"] // branch["tile"]

            def tile(i, carry, branch=branch, per=per):
                rows = picked(branch, offs[branch["level"]], i)
                at = pl.multiple_of(branch["first"] + lax.div(i, per) * branch["seg_k"], 128)
                visit(branch, rows, q_tm[rows, :], at)
                return carry

            lax.fori_loop(0, branch["segs"] * per, tile, 0)

    def attend(top_lanes):
        def visit(branch, rows, queries, at):
            ids = queries[:, ID_Q : ID_Q + 1]
            low = (queries + top_lanes).astype(BF)
            mixed = None
            for begin, step in pieces_of(branch["seg_k"], 1024):
                to = pl.ds(at + begin, step)
                weights = jnp.exp2(dot_nt(low, kall[to, :]) * factor)
                weights = jnp.where(ids == kid[:, to], weights, 0.0).astype(BF)
                more = dot_nn(weights, vall[to, :])
                mixed = more if mixed is None else mixed + more
            if branch["level"]:
                mixed = st_ref[rows, :] + mixed
            st_ref[rows, :] = mixed

        scan(visit)

    attend(split3(-top, lane))
    step = min(512, plan.tokens)

    def least(n, low):
        at = pl.ds(pl.multiple_of(n * step, step), step)
        state = st_ref[at, :]
        st_ref[at, :] = jnp.where(iota((step, LANES), 1) == ID_Q, top, state)
        return jnp.minimum(low, jnp.min(state, 0, keepdims=True))

    weight = lax.fori_loop(0, plan.tokens // step, least, jnp.full((1, LANES), jnp.inf, F32), unroll=2)
    weight = jnp.min(jnp.where(lane == ONE_LANE, weight, jnp.inf))

    @pl.when(jnp.logical_not(weight > 2.0**-60))
    def _():
        def clear(n, carry):
            st_ref[pl.ds(pl.multiple_of(n * step, step), step), :] = jnp.full((step, LANES), NEG, F32)
            return carry

        def largest(branch, rows, queries, at):
            low = queries.astype(BF)
            best = st_ref[rows, :]
            for begin, step in pieces_of(branch["seg_k"], 256):
                to = pl.ds(at + begin, step)
                scores = jnp.where(queries[:, ID_Q : ID_Q + 1] == kid[:, to], dot_nt(low, kall[to, :]), NEG)
                best = jnp.maximum(best, jnp.max(scores, 1, keepdims=True))
            st_ref[rows, :] = best

        def settle(n, carry):
            at = pl.ds(pl.multiple_of(n * step, step), step)
            own = st_ref[at, :]
            tops[at, :] = own
            wide = iota((step, LANES), 1)
            q_tm[at, :] = q_tm[at, :] + split3(-own, wide)
            return carry

        def restore(n, carry):
            at = pl.ds(pl.multiple_of(n * step, step), step)
            st_ref[at, :] = jnp.where(iota((step, LANES), 1) == ID_Q, tops[at, :], st_ref[at, :])
            return carry

        tops = k_tm
        lax.fori_loop(0, plan.tokens // step, clear, 0)
        scan(largest)
        lax.fori_loop(0, plan.tokens // step, settle, 0)
        attend(jnp.zeros((1, LANES), F32))
        lax.fori_loop(0, plan.tokens // step, restore, 0)


def far_kernel(plan, meta, lens, offsets, st_in, qf_ref, kf_ref, vf_ref, *rest):
    halos, (o_ref, st_ref, kall, vall) = rest[:-4], rest[-4:]
    base, head = meta[0], meta[1]
    starts = slide_starts(lens)
    offs = [offsets[b["level"], head] for b in plan.branches]
    factor = plan.factor
    step = min(512, plan.tokens)

    def carry_over(n, carry):
        at = pl.ds(pl.multiple_of(n * step, step), step)
        st_ref[at, :] = st_in[at, :]
        return carry

    lax.fori_loop(0, plan.tokens // step, carry_over, 0, unroll=2)
    if plan.far:
        far_keys(plan, base, offs, starts, halos, kf_ref, vf_ref, kall, vall)
    for branch in plan.far:
        off, tile, wide = offs[branch["level"]], branch["tile"], branch["seg_k"]
        pos, gate = branch_pos(plan, branch, base, off, 0, wide)
        ids = ids_of(pos, starts, gate)
        keys = kall[branch["begin"] : branch["begin"] + wide, :]
        values = vall[branch["begin"] : branch["begin"] + wide, :]
        for i in range(branch["seg_q"] // tile):
            own = branch["own"] + i * tile
            queries = qf_ref[own : own + tile, :]
            rows = picked(branch, off, i)
            scores = dot_nt(queries, keys)
            scores = jnp.where(queries[:, ID_Q : ID_Q + 1].astype(F32) == ids, scores, NEG)
            top = jnp.max(scores, 1, keepdims=True)
            mixed = dot_nn(jnp.exp2((scores - top) * factor).astype(BF), values)
            old = st_ref[rows, :]
            old_top = old[:, ID_Q : ID_Q + 1]
            new_top = jnp.maximum(old_top, top)
            mixed = old * jnp.exp2((old_top - new_top) * factor) + mixed * jnp.exp2((top - new_top) * factor)
            st_ref[rows, :] = jnp.where(iota((tile, LANES), 1) == ID_Q, new_top, mixed)
    eye = jnp.where(iota((plan.size, LANES), 0) == iota((plan.size, LANES), 1), 1.0, 0.0).astype(BF)

    def finish(n, carry):
        at = pl.ds(pl.multiple_of(n * plan.tq, plan.tq), plan.tq)
        state = st_ref[at, :]
        weight = state[:, ONE_LANE : ONE_LANE + 1]
        top = state[:, ID_Q : ID_Q + 1]
        attn = state * (1.0 / weight)
        merged = top + jnp.log2(weight) * (1.0 / factor)
        lane = iota((plan.tq, LANES), 1)
        st_ref[at, :] = jnp.where(lane < plan.size, attn, jnp.where(lane == ONE_LANE, merged, 0.0))
        o_ref[plan.slot(n)] = dot_nt(eye, attn.astype(BF)).astype(BF)
        return carry

    lax.fori_loop(0, plan.blocks, finish, 0, unroll=4)


def back_tile(plan, branch, queries, grads, keys_at, kall, vall, k_fm, linked, dk_acc, dv_acc):
    dq = None
    for begin, step in pieces_of(branch["seg_k"], 256):
        to = pl.ds(keys_at + begin, step)
        part = slice(begin, begin + step)
        keys = kall[to, :]
        probs = jnp.where(linked(keys), jnp.exp2(dot_nt(keys, queries) * plan.factor), 0.0)
        dv_acc[part, :] += dot_nn(probs.astype(BF), grads)
        moved = (probs * dot_nt(vall[to, :], grads)).astype(BF)
        dk_acc[part, :] += dot_nn(moved, queries)
        more = dot_nn(k_fm[:, part], moved)
        dq = more if dq is None else dq + more
    return dq


def far_back_kernel(
    plan, meta, lens, offsets, st_ref, do_ref, qf_ref, kf_ref, vf_ref, *rest,
):
    sides = 1 if plan.paired else 2
    halos, (do_tm, dqf_ref, dkf_ref, dvf_ref), rest = rest[:sides], rest[sides : sides + 4], rest[sides + 4 :]
    halo_outs, (kall, vall, k_fm, dk_acc, dv_acc) = rest[:sides], rest[sides:]
    base, head = meta[0], meta[1]
    starts = slide_starts(lens)
    offs = [offsets[b["level"], head] for b in plan.branches]
    size, tq = plan.size, plan.tq
    row, col, hit = placement(size, 1)
    place = jnp.where(hit, 1.0, 0.0).astype(BF)
    lane = iota((tq, LANES), 1)

    def block(n, carry):
        at = pl.ds(pl.multiple_of(n * tq, tq), tq)
        grads = dot_tn(jnp.concatenate([do_ref[plan.slot(n)], jnp.zeros((16, tq), BF)], 0), place)
        dots = jnp.sum(jnp.where(lane < size, grads * st_ref[at, :], 0.0), 1, keepdims=True)
        do_tm[at, :] = grads + split3(-dots, lane)
        return carry

    lax.fori_loop(0, plan.blocks, block, 0, unroll=4)
    if plan.far:
        far_keys(plan, base, offs, starts, halos, kf_ref, vf_ref, kall, vall)
    eye = jnp.where(iota((LANES, LANES), 0) == iota((LANES, LANES), 1), 1.0, 0.0).astype(BF)
    for branch in plan.far:
        off, tile, wide, begin = offs[branch["level"]], branch["tile"], branch["seg_k"], branch["begin"]
        k_fm[:, :wide] = dot_nt(eye, kall[begin : begin + wide, :]).astype(BF)
        dk_acc[:wide, :] = jnp.zeros((wide, LANES), F32)
        dv_acc[:wide, :] = jnp.zeros((wide, LANES), F32)
        extra, count = branch["extra"], branch["seg_q"]
        for i in range(count // tile):
            own = branch["own"] + i * tile
            rows = picked(branch, off, i)
            wide_lane = iota((tile, LANES), 1)
            merged = st_ref[rows, :][:, ONE_LANE : ONE_LANE + 1]
            queries = jnp.where(wide_lane == ID_Q, 0.0, qf_ref[own : own + tile, :].astype(F32))
            queries = (queries + split3(-merged, wide_lane)).astype(BF)
            grads = do_tm[rows, :].astype(BF)
            pos, _ = branch_pos(plan, branch, base, off, extra + i * tile, tile)
            ids = ids_of(pos, starts)
            linked = lambda keys: keys[:, ID_K : ID_K + 1].astype(F32) == ids
            dq = back_tile(plan, branch, queries, grads, begin, kall, vall, k_fm, linked, dk_acc, dv_acc)
            dqf_ref[own : own + tile, :] = dq.T
        own = slice(branch["own"], branch["own"] + count)
        dkf_ref[own, :] = dk_acc[extra : extra + count, :]
        dvf_ref[own, :] = dv_acc[extra : extra + count, :]
        for side, ref in enumerate(halo_outs):
            at = side * (extra + count)
            if plan.paired:
                at = pl.multiple_of((1 - meta[2]) * (extra + count), 128)
            to = slice(branch["sel"], branch["sel"] + extra)
            dk = (dk_acc[pl.ds(at, extra), :] * size**-0.5).astype(BF)
            ref[:size, to] = dot_nt(eye[:size], dk).astype(BF)
            ref[size:, to] = dot_nt(eye[:size], dv_acc[pl.ds(at, extra), :].astype(BF)).astype(BF)


def near_back_kernel(
    plan, meta, lens, offsets, x_ref, st_ref, do_tm, dqf_ref, dkf_ref, dvf_ref, *rest,
):
    backs, (dx_ref, q_tm, k_tm, v_tm, dq_tm, dk_tm, dv_tm, kall, vall, k_fm, qid, dk_acc, dv_acc) = rest[:-13], rest[-13:]
    base, head = meta[0], meta[1]
    starts = slide_starts(lens)
    offs = [offsets[b["level"], head] for b in plan.branches]
    size, tq = plan.size, plan.tq
    lane = iota((tq, LANES), 1)
    to_rows(
        plan, base, starts, x_ref, q_tm, k_tm, v_tm,
        lambda n, at: split3(-st_ref[at, :][:, ONE_LANE : ONE_LANE + 1], lane),
    )
    gather_near(plan, offs, k_tm, v_tm, kall, vall, plan.near)
    eye = jnp.where(iota((LANES, LANES), 0) == iota((LANES, LANES), 1), 1.0, 0.0).astype(BF)
    for branch in plan.near:
        off, first, wide, tile = offs[branch["level"]], branch["first"], branch["seg_k"], branch["tile"]
        count = branch["segs"] * branch["seg_q"]
        per = branch["seg_q"] // tile
        pos, _ = branch_pos(plan, branch, base, off, 0, count)
        qid[:, :count] = ids_of(pos, starts)

        def segment(seg, carry, branch=branch, off=off, first=first, wide=wide, tile=tile, per=per):
            keys_at = pl.multiple_of(first + seg * wide, 128)
            k_fm[:, :wide] = dot_nt(eye, kall[pl.ds(keys_at, wide), :]).astype(BF)
            dk_acc[:wide, :] = jnp.zeros((wide, LANES), F32)
            dv_acc[:wide, :] = jnp.zeros((wide, LANES), F32)

            def one(j, carry):
                i = seg * per + j
                rows = picked(branch, off, i)
                queries = q_tm[rows, :].astype(BF)
                grads = do_tm[rows, :].astype(BF)
                ids = qid[:, pl.ds(pl.multiple_of(i * tile, tile), tile)]
                linked = lambda keys: keys[:, ID_K : ID_K + 1].astype(F32) == ids
                dq = back_tile(plan, branch, queries, grads, keys_at, kall, vall, k_fm, linked, dk_acc, dv_acc).T
                if branch["level"]:
                    dq = dq_tm[rows, :] + dq
                dq_tm[rows, :] = dq
                return carry

            lax.fori_loop(0, per, one, 0)
            step = min(256, branch["seg_q"])
            for c in range(branch["seg_q"] // step):
                begin = c * step
                if branch["rate"] == 1:
                    to = pl.ds(pl.multiple_of(seg * branch["seg_q"] + begin, step), step)
                    dk_tm[to, :] = dk_acc[begin : begin + step, :]
                    dv_tm[to, :] = dv_acc[begin : begin + step, :]
                else:
                    to = pl.ds(off + (seg * branch["seg_q"] + begin) * branch["rate"], step, stride=branch["rate"])
                    dk_tm[to, :] += dk_acc[begin : begin + step, :]
                    dv_tm[to, :] += dv_acc[begin : begin + step, :]
            return carry

        lax.fori_loop(0, branch["segs"], segment, 0)
    row, col, hit = placement(size, 2)
    place = jnp.where(hit, 1.0, 0.0).astype(BF)[: 2 * size]
    for branch in plan.far:
        off, rate, extra, count = offs[branch["level"]], branch["rate"], branch["extra"], branch["seg_q"]
        rows = pl.ds(off, count, stride=rate)
        own = slice(branch["own"], branch["own"] + count)
        for total, part in ((dq_tm, dqf_ref), (dk_tm, dkf_ref), (dv_tm, dvf_ref)):
            total[rows, :] += part[own, :]
        begins = [plan.tokens - plan.halo, 0]
        if plan.paired:
            begins = [(1 - meta[2]) * (plan.tokens - plan.halo)]
        for begin, ref in zip(begins, backs):
            more = dot_tn(ref[:, branch["sel"] : branch["sel"] + extra], place)
            rows = pl.ds(begin + off, extra, stride=rate)
            dk_tm[rows, :] += more[:, :LANES] * size**0.5
            dv_tm[rows, :] += more[:, LANES:]
    small_eye = eye[:size]

    def finish(n, carry):
        at = pl.ds(pl.multiple_of(n * tq, tq), tq)
        slot = plan.slot(n)
        dx_ref[slot, :size, :] = dot_nt(small_eye, (dq_tm[at, :] * size**-0.5).astype(BF)).astype(BF)
        dx_ref[slot, size : 2 * size, :] = dot_nt(small_eye, (dk_tm[at, :] * size**-0.5).astype(BF)).astype(BF)
        dx_ref[slot, 2 * size :, :] = dot_nt(small_eye, dv_tm[at, :].astype(BF)).astype(BF)
        return carry

    lax.fori_loop(0, plan.blocks, finish, 0, unroll=4)


SMEM = pl.BlockSpec(memory_space=pltpu.SMEM)
VMEM = pl.BlockSpec(memory_space=pltpu.VMEM)
PARAMS = pltpu.CompilerParams(vmem_limit_bytes=60 << 20)


def struct(shape, kind):
    return jax.ShapeDtypeStruct(shape, kind)


def kernel_call(name, kernel, ins, outs, scratch, flops):
    return pl.pallas_call(
        kernel,
        out_shape=tuple(struct(*out) for out in outs),
        in_specs=[SMEM] * 3 + [VMEM] * (len(ins) - 3),
        out_specs=(VMEM,) * len(outs),
        scratch_shapes=[pltpu.VMEM(*s) for s in scratch],
        compiler_params=PARAMS,
        cost_estimate=pl.CostEstimate(flops=flops, bytes_accessed=4 << 20, transcendentals=0),
        name=name,
    )(*ins)


def near_call(plan, meta, lens, offsets, x):
    rows, keys = ((plan.tokens, LANES), F32), ((plan.near_keys, LANES), BF)
    own = ((plan.own, LANES), BF)
    return kernel_call(
        "near", functools.partial(near_kernel, plan), (meta, lens, offsets, x), (rows, own, own, own),
        (rows, rows, rows, keys, keys, ((1, plan.near_keys), F32)), 20_000_000_000,
    )


def far_call(plan, meta, lens, offsets, state, own, halo):
    keys = ((plan.far_keys, LANES), BF)
    return kernel_call(
        "far", functools.partial(far_kernel, plan), (meta, lens, offsets, state, *own, *halo),
        (((plan.blocks, plan.size, plan.tq), BF), ((plan.tokens, LANES), F32)), (keys, keys), 4_000_000_000,
    )


def far_back_call(plan, meta, lens, offsets, state, do, own, halo):
    keys = ((plan.far_keys, LANES), BF)
    part, side = ((plan.own, LANES), F32), ((2 * plan.size, max(plan.sel, LANES)), BF)
    acc = ((plan.widest, LANES), F32)
    return kernel_call(
        "far_back", functools.partial(far_back_kernel, plan), (meta, lens, offsets, state, do, *own, *halo),
        (((plan.tokens, LANES), F32), part, part, part) + (side,) * (1 if plan.paired else 2),
        (keys, keys, ((LANES, plan.widest), BF), acc, acc), 4_000_000_000,
    )


def near_back_call(plan, meta, lens, offsets, x, state, do_rows, parts, back):
    rows, keys = ((plan.tokens, LANES), F32), ((plan.near_keys, LANES), BF)
    acc = ((plan.widest, LANES), F32)
    return kernel_call(
        "near_back", functools.partial(near_back_kernel, plan),
        (meta, lens, offsets, x, state, do_rows, *parts, *back),
        (((plan.blocks, 3 * plan.size, plan.tq), BF),),
        (rows,) * 6 + (keys, keys, ((LANES, plan.widest), BF), ((1, plan.tokens), F32), acc, acc), 40_000_000_000,
    )[0]


def near_rows(values, norm_gain, norm_shift):
    centred = values - jnp.mean(values, 1, keepdims=True)
    inverse = lax.rsqrt(jnp.mean(centred * centred, 1, keepdims=True) + EPS)
    normed = centred * inverse
    return normed * norm_gain + norm_shift, normed, inverse


def back_rows(grad_out, normed, inverse, norm_gain):
    grad_norm = grad_out * norm_gain
    return inverse * (
        grad_norm
        - jnp.mean(grad_norm, 1, keepdims=True)
        - normed * jnp.mean(grad_norm * normed, 1, keepdims=True)
    )


def own_columns(size, unit, core):
    row, col = iota((size, size), 0), iota((size, size), 1)
    half = size // 2
    other = row >= half
    place = jnp.where(other, row - half, row)
    whole = jnp.floor((place.astype(F32) + 0.5) * (1.0 / unit)).astype(jnp.int32)
    parity = jnp.where(other, 1 - core, core)
    return jnp.where(col == place + unit * (whole + parity), 1.0, 0.0).astype(BF)


def middle_kernel(
    unit_up, unit, core_ref, attn_ref, tiles_ref, out_w, out_b, gain, shift, up_w, up_b, down_w, down_b, g_ref,
    y_ref, res_ref, ag_ref, common_ref, mine_ref, theirs_ref, sums_ref, up_sum_ref,
    pick_up, normed_s, lifted_s, inverse_s, out_s, back_s,
):
    step, steps = pl.program_id(0), pl.num_programs(0)
    width = tiles_ref.shape[1]
    chunk = up_w.shape[1]
    half = chunk // 2
    core = core_ref[0]
    hidden_sel = steps * half

    @pl.when(step == 0)
    def _():
        pick_up[...] = own_columns(chunk, unit_up, core)
        residual = tiles_ref[...].astype(F32) + dot_tn(attn_ref[...], out_w[...]) + out_b[...]
        lifted, normed, inverse = near_rows(residual, gain[...], shift[...])
        low = lifted.astype(BF)
        lifted_s[...] = low
        normed_s[...] = normed
        inverse_s[...] = jnp.broadcast_to(inverse, inverse_s.shape)
        out_s[...] = residual + down_b[...]
        back_s[...] = jnp.zeros_like(back_s)
        common_ref[pl.ds(steps * chunk, width), :] = low.T
        pick = own_columns(width, unit, core)
        picked_g = dot_nt(pick, g_ref[...]).astype(BF)
        mine_ref[pl.ds(hidden_sel, width // 2), :] = picked_g[: width // 2]
        theirs_ref[pl.ds(hidden_sel, width // 2), :] = picked_g[width // 2 :]

    lifted = lifted_s[...]
    gate_in = dot_nn(lifted, up_w[...]) + up_b[...]
    cdf = 0.5 + 0.5 * lax.erf(gate_in * (0.5**0.5))
    act = (gate_in * cdf).astype(BF)
    slope = cdf + gate_in * (jnp.exp(-0.5 * gate_in * gate_in) * (1.0 / math.sqrt(2.0 * math.pi)))
    gate_grad = (dot_nt(g_ref[...], down_w[...]) * slope).astype(BF)
    out_s[...] += dot_nn(act, down_w[...])
    back_s[...] += dot_nt(gate_grad, up_w[...])
    up_sum_ref[...] = jnp.sum(gate_grad.astype(F32), 0, keepdims=True)
    common_ref[pl.ds(pl.multiple_of(step * chunk, chunk), chunk), :] = act.T
    picked_gate = dot_nt(pick_up[...], gate_grad).astype(BF)
    at = pl.ds(pl.multiple_of(step * half, half), half)
    mine_ref[at, :] = picked_gate[:half]
    theirs_ref[at, :] = picked_gate[half:]

    @pl.when(step == steps - 1)
    def _():
        y_ref[...] = out_s[...].astype(BF)
        grads = g_ref[...].astype(F32)
        lifted_grad = back_s[...]
        normed = normed_s[...]
        residual_grad = grads + back_rows(lifted_grad, normed, inverse_s[:, :1], gain[...])
        res_ref[...] = residual_grad
        low = residual_grad.astype(BF)
        ag_ref[...] = dot_nt(out_w[...], low).astype(BF)
        pick = own_columns(width, unit, core)
        picked_p = dot_nt(pick, low).astype(BF)
        at = pl.ds(hidden_sel + width // 2, width // 2)
        mine_ref[at, :] = picked_p[: width // 2]
        theirs_ref[at, :] = picked_p[width // 2 :]
        sums_ref[0:1, :] = jnp.sum(grads, 0, keepdims=True)
        sums_ref[1:2, :] = jnp.sum(residual_grad, 0, keepdims=True)
        sums_ref[2:3, :] = jnp.sum(lifted_grad * normed, 0, keepdims=True)
        sums_ref[3:4, :] = jnp.sum(lifted_grad, 0, keepdims=True)
        sums_ref[4:8, :] = jnp.zeros((4, width), F32)


def middle_call(devices, core, attn_t, tiles, out_w, out_b, gain, shift, up_w, up_b, down_w, down_b, g):
    tq, width = tiles.shape
    hidden = up_w.shape[1]
    steps = hidden // width
    whole = lambda *shape: pl.BlockSpec(shape, lambda j: (0,) * len(shape))
    vec = whole(1, width)
    sel = hidden // 2 + width
    return pl.pallas_call(
        functools.partial(middle_kernel, hidden // devices, width // devices),
        grid=(steps,),
        in_specs=[
            SMEM, whole(width, tq), whole(tq, width), whole(width, width), vec, vec, vec,
            pl.BlockSpec((width, width), lambda j: (0, j)), pl.BlockSpec((1, width), lambda j: (0, j)),
            pl.BlockSpec((width, width), lambda j: (j, 0)), vec, whole(tq, width),
        ],
        out_specs=(
            whole(tq, width), whole(tq, width), whole(width, tq), whole(hidden + width, tq), whole(sel, tq),
            whole(sel, tq), whole(8, width), pl.BlockSpec((1, width), lambda j: (0, j)),
        ),
        out_shape=(
            jax.ShapeDtypeStruct((tq, width), BF),
            jax.ShapeDtypeStruct((tq, width), F32),
            jax.ShapeDtypeStruct((width, tq), BF),
            jax.ShapeDtypeStruct((hidden + width, tq), BF),
            jax.ShapeDtypeStruct((sel, tq), BF),
            jax.ShapeDtypeStruct((sel, tq), BF),
            jax.ShapeDtypeStruct((8, width), F32),
            jax.ShapeDtypeStruct((1, hidden), F32),
        ),
        scratch_shapes=[
            pltpu.VMEM((width, width), BF), pltpu.VMEM((tq, width), F32), pltpu.VMEM((tq, width), BF),
            pltpu.VMEM((tq, LANES), F32), pltpu.VMEM((tq, width), F32), pltpu.VMEM((tq, width), F32),
        ],
        compiler_params=PARAMS,
        cost_estimate=pl.CostEstimate(flops=14 * tq * width * hidden, bytes_accessed=20 << 20, transcendentals=0),
        name="middle",
    )(core, attn_t, tiles, out_w, out_b, gain, shift, up_w, up_b, down_w, down_b, g)


def weights_kernel(unit_up, unit, meta, attn_a, attn_b, common_a, common_b, sel_a, sel_b, *rest):
    first_s, second_refs, second_s = rest[0], rest[1:5], rest[5]
    width = attn_a.shape[0]
    hidden = common_a.shape[0] - width
    chips = width // (2 * unit)

    def spot(chip):
        return (chip // 8) * 2 + chip % 2, chip // 2 % 4

    lifted = slice(hidden, hidden + width)
    group = width // (2 * unit_up)
    for step in range(hidden // width):
        rows = slice(step * width // 2, (step + 1) * width // 2)
        part = dot_nt(sel_a[rows, :], common_a[lifted, :]) + dot_nt(sel_b[rows, :], common_b[lifted, :])
        for i in range(group):
            plane, line = spot(step * group + i)
            first_s[plane, line, :unit_up, :] = part[i * unit_up : (i + 1) * unit_up].astype(BF)
    rows_out = slice(hidden // 2 + width // 2, hidden // 2 + width)
    rows = slice(hidden // 2, hidden // 2 + width // 2)
    out = dot_nt(sel_a[rows_out, :], attn_a[...]) + dot_nt(sel_b[rows_out, :], attn_b[...])
    held = [out]
    for step in range(hidden // width):
        cols = slice(step * width, (step + 1) * width)
        part = dot_nt(sel_a[rows, :], common_a[cols, :]) + dot_nt(sel_b[rows, :], common_b[cols, :])
        if step < FIRST_DOWN:
            held.append(part)
            continue
        at = (step - FIRST_DOWN) * width
        for chip in range(chips):
            plane, line = spot(chip)
            second_s[line, plane, :, at : at + width] = part[chip * unit : (chip + 1) * unit].astype(BF)
    for chip in range(chips):
        plane, line = spot(chip)
        at = slice(chip * unit, (chip + 1) * unit)
        first_s[plane, line, unit_up:, :] = jnp.concatenate([part[at] for part in held], 0).astype(BF)
    for k in range(4):
        second_refs[k][...] = second_s[meta[5] ^ k]


def weights_call(devices, meta, attn_a, attn_b, common_a, common_b, sel_a, sel_b):
    width, tq = attn_a.shape
    hidden = common_a.shape[0] - width
    unit_up, unit = hidden // devices, width // devices
    first = (4, 4, unit_up + (1 + FIRST_DOWN) * unit, width)
    second = (4, unit, hidden - FIRST_DOWN * width)
    outs = pl.pallas_call(
        functools.partial(weights_kernel, unit_up, unit),
        in_specs=[SMEM] + [VMEM] * 6,
        out_specs=(VMEM,) * 5,
        out_shape=(jax.ShapeDtypeStruct(first, BF),) + (jax.ShapeDtypeStruct(second, BF),) * 4,
        scratch_shapes=[pltpu.VMEM((4,) + second, BF)],
        compiler_params=PARAMS,
        cost_estimate=pl.CostEstimate(flops=4 * tq * width * hidden, bytes_accessed=14 << 20, transcendentals=0),
        name="weights",
    )(meta, attn_a, attn_b, common_a, common_b, sel_a, sel_b)
    return outs[0], outs[1:]


def fold_kernel(meta, first_ref, own, got1, got2, got3, *outs):
    plane, line = meta[4], meta[5]
    for k in range(4):
        at = line ^ k
        total = first_ref[0, at].astype(F32)
        for i in range(1, 4):
            total += first_ref[i, at].astype(F32)
        outs[k][...] = total.astype(BF)
        at = plane ^ k
        total = own[at].astype(F32) + got1[at].astype(F32) + got2[at].astype(F32) + got3[at].astype(F32)
        outs[4 + k][...] = total.astype(BF)


def fold_call(meta, first, second):
    shapes = [jax.ShapeDtypeStruct(first.shape[2:], BF)] * 4 + [jax.ShapeDtypeStruct(second[0].shape[1:], BF)] * 4
    outs = pl.pallas_call(
        fold_kernel,
        in_specs=[SMEM] + [VMEM] * 5,
        out_specs=(VMEM,) * 8,
        out_shape=tuple(shapes),
        compiler_params=PARAMS,
        name="fold",
    )(meta, first, *second)
    return outs[:4], outs[4:]


def last_kernel(unit_up, unit, *refs):
    first, second, (up_ref, out_ref, down_ref) = refs[:4], refs[4:8], refs[8:]
    total = first[0][...].astype(F32)
    for ref in first[1:]:
        total += ref[...].astype(F32)
    up_ref[...] = total[:unit_up]
    out_ref[...] = total[unit_up : unit_up + unit]
    width = total.shape[1]
    for i in range(FIRST_DOWN):
        at = unit_up + (1 + i) * unit
        down_ref[:, i * width : (i + 1) * width] = total[at : at + unit]
    width = FIRST_DOWN * width
    total = second[0][...].astype(F32)
    for ref in second[1:]:
        total += ref[...].astype(F32)
    down_ref[:, width:] = total


def last_call(unit_up, unit, first, second):
    width = first[0].shape[1]
    hidden = FIRST_DOWN * width + second[0].shape[1]
    return pl.pallas_call(
        functools.partial(last_kernel, unit_up, unit),
        in_specs=[VMEM] * 8,
        out_specs=(VMEM,) * 3,
        out_shape=tuple(jax.ShapeDtypeStruct(s, F32) for s in ((unit_up, width), (unit, width), (unit, hidden))),
        compiler_params=PARAMS,
        name="last",
    )(*first, *second)


def enter_kernel(tiles_ref, gain, shift, w_ref, query_b, value_b, x_ref, npre_ref, low_s):
    part = pl.program_id(0)

    @pl.when((part == 0) & (pl.program_id(1) == 0))
    def _():
        scaled, normed, _ = near_rows(tiles_ref[...].astype(F32), gain[...], shift[...])
        low_s[...] = scaled.astype(BF)
        npre_ref[...] = normed.astype(BF)

    bias = jnp.where(part == 0, query_b[...], jnp.where(part == 2, value_b[...], 0.0))
    joined = (dot_nn(low_s[...], w_ref[...]) + bias).astype(BF).T
    size = x_ref.shape[2]
    for i in range(x_ref.shape[0]):
        x_ref[i, 0] = joined[i * size : (i + 1) * size]


def enter_call(heads, tiles, gain, shift, weight, query_b, value_b):
    tq, width = tiles.shape
    size = width // heads
    half = width // 2
    whole = lambda *shape: pl.BlockSpec(shape, lambda i, j: (0,) * len(shape))
    vec = whole(1, width)
    bias = pl.BlockSpec((1, half), lambda i, j: (0, j))
    return pl.pallas_call(
        enter_kernel,
        grid=(3, 2),
        in_specs=[whole(tq, width), vec, vec, pl.BlockSpec((width, half), lambda i, j: (0, i * 2 + j)), bias, bias],
        out_specs=(pl.BlockSpec((heads // 2, 1, size, tq), lambda i, j: (j, i, 0, 0)), whole(tq, width)),
        out_shape=(jax.ShapeDtypeStruct((heads, 3, size, tq), BF), jax.ShapeDtypeStruct((tq, width), BF)),
        scratch_shapes=[pltpu.VMEM((tq, width), BF)],
        compiler_params=PARAMS,
        name="enter",
    )(tiles, gain, shift, weight, query_b, value_b)


def leave_kernel(tiles_ref, gain, w_ref, jg_ref, res_ref, out_ref, acc):
    first = (pl.program_id(0) == 0) & (pl.program_id(1) == 0)

    @pl.when(first)
    def _():
        acc[...] = jnp.zeros_like(acc)

    heads, size = jg_ref.shape[0], jg_ref.shape[2]
    grads = jnp.concatenate([jg_ref[i, 0] for i in range(heads)], 0)
    acc[...] += dot_nt(grads.T, w_ref[...])

    @pl.when((pl.program_id(0) == 2) & (pl.program_id(1) == 1))
    def _():
        _, normed, inverse = near_rows(tiles_ref[...].astype(F32), gain[...], gain[...])
        out_ref[...] = (res_ref[...] + back_rows(acc[...], normed, inverse, gain[...])).astype(BF)


def leave_call(tiles, gain, weight, joined_grad, residual_grad):
    tq, width = tiles.shape
    heads, _, size, _ = joined_grad.shape
    half = width // 2
    whole = lambda *shape: pl.BlockSpec(shape, lambda i, j: (0,) * len(shape))
    return pl.pallas_call(
        leave_kernel,
        grid=(3, 2),
        in_specs=[
            whole(tq, width), whole(1, width), pl.BlockSpec((width, half), lambda i, j: (0, i * 2 + j)),
            pl.BlockSpec((heads // 2, 1, size, tq), lambda i, j: (j, i, 0, 0)), whole(tq, width),
        ],
        out_specs=whole(tq, width),
        out_shape=jax.ShapeDtypeStruct((tq, width), BF),
        scratch_shapes=[pltpu.VMEM((tq, width), F32)],
        compiler_params=PARAMS,
        name="leave",
    )(tiles, gain, weight, joined_grad, residual_grad)


def halo_hits(plan, offs, first, dims):
    wide = max(plan.sel, LANES)
    shape = (plan.tq, wide)
    token, col = iota(shape, 0) + first, iota(shape, 1)
    hit = col < 0
    for branch in plan.branches:
        if branch["extra"]:
            at = col - branch["sel"]
            inside = (at >= 0) & (at < branch["extra"])
            hit |= inside & (token == at * branch["rate"] + offs[branch["level"]])
    return jnp.where(hit, 1.0, 0.0).astype(BF)


def halo_blocks(plan):
    count = plan.halo // plan.tq
    for i in range(count):
        yield 0, plan.blocks - count + i, i * plan.tq
        yield 1, i, i * plan.tq


def static_slot(plan, block):
    return block % plan.groups * plan.members + block // plan.groups


def select_kernel(plan, meta, offsets, x_ref, *outs):
    offs = [offsets[b["level"], meta[1]] for b in plan.branches]
    if plan.paired:
        count = plan.halo // plan.tq
        total = jnp.zeros((2 * plan.size, max(plan.sel, LANES)), F32)
        for i in range(count):
            block = (1 - meta[2]) * (plan.blocks - count) + i
            total += dot_nn(x_ref[plan.slot(block), plan.size :, :], halo_hits(plan, offs, i * plan.tq, None))
        outs[0][...] = total.astype(BF)
        return
    last_ref, first_ref = outs
    total = [jnp.zeros((2 * plan.size, max(plan.sel, LANES)), F32) for _ in range(2)]
    for side, block, first in halo_blocks(plan):
        hits = halo_hits(plan, offs, first, None)
        total[side] += dot_nn(x_ref[static_slot(plan, block), plan.size :, :], hits)
    last_ref[...] = total[0].astype(BF)
    first_ref[...] = total[1].astype(BF)


def select_call(plan, meta, offsets, x):
    shape = jax.ShapeDtypeStruct((2 * plan.size, max(plan.sel, LANES)), BF)
    return pl.pallas_call(
        functools.partial(select_kernel, plan),
        in_specs=[SMEM, SMEM, VMEM],
        out_specs=(VMEM,) * (1 if plan.paired else 2),
        out_shape=(shape,) * (1 if plan.paired else 2),
        compiler_params=PARAMS,
        name="select",
    )(meta, offsets, x)


def to_owners(vector, owner, lane_of, devices):
    count = vector.shape[1]
    held = jnp.where(iota((devices, count), 0) == owner, vector, 0.0)
    hits = jnp.where(iota((count, LANES), 1) == lane_of, 1.0, 0.0)
    return lax.dot_general(
        held, hits, (((1,), (0,)), ((), ())), precision=lax.Precision.HIGHEST, preferred_element_type=F32
    )


def cut(index, unit):
    whole = jnp.floor((index.astype(F32) + 0.5) * (1.0 / unit)).astype(jnp.int32)
    return whole, index - whole * unit


def head_kernel(devices, meta, dx_ref, near_ref, w_ref, gain, shift, sums_ref, up_ref, keep_ref, give_ref, small_ref, acc, col_s, row_s):
    step, steps = pl.program_id(0), pl.num_programs(0)
    tq = dx_ref.shape[2]
    rows = dx_ref.shape[1]
    per = near_ref.shape[0] // tq
    size = rows // 3
    width = near_ref.shape[1]

    @pl.when(step == 0)
    def _():
        acc[...] = jnp.zeros_like(acc)
        col_s[...] = jnp.zeros_like(col_s)
        row_s[...] = jnp.zeros_like(row_s)

    for i in range(per):
        grads = dx_ref[i]
        acc[...] += dot_nn(grads, near_ref[i * tq : (i + 1) * tq, :])
        col_s[...] += jnp.broadcast_to(jnp.sum(grads.astype(F32), 1, keepdims=True), col_s.shape)
        row_s[...] += dot_nt(jnp.ones((8, tq), BF), grads)

    @pl.when(step == steps - 1)
    def _():
        grp, head = meta[2], meta[1]
        plain = acc[...]
        weight = plain * gain[...] + col_s[:, :1] * shift[...]
        for part in range(3):
            lower = weight[part * size : part * size + size // 2]
            upper = weight[part * size + size // 2 : (part + 1) * size]
            keep_ref[part] = jnp.where(grp == 0, lower, upper).astype(BF)
            give_ref[part] = jnp.where(grp == 0, upper, lower).astype(BF)
        own = w_ref[...].astype(F32)
        gain_part = jnp.sum(own * plain, 0, keepdims=True)
        shift_part = jnp.sum(own * col_s[:, :1], 0, keepdims=True)
        unit = width // devices
        owner = cut(iota((1, width), 1), unit)[0]
        lane = cut(iota((width, 1), 0), unit)[1]
        small_ref[:, 0, :] = to_owners(gain_part, owner, lane, devices)
        small_ref[:, 1, :] = to_owners(shift_part, owner, lane, devices)
        held = jnp.zeros((devices, LANES), F32)
        for i in range(4):
            held += to_owners(sums_ref[i : i + 1, :], owner, lane + i * unit, devices)
        small_ref[:, 2, :] = held
        hidden = up_ref.shape[1]
        unit_up = hidden // devices
        held = jnp.zeros((devices, LANES), F32)
        for i in range(hidden // width):
            owner_up = cut(iota((1, width), 1) + i * width, unit_up)[0]
            lane_up = cut(iota((width, 1), 0) + i * width, unit_up)[1]
            held += to_owners(up_ref[:, i * width : (i + 1) * width], owner_up, lane_up, devices)
        small_ref[:, 3, :] = held
        line = row_s[0:1, :]
        for i, part in enumerate((0, 2)):
            index = iota((1, rows), 1) - part * size
            inside = (index >= 0) & (index < size)
            owner_h = jnp.where(inside, 2 * head + cut(index, size // 2)[0], -1)
            lane_h = cut(iota((rows, 1), 0), size // 2)[1]
            small_ref[:, 4 + i, :] = to_owners(line, owner_h, lane_h, devices)
        small_ref[:, 6, :] = jnp.zeros((devices, LANES), F32)
        small_ref[:, 7, :] = jnp.zeros((devices, LANES), F32)


def head_call(devices, meta, dx, npre_all, own_w, gain, shift, sums, up_sums):
    blocks, rows, tq = dx.shape
    width = npre_all.shape[1]
    per = blocks // 4
    whole = lambda *shape: pl.BlockSpec(shape, lambda i: (0,) * len(shape))
    return pl.pallas_call(
        functools.partial(head_kernel, devices),
        grid=(4,),
        in_specs=[
            SMEM, pl.BlockSpec((per, rows, tq), lambda i: (i, 0, 0)), pl.BlockSpec((per * tq, width), lambda i: (i, 0)),
            whole(rows, width), whole(1, width), whole(1, width), whole(8, width), whole(1, up_sums.shape[1]),
        ],
        out_specs=(whole(3, rows // 6, width), whole(3, rows // 6, width), whole(devices, 8, LANES)),
        out_shape=(
            jax.ShapeDtypeStruct((3, rows // 6, width), BF),
            jax.ShapeDtypeStruct((3, rows // 6, width), BF),
            jax.ShapeDtypeStruct((devices, 8, LANES), F32),
        ),
        scratch_shapes=[
            pltpu.VMEM((rows, width), F32), pltpu.VMEM((rows, LANES), F32), pltpu.VMEM((8, rows), F32),
        ],
        compiler_params=PARAMS,
        cost_estimate=pl.CostEstimate(flops=6_000_000_000, bytes_accessed=8 << 20, transcendentals=0),
        name="head",
    )(meta, dx, npre_all, own_w, gain, shift, sums, up_sums)


def units_kernel(meta, keep, got, *outs):
    for slot, ref in enumerate(outs):
        part = meta[6 + slot]
        ref[...] = (keep[part].astype(F32) + got[part].astype(F32)).astype(BF)


def units_call(meta, keep, got):
    return pl.pallas_call(
        units_kernel,
        in_specs=[SMEM, VMEM, VMEM],
        out_specs=(VMEM,) * 3,
        out_shape=(jax.ShapeDtypeStruct(keep.shape[1:], BF),) * 3,
        compiler_params=PARAMS,
        name="units",
    )(meta, keep, got)


def layer_norm_rows(values, norm_gain, norm_shift):
    row_mean = jnp.mean(values, -1, keepdims=True)
    centred = values - row_mean
    inverse = lax.rsqrt(jnp.mean(centred * centred, -1, keepdims=True) + EPS)
    normed = centred * inverse
    return (normed * norm_gain + norm_shift, normed, inverse)


def norm_back(grad_out, normed, inverse, norm_gain):
    grad_norm = grad_out * norm_gain
    grad_in = inverse * (
        grad_norm
        - jnp.mean(grad_norm, -1, keepdims=True)
        - normed * jnp.mean(grad_norm * normed, -1, keepdims=True)
    )
    return (grad_in, jnp.sum(grad_out * normed, 0), jnp.sum(grad_out, 0))


def swap(values, axes):
    return lax.all_to_all(values, axes, 0, 0, tiled=True)


def scatter_sum(values, orders):
    sizes = {name: lax.axis_size(name) for name in ALL}
    left = list(ALL)
    rows, cols = values.shape[1:]
    for stage, axes in enumerate(orders):
        values = values.reshape([sizes[name] for name in left] + [rows, cols])
        rest = [name for name in left if name not in axes]
        order = [left.index(name) for name in list(axes) + rest]
        values = values.transpose(order + [len(left), len(left) + 1])
        count = math.prod(sizes[name] for name in axes)
        values = values.reshape((count, -1, rows, cols))
        if count > 1:
            values = swap(values, axes)
            values = jnp.sum(values.astype(F32), 0)
            if stage < len(orders) - 1:
                values = values.astype(BF)
        left = rest
    return values.reshape(rows, cols).astype(F32)


def to_neighbours(pieces, count):
    if count == 2:
        return (lax.ppermute(pieces[0], "grp", [(0, 1), (1, 0)]),)
    return (
        lax.ppermute(pieces[0], "grp", [(i, i + 1) for i in range(count - 1)]),
        lax.ppermute(pieces[1], "grp", [(i + 1, i) for i in range(count - 1)]),
    )


def from_neighbours(pieces, count):
    return to_neighbours(pieces[::-1], count)[::-1]


def share_columns(weight_t, sums, width):
    members, size = lax.axis_size(GROUP), weight_t.shape[1]
    head = lax.axis_index(GROUP)
    full = jnp.zeros((3, members) + weight_t.shape[1:], F32)
    full = lax.dynamic_update_slice(full, weight_t[:, None], (0, head, 0, 0))
    full_sums = lax.dynamic_update_slice(jnp.zeros((3, members, size), F32), sums[:, None], (0, head, 0))
    weight = lax.psum_scatter(full.reshape(3 * members * size, width), ALL, scatter_dimension=0, tiled=True)
    sums = lax.psum_scatter(full_sums.reshape(3, members * size), ALL, scatter_dimension=1, tiled=True)
    return weight, sums[0], sums[2]


def body(
    tile_embed,
    slide_lengths,
    head_offsets,
    pre_gain,
    pre_shift,
    qkv_weight,
    query_bias,
    value_bias,
    out_weight,
    out_bias,
    post_gain,
    post_shift,
    up_weight,
    up_bias,
    down_weight,
    down_bias,
    out_grad,
):
    width = qkv_weight.shape[0]
    hidden = up_weight.shape[1]
    heads = head_offsets.shape[1]
    size = width // heads
    tq = tile_embed.shape[1]
    br, groups = lax.axis_size("br"), lax.axis_size("grp")
    members = heads // br
    devices = heads * groups
    plan = Plan(heads, size, head_offsets.shape[0], br, members, tq, devices * tq)
    head = lax.axis_index(GROUP)
    base = lax.axis_index("grp") * plan.tokens
    meta = jnp.stack([base, head, lax.axis_index("grp")]).astype(jnp.int32)

    tiles = tile_embed[0].astype(F32)
    pre_out, normed_pre, inverse_pre = layer_norm_rows(tiles, pre_gain, pre_shift)
    normed_low = pre_out.astype(BF)
    bias_col = jnp.concatenate([query_bias, jnp.zeros_like(query_bias), value_bias], 1).reshape(-1, 1)
    joined_t = (
        lax.dot_general(qkv_weight, normed_low, (((0,), (1,)), ((), ())), preferred_element_type=F32) + bias_col
    ).astype(BF)
    x = joined_t.reshape(3, heads, size, tq).transpose(1, 0, 2, 3).reshape(heads, 3 * size, tq)
    x = swap(x, GROUP)
    normed_all = lax.all_gather(normed_low, GROUP, axis=0, tiled=True)

    halo = to_neighbours(select_call(plan, meta, head_offsets, x), groups)
    state, *own = near_call(plan, meta, slide_lengths, head_offsets, x)
    mixed, state = far_call(plan, meta, slide_lengths, head_offsets, state, own, halo)
    attn_t = swap(mixed, GROUP).reshape(width, tq)

    projected = lax.dot_general(attn_t, out_weight, (((0,), (0,)), ((), ())), preferred_element_type=F32)
    residual = tiles + projected + out_bias
    post_out, normed_post, inverse_post = layer_norm_rows(residual, post_gain, post_shift)
    lifted = post_out.astype(BF)
    gate_in = jnp.dot(lifted, up_weight, preferred_element_type=F32) + up_bias
    act_float, gelu_pull = jax.vjp(lambda v: jax.nn.gelu(v, approximate=False), gate_in)
    act_low = act_float.astype(BF)
    layer_out = (residual + jnp.dot(act_low, down_weight, preferred_element_type=F32) + down_bias).astype(BF)[None]
    grad_low = out_grad[0]
    grad_float = grad_low.astype(F32)
    act_grad = lax.dot_general(grad_low, down_weight, (((1,), (1,)), ((), ())), preferred_element_type=F32)
    gate_grad = gelu_pull(act_grad)[0].astype(BF)
    lifted_grad = lax.dot_general(gate_grad, up_weight, (((1,), (1,)), ((), ())), preferred_element_type=F32)
    norm_part, post_gain_sum, post_shift_sum = norm_back(lifted_grad, normed_post, inverse_post, post_gain)
    residual_grad = grad_float + norm_part
    proj_grad = residual_grad.astype(BF)
    attn_grad_t = lax.dot_general(
        out_weight, proj_grad, (((1,), (1,)), ((), ())), preferred_element_type=F32
    ).astype(BF)
    do = swap(attn_grad_t.reshape(heads, size, tq), GROUP)

    tokens = (((0,), (0,)), ((), ()))
    up_part = lax.dot_general(gate_grad, lifted, tokens, preferred_element_type=F32).astype(BF)
    down_part = lax.dot_general(grad_low, act_low, tokens, preferred_element_type=F32).astype(BF)
    out_part = lax.dot_general(proj_grad, attn_t, (((0,), (1,)), ((), ())), preferred_element_type=F32).astype(BF)
    vectors = [
        jnp.sum(gate_grad.astype(F32), 0).reshape(devices, -1),
        jnp.sum(grad_float, 0).reshape(devices, -1),
        jnp.sum(residual_grad, 0).reshape(devices, -1),
        post_gain_sum.reshape(devices, -1),
        post_shift_sum.reshape(devices, -1),
    ]
    ends = [0]
    for vector in vectors:
        ends.append(ends[-1] + vector.shape[1])
    small = jnp.concatenate(vectors, 1)
    small = jnp.pad(small[:, None, :], ((0, 0), (0, 7), (0, width - small.shape[1]))).astype(BF)
    misc = jnp.concatenate([out_part.reshape(devices, -1, width), small], 1)
    first, second = (("s0",), ("br", "s1"), ("grp", "s2")), (("s0",), ("grp", "s2"), ("br", "s1"))
    up_own = scatter_sum(up_part.reshape(devices, -1, width), first)
    down_own = scatter_sum(down_part.reshape(devices, -1, hidden), second)
    misc_own = scatter_sum(misc, first)
    unit = width // devices
    small_own = misc_own[unit]
    small_own = [small_own[None, ends[i] : ends[i + 1]] for i in range(len(vectors))]

    rows, dq, dk, dv, *sides = far_back_call(plan, meta, slide_lengths, head_offsets, state, do, own, halo)
    back = from_neighbours(sides, groups)
    dx = near_back_call(plan, meta, slide_lengths, head_offsets, x, state, rows, (dq, dk, dv), back)
    joined_grad_t = swap(dx, GROUP).reshape(heads, 3, size, tq).transpose(1, 0, 2, 3).reshape(3 * width, tq)
    weight_t = jnp.einsum(
        "nct,ntd->cd", dx, normed_all.reshape(heads, tq, width), preferred_element_type=F32
    ).reshape(3, size, width)
    head_sums = jnp.sum(dx.astype(F32), (0, 2)).reshape(3, size)
    qkv_own, query_own, value_own = share_columns(weight_t, head_sums, width)
    normed_grad = lax.dot_general(joined_grad_t, qkv_weight, (((0,), (1,)), ((), ())), preferred_element_type=F32)
    tile_part, pre_gain_sum, pre_shift_sum = norm_back(normed_grad, normed_pre, inverse_pre, pre_gain)
    tile_grad = (residual_grad + tile_part).astype(BF)[None]
    last = jnp.stack([pre_gain_sum, pre_shift_sum]).reshape(2, devices, unit).transpose(1, 0, 2)
    last = jnp.pad(last, ((0, 0), (0, 6), (0, LANES - unit)))
    last = jnp.sum(swap(last, ALL).reshape(devices, 8, LANES), 0)
    return (
        layer_out,
        tile_grad,
        last[0:1, :unit],
        last[1:2, :unit],
        qkv_own.T,
        query_own[None],
        value_own[None],
        misc_own[:unit].T,
        small_own[2],
        small_own[3],
        small_own[4],
        up_own.T,
        small_own[0],
        down_own.T,
        small_own[1],
    )


def across(piece, axes, k):
    return lax.ppermute(piece, axes, [(i, i ^ k) for i in range(4)])


def owner_places():
    sizes = [lax.axis_size(name) for name in ALL]
    inner = sizes[2] * sizes[3] * sizes[4]
    place = {}
    for br in range(sizes[0]):
        for grp in range(sizes[1]):
            for sub in range(inner):
                place[(br * inner + sub) * sizes[1] + grp] = (br * sizes[1] + grp) * inner + sub
    return place


def unit_routes():
    place = owner_places()
    devices = len(place)
    for slot in range(3):
        route, part_of = [], [0] * devices
        for owner in range(devices):
            part, which = divmod(3 * owner + slot, devices)
            route.append((place[which], owner))
            part_of[place[which]] = part
        yield route, part_of


def fast_body(
    tile_embed, slide_lengths, head_offsets, pre_gain, pre_shift, qkv_weight, query_bias, value_bias, out_weight,
    out_bias, post_gain, post_shift, up_weight, up_bias, down_weight, down_bias, out_grad,
):
    width = qkv_weight.shape[0]
    heads = head_offsets.shape[1]
    size = width // heads
    tq = tile_embed.shape[1]
    br, groups = lax.axis_size("br"), lax.axis_size("grp")
    members = heads // br
    devices = heads * groups
    plan = Plan(heads, size, head_offsets.shape[0], br, members, tq, devices * tq)
    head = lax.axis_index(GROUP)
    group = lax.axis_index("grp")
    core = lax.axis_index("s0")
    meta = [group * plan.tokens, head, group, core, lax.axis_index(("br", "s1")), lax.axis_index(("grp", "s2"))]
    here = lax.axis_index(ALL)
    routes = []
    for route, part_of in unit_routes():
        routes.append(route)
        meta.append(jnp.array(part_of, jnp.int32)[here])
    meta = jnp.stack(meta).astype(jnp.int32)
    tiles = tile_embed[0]
    own_w = jnp.concatenate(
        [lax.dynamic_slice_in_dim(qkv_weight, part * width + head * size, size, 1) for part in range(3)], 1
    ).T
    pair = [(0, 1), (1, 0)]
    plane, line = ("br", "s1"), ("grp", "s2")

    x, npre = enter_call(heads, tiles, pre_gain, pre_shift, qkv_weight, query_bias, value_bias)
    x = swap(x.reshape(heads, 3 * size, tq), GROUP)
    x, npre, own_w, meta = lax.optimization_barrier((x, npre, own_w, meta))
    halo = to_neighbours(select_call(plan, meta, head_offsets, x), groups)
    state, *own = near_call(plan, meta, slide_lengths, head_offsets, x)
    mixed, state = far_call(plan, meta, slide_lengths, head_offsets, state, own, halo)
    attn_t = swap(mixed, GROUP).reshape(width, tq)
    npre_all = lax.all_gather(npre, GROUP, axis=0, tiled=True)
    attn_t, npre_all = lax.optimization_barrier((attn_t, npre_all))

    attn_b = lax.ppermute(attn_t, "s0", pair)
    layer_out, residual_grad, attn_grad_t, common, sel, sel_give, sums, up_sums = middle_call(
        devices, core[None].astype(jnp.int32), attn_t, tiles, out_weight, out_bias, post_gain, post_shift,
        up_weight, up_bias, down_weight, down_bias, out_grad[0],
    )
    do = swap(attn_grad_t.reshape(heads, size, tq), GROUP)
    common_b = lax.ppermute(common, "s0", pair)
    sel_b = lax.ppermute(sel_give, "s0", pair)
    first, second = weights_call(devices, meta, attn_t, attn_b, common, common_b, sel, sel_b)
    do, first, second = lax.optimization_barrier((do, first, second))
    first = swap(first, plane)
    second = [second[0]] + [across(second[k], line, k) for k in (1, 2, 3)]
    rows, dq, dk, dv, *sides = far_back_call(plan, meta, slide_lengths, head_offsets, state, do, own, halo)
    back = from_neighbours(sides, groups)
    dx = near_back_call(plan, meta, slide_lengths, head_offsets, x, state, rows, (dq, dk, dv), back)
    dx, first, second = lax.optimization_barrier((dx, first, second))
    joined_grad = swap(dx, GROUP).reshape(heads, 3, size, tq)
    keep, give, small = head_call(devices, meta, dx, npre_all, own_w, pre_gain, pre_shift, sums, up_sums)
    joined_grad, small = lax.optimization_barrier((joined_grad, small))
    small = jnp.sum(swap(small, ALL), 0)
    units = units_call(meta, keep, lax.ppermute(give, "grp", pair))
    units = [lax.ppermute(unit, ALL, route) for unit, route in zip(units, routes)]
    qkv_own = jnp.concatenate(units).astype(F32)
    first, second = fold_call(meta, first, second)
    first = [first[0]] + [across(first[k], line, k) for k in (1, 2, 3)]
    second = [second[0]] + [across(second[k], plane, k) for k in (1, 2, 3)]
    tile_grad = leave_call(tiles, pre_gain, qkv_weight, joined_grad, residual_grad)
    unit_up, unit = up_weight.shape[1] // devices, width // devices
    up_own, out_own, down_own = last_call(unit_up, unit, first, second)
    return (
        layer_out[None],
        tile_grad[None],
        small[0:1, :unit],
        small[1:2, :unit],
        qkv_own.T,
        small[4:5, :unit],
        small[5:6, :unit],
        out_own.T,
        small[2:3, unit : 2 * unit],
        small[2:3, 2 * unit : 3 * unit],
        small[2:3, 3 * unit : 4 * unit],
        up_own.T,
        small[3:4, :unit_up],
        down_own.T,
        small[2:3, :unit],
    )


def solution(mesh):
    br, rows = mesh.shape["br"], mesh.shape["rows"]

    def run(*args):
        members = args[2].shape[1] // br
        shape = (br, rows // members, members // 4, 2, 2)
        split = jax.sharding.Mesh(mesh.devices.reshape(shape), ALL)
        tokens = P(("grp", "s2", "s1", "s0"), "br", None)
        owned = P(None, ALL)
        return jax.shard_map(
            fast_body if shape == (2, 2, 2, 2, 2) else body,
            mesh=split,
            in_specs=(tokens,) + (P(),) * 15 + (tokens,),
            out_specs=(tokens, tokens) + (owned,) * 13,
            check_vma=False,
        )(*args)

    return run
```

```python
import functools
import math

import jax
import jax.numpy as jnp
from jax import lax
from jax.experimental import pallas as pl
from jax.experimental.pallas import tpu as pltpu
from jax.sharding import PartitionSpec as P

SEG_BASE = 1024
DOC_MOST = 2048
LANES = 128
BF = jnp.bfloat16
F32 = jnp.float32
NEG = -1e30
EPS = 1e-05
ALL = ("br", "grp", "s2", "s1", "s0")
GROUP = ("br", "s2", "s1", "s0")
FIRST_DOWN = 2
ONE_LANE = 48
ID_Q = 51
ID_K = 52


class Plan:
    def __init__(self, heads, head_size, branches, groups, members, tq, total):
        self.heads, self.size, self.groups, self.members, self.tq = heads, head_size, groups, members, tq
        self.blocks = groups * members
        self.paired = groups * members * tq * 2 == total
        self.tokens = self.blocks * tq
        self.total = total
        self.halo = min(DOC_MOST, self.tokens)
        self.factor = math.log2(math.e) * head_size**-0.5
        self.branches = []
        keys, sel = 0, 0
        for level in range(branches):
            rate = 2**level
            span = min(SEG_BASE * rate, total)
            near = span <= self.tokens
            extra = 0 if near else self.halo // rate
            segs = self.tokens // span if near else 1
            seg_q = self.tokens // rate // segs
            seg_k = seg_q + 2 * extra
            self.branches.append(
                dict(
                    level=level, rate=rate, span=span, near=near, extra=extra, segs=segs,
                    seg_q=seg_q, seg_k=seg_k, tile=min(1024, seg_q), first=keys, sel=sel,
                )
            )
            keys += segs * seg_k
            sel += extra
        self.sel = sel
        self.near = [b for b in self.branches if b["near"]]
        self.far = [b for b in self.branches if not b["near"]]
        self.near_keys = sum(b["segs"] * b["seg_k"] for b in self.near)
        self.far_keys, self.own = 0, 0
        for b in self.far:
            b["begin"], b["own"] = self.far_keys, self.own
            self.far_keys += b["seg_k"]
            self.own += b["seg_q"]
        self.widest = max(b["seg_k"] for b in self.branches)

    def slot(self, block):
        return lax.rem(block, self.groups) * self.members + lax.div(block, self.groups)


def dot_nt(a, b):
    return lax.dot_general(a, b, (((1,), (1,)), ((), ())), preferred_element_type=F32)


def dot_tn(a, b):
    return lax.dot_general(a, b, (((0,), (0,)), ((), ())), preferred_element_type=F32)


def dot_nn(a, b):
    return lax.dot_general(a, b, (((1,), (0,)), ((), ())), preferred_element_type=F32)


def iota(shape, dim):
    return lax.broadcasted_iota(jnp.int32, shape, dim)


def placement(size, parts):
    shape = (parts * size + 16, parts * LANES)
    row, col = iota(shape, 0), iota(shape, 1)
    hit = col < 0
    for part in range(parts):
        hit |= (row >= part * size) & (row < (part + 1) * size) & (col == row - part * size + part * LANES)
    return row, col, hit


def ids_of(pos, starts, gate=None):
    found = jnp.zeros(pos.shape, jnp.int32)
    for start in starts:
        found += jnp.where(pos >= start, 1, 0)
    if gate is not None:
        found = jnp.where(gate, found, -1)
    return found.astype(F32)


def slide_starts(lens_ref):
    starts, at = [], jnp.int32(0)
    for i in range(lens_ref.shape[0]):
        starts.append(at)
        at = at + lens_ref[i]
    return starts


def branch_pos(plan, branch, base, off, first, count):
    start = base - branch["extra"] * branch["rate"] + off
    pos = start + branch["rate"] * (first + iota((1, count), 1))
    if branch["near"]:
        return pos, None
    shift = int(math.log2(branch["span"]))
    return pos, lax.shift_right_arithmetic(pos, shift) == lax.shift_right_arithmetic(base, shift)


def to_rows(plan, base, starts, x_ref, q_tm, k_tm, v_tm, extra_q=None):
    size, tq = plan.size, plan.tq
    row, col, hit = placement(size, 3)
    hit |= (row == 3 * size) & ((col == ID_Q) | (col == LANES + ID_K))
    place = jnp.where(hit, 1.0, 0.0).astype(BF)
    lane = iota((1, 3 * LANES), 1)
    in_k, in_v = lane - LANES, lane - 2 * LANES
    ones = jnp.where(
        ((in_k >= ONE_LANE) & (in_k < ONE_LANE + 3)) | ((in_v >= ONE_LANE) & (in_v < ONE_LANE + 3)), 1.0, 0.0
    )

    def block(n, carry):
        pos = base + n * tq + iota((1, tq), 1)
        ids = jnp.where(iota((16, tq), 0) == 0, ids_of(pos, starts), 0.0).astype(BF)
        full = jnp.concatenate([x_ref[plan.slot(n)], ids], 0)
        rows = dot_tn(full, place) + ones
        at = pl.ds(pl.multiple_of(n * tq, tq), tq)
        queries = rows[:, :LANES]
        if extra_q is not None:
            queries = queries + extra_q(n, at)
        q_tm[at, :] = queries
        k_tm[at, :] = rows[:, LANES : 2 * LANES]
        v_tm[at, :] = rows[:, 2 * LANES :]
        if extra_q is not None:
            return carry
        squares = [jnp.square(full[i * size : (i + 1) * size].astype(F32)) for i in range(2)]
        return tuple(jnp.maximum(a, jnp.sum(b, 0, keepdims=True)) for a, b in zip(carry, squares))

    start = (jnp.zeros((1, tq), F32),) * 2 if extra_q is None else 0
    most = lax.fori_loop(0, plan.blocks, block, start, unroll=4)
    if extra_q is None:
        return jnp.sqrt(jnp.max(most[0], 1, keepdims=True) * jnp.max(most[1], 1, keepdims=True)) * 1.0001
    return None


def gather_near(plan, offs, k_tm, v_tm, kall, vall, branches):
    for branch in branches:
        rate, first, off = branch["rate"], branch["first"], offs[branch["level"]]
        count = plan.tokens // rate
        step = min(256, count)

        def chunk(i, carry, rate=rate, first=first, off=off, step=step):
            rows = pl.ds(off + i * step * rate, step, stride=rate) if rate > 1 else pl.ds(i * step, step)
            to = pl.ds(pl.multiple_of(first + i * step, step), step)
            kall[to, :] = k_tm[rows, :].astype(BF)
            vall[to, :] = v_tm[rows, :].astype(BF)
            return carry

        lax.fori_loop(0, count // step, chunk, 0, unroll=min(4, count // step))


def far_keys(plan, base, offs, starts, halos, k_far, v_far, kall, vall):
    size = plan.size
    row, col, hit = placement(size, 2)
    hit |= (row == 2 * size) & (col == ID_K)
    place = jnp.where(hit, 1.0, 0.0).astype(BF)
    lane = iota((1, 2 * LANES), 1)
    in_v = lane - LANES
    ones = jnp.where(
        ((lane >= ONE_LANE) & (lane < ONE_LANE + 3)) | ((in_v >= ONE_LANE) & (in_v < ONE_LANE + 3)), 1.0, 0.0
    )
    for branch in plan.far:
        extra, first, own, count = branch["extra"], branch["begin"], branch["own"], branch["seg_q"]
        kall[first + extra : first + extra + count, :] = k_far[own : own + count, :]
        vall[first + extra : first + extra + count, :] = v_far[own : own + count, :]
        for side, ref in enumerate((halos[0], halos[-1])):
            begin = side * (extra + count)
            pos, gate = branch_pos(plan, branch, base, offs[branch["level"]], begin, extra)
            ids = jnp.where(iota((16, extra), 0) == 0, ids_of(pos, starts, gate), 0.0).astype(BF)
            piece = ref[:, branch["sel"] : branch["sel"] + extra]
            rows = dot_tn(jnp.concatenate([piece, ids], 0), place) + ones
            kall[first + begin : first + begin + extra, :] = rows[:, :LANES].astype(BF)
            vall[first + begin : first + begin + extra, :] = rows[:, LANES:].astype(BF)


def picked(branch, off, i):
    tile, rate = branch["tile"], branch["rate"]
    if rate == 1:
        return pl.ds(pl.multiple_of(i * tile, tile), tile)
    return pl.ds(off + i * tile * rate, tile, stride=rate)


def pieces_of(wide, most):
    step = next(n for n in (most, 512, 256, 128) if wide % n == 0)
    return [(at, step) for at in range(0, wide, step)]


def split3(column, lane):
    high = column.astype(BF).astype(F32)
    rest = column - high
    mid = rest.astype(BF).astype(F32)
    low = rest - mid
    return jnp.where(
        lane == ONE_LANE, high, jnp.where(lane == ONE_LANE + 1, mid, jnp.where(lane == ONE_LANE + 2, low, 0.0))
    )


def near_kernel(plan, meta, lens, offsets, x_ref, st_ref, qf_ref, kf_ref, vf_ref, q_tm, k_tm, v_tm, kall, vall, kid):
    base, head = meta[0], meta[1]
    starts = slide_starts(lens)
    offs = [offsets[b["level"], head] for b in plan.branches]
    top = to_rows(plan, base, starts, x_ref, q_tm, k_tm, v_tm)
    gather_near(plan, offs, k_tm, v_tm, kall, vall, plan.near)
    for branch in plan.far:
        rows = pl.ds(offs[branch["level"]], branch["seg_q"], stride=branch["rate"])
        own = slice(branch["own"], branch["own"] + branch["seg_q"])
        for ref, source in ((qf_ref, q_tm), (kf_ref, k_tm), (vf_ref, v_tm)):
            ref[own, :] = source[rows, :].astype(BF)
    for branch in plan.near:
        first, total = branch["first"], branch["segs"] * branch["seg_k"]
        pos, gate = branch_pos(plan, branch, base, offs[branch["level"]], 0, total)
        kid[:, first : first + total] = ids_of(pos, starts, gate)
    factor = plan.factor
    lane = iota((1, LANES), 1)

    def scan(visit):
        for branch in plan.near:
            per = branch["seg_q"] // branch["tile"]

            def tile(i, carry, branch=branch, per=per):
                rows = picked(branch, offs[branch["level"]], i)
                at = pl.multiple_of(branch["first"] + lax.div(i, per) * branch["seg_k"], 128)
                visit(branch, rows, q_tm[rows, :], at)
                return carry

            lax.fori_loop(0, branch["segs"] * per, tile, 0)

    def attend(top_lanes):
        def visit(branch, rows, queries, at):
            ids = queries[:, ID_Q : ID_Q + 1]
            low = (queries + top_lanes).astype(BF)
            mixed = None
            for begin, step in pieces_of(branch["seg_k"], 1024):
                to = pl.ds(at + begin, step)
                weights = jnp.exp2(dot_nt(low, kall[to, :]) * factor)
                weights = jnp.where(ids == kid[:, to], weights, 0.0).astype(BF)
                more = dot_nn(weights, vall[to, :])
                mixed = more if mixed is None else mixed + more
            if branch["level"]:
                mixed = st_ref[rows, :] + mixed
            st_ref[rows, :] = mixed

        scan(visit)

    attend(split3(-top, lane))
    step = min(512, plan.tokens)

    def least(n, low):
        at = pl.ds(pl.multiple_of(n * step, step), step)
        state = st_ref[at, :]
        st_ref[at, :] = jnp.where(iota((step, LANES), 1) == ID_Q, top, state)
        return jnp.minimum(low, jnp.min(state, 0, keepdims=True))

    weight = lax.fori_loop(0, plan.tokens // step, least, jnp.full((1, LANES), jnp.inf, F32), unroll=2)
    weight = jnp.min(jnp.where(lane == ONE_LANE, weight, jnp.inf))

    @pl.when(jnp.logical_not(weight > 2.0**-60))
    def _():
        def clear(n, carry):
            st_ref[pl.ds(pl.multiple_of(n * step, step), step), :] = jnp.full((step, LANES), NEG, F32)
            return carry

        def largest(branch, rows, queries, at):
            low = queries.astype(BF)
            best = st_ref[rows, :]
            for begin, step in pieces_of(branch["seg_k"], 256):
                to = pl.ds(at + begin, step)
                scores = jnp.where(queries[:, ID_Q : ID_Q + 1] == kid[:, to], dot_nt(low, kall[to, :]), NEG)
                best = jnp.maximum(best, jnp.max(scores, 1, keepdims=True))
            st_ref[rows, :] = best

        def settle(n, carry):
            at = pl.ds(pl.multiple_of(n * step, step), step)
            own = st_ref[at, :]
            tops[at, :] = own
            wide = iota((step, LANES), 1)
            q_tm[at, :] = q_tm[at, :] + split3(-own, wide)
            return carry

        def restore(n, carry):
            at = pl.ds(pl.multiple_of(n * step, step), step)
            st_ref[at, :] = jnp.where(iota((step, LANES), 1) == ID_Q, tops[at, :], st_ref[at, :])
            return carry

        tops = k_tm
        lax.fori_loop(0, plan.tokens // step, clear, 0)
        scan(largest)
        lax.fori_loop(0, plan.tokens // step, settle, 0)
        attend(jnp.zeros((1, LANES), F32))
        lax.fori_loop(0, plan.tokens // step, restore, 0)


def far_kernel(plan, meta, lens, offsets, st_in, qf_ref, kf_ref, vf_ref, *rest):
    halos, (o_ref, st_ref, kall, vall) = rest[:-4], rest[-4:]
    base, head = meta[0], meta[1]
    starts = slide_starts(lens)
    offs = [offsets[b["level"], head] for b in plan.branches]
    factor = plan.factor
    step = min(512, plan.tokens)

    def carry_over(n, carry):
        at = pl.ds(pl.multiple_of(n * step, step), step)
        st_ref[at, :] = st_in[at, :]
        return carry

    lax.fori_loop(0, plan.tokens // step, carry_over, 0, unroll=2)
    if plan.far:
        far_keys(plan, base, offs, starts, halos, kf_ref, vf_ref, kall, vall)
    for branch in plan.far:
        off, tile, wide = offs[branch["level"]], branch["tile"], branch["seg_k"]
        pos, gate = branch_pos(plan, branch, base, off, 0, wide)
        ids = ids_of(pos, starts, gate)
        keys = kall[branch["begin"] : branch["begin"] + wide, :]
        values = vall[branch["begin"] : branch["begin"] + wide, :]
        for i in range(branch["seg_q"] // tile):
            own = branch["own"] + i * tile
            queries = qf_ref[own : own + tile, :]
            rows = picked(branch, off, i)
            scores = dot_nt(queries, keys)
            scores = jnp.where(queries[:, ID_Q : ID_Q + 1].astype(F32) == ids, scores, NEG)
            top = jnp.max(scores, 1, keepdims=True)
            mixed = dot_nn(jnp.exp2((scores - top) * factor).astype(BF), values)
            old = st_ref[rows, :]
            old_top = old[:, ID_Q : ID_Q + 1]
            new_top = jnp.maximum(old_top, top)
            mixed = old * jnp.exp2((old_top - new_top) * factor) + mixed * jnp.exp2((top - new_top) * factor)
            st_ref[rows, :] = jnp.where(iota((tile, LANES), 1) == ID_Q, new_top, mixed)
    eye = jnp.where(iota((plan.size, LANES), 0) == iota((plan.size, LANES), 1), 1.0, 0.0).astype(BF)

    def finish(n, carry):
        at = pl.ds(pl.multiple_of(n * plan.tq, plan.tq), plan.tq)
        state = st_ref[at, :]
        weight = state[:, ONE_LANE : ONE_LANE + 1]
        top = state[:, ID_Q : ID_Q + 1]
        attn = state * (1.0 / weight)
        merged = top + jnp.log2(weight) * (1.0 / factor)
        lane = iota((plan.tq, LANES), 1)
        st_ref[at, :] = jnp.where(lane < plan.size, attn, jnp.where(lane == ONE_LANE, merged, 0.0))
        o_ref[plan.slot(n)] = dot_nt(eye, attn.astype(BF)).astype(BF)
        return carry

    lax.fori_loop(0, plan.blocks, finish, 0, unroll=4)


def back_tile(plan, branch, queries, grads, keys_at, kall, vall, k_fm, linked, dk_acc, dv_acc):
    dq = None
    for begin, step in pieces_of(branch["seg_k"], 256):
        to = pl.ds(keys_at + begin, step)
        part = slice(begin, begin + step)
        keys = kall[to, :]
        probs = jnp.where(linked(keys), jnp.exp2(dot_nt(keys, queries) * plan.factor), 0.0)
        dv_acc[part, :] += dot_nn(probs.astype(BF), grads)
        moved = (probs * dot_nt(vall[to, :], grads)).astype(BF)
        dk_acc[part, :] += dot_nn(moved, queries)
        more = dot_nn(k_fm[:, part], moved)
        dq = more if dq is None else dq + more
    return dq


def far_back_kernel(
    plan, meta, lens, offsets, st_ref, do_ref, qf_ref, kf_ref, vf_ref, *rest,
):
    sides = 1 if plan.paired else 2
    halos, (do_tm, dqf_ref, dkf_ref, dvf_ref), rest = rest[:sides], rest[sides : sides + 4], rest[sides + 4 :]
    halo_outs, (kall, vall, k_fm, dk_acc, dv_acc) = rest[:sides], rest[sides:]
    base, head = meta[0], meta[1]
    starts = slide_starts(lens)
    offs = [offsets[b["level"], head] for b in plan.branches]
    size, tq = plan.size, plan.tq
    row, col, hit = placement(size, 1)
    place = jnp.where(hit, 1.0, 0.0).astype(BF)
    lane = iota((tq, LANES), 1)

    def block(n, carry):
        at = pl.ds(pl.multiple_of(n * tq, tq), tq)
        grads = dot_tn(jnp.concatenate([do_ref[plan.slot(n)], jnp.zeros((16, tq), BF)], 0), place)
        dots = jnp.sum(jnp.where(lane < size, grads * st_ref[at, :], 0.0), 1, keepdims=True)
        do_tm[at, :] = grads + split3(-dots, lane)
        return carry

    lax.fori_loop(0, plan.blocks, block, 0, unroll=4)
    if plan.far:
        far_keys(plan, base, offs, starts, halos, kf_ref, vf_ref, kall, vall)
    eye = jnp.where(iota((LANES, LANES), 0) == iota((LANES, LANES), 1), 1.0, 0.0).astype(BF)
    for branch in plan.far:
        off, tile, wide, begin = offs[branch["level"]], branch["tile"], branch["seg_k"], branch["begin"]
        k_fm[:, :wide] = dot_nt(eye, kall[begin : begin + wide, :]).astype(BF)
        dk_acc[:wide, :] = jnp.zeros((wide, LANES), F32)
        dv_acc[:wide, :] = jnp.zeros((wide, LANES), F32)
        extra, count = branch["extra"], branch["seg_q"]
        for i in range(count // tile):
            own = branch["own"] + i * tile
            rows = picked(branch, off, i)
            wide_lane = iota((tile, LANES), 1)
            merged = st_ref[rows, :][:, ONE_LANE : ONE_LANE + 1]
            queries = jnp.where(wide_lane == ID_Q, 0.0, qf_ref[own : own + tile, :].astype(F32))
            queries = (queries + split3(-merged, wide_lane)).astype(BF)
            grads = do_tm[rows, :].astype(BF)
            pos, _ = branch_pos(plan, branch, base, off, extra + i * tile, tile)
            ids = ids_of(pos, starts)
            linked = lambda keys: keys[:, ID_K : ID_K + 1].astype(F32) == ids
            dq = back_tile(plan, branch, queries, grads, begin, kall, vall, k_fm, linked, dk_acc, dv_acc)
            dqf_ref[own : own + tile, :] = dq.T
        own = slice(branch["own"], branch["own"] + count)
        dkf_ref[own, :] = dk_acc[extra : extra + count, :]
        dvf_ref[own, :] = dv_acc[extra : extra + count, :]
        for side, ref in enumerate(halo_outs):
            at = side * (extra + count)
            if plan.paired:
                at = pl.multiple_of((1 - meta[2]) * (extra + count), 128)
            to = slice(branch["sel"], branch["sel"] + extra)
            dk = (dk_acc[pl.ds(at, extra), :] * size**-0.5).astype(BF)
            ref[:size, to] = dot_nt(eye[:size], dk).astype(BF)
            ref[size:, to] = dot_nt(eye[:size], dv_acc[pl.ds(at, extra), :].astype(BF)).astype(BF)


def near_back_kernel(
    plan, meta, lens, offsets, x_ref, st_ref, do_tm, dqf_ref, dkf_ref, dvf_ref, *rest,
):
    backs, (dx_ref, q_tm, k_tm, v_tm, dq_tm, dk_tm, dv_tm, kall, vall, k_fm, qid, dk_acc, dv_acc) = rest[:-13], rest[-13:]
    base, head = meta[0], meta[1]
    starts = slide_starts(lens)
    offs = [offsets[b["level"], head] for b in plan.branches]
    size, tq = plan.size, plan.tq
    lane = iota((tq, LANES), 1)
    to_rows(
        plan, base, starts, x_ref, q_tm, k_tm, v_tm,
        lambda n, at: split3(-st_ref[at, :][:, ONE_LANE : ONE_LANE + 1], lane),
    )
    gather_near(plan, offs, k_tm, v_tm, kall, vall, plan.near)
    eye = jnp.where(iota((LANES, LANES), 0) == iota((LANES, LANES), 1), 1.0, 0.0).astype(BF)
    for branch in plan.near:
        off, first, wide, tile = offs[branch["level"]], branch["first"], branch["seg_k"], branch["tile"]
        count = branch["segs"] * branch["seg_q"]
        per = branch["seg_q"] // tile
        pos, _ = branch_pos(plan, branch, base, off, 0, count)
        qid[:, :count] = ids_of(pos, starts)

        def segment(seg, carry, branch=branch, off=off, first=first, wide=wide, tile=tile, per=per):
            keys_at = pl.multiple_of(first + seg * wide, 128)
            k_fm[:, :wide] = dot_nt(eye, kall[pl.ds(keys_at, wide), :]).astype(BF)
            dk_acc[:wide, :] = jnp.zeros((wide, LANES), F32)
            dv_acc[:wide, :] = jnp.zeros((wide, LANES), F32)

            def one(j, carry):
                i = seg * per + j
                rows = picked(branch, off, i)
                queries = q_tm[rows, :].astype(BF)
                grads = do_tm[rows, :].astype(BF)
                ids = qid[:, pl.ds(pl.multiple_of(i * tile, tile), tile)]
                linked = lambda keys: keys[:, ID_K : ID_K + 1].astype(F32) == ids
                dq = back_tile(plan, branch, queries, grads, keys_at, kall, vall, k_fm, linked, dk_acc, dv_acc).T
                if branch["level"]:
                    dq = dq_tm[rows, :] + dq
                dq_tm[rows, :] = dq
                return carry

            lax.fori_loop(0, per, one, 0)
            step = min(256, branch["seg_q"])
            for c in range(branch["seg_q"] // step):
                begin = c * step
                if branch["rate"] == 1:
                    to = pl.ds(pl.multiple_of(seg * branch["seg_q"] + begin, step), step)
                    dk_tm[to, :] = dk_acc[begin : begin + step, :]
                    dv_tm[to, :] = dv_acc[begin : begin + step, :]
                else:
                    to = pl.ds(off + (seg * branch["seg_q"] + begin) * branch["rate"], step, stride=branch["rate"])
                    dk_tm[to, :] += dk_acc[begin : begin + step, :]
                    dv_tm[to, :] += dv_acc[begin : begin + step, :]
            return carry

        lax.fori_loop(0, branch["segs"], segment, 0)
    row, col, hit = placement(size, 2)
    place = jnp.where(hit, 1.0, 0.0).astype(BF)[: 2 * size]
    for branch in plan.far:
        off, rate, extra, count = offs[branch["level"]], branch["rate"], branch["extra"], branch["seg_q"]
        rows = pl.ds(off, count, stride=rate)
        own = slice(branch["own"], branch["own"] + count)
        for total, part in ((dq_tm, dqf_ref), (dk_tm, dkf_ref), (dv_tm, dvf_ref)):
            total[rows, :] += part[own, :]
        begins = [plan.tokens - plan.halo, 0]
        if plan.paired:
            begins = [(1 - meta[2]) * (plan.tokens - plan.halo)]
        for begin, ref in zip(begins, backs):
            more = dot_tn(ref[:, branch["sel"] : branch["sel"] + extra], place)
            rows = pl.ds(begin + off, extra, stride=rate)
            dk_tm[rows, :] += more[:, :LANES] * size**0.5
            dv_tm[rows, :] += more[:, LANES:]
    small_eye = eye[:size]

    def finish(n, carry):
        at = pl.ds(pl.multiple_of(n * tq, tq), tq)
        slot = plan.slot(n)
        dx_ref[slot, :size, :] = dot_nt(small_eye, (dq_tm[at, :] * size**-0.5).astype(BF)).astype(BF)
        dx_ref[slot, size : 2 * size, :] = dot_nt(small_eye, (dk_tm[at, :] * size**-0.5).astype(BF)).astype(BF)
        dx_ref[slot, 2 * size :, :] = dot_nt(small_eye, dv_tm[at, :].astype(BF)).astype(BF)
        return carry

    lax.fori_loop(0, plan.blocks, finish, 0, unroll=4)


SMEM = pl.BlockSpec(memory_space=pltpu.SMEM)
VMEM = pl.BlockSpec(memory_space=pltpu.VMEM)
TINY = pl.CostEstimate(flops=1000, bytes_accessed=1000, transcendentals=0)
PARAMS = pltpu.CompilerParams(vmem_limit_bytes=60 << 20)


def struct(shape, kind):
    return jax.ShapeDtypeStruct(shape, kind)


def kernel_call(name, kernel, ins, outs, scratch, flops):
    return pl.pallas_call(
        kernel,
        out_shape=tuple(struct(*out) for out in outs),
        in_specs=[SMEM] * 3 + [VMEM] * (len(ins) - 3),
        out_specs=(VMEM,) * len(outs),
        scratch_shapes=[pltpu.VMEM(*s) for s in scratch],
        compiler_params=PARAMS,
        cost_estimate=pl.CostEstimate(flops=flops, bytes_accessed=1000, transcendentals=0),
        name=name,
    )(*ins)


def near_call(plan, meta, lens, offsets, x):
    rows, keys = ((plan.tokens, LANES), F32), ((plan.near_keys, LANES), BF)
    own = ((plan.own, LANES), BF)
    return kernel_call(
        "near", functools.partial(near_kernel, plan), (meta, lens, offsets, x), (rows, own, own, own),
        (rows, rows, rows, keys, keys, ((1, plan.near_keys), F32)), 20_000_000_000,
    )


def far_call(plan, meta, lens, offsets, state, own, halo):
    keys = ((plan.far_keys, LANES), BF)
    return kernel_call(
        "far", functools.partial(far_kernel, plan), (meta, lens, offsets, state, *own, *halo),
        (((plan.blocks, plan.size, plan.tq), BF), ((plan.tokens, LANES), F32)), (keys, keys), 4_000_000_000,
    )


def far_back_call(plan, meta, lens, offsets, state, do, own, halo):
    keys = ((plan.far_keys, LANES), BF)
    part, side = ((plan.own, LANES), F32), ((2 * plan.size, max(plan.sel, LANES)), BF)
    acc = ((plan.widest, LANES), F32)
    return kernel_call(
        "far_back", functools.partial(far_back_kernel, plan), (meta, lens, offsets, state, do, *own, *halo),
        (((plan.tokens, LANES), F32), part, part, part) + (side,) * (1 if plan.paired else 2),
        (keys, keys, ((LANES, plan.widest), BF), acc, acc), 4_000_000_000,
    )


def near_back_call(plan, meta, lens, offsets, x, state, do_rows, parts, back):
    rows, keys = ((plan.tokens, LANES), F32), ((plan.near_keys, LANES), BF)
    acc = ((plan.widest, LANES), F32)
    return kernel_call(
        "near_back", functools.partial(near_back_kernel, plan),
        (meta, lens, offsets, x, state, do_rows, *parts, *back),
        (((plan.blocks, 3 * plan.size, plan.tq), BF),),
        (rows,) * 6 + (keys, keys, ((LANES, plan.widest), BF), ((1, plan.tokens), F32), acc, acc), 8_000_000_000,
    )[0]


def near_rows(values, norm_gain, norm_shift):
    centred = values - jnp.mean(values, 1, keepdims=True)
    inverse = lax.rsqrt(jnp.mean(centred * centred, 1, keepdims=True) + EPS)
    normed = centred * inverse
    return normed * norm_gain + norm_shift, normed, inverse


def back_rows(grad_out, normed, inverse, norm_gain):
    grad_norm = grad_out * norm_gain
    return inverse * (
        grad_norm
        - jnp.mean(grad_norm, 1, keepdims=True)
        - normed * jnp.mean(grad_norm * normed, 1, keepdims=True)
    )


def own_columns(size, unit, core):
    row, col = iota((size, size), 0), iota((size, size), 1)
    half = size // 2
    other = row >= half
    place = jnp.where(other, row - half, row)
    whole = jnp.floor((place.astype(F32) + 0.5) * (1.0 / unit)).astype(jnp.int32)
    parity = jnp.where(other, 1 - core, core)
    return jnp.where(col == place + unit * (whole + parity), 1.0, 0.0).astype(BF)


def middle_kernel(
    unit_up, unit, core_ref, attn_ref, tiles_ref, out_w, out_b, gain, shift, up_w, up_b, down_w, down_b, g_ref,
    y_ref, res_ref, ag_ref, common_ref, mine_ref, theirs_ref, sums_ref, up_sum_ref,
    pick_up, normed_s, lifted_s, inverse_s, out_s, back_s,
):
    step, steps = pl.program_id(0), pl.num_programs(0)
    width = tiles_ref.shape[1]
    chunk = up_w.shape[1]
    half = chunk // 2
    core = core_ref[0]
    hidden_sel = steps * half

    @pl.when(step == 0)
    def _():
        pick_up[...] = own_columns(chunk, unit_up, core)
        residual = tiles_ref[...].astype(F32) + dot_tn(attn_ref[...], out_w[...]) + out_b[...]
        lifted, normed, inverse = near_rows(residual, gain[...], shift[...])
        low = lifted.astype(BF)
        lifted_s[...] = low
        normed_s[...] = normed
        inverse_s[...] = jnp.broadcast_to(inverse, inverse_s.shape)
        out_s[...] = residual + down_b[...]
        back_s[...] = jnp.zeros_like(back_s)
        common_ref[pl.ds(steps * chunk, width), :] = low.T
        pick = own_columns(width, unit, core)
        picked_g = dot_nt(pick, g_ref[...]).astype(BF)
        mine_ref[pl.ds(hidden_sel, width // 2), :] = picked_g[: width // 2]
        theirs_ref[pl.ds(hidden_sel, width // 2), :] = picked_g[width // 2 :]

    lifted = lifted_s[...]
    gate_in = dot_nn(lifted, up_w[...]) + up_b[...]
    cdf = 0.5 + 0.5 * lax.erf(gate_in * (0.5**0.5))
    act = (gate_in * cdf).astype(BF)
    slope = cdf + gate_in * (jnp.exp(-0.5 * gate_in * gate_in) * (1.0 / math.sqrt(2.0 * math.pi)))
    gate_grad = (dot_nt(g_ref[...], down_w[...]) * slope).astype(BF)
    out_s[...] += dot_nn(act, down_w[...])
    back_s[...] += dot_nt(gate_grad, up_w[...])
    up_sum_ref[...] = jnp.sum(gate_grad.astype(F32), 0, keepdims=True)
    common_ref[pl.ds(pl.multiple_of(step * chunk, chunk), chunk), :] = act.T
    picked_gate = dot_nt(pick_up[...], gate_grad).astype(BF)
    at = pl.ds(pl.multiple_of(step * half, half), half)
    mine_ref[at, :] = picked_gate[:half]
    theirs_ref[at, :] = picked_gate[half:]

    @pl.when(step == steps - 1)
    def _():
        y_ref[...] = out_s[...].astype(BF)
        grads = g_ref[...].astype(F32)
        lifted_grad = back_s[...]
        normed = normed_s[...]
        residual_grad = grads + back_rows(lifted_grad, normed, inverse_s[:, :1], gain[...])
        res_ref[...] = residual_grad
        low = residual_grad.astype(BF)
        ag_ref[...] = dot_nt(out_w[...], low).astype(BF)
        pick = own_columns(width, unit, core)
        picked_p = dot_nt(pick, low).astype(BF)
        at = pl.ds(hidden_sel + width // 2, width // 2)
        mine_ref[at, :] = picked_p[: width // 2]
        theirs_ref[at, :] = picked_p[width // 2 :]
        sums_ref[0:1, :] = jnp.sum(grads, 0, keepdims=True)
        sums_ref[1:2, :] = jnp.sum(residual_grad, 0, keepdims=True)
        sums_ref[2:3, :] = jnp.sum(lifted_grad * normed, 0, keepdims=True)
        sums_ref[3:4, :] = jnp.sum(lifted_grad, 0, keepdims=True)
        sums_ref[4:8, :] = jnp.zeros((4, width), F32)


def middle_call(devices, core, attn_t, tiles, out_w, out_b, gain, shift, up_w, up_b, down_w, down_b, g):
    tq, width = tiles.shape
    hidden = up_w.shape[1]
    steps = hidden // width
    whole = lambda *shape: pl.BlockSpec(shape, lambda j: (0,) * len(shape))
    vec = whole(1, width)
    sel = hidden // 2 + width
    return pl.pallas_call(
        functools.partial(middle_kernel, hidden // devices, width // devices),
        grid=(steps,),
        in_specs=[
            SMEM, whole(width, tq), whole(tq, width), whole(width, width), vec, vec, vec,
            pl.BlockSpec((width, width), lambda j: (0, j)), pl.BlockSpec((1, width), lambda j: (0, j)),
            pl.BlockSpec((width, width), lambda j: (j, 0)), vec, whole(tq, width),
        ],
        out_specs=(
            whole(tq, width), whole(tq, width), whole(width, tq), whole(hidden + width, tq), whole(sel, tq),
            whole(sel, tq), whole(8, width), pl.BlockSpec((1, width), lambda j: (0, j)),
        ),
        out_shape=(
            jax.ShapeDtypeStruct((tq, width), BF),
            jax.ShapeDtypeStruct((tq, width), F32),
            jax.ShapeDtypeStruct((width, tq), BF),
            jax.ShapeDtypeStruct((hidden + width, tq), BF),
            jax.ShapeDtypeStruct((sel, tq), BF),
            jax.ShapeDtypeStruct((sel, tq), BF),
            jax.ShapeDtypeStruct((8, width), F32),
            jax.ShapeDtypeStruct((1, hidden), F32),
        ),
        scratch_shapes=[
            pltpu.VMEM((width, width), BF), pltpu.VMEM((tq, width), F32), pltpu.VMEM((tq, width), BF),
            pltpu.VMEM((tq, LANES), F32), pltpu.VMEM((tq, width), F32), pltpu.VMEM((tq, width), F32),
        ],
        compiler_params=PARAMS,
        cost_estimate=pl.CostEstimate(flops=14 * tq * width * hidden, bytes_accessed=20 << 20, transcendentals=0),
        name="middle",
    )(core, attn_t, tiles, out_w, out_b, gain, shift, up_w, up_b, down_w, down_b, g)


def weights_kernel(unit_up, unit, meta, attn_a, attn_b, common_a, common_b, sel_a, sel_b, *rest):
    first_s, second_refs, second_s = rest[0], rest[1:5], rest[5]
    width = attn_a.shape[0]
    hidden = common_a.shape[0] - width
    chips = width // (2 * unit)

    def spot(chip):
        return (chip // 8) * 2 + chip % 2, chip // 2 % 4

    lifted = slice(hidden, hidden + width)
    group = width // (2 * unit_up)
    for step in range(hidden // width):
        rows = slice(step * width // 2, (step + 1) * width // 2)
        part = dot_nt(sel_a[rows, :], common_a[lifted, :]) + dot_nt(sel_b[rows, :], common_b[lifted, :])
        for i in range(group):
            plane, line = spot(step * group + i)
            first_s[plane, line, :unit_up, :] = part[i * unit_up : (i + 1) * unit_up].astype(BF)
    rows_out = slice(hidden // 2 + width // 2, hidden // 2 + width)
    rows = slice(hidden // 2, hidden // 2 + width // 2)
    out = dot_nt(sel_a[rows_out, :], attn_a[...]) + dot_nt(sel_b[rows_out, :], attn_b[...])
    held = [out]
    for step in range(hidden // width):
        cols = slice(step * width, (step + 1) * width)
        part = dot_nt(sel_a[rows, :], common_a[cols, :]) + dot_nt(sel_b[rows, :], common_b[cols, :])
        if step < FIRST_DOWN:
            held.append(part)
            continue
        at = (step - FIRST_DOWN) * width
        for chip in range(chips):
            plane, line = spot(chip)
            second_s[line, plane, :, at : at + width] = part[chip * unit : (chip + 1) * unit].astype(BF)
    for chip in range(chips):
        plane, line = spot(chip)
        at = slice(chip * unit, (chip + 1) * unit)
        first_s[plane, line, unit_up:, :] = jnp.concatenate([part[at] for part in held], 0).astype(BF)
    for k in range(4):
        second_refs[k][...] = second_s[meta[5] ^ k]


def weights_call(devices, meta, attn_a, attn_b, common_a, common_b, sel_a, sel_b):
    width, tq = attn_a.shape
    hidden = common_a.shape[0] - width
    unit_up, unit = hidden // devices, width // devices
    first = (4, 4, unit_up + (1 + FIRST_DOWN) * unit, width)
    second = (4, unit, hidden - FIRST_DOWN * width)
    outs = pl.pallas_call(
        functools.partial(weights_kernel, unit_up, unit),
        in_specs=[SMEM] + [VMEM] * 6,
        out_specs=(VMEM,) * 5,
        out_shape=(jax.ShapeDtypeStruct(first, BF),) + (jax.ShapeDtypeStruct(second, BF),) * 4,
        scratch_shapes=[pltpu.VMEM((4,) + second, BF)],
        compiler_params=PARAMS,
        cost_estimate=pl.CostEstimate(flops=4 * tq * width * hidden, bytes_accessed=14 << 20, transcendentals=0),
        name="weights",
    )(meta, attn_a, attn_b, common_a, common_b, sel_a, sel_b)
    return outs[0], outs[1:]


def fold_kernel(meta, first_ref, own, got1, got2, got3, *outs):
    plane, line = meta[4], meta[5]
    for k in range(4):
        at = line ^ k
        total = first_ref[0, at].astype(F32)
        for i in range(1, 4):
            total += first_ref[i, at].astype(F32)
        outs[k][...] = total.astype(BF)
        at = plane ^ k
        total = own[at].astype(F32) + got1[at].astype(F32) + got2[at].astype(F32) + got3[at].astype(F32)
        outs[4 + k][...] = total.astype(BF)


def fold_call(meta, first, second):
    shapes = [jax.ShapeDtypeStruct(first.shape[2:], BF)] * 4 + [jax.ShapeDtypeStruct(second[0].shape[1:], BF)] * 4
    outs = pl.pallas_call(
        fold_kernel,
        in_specs=[SMEM] + [VMEM] * 5,
        out_specs=(VMEM,) * 8,
        out_shape=tuple(shapes),
        compiler_params=PARAMS,
        cost_estimate=TINY,
        name="fold",
    )(meta, first, *second)
    return outs[:4], outs[4:]


def last_kernel(unit_up, unit, meta, *refs):
    columns, first, second, outs = refs[:4], refs[4:8], refs[8:12], refs[12:]
    qkv_ref, up_ref, out_ref, down_ref, held = outs
    size = columns[0].shape[0]
    held[...] = jnp.zeros_like(held)
    for i, ref in enumerate(columns):
        at = pl.multiple_of(meta[10 + i] + size // 2, 8)
        held[pl.ds(at, size), :] += ref[...].astype(F32)
    qkv_ref[...] = held[size // 2 : size // 2 + qkv_ref.shape[0], :]
    total = first[0][...].astype(F32)
    for ref in first[1:]:
        total += ref[...].astype(F32)
    up_ref[...] = total[:unit_up]
    out_ref[...] = total[unit_up : unit_up + unit]
    width = total.shape[1]
    for i in range(FIRST_DOWN):
        at = unit_up + (1 + i) * unit
        down_ref[:, i * width : (i + 1) * width] = total[at : at + unit]
    width = FIRST_DOWN * width
    total = second[0][...].astype(F32)
    for ref in second[1:]:
        total += ref[...].astype(F32)
    down_ref[:, width:] = total


def last_call(meta, unit_qkv, unit_up, unit, columns, first, second):
    size, width = columns[0].shape
    hidden = FIRST_DOWN * width + second[0].shape[1]
    outs = ((unit_qkv, width), (unit_up, width), (unit, width), (unit, hidden))
    return pl.pallas_call(
        functools.partial(last_kernel, unit_up, unit),
        in_specs=[SMEM] + [VMEM] * 12,
        out_specs=(VMEM,) * 4,
        out_shape=tuple(jax.ShapeDtypeStruct(s, F32) for s in outs),
        scratch_shapes=[pltpu.VMEM((unit_qkv + size, width), F32)],
        compiler_params=PARAMS,
        cost_estimate=TINY,
        name="last",
    )(meta, *columns, *first, *second)


def enter_kernel(tiles_ref, gain, shift, w_ref, query_b, value_b, x_ref, npre_ref, low_s):
    part = pl.program_id(0)

    @pl.when(part == 0)
    def _():
        scaled, normed, _ = near_rows(tiles_ref[...].astype(F32), gain[...], shift[...])
        low_s[...] = scaled.astype(BF)
        npre_ref[...] = normed.astype(BF)

    bias = jnp.where(part == 0, query_b[...], jnp.where(part == 2, value_b[...], 0.0))
    joined = (dot_nn(low_s[...], w_ref[...]) + bias).T
    heads, _, size, tq = x_ref.shape
    x_ref[:, 0] = joined.astype(BF).reshape(heads, size, tq)


def enter_call(heads, tiles, gain, shift, weight, query_b, value_b):
    tq, width = tiles.shape
    size = width // heads
    whole = lambda *shape: pl.BlockSpec(shape, lambda i: (0,) * len(shape))
    vec = whole(1, width)
    return pl.pallas_call(
        enter_kernel,
        grid=(3,),
        in_specs=[whole(tq, width), vec, vec, pl.BlockSpec((width, width), lambda i: (0, i)), vec, vec],
        out_specs=(pl.BlockSpec((heads, 1, size, tq), lambda i: (0, i, 0, 0)), whole(tq, width)),
        out_shape=(jax.ShapeDtypeStruct((heads, 3, size, tq), BF), jax.ShapeDtypeStruct((tq, width), BF)),
        scratch_shapes=[pltpu.VMEM((tq, width), BF)],
        compiler_params=PARAMS,
        name="enter",
    )(tiles, gain, shift, weight, query_b, value_b)


def leave_kernel(tiles_ref, gain, w_ref, jg_ref, res_ref, out_ref, acc):
    part = pl.program_id(0)
    width, tq = acc.shape
    more = dot_nn(w_ref[...], jg_ref[:, 0].reshape(width, tq))

    @pl.when(part == 0)
    def _():
        acc[...] = more

    @pl.when(part == 1)
    def _():
        acc[...] += more

    @pl.when(part == 2)
    def _():
        _, normed, inverse = near_rows(tiles_ref[...].astype(F32), gain[...], gain[...])
        grads = (acc[...] + more).T
        out_ref[...] = (res_ref[...] + back_rows(grads, normed, inverse, gain[...])).astype(BF)


def leave_call(tiles, gain, weight, joined_grad, residual_grad):
    tq, width = tiles.shape
    heads, _, size, _ = joined_grad.shape
    whole = lambda *shape: pl.BlockSpec(shape, lambda i: (0,) * len(shape))
    return pl.pallas_call(
        leave_kernel,
        grid=(3,),
        in_specs=[
            whole(tq, width), whole(1, width), pl.BlockSpec((width, width), lambda i: (0, i)),
            pl.BlockSpec((heads, 1, size, tq), lambda i: (0, i, 0, 0)), whole(tq, width),
        ],
        out_specs=whole(tq, width),
        out_shape=jax.ShapeDtypeStruct((tq, width), BF),
        scratch_shapes=[pltpu.VMEM((width, tq), F32)],
        compiler_params=PARAMS,
        cost_estimate=TINY,
        name="leave",
    )(tiles, gain, weight, joined_grad, residual_grad)


def halo_hits(plan, offs, first, dims):
    wide = max(plan.sel, LANES)
    shape = (plan.tq, wide)
    token, col = iota(shape, 0) + first, iota(shape, 1)
    hit = col < 0
    for branch in plan.branches:
        if branch["extra"]:
            at = col - branch["sel"]
            inside = (at >= 0) & (at < branch["extra"])
            hit |= inside & (token == at * branch["rate"] + offs[branch["level"]])
    return jnp.where(hit, 1.0, 0.0).astype(BF)


def halo_blocks(plan):
    count = plan.halo // plan.tq
    for i in range(count):
        yield 0, plan.blocks - count + i, i * plan.tq
        yield 1, i, i * plan.tq


def static_slot(plan, block):
    return block % plan.groups * plan.members + block // plan.groups


def select_kernel(plan, meta, offsets, x_ref, *outs):
    offs = [offsets[b["level"], meta[1]] for b in plan.branches]
    if plan.paired:
        count = plan.halo // plan.tq
        total = jnp.zeros((2 * plan.size, max(plan.sel, LANES)), F32)
        for i in range(count):
            block = (1 - meta[2]) * (plan.blocks - count) + i
            total += dot_nn(x_ref[plan.slot(block), plan.size :, :], halo_hits(plan, offs, i * plan.tq, None))
        outs[0][...] = total.astype(BF)
        return
    last_ref, first_ref = outs
    total = [jnp.zeros((2 * plan.size, max(plan.sel, LANES)), F32) for _ in range(2)]
    for side, block, first in halo_blocks(plan):
        hits = halo_hits(plan, offs, first, None)
        total[side] += dot_nn(x_ref[static_slot(plan, block), plan.size :, :], hits)
    last_ref[...] = total[0].astype(BF)
    first_ref[...] = total[1].astype(BF)


def select_call(plan, meta, offsets, x):
    shape = jax.ShapeDtypeStruct((2 * plan.size, max(plan.sel, LANES)), BF)
    return pl.pallas_call(
        functools.partial(select_kernel, plan),
        in_specs=[SMEM, SMEM, VMEM],
        out_specs=(VMEM,) * (1 if plan.paired else 2),
        out_shape=(shape,) * (1 if plan.paired else 2),
        compiler_params=PARAMS,
        name="select",
    )(meta, offsets, x)


def to_owners(vector, owner, lane_of, devices):
    count = vector.shape[1]
    held = jnp.where(iota((devices, count), 0) == owner, vector, 0.0)
    hits = jnp.where(iota((count, LANES), 1) == lane_of, 1.0, 0.0)
    return lax.dot_general(
        held, hits, (((1,), (0,)), ((), ())), precision=lax.Precision.HIGHEST, preferred_element_type=F32
    )


def cut(index, unit):
    whole = jnp.floor((index.astype(F32) + 0.5) * (1.0 / unit)).astype(jnp.int32)
    return whole, index - whole * unit


def head_kernel(devices, meta, dx_ref, near_ref, w_ref, gain, shift, sums_ref, up_ref, *rest):
    column_refs, (small_ref, acc, col_s, row_s) = rest[:-4], rest[-4:]
    step, steps = pl.program_id(0), pl.num_programs(0)
    tq = dx_ref.shape[2]
    rows = dx_ref.shape[1]
    per = near_ref.shape[0] // tq
    size = rows // 3
    width = near_ref.shape[1]

    @pl.when(step == 0)
    def _():
        acc[...] = jnp.zeros_like(acc)
        col_s[...] = jnp.zeros_like(col_s)
        row_s[...] = jnp.zeros_like(row_s)

    for i in range(per):
        grads = dx_ref[i]
        acc[...] += dot_nn(grads, near_ref[i * tq : (i + 1) * tq, :])
        col_s[...] += jnp.broadcast_to(jnp.sum(grads.astype(F32), 1, keepdims=True), col_s.shape)
        row_s[...] += dot_nt(jnp.ones((8, tq), BF), grads)

    @pl.when(step == steps - 1)
    def _():
        head = meta[1]
        plain = acc[...]
        weight = plain * gain[...] + col_s[:, :1] * shift[...]
        acc[...] = weight
        for i, ref in enumerate(column_refs):
            at = pl.multiple_of(meta[6 + i] * size, 8)
            ref[...] = acc[pl.ds(at, size), :].astype(BF)
        own = w_ref[...].astype(F32)
        gain_part = jnp.sum(own * plain, 0, keepdims=True)
        shift_part = jnp.sum(own * col_s[:, :1], 0, keepdims=True)
        unit = width // devices
        owner = cut(iota((1, width), 1), unit)[0]
        lane = cut(iota((width, 1), 0), unit)[1]
        small_ref[:, 0, :] = to_owners(gain_part, owner, lane, devices)
        small_ref[:, 1, :] = to_owners(shift_part, owner, lane, devices)
        held = jnp.zeros((devices, LANES), F32)
        for i in range(4):
            held += to_owners(sums_ref[i : i + 1, :], owner, lane + i * unit, devices)
        small_ref[:, 2, :] = held
        hidden = up_ref.shape[1]
        unit_up = hidden // devices
        held = jnp.zeros((devices, LANES), F32)
        for i in range(hidden // width):
            owner_up = cut(iota((1, width), 1) + i * width, unit_up)[0]
            lane_up = cut(iota((width, 1), 0) + i * width, unit_up)[1]
            held += to_owners(up_ref[:, i * width : (i + 1) * width], owner_up, lane_up, devices)
        small_ref[:, 3, :] = held
        line = row_s[0:1, :]
        for i, part in enumerate((0, 2)):
            index = iota((1, rows), 1) - part * size
            inside = (index >= 0) & (index < size)
            owner_h = jnp.where(inside, 2 * head + cut(index, size // 2)[0], -1)
            lane_h = cut(iota((rows, 1), 0), size // 2)[1]
            small_ref[:, 4 + i, :] = to_owners(line, owner_h, lane_h, devices)
        small_ref[:, 6, :] = jnp.zeros((devices, LANES), F32)
        small_ref[:, 7, :] = jnp.zeros((devices, LANES), F32)


def head_call(devices, meta, dx, npre_all, own_w, gain, shift, sums, up_sums):
    blocks, rows, tq = dx.shape
    width = npre_all.shape[1]
    per = blocks // 4
    whole = lambda *shape: pl.BlockSpec(shape, lambda i: (0,) * len(shape))
    return pl.pallas_call(
        functools.partial(head_kernel, devices),
        grid=(4,),
        in_specs=[
            SMEM, pl.BlockSpec((per, rows, tq), lambda i: (i, 0, 0)), pl.BlockSpec((per * tq, width), lambda i: (i, 0)),
            whole(rows, width), whole(1, width), whole(1, width), whole(8, width), whole(1, up_sums.shape[1]),
        ],
        out_specs=(whole(rows // 3, width),) * 4 + (whole(devices, 8, LANES),),
        out_shape=(jax.ShapeDtypeStruct((rows // 3, width), BF),) * 4
        + (jax.ShapeDtypeStruct((devices, 8, LANES), F32),),
        scratch_shapes=[
            pltpu.VMEM((rows, width), F32), pltpu.VMEM((rows, LANES), F32), pltpu.VMEM((8, rows), F32),
        ],
        compiler_params=PARAMS,
        cost_estimate=TINY,
        name="head",
    )(meta, dx, npre_all, own_w, gain, shift, sums, up_sums)


def layer_norm_rows(values, norm_gain, norm_shift):
    row_mean = jnp.mean(values, -1, keepdims=True)
    centred = values - row_mean
    inverse = lax.rsqrt(jnp.mean(centred * centred, -1, keepdims=True) + EPS)
    normed = centred * inverse
    return (normed * norm_gain + norm_shift, normed, inverse)


def norm_back(grad_out, normed, inverse, norm_gain):
    grad_norm = grad_out * norm_gain
    grad_in = inverse * (
        grad_norm
        - jnp.mean(grad_norm, -1, keepdims=True)
        - normed * jnp.mean(grad_norm * normed, -1, keepdims=True)
    )
    return (grad_in, jnp.sum(grad_out * normed, 0), jnp.sum(grad_out, 0))


def swap(values, axes):
    return lax.all_to_all(values, axes, 0, 0, tiled=True)


def scatter_sum(values, orders):
    sizes = {name: lax.axis_size(name) for name in ALL}
    left = list(ALL)
    rows, cols = values.shape[1:]
    for stage, axes in enumerate(orders):
        values = values.reshape([sizes[name] for name in left] + [rows, cols])
        rest = [name for name in left if name not in axes]
        order = [left.index(name) for name in list(axes) + rest]
        values = values.transpose(order + [len(left), len(left) + 1])
        count = math.prod(sizes[name] for name in axes)
        values = values.reshape((count, -1, rows, cols))
        if count > 1:
            values = swap(values, axes)
            values = jnp.sum(values.astype(F32), 0)
            if stage < len(orders) - 1:
                values = values.astype(BF)
        left = rest
    return values.reshape(rows, cols).astype(F32)


def to_neighbours(pieces, count):
    if count == 2:
        return (lax.ppermute(pieces[0], "grp", [(0, 1), (1, 0)]),)
    return (
        lax.ppermute(pieces[0], "grp", [(i, i + 1) for i in range(count - 1)]),
        lax.ppermute(pieces[1], "grp", [(i + 1, i) for i in range(count - 1)]),
    )


def from_neighbours(pieces, count):
    return to_neighbours(pieces[::-1], count)[::-1]


def share_columns(weight_t, sums, width):
    members, size = lax.axis_size(GROUP), weight_t.shape[1]
    head = lax.axis_index(GROUP)
    full = jnp.zeros((3, members) + weight_t.shape[1:], F32)
    full = lax.dynamic_update_slice(full, weight_t[:, None], (0, head, 0, 0))
    full_sums = lax.dynamic_update_slice(jnp.zeros((3, members, size), F32), sums[:, None], (0, head, 0))
    weight = lax.psum_scatter(full.reshape(3 * members * size, width), ALL, scatter_dimension=0, tiled=True)
    sums = lax.psum_scatter(full_sums.reshape(3, members * size), ALL, scatter_dimension=1, tiled=True)
    return weight, sums[0], sums[2]


def body(
    tile_embed,
    slide_lengths,
    head_offsets,
    pre_gain,
    pre_shift,
    qkv_weight,
    query_bias,
    value_bias,
    out_weight,
    out_bias,
    post_gain,
    post_shift,
    up_weight,
    up_bias,
    down_weight,
    down_bias,
    out_grad,
):
    width = qkv_weight.shape[0]
    hidden = up_weight.shape[1]
    heads = head_offsets.shape[1]
    size = width // heads
    tq = tile_embed.shape[1]
    br, groups = lax.axis_size("br"), lax.axis_size("grp")
    members = heads // br
    devices = heads * groups
    plan = Plan(heads, size, head_offsets.shape[0], br, members, tq, devices * tq)
    head = lax.axis_index(GROUP)
    base = lax.axis_index("grp") * plan.tokens
    meta = jnp.stack([base, head, lax.axis_index("grp")]).astype(jnp.int32)

    tiles = tile_embed[0].astype(F32)
    pre_out, normed_pre, inverse_pre = layer_norm_rows(tiles, pre_gain, pre_shift)
    normed_low = pre_out.astype(BF)
    bias_col = jnp.concatenate([query_bias, jnp.zeros_like(query_bias), value_bias], 1).reshape(-1, 1)
    joined_t = (
        lax.dot_general(qkv_weight, normed_low, (((0,), (1,)), ((), ())), preferred_element_type=F32) + bias_col
    ).astype(BF)
    x = joined_t.reshape(3, heads, size, tq).transpose(1, 0, 2, 3).reshape(heads, 3 * size, tq)
    x = swap(x, GROUP)
    normed_all = lax.all_gather(normed_low, GROUP, axis=0, tiled=True)

    halo = to_neighbours(select_call(plan, meta, head_offsets, x), groups)
    state, *own = near_call(plan, meta, slide_lengths, head_offsets, x)
    mixed, state = far_call(plan, meta, slide_lengths, head_offsets, state, own, halo)
    attn_t = swap(mixed, GROUP).reshape(width, tq)

    projected = lax.dot_general(attn_t, out_weight, (((0,), (0,)), ((), ())), preferred_element_type=F32)
    residual = tiles + projected + out_bias
    post_out, normed_post, inverse_post = layer_norm_rows(residual, post_gain, post_shift)
    lifted = post_out.astype(BF)
    gate_in = jnp.dot(lifted, up_weight, preferred_element_type=F32) + up_bias
    act_float, gelu_pull = jax.vjp(lambda v: jax.nn.gelu(v, approximate=False), gate_in)
    act_low = act_float.astype(BF)
    layer_out = (residual + jnp.dot(act_low, down_weight, preferred_element_type=F32) + down_bias).astype(BF)[None]
    grad_low = out_grad[0]
    grad_float = grad_low.astype(F32)
    act_grad = lax.dot_general(grad_low, down_weight, (((1,), (1,)), ((), ())), preferred_element_type=F32)
    gate_grad = gelu_pull(act_grad)[0].astype(BF)
    lifted_grad = lax.dot_general(gate_grad, up_weight, (((1,), (1,)), ((), ())), preferred_element_type=F32)
    norm_part, post_gain_sum, post_shift_sum = norm_back(lifted_grad, normed_post, inverse_post, post_gain)
    residual_grad = grad_float + norm_part
    proj_grad = residual_grad.astype(BF)
    attn_grad_t = lax.dot_general(
        out_weight, proj_grad, (((1,), (1,)), ((), ())), preferred_element_type=F32
    ).astype(BF)
    do = swap(attn_grad_t.reshape(heads, size, tq), GROUP)

    tokens = (((0,), (0,)), ((), ()))
    up_part = lax.dot_general(gate_grad, lifted, tokens, preferred_element_type=F32).astype(BF)
    down_part = lax.dot_general(grad_low, act_low, tokens, preferred_element_type=F32).astype(BF)
    out_part = lax.dot_general(proj_grad, attn_t, (((0,), (1,)), ((), ())), preferred_element_type=F32).astype(BF)
    vectors = [
        jnp.sum(gate_grad.astype(F32), 0).reshape(devices, -1),
        jnp.sum(grad_float, 0).reshape(devices, -1),
        jnp.sum(residual_grad, 0).reshape(devices, -1),
        post_gain_sum.reshape(devices, -1),
        post_shift_sum.reshape(devices, -1),
    ]
    ends = [0]
    for vector in vectors:
        ends.append(ends[-1] + vector.shape[1])
    small = jnp.concatenate(vectors, 1)
    small = jnp.pad(small[:, None, :], ((0, 0), (0, 7), (0, width - small.shape[1]))).astype(BF)
    misc = jnp.concatenate([out_part.reshape(devices, -1, width), small], 1)
    first, second = (("s0",), ("br", "s1"), ("grp", "s2")), (("s0",), ("grp", "s2"), ("br", "s1"))
    up_own = scatter_sum(up_part.reshape(devices, -1, width), first)
    down_own = scatter_sum(down_part.reshape(devices, -1, hidden), second)
    misc_own = scatter_sum(misc, first)
    unit = width // devices
    small_own = misc_own[unit]
    small_own = [small_own[None, ends[i] : ends[i + 1]] for i in range(len(vectors))]

    rows, dq, dk, dv, *sides = far_back_call(plan, meta, slide_lengths, head_offsets, state, do, own, halo)
    back = from_neighbours(sides, groups)
    dx = near_back_call(plan, meta, slide_lengths, head_offsets, x, state, rows, (dq, dk, dv), back)
    joined_grad_t = swap(dx, GROUP).reshape(heads, 3, size, tq).transpose(1, 0, 2, 3).reshape(3 * width, tq)
    weight_t = jnp.einsum(
        "nct,ntd->cd", dx, normed_all.reshape(heads, tq, width), preferred_element_type=F32
    ).reshape(3, size, width)
    head_sums = jnp.sum(dx.astype(F32), (0, 2)).reshape(3, size)
    qkv_own, query_own, value_own = share_columns(weight_t, head_sums, width)
    normed_grad = lax.dot_general(joined_grad_t, qkv_weight, (((0,), (1,)), ((), ())), preferred_element_type=F32)
    tile_part, pre_gain_sum, pre_shift_sum = norm_back(normed_grad, normed_pre, inverse_pre, pre_gain)
    tile_grad = (residual_grad + tile_part).astype(BF)[None]
    last = jnp.stack([pre_gain_sum, pre_shift_sum]).reshape(2, devices, unit).transpose(1, 0, 2)
    last = jnp.pad(last, ((0, 0), (0, 6), (0, LANES - unit)))
    last = jnp.sum(swap(last, ALL).reshape(devices, 8, LANES), 0)
    return (
        layer_out,
        tile_grad,
        last[0:1, :unit],
        last[1:2, :unit],
        qkv_own.T,
        query_own[None],
        value_own[None],
        misc_own[:unit].T,
        small_own[2],
        small_own[3],
        small_own[4],
        up_own.T,
        small_own[0],
        down_own.T,
        small_own[1],
    )


def across(piece, axes, k):
    return lax.ppermute(piece, axes, [(i, i ^ k) for i in range(4)])


def matchings(edges, count):
    edges, found = list(edges), []
    while edges:
        by_source = {}
        for edge in edges:
            by_source.setdefault(edge[0], []).append(edge)
        taken = {}

        def place(source, seen):
            for edge in by_source[source]:
                if edge[1] not in seen:
                    seen.add(edge[1])
                    if edge[1] not in taken or place(taken[edge[1]][0], seen):
                        taken[edge[1]] = edge
                        return True
            return False

        for source in range(count):
            place(source, set())
        found.append(sorted(taken.values()))
        for edge in taken.values():
            edges.remove(edge)
    return found


def column_routes(heads, size, unit):
    sizes = [lax.axis_size(name) for name in ALL]
    inner = sizes[2] * sizes[3] * sizes[4]
    edges = []
    for head in range(heads):
        for grp in range(sizes[1]):
            source = (head // inner * sizes[1] + grp) * inner + head % inner
            for part in range(3):
                start = (part * heads + head) * size
                for owner in sorted({start // unit, (start + size - 1) // unit}):
                    edges.append((source, owner, (part, start - owner * unit)))
    devices = heads * sizes[1]
    for matching in matchings(edges, devices):
        route = [edge[:2] for edge in matching]
        part_of, begin_of = [0] * devices, [0] * devices
        for source, owner, (part, begin) in matching:
            part_of[source], begin_of[owner] = part, begin
        yield route, part_of, begin_of


def fast_body(
    tile_embed, slide_lengths, head_offsets, pre_gain, pre_shift, qkv_weight, query_bias, value_bias, out_weight,
    out_bias, post_gain, post_shift, up_weight, up_bias, down_weight, down_bias, out_grad,
):
    width = qkv_weight.shape[0]
    heads = head_offsets.shape[1]
    size = width // heads
    tq = tile_embed.shape[1]
    br, groups = lax.axis_size("br"), lax.axis_size("grp")
    members = heads // br
    devices = heads * groups
    plan = Plan(heads, size, head_offsets.shape[0], br, members, tq, devices * tq)
    head = lax.axis_index(GROUP)
    group = lax.axis_index("grp")
    core = lax.axis_index("s0")
    meta = [group * plan.tokens, head, group, core, lax.axis_index(("br", "s1")), lax.axis_index(("grp", "s2"))]
    routes = list(column_routes(heads, size, 3 * width // devices))
    table = jnp.array([parts for _, parts, _ in routes] + [begins for _, _, begins in routes], jnp.int32)
    meta.extend(lax.dynamic_index_in_dim(table, lax.axis_index(ALL), 1, False))
    meta = jnp.stack(meta).astype(jnp.int32)
    tiles = tile_embed[0]
    own_w = jnp.concatenate(
        [lax.dynamic_slice_in_dim(qkv_weight, part * width + head * size, size, 1) for part in range(3)], 1
    ).T
    pair = [(0, 1), (1, 0)]
    plane, line = ("br", "s1"), ("grp", "s2")

    x, npre = enter_call(heads, tiles, pre_gain, pre_shift, qkv_weight, query_bias, value_bias)
    x = swap(x.reshape(heads, 3 * size, tq), GROUP)
    x, npre, own_w, meta = lax.optimization_barrier((x, npre, own_w, meta))
    halo = to_neighbours(select_call(plan, meta, head_offsets, x), groups)
    state, *own = near_call(plan, meta, slide_lengths, head_offsets, x)
    mixed, state = far_call(plan, meta, slide_lengths, head_offsets, state, own, halo)
    attn_t = swap(mixed, GROUP).reshape(width, tq)
    npre_all = lax.all_gather(npre, GROUP, axis=0, tiled=True)
    attn_t, npre_all = lax.optimization_barrier((attn_t, npre_all))

    attn_b = lax.ppermute(attn_t, "s0", pair)
    layer_out, residual_grad, attn_grad_t, common, sel, sel_give, sums, up_sums = middle_call(
        devices, core[None].astype(jnp.int32), attn_t, tiles, out_weight, out_bias, post_gain, post_shift,
        up_weight, up_bias, down_weight, down_bias, out_grad[0],
    )
    do = swap(attn_grad_t.reshape(heads, size, tq), GROUP)
    common_b = lax.ppermute(common, "s0", pair)
    sel_b = lax.ppermute(sel_give, "s0", pair)
    first, second = weights_call(devices, meta, attn_t, attn_b, common, common_b, sel, sel_b)
    do, first, second = lax.optimization_barrier((do, first, second))
    first = swap(first, plane)
    second = [second[0]] + [across(second[k], line, k) for k in (1, 2, 3)]
    rows, dq, dk, dv, *sides = far_back_call(plan, meta, slide_lengths, head_offsets, state, do, own, halo)
    back = from_neighbours(sides, groups)
    dx = near_back_call(plan, meta, slide_lengths, head_offsets, x, state, rows, (dq, dk, dv), back)
    dx, first, second = lax.optimization_barrier((dx, first, second))
    first, second = fold_call(meta, first, second)
    dx, first, second = lax.optimization_barrier((dx, first, second))
    first = [first[0]] + [across(first[k], line, k) for k in (1, 2, 3)]
    joined_grad = swap(dx, GROUP).reshape(heads, 3, size, tq)
    *columns, small = head_call(devices, meta, dx, npre_all, own_w, pre_gain, pre_shift, sums, up_sums)
    columns = [lax.ppermute(piece, ALL, route) for piece, (route, _, _) in zip(columns, routes)]
    second = [second[0]] + [across(second[k], plane, k) for k in (1, 2, 3)]
    joined_grad, small, second = lax.optimization_barrier((joined_grad, small, second))
    small = jnp.sum(swap(small, ALL), 0)
    joined_grad, first = lax.optimization_barrier((joined_grad, first))
    tile_grad = leave_call(tiles, pre_gain, qkv_weight, joined_grad, residual_grad)
    unit_up, unit = up_weight.shape[1] // devices, width // devices
    qkv_own, up_own, out_own, down_own = last_call(meta, 3 * unit, unit_up, unit, columns, first, second)
    return (
        layer_out[None],
        tile_grad[None],
        small[0:1, :unit],
        small[1:2, :unit],
        qkv_own.T,
        small[4:5, :unit],
        small[5:6, :unit],
        out_own.T,
        small[2:3, unit : 2 * unit],
        small[2:3, 2 * unit : 3 * unit],
        small[2:3, 3 * unit : 4 * unit],
        up_own.T,
        small[3:4, :unit_up],
        down_own.T,
        small[2:3, :unit],
    )


def solution(mesh):
    br, rows = mesh.shape["br"], mesh.shape["rows"]

    def run(*args):
        members = args[2].shape[1] // br
        shape = (br, rows // members, members // 4, 2, 2)
        split = jax.sharding.Mesh(mesh.devices.reshape(shape), ALL)
        tokens = P(("grp", "s2", "s1", "s0"), "br", None)
        owned = P(None, ALL)
        return jax.shard_map(
            fast_body if shape == (2, 2, 2, 2, 2) else body,
            mesh=split,
            in_specs=(tokens,) + (P(),) * 15 + (tokens,),
            out_specs=(tokens, tokens) + (owned,) * 13,
            check_vma=False,
        )(*args)

    return run
```

```python
import functools
import math

import jax
import jax.numpy as jnp
from jax import lax
from jax.experimental import pallas as pl
from jax.experimental.pallas import tpu as pltpu
from jax.sharding import PartitionSpec as P

SEG_BASE = 1024
DOC_MOST = 2048
LANES = 128
BF = jnp.bfloat16
F32 = jnp.float32
NEG = -1e30
EPS = 1e-05
ALL = ("br", "grp", "s2", "s1", "s0")
GROUP = ("br", "s2", "s1", "s0")
FIRST_DOWN = 2
ONE_LANE = 48
ID_Q = 51
ID_K = 52


class Plan:
    def __init__(self, heads, head_size, branches, groups, members, tq, total):
        self.heads, self.size, self.groups, self.members, self.tq = heads, head_size, groups, members, tq
        self.blocks = groups * members
        self.paired = groups * members * tq * 2 == total
        self.tokens = self.blocks * tq
        self.total = total
        self.halo = min(DOC_MOST, self.tokens)
        self.factor = math.log2(math.e) * head_size**-0.5
        self.branches = []
        keys, sel = 0, 0
        for level in range(branches):
            rate = 2**level
            span = min(SEG_BASE * rate, total)
            near = span <= self.tokens
            extra = 0 if near else self.halo // rate
            segs = self.tokens // span if near else 1
            seg_q = self.tokens // rate // segs
            seg_k = seg_q + 2 * extra
            self.branches.append(
                dict(
                    level=level, rate=rate, span=span, near=near, extra=extra, segs=segs,
                    seg_q=seg_q, seg_k=seg_k, tile=min(1024, seg_q), first=keys, sel=sel,
                )
            )
            keys += segs * seg_k
            sel += extra
        self.sel = sel
        self.near = [b for b in self.branches if b["near"]]
        self.far = [b for b in self.branches if not b["near"]]
        self.near_keys = sum(b["segs"] * b["seg_k"] for b in self.near)
        self.far_keys, self.own = 0, 0
        for b in self.far:
            b["begin"], b["own"] = self.far_keys, self.own
            self.far_keys += b["seg_k"]
            self.own += b["seg_q"]
        self.widest = max(b["seg_k"] for b in self.branches)

    def slot(self, block):
        return lax.rem(block, self.groups) * self.members + lax.div(block, self.groups)


def dot_nt(a, b):
    return lax.dot_general(a, b, (((1,), (1,)), ((), ())), preferred_element_type=F32)


def dot_tn(a, b):
    return lax.dot_general(a, b, (((0,), (0,)), ((), ())), preferred_element_type=F32)


def dot_nn(a, b):
    return lax.dot_general(a, b, (((1,), (0,)), ((), ())), preferred_element_type=F32)


def iota(shape, dim):
    return lax.broadcasted_iota(jnp.int32, shape, dim)


def placement(size, parts):
    shape = (parts * size + 16, parts * LANES)
    row, col = iota(shape, 0), iota(shape, 1)
    hit = col < 0
    for part in range(parts):
        hit |= (row >= part * size) & (row < (part + 1) * size) & (col == row - part * size + part * LANES)
    return row, col, hit


def ids_of(pos, starts, gate=None):
    found = jnp.zeros(pos.shape, jnp.int32)
    for start in starts:
        found += jnp.where(pos >= start, 1, 0)
    if gate is not None:
        found = jnp.where(gate, found, -1)
    return found.astype(F32)


def slide_starts(lens_ref):
    starts, at = [], jnp.int32(0)
    for i in range(lens_ref.shape[0]):
        starts.append(at)
        at = at + lens_ref[i]
    return starts


def branch_pos(plan, branch, base, off, first, count):
    start = base - branch["extra"] * branch["rate"] + off
    pos = start + branch["rate"] * (first + iota((1, count), 1))
    if branch["near"]:
        return pos, None
    shift = int(math.log2(branch["span"]))
    return pos, lax.shift_right_arithmetic(pos, shift) == lax.shift_right_arithmetic(base, shift)


def to_rows(plan, base, starts, x_ref, q_tm, k_tm, v_tm, extra_q=None):
    size, tq = plan.size, plan.tq
    row, col, hit = placement(size, 3)
    hit |= (row == 3 * size) & ((col == ID_Q) | (col == LANES + ID_K))
    place = jnp.where(hit, 1.0, 0.0).astype(BF)
    lane = iota((1, 3 * LANES), 1)
    in_k, in_v = lane - LANES, lane - 2 * LANES
    ones = jnp.where(
        ((in_k >= ONE_LANE) & (in_k < ONE_LANE + 3)) | ((in_v >= ONE_LANE) & (in_v < ONE_LANE + 3)), 1.0, 0.0
    )

    def block(n, carry):
        pos = base + n * tq + iota((1, tq), 1)
        ids = jnp.where(iota((16, tq), 0) == 0, ids_of(pos, starts), 0.0).astype(BF)
        full = jnp.concatenate([x_ref[plan.slot(n)], ids], 0)
        rows = dot_tn(full, place) + ones
        at = pl.ds(pl.multiple_of(n * tq, tq), tq)
        queries = rows[:, :LANES]
        if extra_q is not None:
            queries = queries + extra_q(n, at)
        q_tm[at, :] = queries
        k_tm[at, :] = rows[:, LANES : 2 * LANES]
        v_tm[at, :] = rows[:, 2 * LANES :]
        if extra_q is not None:
            return carry
        squares = [jnp.square(full[i * size : (i + 1) * size].astype(F32)) for i in range(2)]
        return tuple(jnp.maximum(a, jnp.sum(b, 0, keepdims=True)) for a, b in zip(carry, squares))

    start = (jnp.zeros((1, tq), F32),) * 2 if extra_q is None else 0
    most = lax.fori_loop(0, plan.blocks, block, start, unroll=4)
    if extra_q is None:
        return jnp.sqrt(jnp.max(most[0], 1, keepdims=True) * jnp.max(most[1], 1, keepdims=True)) * 1.0001
    return None


def gather_near(plan, offs, k_tm, v_tm, kall, vall, branches):
    for branch in branches:
        rate, first, off = branch["rate"], branch["first"], offs[branch["level"]]
        count = plan.tokens // rate
        step = min(256, count)

        def chunk(i, carry, rate=rate, first=first, off=off, step=step):
            rows = pl.ds(off + i * step * rate, step, stride=rate) if rate > 1 else pl.ds(i * step, step)
            to = pl.ds(pl.multiple_of(first + i * step, step), step)
            kall[to, :] = k_tm[rows, :].astype(BF)
            vall[to, :] = v_tm[rows, :].astype(BF)
            return carry

        lax.fori_loop(0, count // step, chunk, 0, unroll=min(4, count // step))


def far_keys(plan, base, offs, starts, halos, k_far, v_far, kall, vall):
    size = plan.size
    row, col, hit = placement(size, 2)
    hit |= (row == 2 * size) & (col == ID_K)
    place = jnp.where(hit, 1.0, 0.0).astype(BF)
    lane = iota((1, 2 * LANES), 1)
    in_v = lane - LANES
    ones = jnp.where(
        ((lane >= ONE_LANE) & (lane < ONE_LANE + 3)) | ((in_v >= ONE_LANE) & (in_v < ONE_LANE + 3)), 1.0, 0.0
    )
    for branch in plan.far:
        extra, first, own, count = branch["extra"], branch["begin"], branch["own"], branch["seg_q"]
        kall[first + extra : first + extra + count, :] = k_far[own : own + count, :]
        vall[first + extra : first + extra + count, :] = v_far[own : own + count, :]
        for side, ref in enumerate((halos[0], halos[-1])):
            begin = side * (extra + count)
            pos, gate = branch_pos(plan, branch, base, offs[branch["level"]], begin, extra)
            ids = jnp.where(iota((16, extra), 0) == 0, ids_of(pos, starts, gate), 0.0).astype(BF)
            piece = ref[:, branch["sel"] : branch["sel"] + extra]
            rows = dot_tn(jnp.concatenate([piece, ids], 0), place) + ones
            kall[first + begin : first + begin + extra, :] = rows[:, :LANES].astype(BF)
            vall[first + begin : first + begin + extra, :] = rows[:, LANES:].astype(BF)


def picked(branch, off, i):
    tile, rate = branch["tile"], branch["rate"]
    if rate == 1:
        return pl.ds(pl.multiple_of(i * tile, tile), tile)
    return pl.ds(off + i * tile * rate, tile, stride=rate)


def pieces_of(wide, most):
    step = next(n for n in (most, 512, 256, 128) if wide % n == 0)
    return [(at, step) for at in range(0, wide, step)]


def split3(column, lane):
    high = column.astype(BF).astype(F32)
    rest = column - high
    mid = rest.astype(BF).astype(F32)
    low = rest - mid
    return jnp.where(
        lane == ONE_LANE, high, jnp.where(lane == ONE_LANE + 1, mid, jnp.where(lane == ONE_LANE + 2, low, 0.0))
    )


def near_kernel(plan, meta, lens, offsets, x_ref, st_ref, qf_ref, kf_ref, vf_ref, q_tm, k_tm, v_tm, kall, vall, kid):
    base, head = meta[0], meta[1]
    starts = slide_starts(lens)
    offs = [offsets[b["level"], head] for b in plan.branches]
    top = to_rows(plan, base, starts, x_ref, q_tm, k_tm, v_tm)
    gather_near(plan, offs, k_tm, v_tm, kall, vall, plan.near)
    for branch in plan.far:
        rows = pl.ds(offs[branch["level"]], branch["seg_q"], stride=branch["rate"])
        own = slice(branch["own"], branch["own"] + branch["seg_q"])
        for ref, source in ((qf_ref, q_tm), (kf_ref, k_tm), (vf_ref, v_tm)):
            ref[own, :] = source[rows, :].astype(BF)
    for branch in plan.near:
        first, total = branch["first"], branch["segs"] * branch["seg_k"]
        pos, gate = branch_pos(plan, branch, base, offs[branch["level"]], 0, total)
        kid[:, first : first + total] = ids_of(pos, starts, gate)
    factor = plan.factor
    lane = iota((1, LANES), 1)

    def scan(visit):
        for branch in plan.near:
            per = branch["seg_q"] // branch["tile"]

            def tile(i, carry, branch=branch, per=per):
                rows = picked(branch, offs[branch["level"]], i)
                at = pl.multiple_of(branch["first"] + lax.div(i, per) * branch["seg_k"], 128)
                visit(branch, rows, q_tm[rows, :], at)
                return carry

            lax.fori_loop(0, branch["segs"] * per, tile, 0)

    def attend(top_lanes):
        def visit(branch, rows, queries, at):
            ids = queries[:, ID_Q : ID_Q + 1]
            low = (queries + top_lanes).astype(BF)
            mixed = None
            for begin, step in pieces_of(branch["seg_k"], 1024):
                to = pl.ds(at + begin, step)
                weights = jnp.exp2(dot_nt(low, kall[to, :]) * factor)
                weights = jnp.where(ids == kid[:, to], weights, 0.0).astype(BF)
                more = dot_nn(weights, vall[to, :])
                mixed = more if mixed is None else mixed + more
            if branch["level"]:
                mixed = st_ref[rows, :] + mixed
            st_ref[rows, :] = mixed

        scan(visit)

    attend(split3(-top, lane))
    step = min(512, plan.tokens)

    def least(n, low):
        at = pl.ds(pl.multiple_of(n * step, step), step)
        state = st_ref[at, :]
        st_ref[at, :] = jnp.where(iota((step, LANES), 1) == ID_Q, top, state)
        return jnp.minimum(low, jnp.min(state, 0, keepdims=True))

    weight = lax.fori_loop(0, plan.tokens // step, least, jnp.full((1, LANES), jnp.inf, F32), unroll=2)
    weight = jnp.min(jnp.where(lane == ONE_LANE, weight, jnp.inf))

    @pl.when(jnp.logical_not(weight > 2.0**-60))
    def _():
        def clear(n, carry):
            st_ref[pl.ds(pl.multiple_of(n * step, step), step), :] = jnp.full((step, LANES), NEG, F32)
            return carry

        def largest(branch, rows, queries, at):
            low = queries.astype(BF)
            best = st_ref[rows, :]
            for begin, step in pieces_of(branch["seg_k"], 256):
                to = pl.ds(at + begin, step)
                scores = jnp.where(queries[:, ID_Q : ID_Q + 1] == kid[:, to], dot_nt(low, kall[to, :]), NEG)
                best = jnp.maximum(best, jnp.max(scores, 1, keepdims=True))
            st_ref[rows, :] = best

        def settle(n, carry):
            at = pl.ds(pl.multiple_of(n * step, step), step)
            own = st_ref[at, :]
            tops[at, :] = own
            wide = iota((step, LANES), 1)
            q_tm[at, :] = q_tm[at, :] + split3(-own, wide)
            return carry

        def restore(n, carry):
            at = pl.ds(pl.multiple_of(n * step, step), step)
            st_ref[at, :] = jnp.where(iota((step, LANES), 1) == ID_Q, tops[at, :], st_ref[at, :])
            return carry

        tops = k_tm
        lax.fori_loop(0, plan.tokens // step, clear, 0)
        scan(largest)
        lax.fori_loop(0, plan.tokens // step, settle, 0)
        attend(jnp.zeros((1, LANES), F32))
        lax.fori_loop(0, plan.tokens // step, restore, 0)


def far_kernel(plan, meta, lens, offsets, st_in, qf_ref, kf_ref, vf_ref, *rest):
    halos, (o_ref, st_ref, kall, vall) = rest[:-4], rest[-4:]
    base, head = meta[0], meta[1]
    starts = slide_starts(lens)
    offs = [offsets[b["level"], head] for b in plan.branches]
    factor = plan.factor
    step = min(512, plan.tokens)

    def carry_over(n, carry):
        at = pl.ds(pl.multiple_of(n * step, step), step)
        st_ref[at, :] = st_in[at, :]
        return carry

    lax.fori_loop(0, plan.tokens // step, carry_over, 0, unroll=2)
    if plan.far:
        far_keys(plan, base, offs, starts, halos, kf_ref, vf_ref, kall, vall)
    for branch in plan.far:
        off, tile, wide = offs[branch["level"]], branch["tile"], branch["seg_k"]
        pos, gate = branch_pos(plan, branch, base, off, 0, wide)
        ids = ids_of(pos, starts, gate)
        keys = kall[branch["begin"] : branch["begin"] + wide, :]
        values = vall[branch["begin"] : branch["begin"] + wide, :]
        for i in range(branch["seg_q"] // tile):
            own = branch["own"] + i * tile
            queries = qf_ref[own : own + tile, :]
            rows = picked(branch, off, i)
            scores = dot_nt(queries, keys)
            scores = jnp.where(queries[:, ID_Q : ID_Q + 1].astype(F32) == ids, scores, NEG)
            top = jnp.max(scores, 1, keepdims=True)
            mixed = dot_nn(jnp.exp2((scores - top) * factor).astype(BF), values)
            old = st_ref[rows, :]
            old_top = old[:, ID_Q : ID_Q + 1]
            new_top = jnp.maximum(old_top, top)
            mixed = old * jnp.exp2((old_top - new_top) * factor) + mixed * jnp.exp2((top - new_top) * factor)
            st_ref[rows, :] = jnp.where(iota((tile, LANES), 1) == ID_Q, new_top, mixed)
    eye = jnp.where(iota((plan.size, LANES), 0) == iota((plan.size, LANES), 1), 1.0, 0.0).astype(BF)

    def finish(n, carry):
        at = pl.ds(pl.multiple_of(n * plan.tq, plan.tq), plan.tq)
        state = st_ref[at, :]
        weight = state[:, ONE_LANE : ONE_LANE + 1]
        top = state[:, ID_Q : ID_Q + 1]
        attn = state * (1.0 / weight)
        merged = top + jnp.log2(weight) * (1.0 / factor)
        lane = iota((plan.tq, LANES), 1)
        st_ref[at, :] = jnp.where(lane < plan.size, attn, jnp.where(lane == ONE_LANE, merged, 0.0))
        o_ref[plan.slot(n)] = dot_nt(eye, attn.astype(BF)).astype(BF)
        return carry

    lax.fori_loop(0, plan.blocks, finish, 0, unroll=4)


def back_tile(plan, branch, queries, grads, keys_at, kall, vall, k_fm, linked, dk_acc, dv_acc):
    dq = None
    for begin, step in pieces_of(branch["seg_k"], 256):
        to = pl.ds(keys_at + begin, step)
        part = slice(begin, begin + step)
        keys = kall[to, :]
        probs = jnp.where(linked(keys), jnp.exp2(dot_nt(keys, queries) * plan.factor), 0.0)
        dv_acc[part, :] += dot_nn(probs.astype(BF), grads)
        moved = (probs * dot_nt(vall[to, :], grads)).astype(BF)
        dk_acc[part, :] += dot_nn(moved, queries)
        more = dot_nn(k_fm[:, part], moved)
        dq = more if dq is None else dq + more
    return dq


def far_back_kernel(
    plan, meta, lens, offsets, st_ref, do_ref, qf_ref, kf_ref, vf_ref, *rest,
):
    sides = 1 if plan.paired else 2
    halos, (do_tm, dqf_ref, dkf_ref, dvf_ref), rest = rest[:sides], rest[sides : sides + 4], rest[sides + 4 :]
    halo_outs, (kall, vall, k_fm, dk_acc, dv_acc) = rest[:sides], rest[sides:]
    base, head = meta[0], meta[1]
    starts = slide_starts(lens)
    offs = [offsets[b["level"], head] for b in plan.branches]
    size, tq = plan.size, plan.tq
    row, col, hit = placement(size, 1)
    place = jnp.where(hit, 1.0, 0.0).astype(BF)
    lane = iota((tq, LANES), 1)

    def block(n, carry):
        at = pl.ds(pl.multiple_of(n * tq, tq), tq)
        grads = dot_tn(jnp.concatenate([do_ref[plan.slot(n)], jnp.zeros((16, tq), BF)], 0), place)
        dots = jnp.sum(jnp.where(lane < size, grads * st_ref[at, :], 0.0), 1, keepdims=True)
        do_tm[at, :] = grads + split3(-dots, lane)
        return carry

    lax.fori_loop(0, plan.blocks, block, 0, unroll=4)
    if plan.far:
        far_keys(plan, base, offs, starts, halos, kf_ref, vf_ref, kall, vall)
    eye = jnp.where(iota((LANES, LANES), 0) == iota((LANES, LANES), 1), 1.0, 0.0).astype(BF)
    for branch in plan.far:
        off, tile, wide, begin = offs[branch["level"]], branch["tile"], branch["seg_k"], branch["begin"]
        k_fm[:, :wide] = dot_nt(eye, kall[begin : begin + wide, :]).astype(BF)
        dk_acc[:wide, :] = jnp.zeros((wide, LANES), F32)
        dv_acc[:wide, :] = jnp.zeros((wide, LANES), F32)
        extra, count = branch["extra"], branch["seg_q"]
        for i in range(count // tile):
            own = branch["own"] + i * tile
            rows = picked(branch, off, i)
            wide_lane = iota((tile, LANES), 1)
            merged = st_ref[rows, :][:, ONE_LANE : ONE_LANE + 1]
            queries = jnp.where(wide_lane == ID_Q, 0.0, qf_ref[own : own + tile, :].astype(F32))
            queries = (queries + split3(-merged, wide_lane)).astype(BF)
            grads = do_tm[rows, :].astype(BF)
            pos, _ = branch_pos(plan, branch, base, off, extra + i * tile, tile)
            ids = ids_of(pos, starts)
            linked = lambda keys: keys[:, ID_K : ID_K + 1].astype(F32) == ids
            dq = back_tile(plan, branch, queries, grads, begin, kall, vall, k_fm, linked, dk_acc, dv_acc)
            dqf_ref[own : own + tile, :] = dq.T
        own = slice(branch["own"], branch["own"] + count)
        dkf_ref[own, :] = dk_acc[extra : extra + count, :]
        dvf_ref[own, :] = dv_acc[extra : extra + count, :]
        for side, ref in enumerate(halo_outs):
            at = side * (extra + count)
            if plan.paired:
                at = pl.multiple_of((1 - meta[2]) * (extra + count), 128)
            to = slice(branch["sel"], branch["sel"] + extra)
            dk = (dk_acc[pl.ds(at, extra), :] * size**-0.5).astype(BF)
            ref[:size, to] = dot_nt(eye[:size], dk).astype(BF)
            ref[size:, to] = dot_nt(eye[:size], dv_acc[pl.ds(at, extra), :].astype(BF)).astype(BF)


def near_back_kernel(
    plan, meta, lens, offsets, x_ref, st_ref, do_tm, dqf_ref, dkf_ref, dvf_ref, *rest,
):
    backs, (dx_ref, q_tm, k_tm, v_tm, dq_tm, dk_tm, dv_tm, kall, vall, k_fm, qid, dk_acc, dv_acc) = rest[:-13], rest[-13:]
    base, head = meta[0], meta[1]
    starts = slide_starts(lens)
    offs = [offsets[b["level"], head] for b in plan.branches]
    size, tq = plan.size, plan.tq
    lane = iota((tq, LANES), 1)
    to_rows(
        plan, base, starts, x_ref, q_tm, k_tm, v_tm,
        lambda n, at: split3(-st_ref[at, :][:, ONE_LANE : ONE_LANE + 1], lane),
    )
    gather_near(plan, offs, k_tm, v_tm, kall, vall, plan.near)
    eye = jnp.where(iota((LANES, LANES), 0) == iota((LANES, LANES), 1), 1.0, 0.0).astype(BF)
    for branch in plan.near:
        off, first, wide, tile = offs[branch["level"]], branch["first"], branch["seg_k"], branch["tile"]
        count = branch["segs"] * branch["seg_q"]
        per = branch["seg_q"] // tile
        pos, _ = branch_pos(plan, branch, base, off, 0, count)
        qid[:, :count] = ids_of(pos, starts)

        def segment(seg, carry, branch=branch, off=off, first=first, wide=wide, tile=tile, per=per):
            keys_at = pl.multiple_of(first + seg * wide, 128)
            k_fm[:, :wide] = dot_nt(eye, kall[pl.ds(keys_at, wide), :]).astype(BF)
            dk_acc[:wide, :] = jnp.zeros((wide, LANES), F32)
            dv_acc[:wide, :] = jnp.zeros((wide, LANES), F32)

            def one(j, carry):
                i = seg * per + j
                rows = picked(branch, off, i)
                queries = q_tm[rows, :].astype(BF)
                grads = do_tm[rows, :].astype(BF)
                ids = qid[:, pl.ds(pl.multiple_of(i * tile, tile), tile)]
                linked = lambda keys: keys[:, ID_K : ID_K + 1].astype(F32) == ids
                dq = back_tile(plan, branch, queries, grads, keys_at, kall, vall, k_fm, linked, dk_acc, dv_acc).T
                if branch["level"]:
                    dq = dq_tm[rows, :] + dq
                dq_tm[rows, :] = dq
                return carry

            lax.fori_loop(0, per, one, 0)
            step = min(256, branch["seg_q"])
            for c in range(branch["seg_q"] // step):
                begin = c * step
                if branch["rate"] == 1:
                    to = pl.ds(pl.multiple_of(seg * branch["seg_q"] + begin, step), step)
                    dk_tm[to, :] = dk_acc[begin : begin + step, :]
                    dv_tm[to, :] = dv_acc[begin : begin + step, :]
                else:
                    to = pl.ds(off + (seg * branch["seg_q"] + begin) * branch["rate"], step, stride=branch["rate"])
                    dk_tm[to, :] += dk_acc[begin : begin + step, :]
                    dv_tm[to, :] += dv_acc[begin : begin + step, :]
            return carry

        lax.fori_loop(0, branch["segs"], segment, 0)
    row, col, hit = placement(size, 2)
    place = jnp.where(hit, 1.0, 0.0).astype(BF)[: 2 * size]
    for branch in plan.far:
        off, rate, extra, count = offs[branch["level"]], branch["rate"], branch["extra"], branch["seg_q"]
        rows = pl.ds(off, count, stride=rate)
        own = slice(branch["own"], branch["own"] + count)
        for total, part in ((dq_tm, dqf_ref), (dk_tm, dkf_ref), (dv_tm, dvf_ref)):
            total[rows, :] += part[own, :]
        begins = [plan.tokens - plan.halo, 0]
        if plan.paired:
            begins = [(1 - meta[2]) * (plan.tokens - plan.halo)]
        for begin, ref in zip(begins, backs):
            more = dot_tn(ref[:, branch["sel"] : branch["sel"] + extra], place)
            rows = pl.ds(begin + off, extra, stride=rate)
            dk_tm[rows, :] += more[:, :LANES] * size**0.5
            dv_tm[rows, :] += more[:, LANES:]
    small_eye = eye[:size]

    def finish(n, carry):
        at = pl.ds(pl.multiple_of(n * tq, tq), tq)
        slot = plan.slot(n)
        dx_ref[slot, :size, :] = dot_nt(small_eye, (dq_tm[at, :] * size**-0.5).astype(BF)).astype(BF)
        dx_ref[slot, size : 2 * size, :] = dot_nt(small_eye, (dk_tm[at, :] * size**-0.5).astype(BF)).astype(BF)
        dx_ref[slot, 2 * size :, :] = dot_nt(small_eye, dv_tm[at, :].astype(BF)).astype(BF)
        return carry

    lax.fori_loop(0, plan.blocks, finish, 0, unroll=4)


SMEM = pl.BlockSpec(memory_space=pltpu.SMEM)
VMEM = pl.BlockSpec(memory_space=pltpu.VMEM)
TINY = pl.CostEstimate(flops=1000, bytes_accessed=1000, transcendentals=0)
PARAMS = pltpu.CompilerParams(vmem_limit_bytes=60 << 20)
ROOMY = pltpu.CompilerParams(vmem_limit_bytes=40 << 20)


def struct(shape, kind):
    return jax.ShapeDtypeStruct(shape, kind)


def kernel_call(name, kernel, ins, outs, scratch, flops):
    return pl.pallas_call(
        kernel,
        out_shape=tuple(struct(*out) for out in outs),
        in_specs=[SMEM] * 3 + [VMEM] * (len(ins) - 3),
        out_specs=(VMEM,) * len(outs),
        scratch_shapes=[pltpu.VMEM(*s) for s in scratch],
        compiler_params=ROOMY,
        cost_estimate=pl.CostEstimate(flops=flops, bytes_accessed=1000, transcendentals=0),
        name=name,
    )(*ins)


def near_call(plan, meta, lens, offsets, x):
    rows, keys = ((plan.tokens, LANES), F32), ((plan.near_keys, LANES), BF)
    own = ((plan.own, LANES), BF)
    return kernel_call(
        "near", functools.partial(near_kernel, plan), (meta, lens, offsets, x), (rows, own, own, own),
        (rows, rows, rows, keys, keys, ((1, plan.near_keys), F32)), 20_000_000_000,
    )


def far_call(plan, meta, lens, offsets, state, own, halo):
    keys = ((plan.far_keys, LANES), BF)
    return kernel_call(
        "far", functools.partial(far_kernel, plan), (meta, lens, offsets, state, *own, *halo),
        (((plan.blocks, plan.size, plan.tq), BF), ((plan.tokens, LANES), F32)), (keys, keys), 4_000_000_000,
    )


def far_back_call(plan, meta, lens, offsets, state, do, own, halo):
    keys = ((plan.far_keys, LANES), BF)
    part, side = ((plan.own, LANES), F32), ((2 * plan.size, max(plan.sel, LANES)), BF)
    acc = ((plan.widest, LANES), F32)
    return kernel_call(
        "far_back", functools.partial(far_back_kernel, plan), (meta, lens, offsets, state, do, *own, *halo),
        (((plan.tokens, LANES), F32), part, part, part) + (side,) * (1 if plan.paired else 2),
        (keys, keys, ((LANES, plan.widest), BF), acc, acc), 4_000_000_000,
    )


def near_back_call(plan, meta, lens, offsets, x, state, do_rows, parts, back):
    rows, keys = ((plan.tokens, LANES), F32), ((plan.near_keys, LANES), BF)
    acc = ((plan.widest, LANES), F32)
    return kernel_call(
        "near_back", functools.partial(near_back_kernel, plan),
        (meta, lens, offsets, x, state, do_rows, *parts, *back),
        (((plan.blocks, 3 * plan.size, plan.tq), BF),),
        (rows,) * 6 + (keys, keys, ((LANES, plan.widest), BF), ((1, plan.tokens), F32), acc, acc), 8_000_000_000,
    )[0]


def near_rows(values, norm_gain, norm_shift):
    centred = values - jnp.mean(values, 1, keepdims=True)
    inverse = lax.rsqrt(jnp.mean(centred * centred, 1, keepdims=True) + EPS)
    normed = centred * inverse
    return normed * norm_gain + norm_shift, normed, inverse


def back_rows(grad_out, normed, inverse, norm_gain):
    grad_norm = grad_out * norm_gain
    return inverse * (
        grad_norm
        - jnp.mean(grad_norm, 1, keepdims=True)
        - normed * jnp.mean(grad_norm * normed, 1, keepdims=True)
    )


def own_columns(size, unit, core):
    row, col = iota((size, size), 0), iota((size, size), 1)
    half = size // 2
    other = row >= half
    place = jnp.where(other, row - half, row)
    whole = jnp.floor((place.astype(F32) + 0.5) * (1.0 / unit)).astype(jnp.int32)
    parity = jnp.where(other, 1 - core, core)
    return jnp.where(col == place + unit * (whole + parity), 1.0, 0.0).astype(BF)


def middle_kernel(
    unit_up, unit, core_ref, attn_ref, tiles_ref, out_w, out_b, gain, shift, up_w, up_b, down_w, down_b, g_ref,
    y_ref, res_ref, ag_ref, common_ref, mine_ref, theirs_ref, sums_ref, up_sum_ref,
    pick_up, normed_s, lifted_s, inverse_s, out_s, back_s,
):
    step, steps = pl.program_id(0), pl.num_programs(0)
    width = tiles_ref.shape[1]
    chunk = up_w.shape[1]
    half = chunk // 2
    core = core_ref[0]
    hidden_sel = steps * half

    @pl.when(step == 0)
    def _():
        pick_up[...] = own_columns(chunk, unit_up, core)
        residual = tiles_ref[...].astype(F32) + dot_tn(attn_ref[...], out_w[...]) + out_b[...]
        lifted, normed, inverse = near_rows(residual, gain[...], shift[...])
        low = lifted.astype(BF)
        lifted_s[...] = low
        normed_s[...] = normed
        inverse_s[...] = jnp.broadcast_to(inverse, inverse_s.shape)
        out_s[...] = residual + down_b[...]
        back_s[...] = jnp.zeros_like(back_s)
        common_ref[pl.ds(steps * chunk, width), :] = low.T
        pick = own_columns(width, unit, core)
        picked_g = dot_nt(pick, g_ref[...]).astype(BF)
        mine_ref[pl.ds(hidden_sel, width // 2), :] = picked_g[: width // 2]
        theirs_ref[pl.ds(hidden_sel, width // 2), :] = picked_g[width // 2 :]

    lifted = lifted_s[...]
    gate_in = dot_nn(lifted, up_w[...]) + up_b[...]
    cdf = 0.5 + 0.5 * lax.erf(gate_in * (0.5**0.5))
    act = (gate_in * cdf).astype(BF)
    slope = cdf + gate_in * (jnp.exp(-0.5 * gate_in * gate_in) * (1.0 / math.sqrt(2.0 * math.pi)))
    gate_grad = (dot_nt(g_ref[...], down_w[...]) * slope).astype(BF)
    out_s[...] += dot_nn(act, down_w[...])
    back_s[...] += dot_nt(gate_grad, up_w[...])
    up_sum_ref[...] = jnp.sum(gate_grad.astype(F32), 0, keepdims=True)
    common_ref[pl.ds(pl.multiple_of(step * chunk, chunk), chunk), :] = act.T
    picked_gate = dot_nt(pick_up[...], gate_grad).astype(BF)
    at = pl.ds(pl.multiple_of(step * half, half), half)
    mine_ref[at, :] = picked_gate[:half]
    theirs_ref[at, :] = picked_gate[half:]

    @pl.when(step == steps - 1)
    def _():
        y_ref[...] = out_s[...].astype(BF)
        grads = g_ref[...].astype(F32)
        lifted_grad = back_s[...]
        normed = normed_s[...]
        residual_grad = grads + back_rows(lifted_grad, normed, inverse_s[:, :1], gain[...])
        res_ref[...] = residual_grad
        low = residual_grad.astype(BF)
        ag_ref[...] = dot_nt(out_w[...], low).astype(BF)
        pick = own_columns(width, unit, core)
        picked_p = dot_nt(pick, low).astype(BF)
        at = pl.ds(hidden_sel + width // 2, width // 2)
        mine_ref[at, :] = picked_p[: width // 2]
        theirs_ref[at, :] = picked_p[width // 2 :]
        sums_ref[0:1, :] = jnp.sum(grads, 0, keepdims=True)
        sums_ref[1:2, :] = jnp.sum(residual_grad, 0, keepdims=True)
        sums_ref[2:3, :] = jnp.sum(lifted_grad * normed, 0, keepdims=True)
        sums_ref[3:4, :] = jnp.sum(lifted_grad, 0, keepdims=True)
        sums_ref[4:8, :] = jnp.zeros((4, width), F32)


def middle_call(devices, core, attn_t, tiles, out_w, out_b, gain, shift, up_w, up_b, down_w, down_b, g):
    tq, width = tiles.shape
    hidden = up_w.shape[1]
    steps = hidden // width
    whole = lambda *shape: pl.BlockSpec(shape, lambda j: (0,) * len(shape))
    vec = whole(1, width)
    sel = hidden // 2 + width
    return pl.pallas_call(
        functools.partial(middle_kernel, hidden // devices, width // devices),
        grid=(steps,),
        in_specs=[
            SMEM, whole(width, tq), whole(tq, width), whole(width, width), vec, vec, vec,
            pl.BlockSpec((width, width), lambda j: (0, j)), pl.BlockSpec((1, width), lambda j: (0, j)),
            pl.BlockSpec((width, width), lambda j: (j, 0)), vec, whole(tq, width),
        ],
        out_specs=(
            whole(tq, width), whole(tq, width), whole(width, tq), whole(hidden + width, tq), whole(sel, tq),
            whole(sel, tq), whole(8, width), pl.BlockSpec((1, width), lambda j: (0, j)),
        ),
        out_shape=(
            jax.ShapeDtypeStruct((tq, width), BF),
            pltpu.HBM((tq, width), F32),
            jax.ShapeDtypeStruct((width, tq), BF),
            pltpu.HBM((hidden + width, tq), BF),
            pltpu.HBM((sel, tq), BF),
            pltpu.HBM((sel, tq), BF),
            pltpu.HBM((8, width), F32),
            pltpu.HBM((1, hidden), F32),
        ),
        scratch_shapes=[
            pltpu.VMEM((width, width), BF), pltpu.VMEM((tq, width), F32), pltpu.VMEM((tq, width), BF),
            pltpu.VMEM((tq, LANES), F32), pltpu.VMEM((tq, width), F32), pltpu.VMEM((tq, width), F32),
        ],
        compiler_params=ROOMY,
        cost_estimate=pl.CostEstimate(flops=14 * tq * width * hidden, bytes_accessed=20 << 20, transcendentals=0),
        name="middle",
    )(core, attn_t, tiles, out_w, out_b, gain, shift, up_w, up_b, down_w, down_b, g)


def weights_kernel(unit_up, unit, meta, attn_a, attn_b, common_a, common_b, sel_a, sel_b, *rest):
    first_ref, second_refs, (first_s, second_s, sems) = rest[0], rest[1:5], rest[5:]
    width = attn_a.shape[0]
    hidden = common_a.shape[0] - width
    chips = width // (2 * unit)

    def spot(chip):
        return (chip // 8) * 2 + chip % 2, chip // 2 % 4

    lifted = slice(hidden, hidden + width)
    group = width // (2 * unit_up)
    for step in range(hidden // width):
        rows = slice(step * width // 2, (step + 1) * width // 2)
        part = dot_nt(sel_a[rows, :], common_a[lifted, :]) + dot_nt(sel_b[rows, :], common_b[lifted, :])
        for i in range(group):
            plane, line = spot(step * group + i)
            first_s[plane, line, :unit_up, :] = part[i * unit_up : (i + 1) * unit_up].astype(BF)
    rows_out = slice(hidden // 2 + width // 2, hidden // 2 + width)
    rows = slice(hidden // 2, hidden // 2 + width // 2)
    out = dot_nt(sel_a[rows_out, :], attn_a[...]) + dot_nt(sel_b[rows_out, :], attn_b[...])
    held = [out]

    def down_part(step):
        cols = slice(step * width, (step + 1) * width)
        return dot_nt(sel_a[rows, :], common_a[cols, :]) + dot_nt(sel_b[rows, :], common_b[cols, :])

    held += [down_part(step) for step in range(FIRST_DOWN)]
    for chip in range(chips):
        plane, line = spot(chip)
        at = slice(chip * unit, (chip + 1) * unit)
        first_s[plane, line, unit_up:, :] = jnp.concatenate([part[at] for part in held], 0).astype(BF)
    copies = [pltpu.make_async_copy(first_s, first_ref, sems.at[4])]
    copies[0].start()
    for step in range(FIRST_DOWN, hidden // width):
        part = down_part(step)
        at = (step - FIRST_DOWN) * width
        for chip in range(chips):
            plane, line = spot(chip)
            second_s[line, plane, :, at : at + width] = part[chip * unit : (chip + 1) * unit].astype(BF)
    for k in range(4):
        copies.append(pltpu.make_async_copy(second_s.at[meta[5] ^ k], second_refs[k], sems.at[k]))
        copies[-1].start()
    for copy in copies:
        copy.wait()


def weights_call(devices, meta, attn_a, attn_b, common_a, common_b, sel_a, sel_b):
    width, tq = attn_a.shape
    hidden = common_a.shape[0] - width
    unit_up, unit = hidden // devices, width // devices
    first = (4, 4, unit_up + (1 + FIRST_DOWN) * unit, width)
    second = (4, unit, hidden - FIRST_DOWN * width)
    outs = pl.pallas_call(
        functools.partial(weights_kernel, unit_up, unit),
        in_specs=[SMEM] + [VMEM] * 6,
        out_specs=(pl.BlockSpec(memory_space=pltpu.HBM),) * 5,
        out_shape=(jax.ShapeDtypeStruct(first, BF),) + (jax.ShapeDtypeStruct(second, BF),) * 4,
        scratch_shapes=[pltpu.VMEM(first, BF), pltpu.VMEM((4,) + second, BF), pltpu.SemaphoreType.DMA((5,))],
        compiler_params=PARAMS,
        cost_estimate=pl.CostEstimate(flops=4 * tq * width * hidden, bytes_accessed=14 << 20, transcendentals=0),
        name="weights",
    )(meta, attn_a, attn_b, common_a, common_b, sel_a, sel_b)
    return outs[0], outs[1:]


def fold_kernel(meta, first_ref, own, got1, got2, got3, *outs):
    plane, line = meta[4], meta[5]
    for k in range(4):
        at = line ^ k
        total = first_ref[0, at].astype(F32)
        for i in range(1, 4):
            total += first_ref[i, at].astype(F32)
        outs[k][...] = total.astype(BF)
        at = plane ^ k
        total = own[at].astype(F32) + got1[at].astype(F32) + got2[at].astype(F32) + got3[at].astype(F32)
        outs[4 + k][...] = total.astype(BF)


def fold_call(meta, first, second):
    shapes = [jax.ShapeDtypeStruct(first.shape[2:], BF)] * 4 + [jax.ShapeDtypeStruct(second[0].shape[1:], BF)] * 4
    outs = pl.pallas_call(
        fold_kernel,
        in_specs=[SMEM] + [VMEM] * 5,
        out_specs=(VMEM,) * 8,
        out_shape=tuple(shapes),
        compiler_params=ROOMY,
        cost_estimate=TINY,
        name="fold",
    )(meta, first, *second)
    return outs[:4], outs[4:]


def last_kernel(unit_up, unit, meta, *refs):
    columns, first, second, outs = refs[:4], refs[4:8], refs[8:12], refs[12:]
    qkv_ref, up_ref, out_ref, down_ref, held = outs
    size = columns[0].shape[0]
    held[...] = jnp.zeros_like(held)
    for i, ref in enumerate(columns):
        at = pl.multiple_of(meta[10 + i] + size // 2, 8)
        held[pl.ds(at, size), :] += ref[...].astype(F32)
    qkv_ref[...] = held[size // 2 : size // 2 + qkv_ref.shape[0], :]
    total = first[0][...].astype(F32)
    for ref in first[1:]:
        total += ref[...].astype(F32)
    up_ref[...] = total[:unit_up]
    out_ref[...] = total[unit_up : unit_up + unit]
    width = total.shape[1]
    for i in range(FIRST_DOWN):
        at = unit_up + (1 + i) * unit
        down_ref[:, i * width : (i + 1) * width] = total[at : at + unit]
    width = FIRST_DOWN * width
    total = second[0][...].astype(F32)
    for ref in second[1:]:
        total += ref[...].astype(F32)
    down_ref[:, width:] = total


def last_call(meta, unit_qkv, unit_up, unit, columns, first, second):
    size, width = columns[0].shape
    hidden = FIRST_DOWN * width + second[0].shape[1]
    outs = ((unit_qkv, width), (unit_up, width), (unit, width), (unit, hidden))
    return pl.pallas_call(
        functools.partial(last_kernel, unit_up, unit),
        in_specs=[SMEM] + [VMEM] * 12,
        out_specs=(VMEM,) * 4,
        out_shape=tuple(jax.ShapeDtypeStruct(s, F32) for s in outs),
        scratch_shapes=[pltpu.VMEM((unit_qkv + size, width), F32)],
        compiler_params=ROOMY,
        cost_estimate=TINY,
        name="last",
    )(meta, *columns, *first, *second)


def enter_kernel(tiles_ref, gain, shift, w_ref, query_b, value_b, x_ref, npre_ref, low_s):
    part = pl.program_id(0)

    @pl.when(part == 0)
    def _():
        scaled, normed, _ = near_rows(tiles_ref[...].astype(F32), gain[...], shift[...])
        low_s[...] = scaled.astype(BF)
        npre_ref[...] = normed.astype(BF)

    bias = jnp.where(part == 0, query_b[...], jnp.where(part == 2, value_b[...], 0.0))
    joined = (dot_nn(low_s[...], w_ref[...]) + bias).T
    heads, _, size, tq = x_ref.shape
    x_ref[:, 0] = joined.astype(BF).reshape(heads, size, tq)


def enter_call(heads, tiles, gain, shift, weight, query_b, value_b):
    tq, width = tiles.shape
    size = width // heads
    whole = lambda *shape: pl.BlockSpec(shape, lambda i: (0,) * len(shape))
    vec = whole(1, width)
    return pl.pallas_call(
        enter_kernel,
        grid=(3,),
        in_specs=[whole(tq, width), vec, vec, pl.BlockSpec((width, width), lambda i: (0, i)), vec, vec],
        out_specs=(pl.BlockSpec((heads, 1, size, tq), lambda i: (0, i, 0, 0)), whole(tq, width)),
        out_shape=(jax.ShapeDtypeStruct((heads, 3, size, tq), BF), jax.ShapeDtypeStruct((tq, width), BF)),
        scratch_shapes=[pltpu.VMEM((tq, width), BF)],
        compiler_params=PARAMS,
        name="enter",
    )(tiles, gain, shift, weight, query_b, value_b)


def leave_kernel(tiles_ref, gain, w_ref, jg_ref, res_ref, out_ref, acc):
    part = pl.program_id(0)
    width, tq = acc.shape
    more = dot_nn(w_ref[...], jg_ref[:, 0].reshape(width, tq))

    @pl.when(part == 0)
    def _():
        acc[...] = more

    @pl.when(part == 1)
    def _():
        acc[...] += more

    @pl.when(part == 2)
    def _():
        _, normed, inverse = near_rows(tiles_ref[...].astype(F32), gain[...], gain[...])
        grads = (acc[...] + more).T
        out_ref[...] = (res_ref[...] + back_rows(grads, normed, inverse, gain[...])).astype(BF)


def leave_call(tiles, gain, weight, joined_grad, residual_grad):
    tq, width = tiles.shape
    heads, _, size, _ = joined_grad.shape
    whole = lambda *shape: pl.BlockSpec(shape, lambda i: (0,) * len(shape))
    return pl.pallas_call(
        leave_kernel,
        grid=(3,),
        in_specs=[
            whole(tq, width), whole(1, width), pl.BlockSpec((width, width), lambda i: (0, i)),
            pl.BlockSpec((heads, 1, size, tq), lambda i: (0, i, 0, 0)), whole(tq, width),
        ],
        out_specs=whole(tq, width),
        out_shape=jax.ShapeDtypeStruct((tq, width), BF),
        scratch_shapes=[pltpu.VMEM((width, tq), F32)],
        compiler_params=PARAMS,
        cost_estimate=TINY,
        name="leave",
    )(tiles, gain, weight, joined_grad, residual_grad)


def halo_hits(plan, offs, first, dims):
    wide = max(plan.sel, LANES)
    shape = (plan.tq, wide)
    token, col = iota(shape, 0) + first, iota(shape, 1)
    hit = col < 0
    for branch in plan.branches:
        if branch["extra"]:
            at = col - branch["sel"]
            inside = (at >= 0) & (at < branch["extra"])
            hit |= inside & (token == at * branch["rate"] + offs[branch["level"]])
    return jnp.where(hit, 1.0, 0.0).astype(BF)


def halo_blocks(plan):
    count = plan.halo // plan.tq
    for i in range(count):
        yield 0, plan.blocks - count + i, i * plan.tq
        yield 1, i, i * plan.tq


def static_slot(plan, block):
    return block % plan.groups * plan.members + block // plan.groups


def select_kernel(plan, meta, offsets, x_ref, *outs):
    offs = [offsets[b["level"], meta[1]] for b in plan.branches]
    if plan.paired:
        count = plan.halo // plan.tq
        total = jnp.zeros((2 * plan.size, max(plan.sel, LANES)), F32)
        for i in range(count):
            block = (1 - meta[2]) * (plan.blocks - count) + i
            total += dot_nn(x_ref[plan.slot(block), plan.size :, :], halo_hits(plan, offs, i * plan.tq, None))
        outs[0][...] = total.astype(BF)
        return
    last_ref, first_ref = outs
    total = [jnp.zeros((2 * plan.size, max(plan.sel, LANES)), F32) for _ in range(2)]
    for side, block, first in halo_blocks(plan):
        hits = halo_hits(plan, offs, first, None)
        total[side] += dot_nn(x_ref[static_slot(plan, block), plan.size :, :], hits)
    last_ref[...] = total[0].astype(BF)
    first_ref[...] = total[1].astype(BF)


def select_call(plan, meta, offsets, x):
    shape = jax.ShapeDtypeStruct((2 * plan.size, max(plan.sel, LANES)), BF)
    return pl.pallas_call(
        functools.partial(select_kernel, plan),
        in_specs=[SMEM, SMEM, VMEM],
        out_specs=(VMEM,) * (1 if plan.paired else 2),
        out_shape=(shape,) * (1 if plan.paired else 2),
        compiler_params=ROOMY,
        name="select",
    )(meta, offsets, x)


def to_owners(vector, owner, lane_of, devices):
    count = vector.shape[1]
    held = jnp.where(iota((devices, count), 0) == owner, vector, 0.0)
    hits = jnp.where(iota((count, LANES), 1) == lane_of, 1.0, 0.0)
    return lax.dot_general(
        held, hits, (((1,), (0,)), ((), ())), precision=lax.Precision.HIGHEST, preferred_element_type=F32
    )


def cut(index, unit):
    whole = jnp.floor((index.astype(F32) + 0.5) * (1.0 / unit)).astype(jnp.int32)
    return whole, index - whole * unit


def head_kernel(devices, meta, dx_ref, near_ref, w_ref, gain, shift, sums_ref, up_ref, *rest):
    column_refs, (small_ref, acc, col_s, row_s) = rest[:-4], rest[-4:]
    step, steps = pl.program_id(0), pl.num_programs(0)
    tq = dx_ref.shape[2]
    rows = dx_ref.shape[1]
    per = near_ref.shape[0] // tq
    size = rows // 3
    width = near_ref.shape[1]

    @pl.when(step == 0)
    def _():
        acc[...] = jnp.zeros_like(acc)
        col_s[...] = jnp.zeros_like(col_s)
        row_s[...] = jnp.zeros_like(row_s)

    for i in range(per):
        grads = dx_ref[i]
        acc[...] += dot_nn(grads, near_ref[i * tq : (i + 1) * tq, :])
        col_s[...] += jnp.broadcast_to(jnp.sum(grads.astype(F32), 1, keepdims=True), col_s.shape)
        row_s[...] += dot_nt(jnp.ones((8, tq), BF), grads)

    @pl.when(step == steps - 1)
    def _():
        head = meta[1]
        plain = acc[...]
        weight = plain * gain[...] + col_s[:, :1] * shift[...]
        acc[...] = weight
        for i, ref in enumerate(column_refs):
            at = pl.multiple_of(meta[6 + i] * size, 8)
            ref[...] = acc[pl.ds(at, size), :].astype(BF)
        own = w_ref[...].astype(F32)
        gain_part = jnp.sum(own * plain, 0, keepdims=True)
        shift_part = jnp.sum(own * col_s[:, :1], 0, keepdims=True)
        unit = width // devices
        owner = cut(iota((1, width), 1), unit)[0]
        lane = cut(iota((width, 1), 0), unit)[1]
        small_ref[:, 0, :] = to_owners(gain_part, owner, lane, devices)
        small_ref[:, 1, :] = to_owners(shift_part, owner, lane, devices)
        held = jnp.zeros((devices, LANES), F32)
        for i in range(4):
            held += to_owners(sums_ref[i : i + 1, :], owner, lane + i * unit, devices)
        small_ref[:, 2, :] = held
        hidden = up_ref.shape[1]
        unit_up = hidden // devices
        held = jnp.zeros((devices, LANES), F32)
        for i in range(hidden // width):
            owner_up = cut(iota((1, width), 1) + i * width, unit_up)[0]
            lane_up = cut(iota((width, 1), 0) + i * width, unit_up)[1]
            held += to_owners(up_ref[:, i * width : (i + 1) * width], owner_up, lane_up, devices)
        small_ref[:, 3, :] = held
        line = row_s[0:1, :]
        for i, part in enumerate((0, 2)):
            index = iota((1, rows), 1) - part * size
            inside = (index >= 0) & (index < size)
            owner_h = jnp.where(inside, 2 * head + cut(index, size // 2)[0], -1)
            lane_h = cut(iota((rows, 1), 0), size // 2)[1]
            small_ref[:, 4 + i, :] = to_owners(line, owner_h, lane_h, devices)
        small_ref[:, 6, :] = jnp.zeros((devices, LANES), F32)
        small_ref[:, 7, :] = jnp.zeros((devices, LANES), F32)


def head_call(devices, meta, dx, npre_all, own_w, gain, shift, sums, up_sums):
    blocks, rows, tq = dx.shape
    width = npre_all.shape[1]
    per = blocks // 4
    whole = lambda *shape: pl.BlockSpec(shape, lambda i: (0,) * len(shape))
    return pl.pallas_call(
        functools.partial(head_kernel, devices),
        grid=(4,),
        in_specs=[
            SMEM, pl.BlockSpec((per, rows, tq), lambda i: (i, 0, 0)), pl.BlockSpec((per * tq, width), lambda i: (i, 0)),
            whole(rows, width), whole(1, width), whole(1, width), whole(8, width), whole(1, up_sums.shape[1]),
        ],
        out_specs=(whole(rows // 3, width),) * 4 + (whole(devices, 8, LANES),),
        out_shape=(jax.ShapeDtypeStruct((rows // 3, width), BF),) * 4
        + (jax.ShapeDtypeStruct((devices, 8, LANES), F32),),
        scratch_shapes=[
            pltpu.VMEM((rows, width), F32), pltpu.VMEM((rows, LANES), F32), pltpu.VMEM((8, rows), F32),
        ],
        compiler_params=PARAMS,
        cost_estimate=TINY,
        name="head",
    )(meta, dx, npre_all, own_w, gain, shift, sums, up_sums)


def layer_norm_rows(values, norm_gain, norm_shift):
    row_mean = jnp.mean(values, -1, keepdims=True)
    centred = values - row_mean
    inverse = lax.rsqrt(jnp.mean(centred * centred, -1, keepdims=True) + EPS)
    normed = centred * inverse
    return (normed * norm_gain + norm_shift, normed, inverse)


def norm_back(grad_out, normed, inverse, norm_gain):
    grad_norm = grad_out * norm_gain
    grad_in = inverse * (
        grad_norm
        - jnp.mean(grad_norm, -1, keepdims=True)
        - normed * jnp.mean(grad_norm * normed, -1, keepdims=True)
    )
    return (grad_in, jnp.sum(grad_out * normed, 0), jnp.sum(grad_out, 0))


def swap(values, axes):
    return lax.all_to_all(values, axes, 0, 0, tiled=True)


def scatter_sum(values, orders):
    sizes = {name: lax.axis_size(name) for name in ALL}
    left = list(ALL)
    rows, cols = values.shape[1:]
    for stage, axes in enumerate(orders):
        values = values.reshape([sizes[name] for name in left] + [rows, cols])
        rest = [name for name in left if name not in axes]
        order = [left.index(name) for name in list(axes) + rest]
        values = values.transpose(order + [len(left), len(left) + 1])
        count = math.prod(sizes[name] for name in axes)
        values = values.reshape((count, -1, rows, cols))
        if count > 1:
            values = swap(values, axes)
            values = jnp.sum(values.astype(F32), 0)
            if stage < len(orders) - 1:
                values = values.astype(BF)
        left = rest
    return values.reshape(rows, cols).astype(F32)


def to_neighbours(pieces, count):
    if count == 2:
        return (lax.ppermute(pieces[0], "grp", [(0, 1), (1, 0)]),)
    return (
        lax.ppermute(pieces[0], "grp", [(i, i + 1) for i in range(count - 1)]),
        lax.ppermute(pieces[1], "grp", [(i + 1, i) for i in range(count - 1)]),
    )


def from_neighbours(pieces, count):
    return to_neighbours(pieces[::-1], count)[::-1]


def share_columns(weight_t, sums, width):
    members, size = lax.axis_size(GROUP), weight_t.shape[1]
    head = lax.axis_index(GROUP)
    full = jnp.zeros((3, members) + weight_t.shape[1:], F32)
    full = lax.dynamic_update_slice(full, weight_t[:, None], (0, head, 0, 0))
    full_sums = lax.dynamic_update_slice(jnp.zeros((3, members, size), F32), sums[:, None], (0, head, 0))
    weight = lax.psum_scatter(full.reshape(3 * members * size, width), ALL, scatter_dimension=0, tiled=True)
    sums = lax.psum_scatter(full_sums.reshape(3, members * size), ALL, scatter_dimension=1, tiled=True)
    return weight, sums[0], sums[2]


def body(
    tile_embed,
    slide_lengths,
    head_offsets,
    pre_gain,
    pre_shift,
    qkv_weight,
    query_bias,
    value_bias,
    out_weight,
    out_bias,
    post_gain,
    post_shift,
    up_weight,
    up_bias,
    down_weight,
    down_bias,
    out_grad,
):
    width = qkv_weight.shape[0]
    hidden = up_weight.shape[1]
    heads = head_offsets.shape[1]
    size = width // heads
    tq = tile_embed.shape[1]
    br, groups = lax.axis_size("br"), lax.axis_size("grp")
    members = heads // br
    devices = heads * groups
    plan = Plan(heads, size, head_offsets.shape[0], br, members, tq, devices * tq)
    head = lax.axis_index(GROUP)
    base = lax.axis_index("grp") * plan.tokens
    meta = jnp.stack([base, head, lax.axis_index("grp")]).astype(jnp.int32)

    tiles = tile_embed[0].astype(F32)
    pre_out, normed_pre, inverse_pre = layer_norm_rows(tiles, pre_gain, pre_shift)
    normed_low = pre_out.astype(BF)
    bias_col = jnp.concatenate([query_bias, jnp.zeros_like(query_bias), value_bias], 1).reshape(-1, 1)
    joined_t = (
        lax.dot_general(qkv_weight, normed_low, (((0,), (1,)), ((), ())), preferred_element_type=F32) + bias_col
    ).astype(BF)
    x = joined_t.reshape(3, heads, size, tq).transpose(1, 0, 2, 3).reshape(heads, 3 * size, tq)
    x = swap(x, GROUP)
    normed_all = lax.all_gather(normed_low, GROUP, axis=0, tiled=True)

    halo = to_neighbours(select_call(plan, meta, head_offsets, x), groups)
    state, *own = near_call(plan, meta, slide_lengths, head_offsets, x)
    mixed, state = far_call(plan, meta, slide_lengths, head_offsets, state, own, halo)
    attn_t = swap(mixed, GROUP).reshape(width, tq)

    projected = lax.dot_general(attn_t, out_weight, (((0,), (0,)), ((), ())), preferred_element_type=F32)
    residual = tiles + projected + out_bias
    post_out, normed_post, inverse_post = layer_norm_rows(residual, post_gain, post_shift)
    lifted = post_out.astype(BF)
    gate_in = jnp.dot(lifted, up_weight, preferred_element_type=F32) + up_bias
    act_float, gelu_pull = jax.vjp(lambda v: jax.nn.gelu(v, approximate=False), gate_in)
    act_low = act_float.astype(BF)
    layer_out = (residual + jnp.dot(act_low, down_weight, preferred_element_type=F32) + down_bias).astype(BF)[None]
    grad_low = out_grad[0]
    grad_float = grad_low.astype(F32)
    act_grad = lax.dot_general(grad_low, down_weight, (((1,), (1,)), ((), ())), preferred_element_type=F32)
    gate_grad = gelu_pull(act_grad)[0].astype(BF)
    lifted_grad = lax.dot_general(gate_grad, up_weight, (((1,), (1,)), ((), ())), preferred_element_type=F32)
    norm_part, post_gain_sum, post_shift_sum = norm_back(lifted_grad, normed_post, inverse_post, post_gain)
    residual_grad = grad_float + norm_part
    proj_grad = residual_grad.astype(BF)
    attn_grad_t = lax.dot_general(
        out_weight, proj_grad, (((1,), (1,)), ((), ())), preferred_element_type=F32
    ).astype(BF)
    do = swap(attn_grad_t.reshape(heads, size, tq), GROUP)

    tokens = (((0,), (0,)), ((), ()))
    up_part = lax.dot_general(gate_grad, lifted, tokens, preferred_element_type=F32).astype(BF)
    down_part = lax.dot_general(grad_low, act_low, tokens, preferred_element_type=F32).astype(BF)
    out_part = lax.dot_general(proj_grad, attn_t, (((0,), (1,)), ((), ())), preferred_element_type=F32).astype(BF)
    vectors = [
        jnp.sum(gate_grad.astype(F32), 0).reshape(devices, -1),
        jnp.sum(grad_float, 0).reshape(devices, -1),
        jnp.sum(residual_grad, 0).reshape(devices, -1),
        post_gain_sum.reshape(devices, -1),
        post_shift_sum.reshape(devices, -1),
    ]
    ends = [0]
    for vector in vectors:
        ends.append(ends[-1] + vector.shape[1])
    small = jnp.concatenate(vectors, 1)
    small = jnp.pad(small[:, None, :], ((0, 0), (0, 7), (0, width - small.shape[1]))).astype(BF)
    misc = jnp.concatenate([out_part.reshape(devices, -1, width), small], 1)
    first, second = (("s0",), ("br", "s1"), ("grp", "s2")), (("s0",), ("grp", "s2"), ("br", "s1"))
    up_own = scatter_sum(up_part.reshape(devices, -1, width), first)
    down_own = scatter_sum(down_part.reshape(devices, -1, hidden), second)
    misc_own = scatter_sum(misc, first)
    unit = width // devices
    small_own = misc_own[unit]
    small_own = [small_own[None, ends[i] : ends[i + 1]] for i in range(len(vectors))]

    rows, dq, dk, dv, *sides = far_back_call(plan, meta, slide_lengths, head_offsets, state, do, own, halo)
    back = from_neighbours(sides, groups)
    dx = near_back_call(plan, meta, slide_lengths, head_offsets, x, state, rows, (dq, dk, dv), back)
    joined_grad_t = swap(dx, GROUP).reshape(heads, 3, size, tq).transpose(1, 0, 2, 3).reshape(3 * width, tq)
    weight_t = jnp.einsum(
        "nct,ntd->cd", dx, normed_all.reshape(heads, tq, width), preferred_element_type=F32
    ).reshape(3, size, width)
    head_sums = jnp.sum(dx.astype(F32), (0, 2)).reshape(3, size)
    qkv_own, query_own, value_own = share_columns(weight_t, head_sums, width)
    normed_grad = lax.dot_general(joined_grad_t, qkv_weight, (((0,), (1,)), ((), ())), preferred_element_type=F32)
    tile_part, pre_gain_sum, pre_shift_sum = norm_back(normed_grad, normed_pre, inverse_pre, pre_gain)
    tile_grad = (residual_grad + tile_part).astype(BF)[None]
    last = jnp.stack([pre_gain_sum, pre_shift_sum]).reshape(2, devices, unit).transpose(1, 0, 2)
    last = jnp.pad(last, ((0, 0), (0, 6), (0, LANES - unit)))
    last = jnp.sum(swap(last, ALL).reshape(devices, 8, LANES), 0)
    return (
        layer_out,
        tile_grad,
        last[0:1, :unit],
        last[1:2, :unit],
        qkv_own.T,
        query_own[None],
        value_own[None],
        misc_own[:unit].T,
        small_own[2],
        small_own[3],
        small_own[4],
        up_own.T,
        small_own[0],
        down_own.T,
        small_own[1],
    )


def across(piece, axes, k):
    return lax.ppermute(piece, axes, [(i, i ^ k) for i in range(4)])


def matchings(edges, count):
    edges, found = list(edges), []
    while edges:
        by_source = {}
        for edge in edges:
            by_source.setdefault(edge[0], []).append(edge)
        taken = {}

        def place(source, seen):
            for edge in by_source[source]:
                if edge[1] not in seen:
                    seen.add(edge[1])
                    if edge[1] not in taken or place(taken[edge[1]][0], seen):
                        taken[edge[1]] = edge
                        return True
            return False

        for source in range(count):
            place(source, set())
        found.append(sorted(taken.values()))
        for edge in taken.values():
            edges.remove(edge)
    return found


def column_routes(heads, size, unit):
    sizes = [lax.axis_size(name) for name in ALL]
    inner = sizes[2] * sizes[3] * sizes[4]
    edges = []
    for head in range(heads):
        for grp in range(sizes[1]):
            source = (head // inner * sizes[1] + grp) * inner + head % inner
            for part in range(3):
                start = (part * heads + head) * size
                for owner in sorted({start // unit, (start + size - 1) // unit}):
                    edges.append((source, owner, (part, start - owner * unit)))
    devices = heads * sizes[1]
    for matching in matchings(edges, devices):
        route = [edge[:2] for edge in matching]
        part_of, begin_of = [0] * devices, [0] * devices
        for source, owner, (part, begin) in matching:
            part_of[source], begin_of[owner] = part, begin
        yield route, part_of, begin_of


def fast_body(
    tile_embed, slide_lengths, head_offsets, pre_gain, pre_shift, qkv_weight, query_bias, value_bias, out_weight,
    out_bias, post_gain, post_shift, up_weight, up_bias, down_weight, down_bias, out_grad,
):
    width = qkv_weight.shape[0]
    heads = head_offsets.shape[1]
    size = width // heads
    tq = tile_embed.shape[1]
    br, groups = lax.axis_size("br"), lax.axis_size("grp")
    members = heads // br
    devices = heads * groups
    plan = Plan(heads, size, head_offsets.shape[0], br, members, tq, devices * tq)
    head = lax.axis_index(GROUP)
    group = lax.axis_index("grp")
    core = lax.axis_index("s0")
    meta = [group * plan.tokens, head, group, core, lax.axis_index(("br", "s1")), lax.axis_index(("grp", "s2"))]
    routes = list(column_routes(heads, size, 3 * width // devices))[::-1]
    table = jnp.array([parts for _, parts, _ in routes] + [begins for _, _, begins in routes], jnp.int32)
    meta.extend(lax.dynamic_index_in_dim(table, lax.axis_index(ALL), 1, False))
    meta = jnp.stack(meta).astype(jnp.int32)
    tiles = tile_embed[0]
    own_w = jnp.concatenate(
        [lax.dynamic_slice_in_dim(qkv_weight, part * width + head * size, size, 1) for part in range(3)], 1
    ).T
    pair = [(0, 1), (1, 0)]
    plane, line = ("br", "s1"), ("grp", "s2")

    x, npre = enter_call(heads, tiles, pre_gain, pre_shift, qkv_weight, query_bias, value_bias)
    x = swap(x.reshape(heads, 3 * size, tq), GROUP)
    x, npre, own_w, meta = lax.optimization_barrier((x, npre, own_w, meta))
    halo = to_neighbours(select_call(plan, meta, head_offsets, x), groups)
    state, *own = near_call(plan, meta, slide_lengths, head_offsets, x)
    mixed, state = far_call(plan, meta, slide_lengths, head_offsets, state, own, halo)
    attn_t = swap(mixed, GROUP).reshape(width, tq)
    npre_all = lax.all_gather(npre, GROUP, axis=0, tiled=True)
    attn_b = lax.ppermute(attn_t, "s0", pair)
    layer_out, residual_grad, attn_grad_t, common, sel, sel_give, sums, up_sums = middle_call(
        devices, core[None].astype(jnp.int32), attn_t, tiles, out_weight, out_bias, post_gain, post_shift,
        up_weight, up_bias, down_weight, down_bias, out_grad[0],
    )
    do = swap(attn_grad_t.reshape(heads, size, tq), GROUP)
    common_b = lax.ppermute(common, "s0", pair)
    sel_b = lax.ppermute(sel_give, "s0", pair)
    first, second = weights_call(devices, meta, attn_t, attn_b, common, common_b, sel, sel_b)
    do, first, second, npre_all = lax.optimization_barrier((do, first, second, npre_all))
    first = swap(first, plane)
    second = [second[0]] + [across(second[k], line, k) for k in (1, 2, 3)]
    rows, dq, dk, dv, *sides = far_back_call(plan, meta, slide_lengths, head_offsets, state, do, own, halo)
    back = from_neighbours(sides, groups)
    dx = near_back_call(plan, meta, slide_lengths, head_offsets, x, state, rows, (dq, dk, dv), back)
    dx, first, second = lax.optimization_barrier((dx, first, second))
    first, second = fold_call(meta, first, second)
    dx, first, second = lax.optimization_barrier((dx, first, second))
    first = [first[0]] + [across(first[k], line, k) for k in (1, 2, 3)]
    joined_grad = swap(dx, GROUP).reshape(heads, 3, size, tq)
    *columns, small = head_call(devices, meta, dx, npre_all, own_w, pre_gain, pre_shift, sums, up_sums)
    *columns, third = lax.optimization_barrier((*columns, second[3]))
    columns = [lax.ppermute(piece, ALL, route) for piece, (route, _, _) in zip(columns, routes)]
    second = [second[0], across(second[1], plane, 1), across(second[2], plane, 2), across(third, plane, 3)]
    joined_grad, small, second = lax.optimization_barrier((joined_grad, small, second))
    small = jnp.sum(swap(small, ALL), 0)
    joined_grad, first = lax.optimization_barrier((joined_grad, first))
    tile_grad = leave_call(tiles, pre_gain, qkv_weight, joined_grad, residual_grad)
    unit_up, unit = up_weight.shape[1] // devices, width // devices
    qkv_own, up_own, out_own, down_own = last_call(meta, 3 * unit, unit_up, unit, columns, first, second)
    return (
        layer_out[None],
        tile_grad[None],
        small[0:1, :unit],
        small[1:2, :unit],
        qkv_own.T,
        small[4:5, :unit],
        small[5:6, :unit],
        out_own.T,
        small[2:3, unit : 2 * unit],
        small[2:3, 2 * unit : 3 * unit],
        small[2:3, 3 * unit : 4 * unit],
        up_own.T,
        small[3:4, :unit_up],
        down_own.T,
        small[2:3, :unit],
    )


def solution(mesh):
    br, rows = mesh.shape["br"], mesh.shape["rows"]

    def run(*args):
        members = args[2].shape[1] // br
        shape = (br, rows // members, members // 4, 2, 2)
        split = jax.sharding.Mesh(mesh.devices.reshape(shape), ALL)
        tokens = P(("grp", "s2", "s1", "s0"), "br", None)
        owned = P(None, ALL)
        return jax.shard_map(
            fast_body if shape == (2, 2, 2, 2, 2) else body,
            mesh=split,
            in_specs=(tokens,) + (P(),) * 15 + (tokens,),
            out_specs=(tokens, tokens) + (owned,) * 13,
            check_vma=False,
        )(*args)

    return run
```

```python
import functools
import math

import jax
import jax.numpy as jnp
import ml_dtypes
import numpy as np
from jax import lax
from jax.experimental import pallas as pl
from jax.experimental.pallas import tpu as pltpu
from jax.sharding import PartitionSpec as P

SEG_BASE = 1024
DOC_MOST = 2048
LANES = 128
BF = jnp.bfloat16
F32 = jnp.float32
NEG = -1e30
EPS = 1e-05
ALL = ("br", "grp", "s2", "s1", "s0")
GROUP = ("br", "s2", "s1", "s0")
FIRST_DOWN = 2
ONE_LANE = 48
ID_Q = 51
ID_K = 52
TWICE = 53


class Plan:
    def __init__(self, heads, head_size, branches, groups, members, tq, total):
        self.heads, self.size, self.groups, self.members, self.tq = heads, head_size, groups, members, tq
        self.blocks = groups * members
        self.paired = groups * members * tq * 2 == total
        self.tokens = self.blocks * tq
        self.total = total
        self.halo = min(DOC_MOST, self.tokens)
        self.factor = math.log2(math.e) * head_size**-0.5
        self.branches = []
        keys, sel = 0, 0
        for level in range(branches):
            rate = 2**level
            span = min(SEG_BASE * rate, total)
            near = span <= self.tokens
            extra = 0 if near else self.halo // rate
            segs = self.tokens // span if near else 1
            seg_q = self.tokens // rate // segs
            seg_k = seg_q + 2 * extra
            flip = 0
            if level == 1 and near and span == 2 * self.branches[0]["span"]:
                segs, seg_q, seg_k, flip = segs * 2, seg_q // 2, seg_k // 2, 1
            self.branches.append(
                dict(
                    level=level, rate=rate, span=span, near=near, extra=extra, segs=segs,
                    seg_q=seg_q, seg_k=seg_k, tile=min(1024, seg_q), first=keys, sel=sel, flip=flip,
                )
            )
            keys += segs * seg_k
            sel += extra
        self.sel = sel
        self.twice = any(b["flip"] for b in self.branches)
        self.near = [b for b in self.branches if b["near"]]
        self.far = [b for b in self.branches if not b["near"]]
        self.near_keys = sum(b["segs"] * b["seg_k"] for b in self.near)
        self.far_keys, self.own = 0, 0
        for b in self.far:
            b["begin"], b["own"] = self.far_keys, self.own
            self.far_keys += b["seg_k"]
            self.own += b["seg_q"]
        self.widest = max(b["seg_k"] for b in self.branches)

    def slot(self, block):
        return lax.rem(block, self.groups) * self.members + lax.div(block, self.groups)


def dot_nt(a, b):
    return lax.dot_general(a, b, (((1,), (1,)), ((), ())), preferred_element_type=F32)


def dot_tn(a, b):
    return lax.dot_general(a, b, (((0,), (0,)), ((), ())), preferred_element_type=F32)


def dot_nn(a, b):
    return lax.dot_general(a, b, (((1,), (0,)), ((), ())), preferred_element_type=F32)


def iota(shape, dim):
    return lax.broadcasted_iota(jnp.int32, shape, dim)


def placement(size, parts):
    shape = (parts * size + 16, parts * LANES)
    row, col = iota(shape, 0), iota(shape, 1)
    hit = col < 0
    for part in range(parts):
        hit |= (row >= part * size) & (row < (part + 1) * size) & (col == row - part * size + part * LANES)
    return row, col, hit


def ids_of(pos, starts, gate=None):
    found = jnp.zeros(pos.shape, jnp.int32)
    for start in starts:
        found += jnp.where(pos >= start, 1, 0)
    if gate is not None:
        found = jnp.where(gate, found, -1)
    return found.astype(F32)


def slide_starts(lens_ref):
    starts, at = [], jnp.int32(0)
    for i in range(lens_ref.shape[0]):
        starts.append(at)
        at = at + lens_ref[i]
    return starts


def branch_pos(plan, branch, base, off, first, count):
    start = base - branch["extra"] * branch["rate"] + off
    pos = start + branch["rate"] * (first + iota((1, count), 1))
    if branch["near"]:
        return pos, None
    shift = int(math.log2(branch["span"]))
    return pos, lax.shift_right_arithmetic(pos, shift) == lax.shift_right_arithmetic(base, shift)


def plain_keys(rows):
    lane = iota(rows.shape, 1)
    return jnp.where((lane >= TWICE) & (lane < TWICE + 3), 0.0, rows)


def to_rows(plan, base, offs, starts, x_ref, q_tm, k_tm, v_tm, extra_q=None):
    size, tq = plan.size, plan.tq
    row, col, hit = placement(size, 3)
    hit |= (row == 3 * size) & ((col == ID_Q) | (col == LANES + ID_K))
    place = jnp.where(hit, 1.0, 0.0).astype(BF)
    lane = iota((1, 3 * LANES), 1)
    in_k, in_v = lane - LANES, lane - 2 * LANES
    ones = jnp.where(
        ((in_k >= ONE_LANE) & (in_k < ONE_LANE + 3)) | ((in_v >= ONE_LANE) & (in_v < ONE_LANE + 3)), 1.0, 0.0
    )

    more = jnp.zeros((1, LANES), F32)
    rest = 1.0 / plan.factor
    for i in range(3 if plan.twice else 0):
        term = float(np.float32(rest).astype(ml_dtypes.bfloat16))
        more = jnp.where(lane[:, :LANES] == TWICE + i, term, more)
        rest -= term
    own = iota((1, LANES), 1)
    both = jnp.where((own >= TWICE) & (own < TWICE + 3), 1.0, 0.0)

    def block(n, carry):
        pos = base + n * tq + iota((1, tq), 1)
        ids = jnp.where(iota((16, tq), 0) == 0, ids_of(pos, starts), 0.0).astype(BF)
        full = jnp.concatenate([x_ref[plan.slot(n)], ids], 0)
        rows = dot_tn(full, place) + ones
        at = pl.ds(pl.multiple_of(n * tq, tq), tq)
        queries = rows[:, :LANES]
        if extra_q is not None:
            queries = queries + extra_q(n, at)
        keys = rows[:, LANES : 2 * LANES]
        if plan.twice:
            member = (iota((tq, 1), 0) & 1) == offs[1]
            queries = jnp.where(member, queries + more, queries)
            keys = jnp.where(member, keys + both, keys)
        q_tm[at, :] = queries
        k_tm[at, :] = keys
        v_tm[at, :] = rows[:, 2 * LANES :]
        if extra_q is not None:
            return carry
        squares = [jnp.square(full[i * size : (i + 1) * size].astype(F32)) for i in range(2)]
        return tuple(jnp.maximum(a, jnp.sum(b, 0, keepdims=True)) for a, b in zip(carry, squares))

    start = (jnp.zeros((1, tq), F32),) * 2 if extra_q is None else 0
    most = lax.fori_loop(0, plan.blocks, block, start, unroll=4)
    if extra_q is None:
        return jnp.sqrt(jnp.max(most[0], 1, keepdims=True) * jnp.max(most[1], 1, keepdims=True)) * 1.0001
    return None


def gather_near(plan, offs, k_tm, v_tm, kall, vall, branches):
    for branch in branches:
        rate, first, off = branch["rate"], branch["first"], offs[branch["level"]]
        count = plan.tokens // rate
        step = min(256, count)

        def chunk(i, carry, rate=rate, first=first, off=off, step=step):
            keys = k_tm[pl.ds(off + i * step * rate, step, stride=rate) if rate > 1 else pl.ds(i * step, step), :]
            rows = pl.ds(off + i * step * rate, step, stride=rate) if rate > 1 else pl.ds(i * step, step)
            to = pl.ds(pl.multiple_of(first + i * step, step), step)
            kall[to, :] = (plain_keys(keys) if rate > 1 else keys).astype(BF)
            vall[to, :] = v_tm[rows, :].astype(BF)
            return carry

        lax.fori_loop(0, count // step, chunk, 0, unroll=min(4, count // step))


def far_keys(plan, base, offs, starts, halos, k_far, v_far, kall, vall):
    size = plan.size
    row, col, hit = placement(size, 2)
    hit |= (row == 2 * size) & (col == ID_K)
    place = jnp.where(hit, 1.0, 0.0).astype(BF)
    lane = iota((1, 2 * LANES), 1)
    in_v = lane - LANES
    ones = jnp.where(
        ((lane >= ONE_LANE) & (lane < ONE_LANE + 3)) | ((in_v >= ONE_LANE) & (in_v < ONE_LANE + 3)), 1.0, 0.0
    )
    for branch in plan.far:
        extra, first, own, count = branch["extra"], branch["begin"], branch["own"], branch["seg_q"]
        kall[first + extra : first + extra + count, :] = k_far[own : own + count, :]
        vall[first + extra : first + extra + count, :] = v_far[own : own + count, :]
        for side, ref in enumerate((halos[0], halos[-1])):
            begin = side * (extra + count)
            pos, gate = branch_pos(plan, branch, base, offs[branch["level"]], begin, extra)
            ids = jnp.where(iota((16, extra), 0) == 0, ids_of(pos, starts, gate), 0.0).astype(BF)
            piece = ref[:, branch["sel"] : branch["sel"] + extra]
            rows = dot_tn(jnp.concatenate([piece, ids], 0), place) + ones
            kall[first + begin : first + begin + extra, :] = rows[:, :LANES].astype(BF)
            vall[first + begin : first + begin + extra, :] = rows[:, LANES:].astype(BF)


def picked(branch, off, i):
    tile, rate = branch["tile"], branch["rate"]
    if rate == 1:
        return pl.ds(pl.multiple_of(i * tile, tile), tile)
    return pl.ds(off + i * tile * rate, tile, stride=rate)


def pieces_of(wide, most):
    step = next(n for n in (most, 512, 256, 128) if wide % n == 0)
    return [(at, step) for at in range(0, wide, step)]


def split3(column, lane):
    high = column.astype(BF).astype(F32)
    rest = column - high
    mid = rest.astype(BF).astype(F32)
    low = rest - mid
    return jnp.where(
        lane == ONE_LANE, high, jnp.where(lane == ONE_LANE + 1, mid, jnp.where(lane == ONE_LANE + 2, low, 0.0))
    )


def near_kernel(plan, meta, lens, offsets, x_ref, st_ref, qf_ref, kf_ref, vf_ref, q_tm, k_tm, v_tm, kall, vall, kid):
    base, head = meta[0], meta[1]
    starts = slide_starts(lens)
    offs = [offsets[b["level"], head] for b in plan.branches]
    top = to_rows(plan, base, offs, starts, x_ref, q_tm, k_tm, v_tm)
    gather_near(plan, offs, k_tm, v_tm, kall, vall, plan.near)
    for branch in plan.far:
        rows = pl.ds(offs[branch["level"]], branch["seg_q"], stride=branch["rate"])
        own = slice(branch["own"], branch["own"] + branch["seg_q"])
        qf_ref[own, :] = q_tm[rows, :].astype(BF)
        kf_ref[own, :] = plain_keys(k_tm[rows, :]).astype(BF)
        vf_ref[own, :] = v_tm[rows, :].astype(BF)
    for branch in plan.near:
        first, total = branch["first"], branch["segs"] * branch["seg_k"]
        pos, gate = branch_pos(plan, branch, base, offs[branch["level"]], 0, total)
        kid[:, first : first + total] = ids_of(pos, starts, gate)
    factor = plan.factor
    lane = iota((1, LANES), 1)

    def scan(visit):
        for branch in plan.near:
            per = branch["seg_q"] // branch["tile"]

            def tile(i, carry, branch=branch, per=per):
                rows = picked(branch, offs[branch["level"]], i)
                at = pl.multiple_of(branch["first"] + (lax.div(i, per) ^ branch["flip"]) * branch["seg_k"], 128)
                visit(branch, rows, q_tm[rows, :], at)
                return carry

            lax.fori_loop(0, branch["segs"] * per, tile, 0, unroll=4 if branch["flip"] else min(2, branch["segs"] * per))

    def attend(top_lanes):
        def visit(branch, rows, queries, at):
            ids = queries[:, ID_Q : ID_Q + 1]
            low = (queries + top_lanes).astype(BF)
            mixed = None
            for begin, step in pieces_of(branch["seg_k"], 1024):
                to = pl.ds(at + begin, step)
                weights = jnp.exp2(dot_nt(low, kall[to, :]) * factor)
                weights = jnp.where(ids == kid[:, to], weights, 0.0).astype(BF)
                more = dot_nn(weights, vall[to, :])
                mixed = more if mixed is None else mixed + more
            if branch["level"]:
                mixed = st_ref[rows, :] + mixed
            st_ref[rows, :] = mixed

        scan(visit)

    attend(split3(-top, lane))
    step = min(512, plan.tokens)

    def least(n, low):
        at = pl.ds(pl.multiple_of(n * step, step), step)
        state = st_ref[at, :]
        st_ref[at, :] = jnp.where(iota((step, LANES), 1) == ID_Q, top, state)
        return jnp.minimum(low, jnp.min(state, 0, keepdims=True))

    weight = lax.fori_loop(0, plan.tokens // step, least, jnp.full((1, LANES), jnp.inf, F32), unroll=2)
    weight = jnp.min(jnp.where(lane == ONE_LANE, weight, jnp.inf))

    @pl.when(jnp.logical_not(weight > 2.0**-60))
    def _():
        def clear(n, carry):
            st_ref[pl.ds(pl.multiple_of(n * step, step), step), :] = jnp.full((step, LANES), NEG, F32)
            return carry

        def largest(branch, rows, queries, at):
            low = queries.astype(BF)
            best = st_ref[rows, :]
            for begin, step in pieces_of(branch["seg_k"], 256):
                to = pl.ds(at + begin, step)
                scores = jnp.where(queries[:, ID_Q : ID_Q + 1] == kid[:, to], dot_nt(low, kall[to, :]), NEG)
                best = jnp.maximum(best, jnp.max(scores, 1, keepdims=True))
            st_ref[rows, :] = best

        def settle(n, carry):
            at = pl.ds(pl.multiple_of(n * step, step), step)
            own = st_ref[at, :]
            tops[at, :] = own
            wide = iota((step, LANES), 1)
            q_tm[at, :] = q_tm[at, :] + split3(-own, wide)
            return carry

        def restore(n, carry):
            at = pl.ds(pl.multiple_of(n * step, step), step)
            st_ref[at, :] = jnp.where(iota((step, LANES), 1) == ID_Q, tops[at, :], st_ref[at, :])
            return carry

        tops = k_tm
        lax.fori_loop(0, plan.tokens // step, clear, 0)
        scan(largest)
        lax.fori_loop(0, plan.tokens // step, settle, 0)
        attend(jnp.zeros((1, LANES), F32))
        lax.fori_loop(0, plan.tokens // step, restore, 0)


def far_kernel(plan, meta, lens, offsets, st_in, qf_ref, kf_ref, vf_ref, *rest):
    halos, (o_ref, st_ref, kall, vall) = rest[:-4], rest[-4:]
    base, head = meta[0], meta[1]
    starts = slide_starts(lens)
    offs = [offsets[b["level"], head] for b in plan.branches]
    factor = plan.factor
    step = min(512, plan.tokens)

    def carry_over(n, carry):
        at = pl.ds(pl.multiple_of(n * step, step), step)
        st_ref[at, :] = st_in[at, :]
        return carry

    lax.fori_loop(0, plan.tokens // step, carry_over, 0, unroll=2)
    if plan.far:
        far_keys(plan, base, offs, starts, halos, kf_ref, vf_ref, kall, vall)
    for branch in plan.far:
        off, tile, wide = offs[branch["level"]], branch["tile"], branch["seg_k"]
        pos, gate = branch_pos(plan, branch, base, off, 0, wide)
        ids = ids_of(pos, starts, gate)
        keys = kall[branch["begin"] : branch["begin"] + wide, :]
        values = vall[branch["begin"] : branch["begin"] + wide, :]
        for i in range(branch["seg_q"] // tile):
            own = branch["own"] + i * tile
            queries = qf_ref[own : own + tile, :]
            rows = picked(branch, off, i)
            scores = dot_nt(queries, keys)
            scores = jnp.where(queries[:, ID_Q : ID_Q + 1].astype(F32) == ids, scores, NEG)
            top = jnp.max(scores, 1, keepdims=True)
            mixed = dot_nn(jnp.exp2((scores - top) * factor).astype(BF), values)
            old = st_ref[rows, :]
            old_top = old[:, ID_Q : ID_Q + 1]
            new_top = jnp.maximum(old_top, top)
            mixed = old * jnp.exp2((old_top - new_top) * factor) + mixed * jnp.exp2((top - new_top) * factor)
            st_ref[rows, :] = jnp.where(iota((tile, LANES), 1) == ID_Q, new_top, mixed)
    eye = jnp.where(iota((plan.size, LANES), 0) == iota((plan.size, LANES), 1), 1.0, 0.0).astype(BF)

    def finish(n, carry):
        at = pl.ds(pl.multiple_of(n * plan.tq, plan.tq), plan.tq)
        state = st_ref[at, :]
        weight = state[:, ONE_LANE : ONE_LANE + 1]
        top = state[:, ID_Q : ID_Q + 1]
        attn = state * (1.0 / weight)
        merged = top + jnp.log2(weight) * (1.0 / factor)
        lane = iota((plan.tq, LANES), 1)
        st_ref[at, :] = jnp.where(lane < plan.size, attn, jnp.where(lane == ONE_LANE, merged, 0.0))
        o_ref[plan.slot(n)] = dot_nt(eye, attn.astype(BF)).astype(BF)
        return carry

    lax.fori_loop(0, plan.blocks, finish, 0, unroll=4)


def back_tile(plan, branch, queries, grads, keys_at, kall, vall, k_fm, linked, dk_acc, dv_acc):
    dq = None
    for begin, step in pieces_of(branch["seg_k"], 256):
        to = pl.ds(keys_at + begin, step)
        part = slice(begin, begin + step)
        keys = kall[to, :]
        probs = jnp.where(linked(keys), jnp.exp2(dot_nt(keys, queries) * plan.factor), 0.0)
        dv_acc[part, :] += dot_nn(probs.astype(BF), grads)
        moved = (probs * dot_nt(vall[to, :], grads)).astype(BF)
        dk_acc[part, :] += dot_nn(moved, queries)
        more = dot_nn(k_fm[:, part], moved)
        dq = more if dq is None else dq + more
    return dq


def far_back_kernel(
    plan, meta, lens, offsets, st_ref, do_ref, qf_ref, kf_ref, vf_ref, *rest,
):
    sides = 1 if plan.paired else 2
    halos, (do_tm, dqf_ref, dkf_ref, dvf_ref), rest = rest[:sides], rest[sides : sides + 4], rest[sides + 4 :]
    halo_outs, (kall, vall, k_fm, dk_acc, dv_acc) = rest[:sides], rest[sides:]
    base, head = meta[0], meta[1]
    starts = slide_starts(lens)
    offs = [offsets[b["level"], head] for b in plan.branches]
    size, tq = plan.size, plan.tq
    row, col, hit = placement(size, 1)
    place = jnp.where(hit, 1.0, 0.0).astype(BF)
    lane = iota((tq, LANES), 1)

    def block(n, carry):
        at = pl.ds(pl.multiple_of(n * tq, tq), tq)
        grads = dot_tn(jnp.concatenate([do_ref[plan.slot(n)], jnp.zeros((16, tq), BF)], 0), place)
        dots = jnp.sum(jnp.where(lane < size, grads * st_ref[at, :], 0.0), 1, keepdims=True)
        do_tm[at, :] = grads + split3(-dots, lane)
        return carry

    lax.fori_loop(0, plan.blocks, block, 0, unroll=4)
    if plan.far:
        far_keys(plan, base, offs, starts, halos, kf_ref, vf_ref, kall, vall)
    eye = jnp.where(iota((LANES, LANES), 0) == iota((LANES, LANES), 1), 1.0, 0.0).astype(BF)
    for branch in plan.far:
        off, tile, wide, begin = offs[branch["level"]], branch["tile"], branch["seg_k"], branch["begin"]
        k_fm[:, :wide] = dot_nt(eye, kall[begin : begin + wide, :]).astype(BF)
        dk_acc[:wide, :] = jnp.zeros((wide, LANES), F32)
        dv_acc[:wide, :] = jnp.zeros((wide, LANES), F32)
        extra, count = branch["extra"], branch["seg_q"]
        for i in range(count // tile):
            own = branch["own"] + i * tile
            rows = picked(branch, off, i)
            wide_lane = iota((tile, LANES), 1)
            merged = st_ref[rows, :][:, ONE_LANE : ONE_LANE + 1]
            queries = jnp.where(wide_lane == ID_Q, 0.0, qf_ref[own : own + tile, :].astype(F32))
            queries = (queries + split3(-merged, wide_lane)).astype(BF)
            grads = do_tm[rows, :].astype(BF)
            pos, _ = branch_pos(plan, branch, base, off, extra + i * tile, tile)
            ids = ids_of(pos, starts)
            linked = lambda keys: keys[:, ID_K : ID_K + 1].astype(F32) == ids
            dq = back_tile(plan, branch, queries, grads, begin, kall, vall, k_fm, linked, dk_acc, dv_acc)
            dqf_ref[own : own + tile, :] = dq.T
        own = slice(branch["own"], branch["own"] + count)
        dkf_ref[own, :] = dk_acc[extra : extra + count, :]
        dvf_ref[own, :] = dv_acc[extra : extra + count, :]
        for side, ref in enumerate(halo_outs):
            at = side * (extra + count)
            if plan.paired:
                at = pl.multiple_of((1 - meta[2]) * (extra + count), 128)
            to = slice(branch["sel"], branch["sel"] + extra)
            dk = (dk_acc[pl.ds(at, extra), :] * size**-0.5).astype(BF)
            ref[:size, to] = dot_nt(eye[:size], dk).astype(BF)
            ref[size:, to] = dot_nt(eye[:size], dv_acc[pl.ds(at, extra), :].astype(BF)).astype(BF)


def near_back_kernel(
    plan, meta, lens, offsets, x_ref, st_ref, do_tm, dqf_ref, dkf_ref, dvf_ref, *rest,
):
    backs, (dx_ref, q_tm, k_tm, v_tm, dq_tm, dk_tm, dv_tm, kall, vall, k_fm, qid, dk_acc, dv_acc) = rest[:-13], rest[-13:]
    base, head = meta[0], meta[1]
    starts = slide_starts(lens)
    offs = [offsets[b["level"], head] for b in plan.branches]
    size, tq = plan.size, plan.tq
    lane = iota((tq, LANES), 1)
    to_rows(
        plan, base, offs, starts, x_ref, q_tm, k_tm, v_tm,
        lambda n, at: split3(-st_ref[at, :][:, ONE_LANE : ONE_LANE + 1], lane),
    )
    gather_near(plan, offs, k_tm, v_tm, kall, vall, plan.near)
    eye = jnp.where(iota((LANES, LANES), 0) == iota((LANES, LANES), 1), 1.0, 0.0).astype(BF)
    for branch in plan.near:
        off, first, wide, tile = offs[branch["level"]], branch["first"], branch["seg_k"], branch["tile"]
        count = branch["segs"] * branch["seg_q"]
        per = branch["seg_q"] // tile
        pos, _ = branch_pos(plan, branch, base, off, 0, count)
        qid[:, :count] = ids_of(pos, starts)

        def segment(seg, carry, branch=branch, off=off, first=first, wide=wide, tile=tile, per=per):
            key_seg = seg ^ branch["flip"]
            keys_at = pl.multiple_of(first + key_seg * wide, 128)
            k_fm[:, :wide] = dot_nt(eye, kall[pl.ds(keys_at, wide), :]).astype(BF)
            dk_acc[:wide, :] = jnp.zeros((wide, LANES), F32)
            dv_acc[:wide, :] = jnp.zeros((wide, LANES), F32)

            def one(j, carry):
                i = seg * per + j
                rows = picked(branch, off, i)
                queries = q_tm[rows, :].astype(BF)
                grads = do_tm[rows, :].astype(BF)
                ids = qid[:, pl.ds(pl.multiple_of(i * tile, tile), tile)]
                linked = lambda keys: keys[:, ID_K : ID_K + 1].astype(F32) == ids
                dq = back_tile(plan, branch, queries, grads, keys_at, kall, vall, k_fm, linked, dk_acc, dv_acc).T
                if branch["level"]:
                    dq = dq_tm[rows, :] + dq
                dq_tm[rows, :] = dq
                return carry

            lax.fori_loop(0, per, one, 0)
            step = min(256, branch["seg_q"])
            for c in range(branch["seg_q"] // step):
                begin = c * step
                if branch["rate"] == 1:
                    to = pl.ds(pl.multiple_of(key_seg * branch["seg_q"] + begin, step), step)
                    dk_tm[to, :] = dk_acc[begin : begin + step, :]
                    dv_tm[to, :] = dv_acc[begin : begin + step, :]
                else:
                    to = pl.ds(off + (key_seg * branch["seg_q"] + begin) * branch["rate"], step, stride=branch["rate"])
                    dk_tm[to, :] += dk_acc[begin : begin + step, :]
                    dv_tm[to, :] += dv_acc[begin : begin + step, :]
            return carry

        lax.fori_loop(0, branch["segs"], segment, 0, unroll=2 if branch["segs"] > 1 else 1)
    row, col, hit = placement(size, 2)
    place = jnp.where(hit, 1.0, 0.0).astype(BF)[: 2 * size]
    for branch in plan.far:
        off, rate, extra, count = offs[branch["level"]], branch["rate"], branch["extra"], branch["seg_q"]
        rows = pl.ds(off, count, stride=rate)
        own = slice(branch["own"], branch["own"] + count)
        for total, part in ((dq_tm, dqf_ref), (dk_tm, dkf_ref), (dv_tm, dvf_ref)):
            total[rows, :] += part[own, :]
        begins = [plan.tokens - plan.halo, 0]
        if plan.paired:
            begins = [(1 - meta[2]) * (plan.tokens - plan.halo)]
        for begin, ref in zip(begins, backs):
            more = dot_tn(ref[:, branch["sel"] : branch["sel"] + extra], place)
            rows = pl.ds(begin + off, extra, stride=rate)
            dk_tm[rows, :] += more[:, :LANES] * size**0.5
            dv_tm[rows, :] += more[:, LANES:]
    small_eye = eye[:size]

    def finish(n, carry):
        at = pl.ds(pl.multiple_of(n * tq, tq), tq)
        slot = plan.slot(n)
        dx_ref[slot, :size, :] = dot_nt(small_eye, (dq_tm[at, :] * size**-0.5).astype(BF)).astype(BF)
        dx_ref[slot, size : 2 * size, :] = dot_nt(small_eye, (dk_tm[at, :] * size**-0.5).astype(BF)).astype(BF)
        dx_ref[slot, 2 * size :, :] = dot_nt(small_eye, dv_tm[at, :].astype(BF)).astype(BF)
        return carry

    lax.fori_loop(0, plan.blocks, finish, 0, unroll=4)


SMEM = pl.BlockSpec(memory_space=pltpu.SMEM)
VMEM = pl.BlockSpec(memory_space=pltpu.VMEM)
TINY = pl.CostEstimate(flops=1000, bytes_accessed=1000, transcendentals=0)
PARAMS = pltpu.CompilerParams(vmem_limit_bytes=60 << 20)
ROOMY = pltpu.CompilerParams(vmem_limit_bytes=40 << 20)


def struct(shape, kind):
    return jax.ShapeDtypeStruct(shape, kind)


def kernel_call(name, kernel, ins, outs, scratch, flops):
    return pl.pallas_call(
        kernel,
        out_shape=tuple(struct(*out) for out in outs),
        in_specs=[SMEM] * 3 + [VMEM] * (len(ins) - 3),
        out_specs=(VMEM,) * len(outs),
        scratch_shapes=[pltpu.VMEM(*s) for s in scratch],
        compiler_params=ROOMY,
        cost_estimate=pl.CostEstimate(flops=flops, bytes_accessed=1000, transcendentals=0),
        name=name,
    )(*ins)


def near_call(plan, meta, lens, offsets, x):
    rows, keys = ((plan.tokens, LANES), F32), ((plan.near_keys, LANES), BF)
    own = ((plan.own, LANES), BF)
    return kernel_call(
        "near", functools.partial(near_kernel, plan), (meta, lens, offsets, x), (rows, own, own, own),
        (rows, rows, rows, keys, keys, ((1, plan.near_keys), F32)), 20_000_000_000,
    )


def far_call(plan, meta, lens, offsets, state, own, halo):
    keys = ((plan.far_keys, LANES), BF)
    return kernel_call(
        "far", functools.partial(far_kernel, plan), (meta, lens, offsets, state, *own, *halo),
        (((plan.blocks, plan.size, plan.tq), BF), ((plan.tokens, LANES), F32)), (keys, keys), 4_000_000_000,
    )


def far_back_call(plan, meta, lens, offsets, state, do, own, halo):
    keys = ((plan.far_keys, LANES), BF)
    part, side = ((plan.own, LANES), F32), ((2 * plan.size, max(plan.sel, LANES)), BF)
    acc = ((plan.widest, LANES), F32)
    return kernel_call(
        "far_back", functools.partial(far_back_kernel, plan), (meta, lens, offsets, state, do, *own, *halo),
        (((plan.tokens, LANES), F32), part, part, part) + (side,) * (1 if plan.paired else 2),
        (keys, keys, ((LANES, plan.widest), BF), acc, acc), 4_000_000_000,
    )


def near_back_call(plan, meta, lens, offsets, x, state, do_rows, parts, back):
    rows, keys = ((plan.tokens, LANES), F32), ((plan.near_keys, LANES), BF)
    acc = ((plan.widest, LANES), F32)
    return kernel_call(
        "near_back", functools.partial(near_back_kernel, plan),
        (meta, lens, offsets, x, state, do_rows, *parts, *back),
        (((plan.blocks, 3 * plan.size, plan.tq), BF),),
        (rows,) * 6 + (keys, keys, ((LANES, plan.widest), BF), ((1, plan.tokens), F32), acc, acc), 8_000_000_000,
    )[0]


def near_rows(values, norm_gain, norm_shift):
    centred = values - jnp.mean(values, 1, keepdims=True)
    inverse = lax.rsqrt(jnp.mean(centred * centred, 1, keepdims=True) + EPS)
    normed = centred * inverse
    return normed * norm_gain + norm_shift, normed, inverse


def back_rows(grad_out, normed, inverse, norm_gain):
    grad_norm = grad_out * norm_gain
    return inverse * (
        grad_norm
        - jnp.mean(grad_norm, 1, keepdims=True)
        - normed * jnp.mean(grad_norm * normed, 1, keepdims=True)
    )


def own_columns(size, unit, core):
    row, col = iota((size, size), 0), iota((size, size), 1)
    half = size // 2
    other = row >= half
    place = jnp.where(other, row - half, row)
    whole = jnp.floor((place.astype(F32) + 0.5) * (1.0 / unit)).astype(jnp.int32)
    parity = jnp.where(other, 1 - core, core)
    return jnp.where(col == place + unit * (whole + parity), 1.0, 0.0).astype(BF)


def middle_kernel(
    unit_up, unit, core_ref, attn_ref, tiles_ref, out_w, out_b, gain, shift, up_w, up_b, down_w, down_b, g_ref,
    y_ref, res_ref, ag_ref, common_ref, mine_ref, theirs_ref, sums_ref, up_sum_ref,
    pick_up, normed_s, lifted_s, inverse_s, out_s, back_s,
):
    step, steps = pl.program_id(0), pl.num_programs(0)
    width = tiles_ref.shape[1]
    chunk = up_w.shape[1]
    half = chunk // 2
    core = core_ref[0]
    hidden_sel = steps * half

    @pl.when(step == 0)
    def _():
        pick_up[...] = own_columns(chunk, unit_up, core)
        residual = tiles_ref[...].astype(F32) + dot_tn(attn_ref[...], out_w[...]) + out_b[...]
        lifted, normed, inverse = near_rows(residual, gain[...], shift[...])
        low = lifted.astype(BF)
        lifted_s[...] = low
        normed_s[...] = normed
        inverse_s[...] = jnp.broadcast_to(inverse, inverse_s.shape)
        out_s[...] = residual + down_b[...]
        back_s[...] = jnp.zeros_like(back_s)
        common_ref[pl.ds(steps * chunk, width), :] = low.T
        pick = own_columns(width, unit, core)
        picked_g = dot_nt(pick, g_ref[...]).astype(BF)
        mine_ref[pl.ds(hidden_sel, width // 2), :] = picked_g[: width // 2]
        theirs_ref[pl.ds(hidden_sel, width // 2), :] = picked_g[width // 2 :]

    lifted = lifted_s[...]
    gate_in = dot_nn(lifted, up_w[...]) + up_b[...]
    cdf = 0.5 + 0.5 * lax.erf(gate_in * (0.5**0.5))
    act = (gate_in * cdf).astype(BF)
    slope = cdf + gate_in * (jnp.exp(-0.5 * gate_in * gate_in) * (1.0 / math.sqrt(2.0 * math.pi)))
    gate_grad = (dot_nt(g_ref[...], down_w[...]) * slope).astype(BF)
    out_s[...] += dot_nn(act, down_w[...])
    back_s[...] += dot_nt(gate_grad, up_w[...])
    up_sum_ref[...] = jnp.sum(gate_grad.astype(F32), 0, keepdims=True)
    common_ref[pl.ds(pl.multiple_of(step * chunk, chunk), chunk), :] = act.T
    picked_gate = dot_nt(pick_up[...], gate_grad).astype(BF)
    at = pl.ds(pl.multiple_of(step * half, half), half)
    mine_ref[at, :] = picked_gate[:half]
    theirs_ref[at, :] = picked_gate[half:]

    @pl.when(step == steps - 1)
    def _():
        y_ref[...] = out_s[...].astype(BF)
        grads = g_ref[...].astype(F32)
        lifted_grad = back_s[...]
        normed = normed_s[...]
        residual_grad = grads + back_rows(lifted_grad, normed, inverse_s[:, :1], gain[...])
        res_ref[...] = residual_grad
        low = residual_grad.astype(BF)
        ag_ref[...] = dot_nt(out_w[...], low).astype(BF)
        pick = own_columns(width, unit, core)
        picked_p = dot_nt(pick, low).astype(BF)
        at = pl.ds(hidden_sel + width // 2, width // 2)
        mine_ref[at, :] = picked_p[: width // 2]
        theirs_ref[at, :] = picked_p[width // 2 :]
        sums_ref[0:1, :] = jnp.sum(grads, 0, keepdims=True)
        sums_ref[1:2, :] = jnp.sum(residual_grad, 0, keepdims=True)
        sums_ref[2:3, :] = jnp.sum(lifted_grad * normed, 0, keepdims=True)
        sums_ref[3:4, :] = jnp.sum(lifted_grad, 0, keepdims=True)
        sums_ref[4:8, :] = jnp.zeros((4, width), F32)


def middle_call(devices, core, attn_t, tiles, out_w, out_b, gain, shift, up_w, up_b, down_w, down_b, g):
    tq, width = tiles.shape
    hidden = up_w.shape[1]
    steps = hidden // width
    whole = lambda *shape: pl.BlockSpec(shape, lambda j: (0,) * len(shape))
    vec = whole(1, width)
    sel = hidden // 2 + width
    return pl.pallas_call(
        functools.partial(middle_kernel, hidden // devices, width // devices),
        grid=(steps,),
        in_specs=[
            SMEM, whole(width, tq), whole(tq, width), whole(width, width), vec, vec, vec,
            pl.BlockSpec((width, width), lambda j: (0, j)), pl.BlockSpec((1, width), lambda j: (0, j)),
            pl.BlockSpec((width, width), lambda j: (j, 0)), vec, whole(tq, width),
        ],
        out_specs=(
            whole(tq, width), whole(tq, width), whole(width, tq), whole(hidden + width, tq), whole(sel, tq),
            whole(sel, tq), whole(8, width), pl.BlockSpec((1, width), lambda j: (0, j)),
        ),
        out_shape=(
            jax.ShapeDtypeStruct((tq, width), BF),
            pltpu.HBM((tq, width), F32),
            jax.ShapeDtypeStruct((width, tq), BF),
            pltpu.HBM((hidden + width, tq), BF),
            pltpu.HBM((sel, tq), BF),
            pltpu.HBM((sel, tq), BF),
            pltpu.HBM((8, width), F32),
            pltpu.HBM((1, hidden), F32),
        ),
        scratch_shapes=[
            pltpu.VMEM((width, width), BF), pltpu.VMEM((tq, width), F32), pltpu.VMEM((tq, width), BF),
            pltpu.VMEM((tq, LANES), F32), pltpu.VMEM((tq, width), F32), pltpu.VMEM((tq, width), F32),
        ],
        compiler_params=ROOMY,
        cost_estimate=pl.CostEstimate(flops=14 * tq * width * hidden, bytes_accessed=20 << 20, transcendentals=0),
        name="middle",
    )(core, attn_t, tiles, out_w, out_b, gain, shift, up_w, up_b, down_w, down_b, g)


def weights_kernel(unit_up, unit, meta, attn_a, attn_b, common_a, common_b, sel_a, sel_b, *rest):
    first_ref, second_refs, (first_s, second_s, sems) = rest[0], rest[1:5], rest[5:]
    width = attn_a.shape[0]
    hidden = common_a.shape[0] - width
    chips = width // (2 * unit)

    def spot(chip):
        return (chip // 8) * 2 + chip % 2, chip // 2 % 4

    lifted = slice(hidden, hidden + width)
    group = width // (2 * unit_up)
    for step in range(hidden // width):
        rows = slice(step * width // 2, (step + 1) * width // 2)
        part = dot_nt(sel_a[rows, :], common_a[lifted, :]) + dot_nt(sel_b[rows, :], common_b[lifted, :])
        for i in range(group):
            plane, line = spot(step * group + i)
            first_s[plane, line, :unit_up, :] = part[i * unit_up : (i + 1) * unit_up].astype(BF)
    rows_out = slice(hidden // 2 + width // 2, hidden // 2 + width)
    rows = slice(hidden // 2, hidden // 2 + width // 2)
    out = dot_nt(sel_a[rows_out, :], attn_a[...]) + dot_nt(sel_b[rows_out, :], attn_b[...])
    held = [out]

    def down_part(step):
        cols = slice(step * width, (step + 1) * width)
        return dot_nt(sel_a[rows, :], common_a[cols, :]) + dot_nt(sel_b[rows, :], common_b[cols, :])

    held += [down_part(step) for step in range(FIRST_DOWN)]
    for chip in range(chips):
        plane, line = spot(chip)
        at = slice(chip * unit, (chip + 1) * unit)
        first_s[plane, line, unit_up:, :] = jnp.concatenate([part[at] for part in held], 0).astype(BF)
    copies = [pltpu.make_async_copy(first_s, first_ref, sems.at[4])]
    copies[0].start()
    for step in range(FIRST_DOWN, hidden // width):
        part = down_part(step)
        at = (step - FIRST_DOWN) * width
        for chip in range(chips):
            plane, line = spot(chip)
            second_s[line, plane, :, at : at + width] = part[chip * unit : (chip + 1) * unit].astype(BF)
    for k in range(4):
        copies.append(pltpu.make_async_copy(second_s.at[meta[5] ^ k], second_refs[k], sems.at[k]))
        copies[-1].start()
    for copy in copies:
        copy.wait()


def weights_call(devices, meta, attn_a, attn_b, common_a, common_b, sel_a, sel_b):
    width, tq = attn_a.shape
    hidden = common_a.shape[0] - width
    unit_up, unit = hidden // devices, width // devices
    first = (4, 4, unit_up + (1 + FIRST_DOWN) * unit, width)
    second = (4, unit, hidden - FIRST_DOWN * width)
    outs = pl.pallas_call(
        functools.partial(weights_kernel, unit_up, unit),
        in_specs=[SMEM] + [VMEM] * 6,
        out_specs=(pl.BlockSpec(memory_space=pltpu.HBM),) * 5,
        out_shape=(jax.ShapeDtypeStruct(first, BF),) + (jax.ShapeDtypeStruct(second, BF),) * 4,
        scratch_shapes=[pltpu.VMEM(first, BF), pltpu.VMEM((4,) + second, BF), pltpu.SemaphoreType.DMA((5,))],
        compiler_params=PARAMS,
        cost_estimate=pl.CostEstimate(flops=4 * tq * width * hidden, bytes_accessed=14 << 20, transcendentals=0),
        name="weights",
    )(meta, attn_a, attn_b, common_a, common_b, sel_a, sel_b)
    return outs[0], outs[1:]


def fold_kernel(meta, first_ref, own, got1, got2, got3, *outs):
    plane, line = meta[4], meta[5]
    for k in range(4):
        at = line ^ k
        total = first_ref[0, at].astype(F32)
        for i in range(1, 4):
            total += first_ref[i, at].astype(F32)
        outs[k][...] = total.astype(BF)
        at = plane ^ k
        total = own[at].astype(F32) + got1[at].astype(F32) + got2[at].astype(F32) + got3[at].astype(F32)
        outs[4 + k][...] = total.astype(BF)


def fold_call(meta, first, second):
    shapes = [jax.ShapeDtypeStruct(first.shape[2:], BF)] * 4 + [jax.ShapeDtypeStruct(second[0].shape[1:], BF)] * 4
    outs = pl.pallas_call(
        fold_kernel,
        in_specs=[SMEM] + [VMEM] * 5,
        out_specs=(VMEM,) * 8,
        out_shape=tuple(shapes),
        compiler_params=ROOMY,
        cost_estimate=TINY,
        name="fold",
    )(meta, first, *second)
    return outs[:4], outs[4:]


def last_kernel(unit_up, unit, meta, *refs):
    columns, first, second, outs = refs[:4], refs[4:8], refs[8:12], refs[12:]
    qkv_ref, up_ref, out_ref, down_ref, held = outs
    size = columns[0].shape[0]
    held[...] = jnp.zeros_like(held)
    for i, ref in enumerate(columns):
        at = pl.multiple_of(meta[10 + i] + size // 2, 8)
        held[pl.ds(at, size), :] += ref[...].astype(F32)
    qkv_ref[...] = held[size // 2 : size // 2 + qkv_ref.shape[0], :]
    total = first[0][...].astype(F32)
    for ref in first[1:]:
        total += ref[...].astype(F32)
    up_ref[...] = total[:unit_up]
    out_ref[...] = total[unit_up : unit_up + unit]
    width = total.shape[1]
    for i in range(FIRST_DOWN):
        at = unit_up + (1 + i) * unit
        down_ref[:, i * width : (i + 1) * width] = total[at : at + unit]
    width = FIRST_DOWN * width
    total = second[0][...].astype(F32)
    for ref in second[1:]:
        total += ref[...].astype(F32)
    down_ref[:, width:] = total


def last_call(meta, unit_qkv, unit_up, unit, columns, first, second):
    size, width = columns[0].shape
    hidden = FIRST_DOWN * width + second[0].shape[1]
    outs = ((unit_qkv, width), (unit_up, width), (unit, width), (unit, hidden))
    return pl.pallas_call(
        functools.partial(last_kernel, unit_up, unit),
        in_specs=[SMEM] + [VMEM] * 12,
        out_specs=(VMEM,) * 4,
        out_shape=tuple(jax.ShapeDtypeStruct(s, F32) for s in outs),
        scratch_shapes=[pltpu.VMEM((unit_qkv + size, width), F32)],
        compiler_params=ROOMY,
        cost_estimate=TINY,
        name="last",
    )(meta, *columns, *first, *second)


def enter_kernel(tiles_ref, gain, shift, w_ref, query_b, value_b, x_ref, npre_ref, low_s):
    part = pl.program_id(0)

    @pl.when(part == 0)
    def _():
        scaled, normed, _ = near_rows(tiles_ref[...].astype(F32), gain[...], shift[...])
        low_s[...] = scaled.astype(BF)
        npre_ref[...] = normed.astype(BF)

    bias = jnp.where(part == 0, query_b[...], jnp.where(part == 2, value_b[...], 0.0))
    joined = (dot_nn(low_s[...], w_ref[...]) + bias).T
    heads, _, size, tq = x_ref.shape
    x_ref[:, 0] = joined.astype(BF).reshape(heads, size, tq)


def enter_call(heads, tiles, gain, shift, weight, query_b, value_b):
    tq, width = tiles.shape
    size = width // heads
    whole = lambda *shape: pl.BlockSpec(shape, lambda i: (0,) * len(shape))
    vec = whole(1, width)
    return pl.pallas_call(
        enter_kernel,
        grid=(3,),
        in_specs=[whole(tq, width), vec, vec, pl.BlockSpec((width, width), lambda i: (0, i)), vec, vec],
        out_specs=(pl.BlockSpec((heads, 1, size, tq), lambda i: (0, i, 0, 0)), whole(tq, width)),
        out_shape=(jax.ShapeDtypeStruct((heads, 3, size, tq), BF), jax.ShapeDtypeStruct((tq, width), BF)),
        scratch_shapes=[pltpu.VMEM((tq, width), BF)],
        compiler_params=PARAMS,
        name="enter",
    )(tiles, gain, shift, weight, query_b, value_b)


def leave_kernel(tiles_ref, gain, w_ref, jg_ref, res_ref, out_ref, acc):
    part = pl.program_id(0)
    width, tq = acc.shape
    more = dot_nn(w_ref[...], jg_ref[:, 0].reshape(width, tq))

    @pl.when(part == 0)
    def _():
        acc[...] = more

    @pl.when(part == 1)
    def _():
        acc[...] += more

    @pl.when(part == 2)
    def _():
        _, normed, inverse = near_rows(tiles_ref[...].astype(F32), gain[...], gain[...])
        grads = (acc[...] + more).T
        out_ref[...] = (res_ref[...] + back_rows(grads, normed, inverse, gain[...])).astype(BF)


def leave_call(tiles, gain, weight, joined_grad, residual_grad):
    tq, width = tiles.shape
    heads, _, size, _ = joined_grad.shape
    whole = lambda *shape: pl.BlockSpec(shape, lambda i: (0,) * len(shape))
    return pl.pallas_call(
        leave_kernel,
        grid=(3,),
        in_specs=[
            whole(tq, width), whole(1, width), pl.BlockSpec((width, width), lambda i: (0, i)),
            pl.BlockSpec((heads, 1, size, tq), lambda i: (0, i, 0, 0)), whole(tq, width),
        ],
        out_specs=whole(tq, width),
        out_shape=jax.ShapeDtypeStruct((tq, width), BF),
        scratch_shapes=[pltpu.VMEM((width, tq), F32)],
        compiler_params=PARAMS,
        cost_estimate=TINY,
        name="leave",
    )(tiles, gain, weight, joined_grad, residual_grad)


def halo_hits(plan, offs, first, dims):
    wide = max(plan.sel, LANES)
    shape = (plan.tq, wide)
    token, col = iota(shape, 0) + first, iota(shape, 1)
    hit = col < 0
    for branch in plan.branches:
        if branch["extra"]:
            at = col - branch["sel"]
            inside = (at >= 0) & (at < branch["extra"])
            hit |= inside & (token == at * branch["rate"] + offs[branch["level"]])
    return jnp.where(hit, 1.0, 0.0).astype(BF)


def halo_blocks(plan):
    count = plan.halo // plan.tq
    for i in range(count):
        yield 0, plan.blocks - count + i, i * plan.tq
        yield 1, i, i * plan.tq


def static_slot(plan, block):
    return block % plan.groups * plan.members + block // plan.groups


def select_kernel(plan, meta, offsets, x_ref, *outs):
    offs = [offsets[b["level"], meta[1]] for b in plan.branches]
    if plan.paired:
        count = plan.halo // plan.tq
        total = jnp.zeros((2 * plan.size, max(plan.sel, LANES)), F32)
        for i in range(count):
            block = (1 - meta[2]) * (plan.blocks - count) + i
            total += dot_nn(x_ref[plan.slot(block), plan.size :, :], halo_hits(plan, offs, i * plan.tq, None))
        outs[0][...] = total.astype(BF)
        return
    last_ref, first_ref = outs
    total = [jnp.zeros((2 * plan.size, max(plan.sel, LANES)), F32) for _ in range(2)]
    for side, block, first in halo_blocks(plan):
        hits = halo_hits(plan, offs, first, None)
        total[side] += dot_nn(x_ref[static_slot(plan, block), plan.size :, :], hits)
    last_ref[...] = total[0].astype(BF)
    first_ref[...] = total[1].astype(BF)


def select_call(plan, meta, offsets, x):
    shape = jax.ShapeDtypeStruct((2 * plan.size, max(plan.sel, LANES)), BF)
    return pl.pallas_call(
        functools.partial(select_kernel, plan),
        in_specs=[SMEM, SMEM, VMEM],
        out_specs=(VMEM,) * (1 if plan.paired else 2),
        out_shape=(shape,) * (1 if plan.paired else 2),
        compiler_params=ROOMY,
        name="select",
    )(meta, offsets, x)


def to_owners(vector, owner, lane_of, devices):
    count = vector.shape[1]
    held = jnp.where(iota((devices, count), 0) == owner, vector, 0.0)
    hits = jnp.where(iota((count, LANES), 1) == lane_of, 1.0, 0.0)
    return lax.dot_general(
        held, hits, (((1,), (0,)), ((), ())), precision=lax.Precision.HIGHEST, preferred_element_type=F32
    )


def cut(index, unit):
    whole = jnp.floor((index.astype(F32) + 0.5) * (1.0 / unit)).astype(jnp.int32)
    return whole, index - whole * unit


def head_kernel(devices, meta, dx_ref, near_ref, w_ref, gain, shift, sums_ref, up_ref, *rest):
    column_refs, (small_ref, acc, col_s, row_s) = rest[:-4], rest[-4:]
    step, steps = pl.program_id(0), pl.num_programs(0)
    tq = dx_ref.shape[2]
    rows = dx_ref.shape[1]
    per = near_ref.shape[0] // tq
    size = rows // 3
    width = near_ref.shape[1]

    @pl.when(step == 0)
    def _():
        acc[...] = jnp.zeros_like(acc)
        col_s[...] = jnp.zeros_like(col_s)
        row_s[...] = jnp.zeros_like(row_s)

    for i in range(per):
        grads = dx_ref[i]
        acc[...] += dot_nn(grads, near_ref[i * tq : (i + 1) * tq, :])
        col_s[...] += jnp.broadcast_to(jnp.sum(grads.astype(F32), 1, keepdims=True), col_s.shape)
        row_s[...] += dot_nt(jnp.ones((8, tq), BF), grads)

    @pl.when(step == steps - 1)
    def _():
        head = meta[1]
        plain = acc[...]
        weight = plain * gain[...] + col_s[:, :1] * shift[...]
        acc[...] = weight
        for i, ref in enumerate(column_refs):
            at = pl.multiple_of(meta[6 + i] * size, 8)
            ref[...] = acc[pl.ds(at, size), :].astype(BF)
        own = w_ref[...].astype(F32)
        gain_part = jnp.sum(own * plain, 0, keepdims=True)
        shift_part = jnp.sum(own * col_s[:, :1], 0, keepdims=True)
        unit = width // devices
        owner = cut(iota((1, width), 1), unit)[0]
        lane = cut(iota((width, 1), 0), unit)[1]
        small_ref[:, 0, :] = to_owners(gain_part, owner, lane, devices)
        small_ref[:, 1, :] = to_owners(shift_part, owner, lane, devices)
        held = jnp.zeros((devices, LANES), F32)
        for i in range(4):
            held += to_owners(sums_ref[i : i + 1, :], owner, lane + i * unit, devices)
        small_ref[:, 2, :] = held
        hidden = up_ref.shape[1]
        unit_up = hidden // devices
        held = jnp.zeros((devices, LANES), F32)
        for i in range(hidden // width):
            owner_up = cut(iota((1, width), 1) + i * width, unit_up)[0]
            lane_up = cut(iota((width, 1), 0) + i * width, unit_up)[1]
            held += to_owners(up_ref[:, i * width : (i + 1) * width], owner_up, lane_up, devices)
        small_ref[:, 3, :] = held
        line = row_s[0:1, :]
        for i, part in enumerate((0, 2)):
            index = iota((1, rows), 1) - part * size
            inside = (index >= 0) & (index < size)
            owner_h = jnp.where(inside, 2 * head + cut(index, size // 2)[0], -1)
            lane_h = cut(iota((rows, 1), 0), size // 2)[1]
            small_ref[:, 4 + i, :] = to_owners(line, owner_h, lane_h, devices)
        small_ref[:, 6, :] = jnp.zeros((devices, LANES), F32)
        small_ref[:, 7, :] = jnp.zeros((devices, LANES), F32)


def head_call(devices, meta, dx, npre_all, own_w, gain, shift, sums, up_sums):
    blocks, rows, tq = dx.shape
    width = npre_all.shape[1]
    per = blocks // 4
    whole = lambda *shape: pl.BlockSpec(shape, lambda i: (0,) * len(shape))
    return pl.pallas_call(
        functools.partial(head_kernel, devices),
        grid=(4,),
        in_specs=[
            SMEM, pl.BlockSpec((per, rows, tq), lambda i: (i, 0, 0)), pl.BlockSpec((per * tq, width), lambda i: (i, 0)),
            whole(rows, width), whole(1, width), whole(1, width), whole(8, width), whole(1, up_sums.shape[1]),
        ],
        out_specs=(whole(rows // 3, width),) * 4 + (whole(devices, 8, LANES),),
        out_shape=(jax.ShapeDtypeStruct((rows // 3, width), BF),) * 4
        + (jax.ShapeDtypeStruct((devices, 8, LANES), F32),),
        scratch_shapes=[
            pltpu.VMEM((rows, width), F32), pltpu.VMEM((rows, LANES), F32), pltpu.VMEM((8, rows), F32),
        ],
        compiler_params=PARAMS,
        cost_estimate=TINY,
        name="head",
    )(meta, dx, npre_all, own_w, gain, shift, sums, up_sums)


def layer_norm_rows(values, norm_gain, norm_shift):
    row_mean = jnp.mean(values, -1, keepdims=True)
    centred = values - row_mean
    inverse = lax.rsqrt(jnp.mean(centred * centred, -1, keepdims=True) + EPS)
    normed = centred * inverse
    return (normed * norm_gain + norm_shift, normed, inverse)


def norm_back(grad_out, normed, inverse, norm_gain):
    grad_norm = grad_out * norm_gain
    grad_in = inverse * (
        grad_norm
        - jnp.mean(grad_norm, -1, keepdims=True)
        - normed * jnp.mean(grad_norm * normed, -1, keepdims=True)
    )
    return (grad_in, jnp.sum(grad_out * normed, 0), jnp.sum(grad_out, 0))


def swap(values, axes):
    return lax.all_to_all(values, axes, 0, 0, tiled=True)


def scatter_sum(values, orders):
    sizes = {name: lax.axis_size(name) for name in ALL}
    left = list(ALL)
    rows, cols = values.shape[1:]
    for stage, axes in enumerate(orders):
        values = values.reshape([sizes[name] for name in left] + [rows, cols])
        rest = [name for name in left if name not in axes]
        order = [left.index(name) for name in list(axes) + rest]
        values = values.transpose(order + [len(left), len(left) + 1])
        count = math.prod(sizes[name] for name in axes)
        values = values.reshape((count, -1, rows, cols))
        if count > 1:
            values = swap(values, axes)
            values = jnp.sum(values.astype(F32), 0)
            if stage < len(orders) - 1:
                values = values.astype(BF)
        left = rest
    return values.reshape(rows, cols).astype(F32)


def to_neighbours(pieces, count):
    if count == 2:
        return (lax.ppermute(pieces[0], "grp", [(0, 1), (1, 0)]),)
    return (
        lax.ppermute(pieces[0], "grp", [(i, i + 1) for i in range(count - 1)]),
        lax.ppermute(pieces[1], "grp", [(i + 1, i) for i in range(count - 1)]),
    )


def from_neighbours(pieces, count):
    return to_neighbours(pieces[::-1], count)[::-1]


def share_columns(weight_t, sums, width):
    members, size = lax.axis_size(GROUP), weight_t.shape[1]
    head = lax.axis_index(GROUP)
    full = jnp.zeros((3, members) + weight_t.shape[1:], F32)
    full = lax.dynamic_update_slice(full, weight_t[:, None], (0, head, 0, 0))
    full_sums = lax.dynamic_update_slice(jnp.zeros((3, members, size), F32), sums[:, None], (0, head, 0))
    weight = lax.psum_scatter(full.reshape(3 * members * size, width), ALL, scatter_dimension=0, tiled=True)
    sums = lax.psum_scatter(full_sums.reshape(3, members * size), ALL, scatter_dimension=1, tiled=True)
    return weight, sums[0], sums[2]


def body(
    tile_embed,
    slide_lengths,
    head_offsets,
    pre_gain,
    pre_shift,
    qkv_weight,
    query_bias,
    value_bias,
    out_weight,
    out_bias,
    post_gain,
    post_shift,
    up_weight,
    up_bias,
    down_weight,
    down_bias,
    out_grad,
):
    width = qkv_weight.shape[0]
    hidden = up_weight.shape[1]
    heads = head_offsets.shape[1]
    size = width // heads
    tq = tile_embed.shape[1]
    br, groups = lax.axis_size("br"), lax.axis_size("grp")
    members = heads // br
    devices = heads * groups
    plan = Plan(heads, size, head_offsets.shape[0], br, members, tq, devices * tq)
    head = lax.axis_index(GROUP)
    base = lax.axis_index("grp") * plan.tokens
    meta = jnp.stack([base, head, lax.axis_index("grp")]).astype(jnp.int32)

    tiles = tile_embed[0].astype(F32)
    pre_out, normed_pre, inverse_pre = layer_norm_rows(tiles, pre_gain, pre_shift)
    normed_low = pre_out.astype(BF)
    bias_col = jnp.concatenate([query_bias, jnp.zeros_like(query_bias), value_bias], 1).reshape(-1, 1)
    joined_t = (
        lax.dot_general(qkv_weight, normed_low, (((0,), (1,)), ((), ())), preferred_element_type=F32) + bias_col
    ).astype(BF)
    x = joined_t.reshape(3, heads, size, tq).transpose(1, 0, 2, 3).reshape(heads, 3 * size, tq)
    x = swap(x, GROUP)
    normed_all = lax.all_gather(normed_low, GROUP, axis=0, tiled=True)

    halo = to_neighbours(select_call(plan, meta, head_offsets, x), groups)
    state, *own = near_call(plan, meta, slide_lengths, head_offsets, x)
    mixed, state = far_call(plan, meta, slide_lengths, head_offsets, state, own, halo)
    attn_t = swap(mixed, GROUP).reshape(width, tq)

    projected = lax.dot_general(attn_t, out_weight, (((0,), (0,)), ((), ())), preferred_element_type=F32)
    residual = tiles + projected + out_bias
    post_out, normed_post, inverse_post = layer_norm_rows(residual, post_gain, post_shift)
    lifted = post_out.astype(BF)
    gate_in = jnp.dot(lifted, up_weight, preferred_element_type=F32) + up_bias
    act_float, gelu_pull = jax.vjp(lambda v: jax.nn.gelu(v, approximate=False), gate_in)
    act_low = act_float.astype(BF)
    layer_out = (residual + jnp.dot(act_low, down_weight, preferred_element_type=F32) + down_bias).astype(BF)[None]
    grad_low = out_grad[0]
    grad_float = grad_low.astype(F32)
    act_grad = lax.dot_general(grad_low, down_weight, (((1,), (1,)), ((), ())), preferred_element_type=F32)
    gate_grad = gelu_pull(act_grad)[0].astype(BF)
    lifted_grad = lax.dot_general(gate_grad, up_weight, (((1,), (1,)), ((), ())), preferred_element_type=F32)
    norm_part, post_gain_sum, post_shift_sum = norm_back(lifted_grad, normed_post, inverse_post, post_gain)
    residual_grad = grad_float + norm_part
    proj_grad = residual_grad.astype(BF)
    attn_grad_t = lax.dot_general(
        out_weight, proj_grad, (((1,), (1,)), ((), ())), preferred_element_type=F32
    ).astype(BF)
    do = swap(attn_grad_t.reshape(heads, size, tq), GROUP)

    tokens = (((0,), (0,)), ((), ()))
    up_part = lax.dot_general(gate_grad, lifted, tokens, preferred_element_type=F32).astype(BF)
    down_part = lax.dot_general(grad_low, act_low, tokens, preferred_element_type=F32).astype(BF)
    out_part = lax.dot_general(proj_grad, attn_t, (((0,), (1,)), ((), ())), preferred_element_type=F32).astype(BF)
    vectors = [
        jnp.sum(gate_grad.astype(F32), 0).reshape(devices, -1),
        jnp.sum(grad_float, 0).reshape(devices, -1),
        jnp.sum(residual_grad, 0).reshape(devices, -1),
        post_gain_sum.reshape(devices, -1),
        post_shift_sum.reshape(devices, -1),
    ]
    ends = [0]
    for vector in vectors:
        ends.append(ends[-1] + vector.shape[1])
    small = jnp.concatenate(vectors, 1)
    small = jnp.pad(small[:, None, :], ((0, 0), (0, 7), (0, width - small.shape[1]))).astype(BF)
    misc = jnp.concatenate([out_part.reshape(devices, -1, width), small], 1)
    first, second = (("s0",), ("br", "s1"), ("grp", "s2")), (("s0",), ("grp", "s2"), ("br", "s1"))
    up_own = scatter_sum(up_part.reshape(devices, -1, width), first)
    down_own = scatter_sum(down_part.reshape(devices, -1, hidden), second)
    misc_own = scatter_sum(misc, first)
    unit = width // devices
    small_own = misc_own[unit]
    small_own = [small_own[None, ends[i] : ends[i + 1]] for i in range(len(vectors))]

    rows, dq, dk, dv, *sides = far_back_call(plan, meta, slide_lengths, head_offsets, state, do, own, halo)
    back = from_neighbours(sides, groups)
    dx = near_back_call(plan, meta, slide_lengths, head_offsets, x, state, rows, (dq, dk, dv), back)
    joined_grad_t = swap(dx, GROUP).reshape(heads, 3, size, tq).transpose(1, 0, 2, 3).reshape(3 * width, tq)
    weight_t = jnp.einsum(
        "nct,ntd->cd", dx, normed_all.reshape(heads, tq, width), preferred_element_type=F32
    ).reshape(3, size, width)
    head_sums = jnp.sum(dx.astype(F32), (0, 2)).reshape(3, size)
    qkv_own, query_own, value_own = share_columns(weight_t, head_sums, width)
    normed_grad = lax.dot_general(joined_grad_t, qkv_weight, (((0,), (1,)), ((), ())), preferred_element_type=F32)
    tile_part, pre_gain_sum, pre_shift_sum = norm_back(normed_grad, normed_pre, inverse_pre, pre_gain)
    tile_grad = (residual_grad + tile_part).astype(BF)[None]
    last = jnp.stack([pre_gain_sum, pre_shift_sum]).reshape(2, devices, unit).transpose(1, 0, 2)
    last = jnp.pad(last, ((0, 0), (0, 6), (0, LANES - unit)))
    last = jnp.sum(swap(last, ALL).reshape(devices, 8, LANES), 0)
    return (
        layer_out,
        tile_grad,
        last[0:1, :unit],
        last[1:2, :unit],
        qkv_own.T,
        query_own[None],
        value_own[None],
        misc_own[:unit].T,
        small_own[2],
        small_own[3],
        small_own[4],
        up_own.T,
        small_own[0],
        down_own.T,
        small_own[1],
    )


def across(piece, axes, k):
    return lax.ppermute(piece, axes, [(i, i ^ k) for i in range(4)])


def matchings(edges, count):
    edges, found = list(edges), []
    while edges:
        by_source = {}
        for edge in edges:
            by_source.setdefault(edge[0], []).append(edge)
        taken = {}

        def place(source, seen):
            for edge in by_source[source]:
                if edge[1] not in seen:
                    seen.add(edge[1])
                    if edge[1] not in taken or place(taken[edge[1]][0], seen):
                        taken[edge[1]] = edge
                        return True
            return False

        for source in range(count):
            place(source, set())
        found.append(sorted(taken.values()))
        for edge in taken.values():
            edges.remove(edge)
    return found


def column_routes(heads, size, unit):
    sizes = [lax.axis_size(name) for name in ALL]
    inner = sizes[2] * sizes[3] * sizes[4]
    edges = []
    for head in range(heads):
        for grp in range(sizes[1]):
            source = (head // inner * sizes[1] + grp) * inner + head % inner
            for part in range(3):
                start = (part * heads + head) * size
                for owner in sorted({start // unit, (start + size - 1) // unit}):
                    edges.append((source, owner, (part, start - owner * unit)))
    devices = heads * sizes[1]
    for matching in matchings(edges, devices):
        route = [edge[:2] for edge in matching]
        part_of, begin_of = [0] * devices, [0] * devices
        for source, owner, (part, begin) in matching:
            part_of[source], begin_of[owner] = part, begin
        yield route, part_of, begin_of


def fast_body(
    tile_embed, slide_lengths, head_offsets, pre_gain, pre_shift, qkv_weight, query_bias, value_bias, out_weight,
    out_bias, post_gain, post_shift, up_weight, up_bias, down_weight, down_bias, out_grad,
):
    width = qkv_weight.shape[0]
    heads = head_offsets.shape[1]
    size = width // heads
    tq = tile_embed.shape[1]
    br, groups = lax.axis_size("br"), lax.axis_size("grp")
    members = heads // br
    devices = heads * groups
    plan = Plan(heads, size, head_offsets.shape[0], br, members, tq, devices * tq)
    head = lax.axis_index(GROUP)
    group = lax.axis_index("grp")
    core = lax.axis_index("s0")
    meta = [group * plan.tokens, head, group, core, lax.axis_index(("br", "s1")), lax.axis_index(("grp", "s2"))]
    routes = list(column_routes(heads, size, 3 * width // devices))[::-1]
    table = jnp.array([parts for _, parts, _ in routes] + [begins for _, _, begins in routes], jnp.int32)
    meta.extend(lax.dynamic_index_in_dim(table, lax.axis_index(ALL), 1, False))
    meta = jnp.stack(meta).astype(jnp.int32)
    tiles = tile_embed[0]
    own_w = jnp.concatenate(
        [lax.dynamic_slice_in_dim(qkv_weight, part * width + head * size, size, 1) for part in range(3)], 1
    ).T
    pair = [(0, 1), (1, 0)]
    plane, line = ("br", "s1"), ("grp", "s2")

    x, npre = enter_call(heads, tiles, pre_gain, pre_shift, qkv_weight, query_bias, value_bias)
    x = swap(x.reshape(heads, 3 * size, tq), GROUP)
    x, npre, own_w, meta = lax.optimization_barrier((x, npre, own_w, meta))
    halo = to_neighbours(select_call(plan, meta, head_offsets, x), groups)
    state, *own = near_call(plan, meta, slide_lengths, head_offsets, x)
    mixed, state = far_call(plan, meta, slide_lengths, head_offsets, state, own, halo)
    attn_t = swap(mixed, GROUP).reshape(width, tq)
    npre_all = lax.all_gather(npre, GROUP, axis=0, tiled=True)
    attn_b = lax.ppermute(attn_t, "s0", pair)
    layer_out, residual_grad, attn_grad_t, common, sel, sel_give, sums, up_sums = middle_call(
        devices, core[None].astype(jnp.int32), attn_t, tiles, out_weight, out_bias, post_gain, post_shift,
        up_weight, up_bias, down_weight, down_bias, out_grad[0],
    )
    do = swap(attn_grad_t.reshape(heads, size, tq), GROUP)
    common_b = lax.ppermute(common, "s0", pair)
    sel_b = lax.ppermute(sel_give, "s0", pair)
    first, second = weights_call(devices, meta, attn_t, attn_b, common, common_b, sel, sel_b)
    do, first, second, npre_all = lax.optimization_barrier((do, first, second, npre_all))
    first = swap(first, plane)
    second = [second[0]] + [across(second[k], line, k) for k in (1, 2, 3)]
    rows, dq, dk, dv, *sides = far_back_call(plan, meta, slide_lengths, head_offsets, state, do, own, halo)
    back = from_neighbours(sides, groups)
    dx = near_back_call(plan, meta, slide_lengths, head_offsets, x, state, rows, (dq, dk, dv), back)
    dx, first, second = lax.optimization_barrier((dx, first, second))
    first, second = fold_call(meta, first, second)
    dx, first, second = lax.optimization_barrier((dx, first, second))
    first = [first[0]] + [across(first[k], line, k) for k in (1, 2, 3)]
    joined_grad = swap(dx, GROUP).reshape(heads, 3, size, tq)
    *columns, small = head_call(devices, meta, dx, npre_all, own_w, pre_gain, pre_shift, sums, up_sums)
    *columns, third = lax.optimization_barrier((*columns, second[3]))
    columns = [lax.ppermute(piece, ALL, route) for piece, (route, _, _) in zip(columns, routes)]
    second = [second[0], across(second[1], plane, 1), across(second[2], plane, 2), across(third, plane, 3)]
    joined_grad, small, second = lax.optimization_barrier((joined_grad, small, second))
    small = jnp.sum(swap(small, ALL), 0)
    joined_grad, first = lax.optimization_barrier((joined_grad, first))
    tile_grad = leave_call(tiles, pre_gain, qkv_weight, joined_grad, residual_grad)
    unit_up, unit = up_weight.shape[1] // devices, width // devices
    qkv_own, up_own, out_own, down_own = last_call(meta, 3 * unit, unit_up, unit, columns, first, second)
    return (
        layer_out[None],
        tile_grad[None],
        small[0:1, :unit],
        small[1:2, :unit],
        qkv_own.T,
        small[4:5, :unit],
        small[5:6, :unit],
        out_own.T,
        small[2:3, unit : 2 * unit],
        small[2:3, 2 * unit : 3 * unit],
        small[2:3, 3 * unit : 4 * unit],
        up_own.T,
        small[3:4, :unit_up],
        down_own.T,
        small[2:3, :unit],
    )


def solution(mesh):
    br, rows = mesh.shape["br"], mesh.shape["rows"]

    def run(*args):
        members = args[2].shape[1] // br
        shape = (br, rows // members, members // 4, 2, 2)
        split = jax.sharding.Mesh(mesh.devices.reshape(shape), ALL)
        tokens = P(("grp", "s2", "s1", "s0"), "br", None)
        owned = P(None, ALL)
        return jax.shard_map(
            fast_body if shape == (2, 2, 2, 2, 2) else body,
            mesh=split,
            in_specs=(tokens,) + (P(),) * 15 + (tokens,),
            out_specs=(tokens, tokens) + (owned,) * 13,
            check_vma=False,
        )(*args)

    return run
```

```python
import functools
import math

import jax
import jax.numpy as jnp
import ml_dtypes
import numpy as np
from jax import lax
from jax.experimental import pallas as pl
from jax.experimental.pallas import tpu as pltpu
from jax.sharding import PartitionSpec as P

SEG_BASE = 1024
DOC_MOST = 2048
LANES = 128
BF = jnp.bfloat16
F32 = jnp.float32
NEG = -1e30
EPS = 1e-05
ALL = ("br", "grp", "s2", "s1", "s0")
GROUP = ("br", "s2", "s1", "s0")
FIRST_DOWN = 2
ONE_LANE = 48
ID_Q = 51
ID_K = 52
TWICE = 53


class Plan:
    def __init__(self, heads, head_size, branches, groups, members, tq, total):
        self.heads, self.size, self.groups, self.members, self.tq = heads, head_size, groups, members, tq
        self.blocks = groups * members
        self.paired = groups * members * tq * 2 == total
        self.tokens = self.blocks * tq
        self.total = total
        self.halo = min(DOC_MOST, self.tokens)
        self.factor = math.log2(math.e) * head_size**-0.5
        self.branches = []
        keys, sel = 0, 0
        for level in range(branches):
            rate = 2**level
            span = min(SEG_BASE * rate, total)
            near = span <= self.tokens
            extra = 0 if near else self.halo // rate
            segs = self.tokens // span if near else 1
            seg_q = self.tokens // rate // segs
            seg_k = seg_q + 2 * extra
            flip = 0
            if level == 1 and near and span == 2 * self.branches[0]["span"]:
                segs, seg_q, seg_k, flip = segs * 2, seg_q // 2, seg_k // 2, 1
            self.branches.append(
                dict(
                    level=level, rate=rate, span=span, near=near, extra=extra, segs=segs,
                    seg_q=seg_q, seg_k=seg_k, tile=min(1024, seg_q), first=keys, sel=sel, flip=flip,
                )
            )
            keys += segs * seg_k
            sel += extra
        self.sel = sel
        self.twice = any(b["flip"] for b in self.branches)
        self.near = [b for b in self.branches if b["near"]]
        self.far = [b for b in self.branches if not b["near"]]
        self.near_keys = sum(b["segs"] * b["seg_k"] for b in self.near)
        self.far_keys, self.own = 0, 0
        for b in self.far:
            b["begin"], b["own"] = self.far_keys, self.own
            self.far_keys += b["seg_k"]
            self.own += b["seg_q"]
        self.widest = max(b["seg_k"] for b in self.branches)

    def slot(self, block):
        return lax.rem(block, self.groups) * self.members + lax.div(block, self.groups)


def dot_nt(a, b):
    return lax.dot_general(a, b, (((1,), (1,)), ((), ())), preferred_element_type=F32)


def dot_tn(a, b):
    return lax.dot_general(a, b, (((0,), (0,)), ((), ())), preferred_element_type=F32)


def dot_nn(a, b):
    return lax.dot_general(a, b, (((1,), (0,)), ((), ())), preferred_element_type=F32)


def iota(shape, dim):
    return lax.broadcasted_iota(jnp.int32, shape, dim)


def placement(size, parts):
    shape = (parts * size + 16, parts * LANES)
    row, col = iota(shape, 0), iota(shape, 1)
    hit = col < 0
    for part in range(parts):
        hit |= (row >= part * size) & (row < (part + 1) * size) & (col == row - part * size + part * LANES)
    return row, col, hit


def ids_of(pos, starts, gate=None):
    found = jnp.zeros(pos.shape, jnp.int32)
    for start in starts:
        found += jnp.where(pos >= start, 1, 0)
    if gate is not None:
        found = jnp.where(gate, found, -1)
    return found.astype(F32)


def slide_starts(lens_ref):
    starts, at = [], jnp.int32(0)
    for i in range(lens_ref.shape[0]):
        starts.append(at)
        at = at + lens_ref[i]
    return starts


def branch_pos(plan, branch, base, off, first, count):
    start = base - branch["extra"] * branch["rate"] + off
    pos = start + branch["rate"] * (first + iota((1, count), 1))
    if branch["near"]:
        return pos, None
    shift = int(math.log2(branch["span"]))
    return pos, lax.shift_right_arithmetic(pos, shift) == lax.shift_right_arithmetic(base, shift)


def plain_keys(rows):
    lane = iota(rows.shape, 1)
    return jnp.where((lane >= TWICE) & (lane < TWICE + 3), 0.0, rows)


def to_rows(plan, base, offs, starts, x_ref, q_tm, k_tm, v_tm, extra_q=None):
    size, tq = plan.size, plan.tq
    row, col, hit = placement(size, 3)
    hit |= (row == 3 * size) & ((col == ID_Q) | (col == LANES + ID_K))
    place = jnp.where(hit, 1.0, 0.0).astype(BF)
    lane = iota((1, 3 * LANES), 1)
    in_k, in_v = lane - LANES, lane - 2 * LANES
    ones = jnp.where(
        ((in_k >= ONE_LANE) & (in_k < ONE_LANE + 3)) | ((in_v >= ONE_LANE) & (in_v < ONE_LANE + 3)), 1.0, 0.0
    )

    more = jnp.zeros((1, LANES), F32)
    rest = 1.0 / plan.factor
    for i in range(3 if plan.twice else 0):
        term = float(np.float32(rest).astype(ml_dtypes.bfloat16))
        more = jnp.where(lane[:, :LANES] == TWICE + i, term, more)
        rest -= term
    own = iota((1, LANES), 1)
    both = jnp.where((own >= TWICE) & (own < TWICE + 3), 1.0, 0.0)

    def block(n, carry):
        pos = base + n * tq + iota((1, tq), 1)
        ids = jnp.where(iota((16, tq), 0) == 0, ids_of(pos, starts), 0.0).astype(BF)
        full = jnp.concatenate([x_ref[plan.slot(n)], ids], 0)
        rows = dot_tn(full, place) + ones
        at = pl.ds(pl.multiple_of(n * tq, tq), tq)
        queries = rows[:, :LANES]
        if extra_q is not None:
            queries = queries + extra_q(n, at)
        keys = rows[:, LANES : 2 * LANES]
        if plan.twice:
            member = (iota((tq, 1), 0) & 1) == offs[1]
            queries = jnp.where(member, queries + more, queries)
            keys = jnp.where(member, keys + both, keys)
        q_tm[at, :] = queries
        k_tm[at, :] = keys
        v_tm[at, :] = rows[:, 2 * LANES :]
        if extra_q is not None:
            return carry
        squares = [jnp.square(full[i * size : (i + 1) * size].astype(F32)) for i in range(2)]
        return tuple(jnp.maximum(a, jnp.sum(b, 0, keepdims=True)) for a, b in zip(carry, squares))

    start = (jnp.zeros((1, tq), F32),) * 2 if extra_q is None else 0
    most = lax.fori_loop(0, plan.blocks, block, start, unroll=4)
    if extra_q is None:
        return jnp.sqrt(jnp.max(most[0], 1, keepdims=True) * jnp.max(most[1], 1, keepdims=True)) * 1.0001
    return None


def gather_near(plan, offs, k_tm, v_tm, kall, vall, branches):
    for branch in branches:
        rate, first, off = branch["rate"], branch["first"], offs[branch["level"]]
        count = plan.tokens // rate
        step = min(256, count)

        def chunk(i, carry, rate=rate, first=first, off=off, step=step):
            keys = k_tm[pl.ds(off + i * step * rate, step, stride=rate) if rate > 1 else pl.ds(i * step, step), :]
            rows = pl.ds(off + i * step * rate, step, stride=rate) if rate > 1 else pl.ds(i * step, step)
            to = pl.ds(pl.multiple_of(first + i * step, step), step)
            kall[to, :] = (plain_keys(keys) if rate > 1 else keys).astype(BF)
            vall[to, :] = v_tm[rows, :].astype(BF)
            return carry

        lax.fori_loop(0, count // step, chunk, 0, unroll=min(4, count // step))


def far_keys(plan, base, offs, starts, halos, k_far, v_far, kall, vall):
    size = plan.size
    row, col, hit = placement(size, 2)
    hit |= (row == 2 * size) & (col == ID_K)
    place = jnp.where(hit, 1.0, 0.0).astype(BF)
    lane = iota((1, 2 * LANES), 1)
    in_v = lane - LANES
    ones = jnp.where(
        ((lane >= ONE_LANE) & (lane < ONE_LANE + 3)) | ((in_v >= ONE_LANE) & (in_v < ONE_LANE + 3)), 1.0, 0.0
    )
    for branch in plan.far:
        extra, first, own, count = branch["extra"], branch["begin"], branch["own"], branch["seg_q"]
        kall[first + extra : first + extra + count, :] = k_far[own : own + count, :]
        vall[first + extra : first + extra + count, :] = v_far[own : own + count, :]
        for side, ref in enumerate((halos[0], halos[-1])):
            begin = side * (extra + count)
            pos, gate = branch_pos(plan, branch, base, offs[branch["level"]], begin, extra)
            ids = jnp.where(iota((16, extra), 0) == 0, ids_of(pos, starts, gate), 0.0).astype(BF)
            piece = ref[:, branch["sel"] : branch["sel"] + extra]
            rows = dot_tn(jnp.concatenate([piece, ids], 0), place) + ones
            kall[first + begin : first + begin + extra, :] = rows[:, :LANES].astype(BF)
            vall[first + begin : first + begin + extra, :] = rows[:, LANES:].astype(BF)


def picked(branch, off, i):
    tile, rate = branch["tile"], branch["rate"]
    if rate == 1:
        return pl.ds(pl.multiple_of(i * tile, tile), tile)
    return pl.ds(off + i * tile * rate, tile, stride=rate)


def pieces_of(wide, most):
    step = next(n for n in (most, 512, 256, 128) if wide % n == 0)
    return [(at, step) for at in range(0, wide, step)]


def split3(column, lane):
    high = column.astype(BF).astype(F32)
    rest = column - high
    mid = rest.astype(BF).astype(F32)
    low = rest - mid
    return jnp.where(
        lane == ONE_LANE, high, jnp.where(lane == ONE_LANE + 1, mid, jnp.where(lane == ONE_LANE + 2, low, 0.0))
    )


def near_kernel(plan, meta, lens, offsets, x_ref, st_ref, qf_ref, kf_ref, vf_ref, q_tm, k_tm, v_tm, kall, vall, kid):
    base, head = meta[0], meta[1]
    starts = slide_starts(lens)
    offs = [offsets[b["level"], head] for b in plan.branches]
    top = to_rows(plan, base, offs, starts, x_ref, q_tm, k_tm, v_tm)
    gather_near(plan, offs, k_tm, v_tm, kall, vall, plan.near)
    for branch in plan.far:
        rows = pl.ds(offs[branch["level"]], branch["seg_q"], stride=branch["rate"])
        own = slice(branch["own"], branch["own"] + branch["seg_q"])
        qf_ref[own, :] = q_tm[rows, :].astype(BF)
        kf_ref[own, :] = plain_keys(k_tm[rows, :]).astype(BF)
        vf_ref[own, :] = v_tm[rows, :].astype(BF)
    for branch in plan.near:
        first, total = branch["first"], branch["segs"] * branch["seg_k"]
        pos, gate = branch_pos(plan, branch, base, offs[branch["level"]], 0, total)
        kid[:, first : first + total] = ids_of(pos, starts, gate)
    factor = plan.factor
    lane = iota((1, LANES), 1)

    def scan(visit):
        for branch in plan.near:
            per = branch["seg_q"] // branch["tile"]

            def tile(i, carry, branch=branch, per=per):
                rows = picked(branch, offs[branch["level"]], i)
                at = pl.multiple_of(branch["first"] + (lax.div(i, per) ^ branch["flip"]) * branch["seg_k"], 128)
                visit(branch, rows, q_tm[rows, :], at)
                return carry

            lax.fori_loop(0, branch["segs"] * per, tile, 0, unroll=4 if branch["flip"] else min(2, branch["segs"] * per))

    def attend(top_lanes):
        def visit(branch, rows, queries, at):
            ids = queries[:, ID_Q : ID_Q + 1]
            low = (queries + top_lanes).astype(BF)
            mixed = None
            for begin, step in pieces_of(branch["seg_k"], 1024):
                to = pl.ds(at + begin, step)
                weights = jnp.exp2(dot_nt(low, kall[to, :]) * factor)
                weights = jnp.where(ids == kid[:, to], weights, 0.0).astype(BF)
                more = dot_nn(weights, vall[to, :])
                mixed = more if mixed is None else mixed + more
            if branch["level"]:
                mixed = st_ref[rows, :] + mixed
            st_ref[rows, :] = mixed

        scan(visit)

    attend(split3(-top, lane))
    step = min(512, plan.tokens)

    def least(n, low):
        at = pl.ds(pl.multiple_of(n * step, step), step)
        state = st_ref[at, :]
        st_ref[at, :] = jnp.where(iota((step, LANES), 1) == ID_Q, top, state)
        return jnp.minimum(low, jnp.min(state, 0, keepdims=True))

    weight = lax.fori_loop(0, plan.tokens // step, least, jnp.full((1, LANES), jnp.inf, F32), unroll=2)
    weight = jnp.min(jnp.where(lane == ONE_LANE, weight, jnp.inf))

    @pl.when(jnp.logical_not(weight > 2.0**-60))
    def _():
        def clear(n, carry):
            st_ref[pl.ds(pl.multiple_of(n * step, step), step), :] = jnp.full((step, LANES), NEG, F32)
            return carry

        def largest(branch, rows, queries, at):
            low = queries.astype(BF)
            best = st_ref[rows, :]
            for begin, step in pieces_of(branch["seg_k"], 256):
                to = pl.ds(at + begin, step)
                scores = jnp.where(queries[:, ID_Q : ID_Q + 1] == kid[:, to], dot_nt(low, kall[to, :]), NEG)
                best = jnp.maximum(best, jnp.max(scores, 1, keepdims=True))
            st_ref[rows, :] = best

        def settle(n, carry):
            at = pl.ds(pl.multiple_of(n * step, step), step)
            own = st_ref[at, :]
            tops[at, :] = own
            wide = iota((step, LANES), 1)
            q_tm[at, :] = q_tm[at, :] + split3(-own, wide)
            return carry

        def restore(n, carry):
            at = pl.ds(pl.multiple_of(n * step, step), step)
            st_ref[at, :] = jnp.where(iota((step, LANES), 1) == ID_Q, tops[at, :], st_ref[at, :])
            return carry

        tops = k_tm
        lax.fori_loop(0, plan.tokens // step, clear, 0)
        scan(largest)
        lax.fori_loop(0, plan.tokens // step, settle, 0)
        attend(jnp.zeros((1, LANES), F32))
        lax.fori_loop(0, plan.tokens // step, restore, 0)


def far_kernel(plan, meta, lens, offsets, st_in, qf_ref, kf_ref, vf_ref, *rest):
    halos, (o_ref, st_ref, kall, vall) = rest[:-4], rest[-4:]
    base, head = meta[0], meta[1]
    starts = slide_starts(lens)
    offs = [offsets[b["level"], head] for b in plan.branches]
    factor = plan.factor
    step = min(512, plan.tokens)

    def carry_over(n, carry):
        at = pl.ds(pl.multiple_of(n * step, step), step)
        st_ref[at, :] = st_in[at, :]
        return carry

    lax.fori_loop(0, plan.tokens // step, carry_over, 0, unroll=2)
    if plan.far:
        far_keys(plan, base, offs, starts, halos, kf_ref, vf_ref, kall, vall)
    for branch in plan.far:
        off, tile, wide = offs[branch["level"]], branch["tile"], branch["seg_k"]
        pos, gate = branch_pos(plan, branch, base, off, 0, wide)
        ids = ids_of(pos, starts, gate)
        keys = kall[branch["begin"] : branch["begin"] + wide, :]
        values = vall[branch["begin"] : branch["begin"] + wide, :]
        for i in range(branch["seg_q"] // tile):
            own = branch["own"] + i * tile
            queries = qf_ref[own : own + tile, :]
            rows = picked(branch, off, i)
            scores = dot_nt(queries, keys)
            scores = jnp.where(queries[:, ID_Q : ID_Q + 1].astype(F32) == ids, scores, NEG)
            top = jnp.max(scores, 1, keepdims=True)
            mixed = dot_nn(jnp.exp2((scores - top) * factor).astype(BF), values)
            old = st_ref[rows, :]
            old_top = old[:, ID_Q : ID_Q + 1]
            new_top = jnp.maximum(old_top, top)
            mixed = old * jnp.exp2((old_top - new_top) * factor) + mixed * jnp.exp2((top - new_top) * factor)
            st_ref[rows, :] = jnp.where(iota((tile, LANES), 1) == ID_Q, new_top, mixed)
    eye = jnp.where(iota((plan.size, LANES), 0) == iota((plan.size, LANES), 1), 1.0, 0.0).astype(BF)

    def finish(n, carry):
        at = pl.ds(pl.multiple_of(n * plan.tq, plan.tq), plan.tq)
        state = st_ref[at, :]
        weight = state[:, ONE_LANE : ONE_LANE + 1]
        top = state[:, ID_Q : ID_Q + 1]
        attn = state * (1.0 / weight)
        merged = top + jnp.log2(weight) * (1.0 / factor)
        lane = iota((plan.tq, LANES), 1)
        st_ref[at, :] = jnp.where(lane < plan.size, attn, jnp.where(lane == ONE_LANE, merged, 0.0))
        o_ref[plan.slot(n)] = dot_nt(eye, attn.astype(BF)).astype(BF)
        return carry

    lax.fori_loop(0, plan.blocks, finish, 0, unroll=4)


def back_tile(plan, branch, queries, grads, keys_at, kall, vall, k_fm, linked, dk_acc, dv_acc):
    dq = None
    for begin, step in pieces_of(branch["seg_k"], 256):
        to = pl.ds(keys_at + begin, step)
        part = slice(begin, begin + step)
        keys = kall[to, :]
        probs = jnp.where(linked(keys), jnp.exp2(dot_nt(keys, queries) * plan.factor), 0.0)
        dv_acc[part, :] += dot_nn(probs.astype(BF), grads)
        moved = (probs * dot_nt(vall[to, :], grads)).astype(BF)
        dk_acc[part, :] += dot_nn(moved, queries)
        more = dot_nn(k_fm[:, part], moved)
        dq = more if dq is None else dq + more
    return dq


def far_back_kernel(
    plan, meta, lens, offsets, st_ref, do_ref, qf_ref, kf_ref, vf_ref, *rest,
):
    sides = 1 if plan.paired else 2
    halos, (do_tm, dqf_ref, dkf_ref, dvf_ref), rest = rest[:sides], rest[sides : sides + 4], rest[sides + 4 :]
    halo_outs, (kall, vall, k_fm, dk_acc, dv_acc) = rest[:sides], rest[sides:]
    base, head = meta[0], meta[1]
    starts = slide_starts(lens)
    offs = [offsets[b["level"], head] for b in plan.branches]
    size, tq = plan.size, plan.tq
    row, col, hit = placement(size, 1)
    place = jnp.where(hit, 1.0, 0.0).astype(BF)
    lane = iota((tq, LANES), 1)

    def block(n, carry):
        at = pl.ds(pl.multiple_of(n * tq, tq), tq)
        grads = dot_tn(jnp.concatenate([do_ref[plan.slot(n)], jnp.zeros((16, tq), BF)], 0), place)
        dots = jnp.sum(jnp.where(lane < size, grads * st_ref[at, :], 0.0), 1, keepdims=True)
        do_tm[at, :] = grads + split3(-dots, lane)
        return carry

    lax.fori_loop(0, plan.blocks, block, 0, unroll=4)
    if plan.far:
        far_keys(plan, base, offs, starts, halos, kf_ref, vf_ref, kall, vall)
    eye = jnp.where(iota((LANES, LANES), 0) == iota((LANES, LANES), 1), 1.0, 0.0).astype(BF)
    for branch in plan.far:
        off, tile, wide, begin = offs[branch["level"]], branch["tile"], branch["seg_k"], branch["begin"]
        k_fm[:, :wide] = dot_nt(eye, kall[begin : begin + wide, :]).astype(BF)
        dk_acc[:wide, :] = jnp.zeros((wide, LANES), F32)
        dv_acc[:wide, :] = jnp.zeros((wide, LANES), F32)
        extra, count = branch["extra"], branch["seg_q"]
        for i in range(count // tile):
            own = branch["own"] + i * tile
            rows = picked(branch, off, i)
            wide_lane = iota((tile, LANES), 1)
            merged = st_ref[rows, :][:, ONE_LANE : ONE_LANE + 1]
            queries = jnp.where(wide_lane == ID_Q, 0.0, qf_ref[own : own + tile, :].astype(F32))
            queries = (queries + split3(-merged, wide_lane)).astype(BF)
            grads = do_tm[rows, :].astype(BF)
            pos, _ = branch_pos(plan, branch, base, off, extra + i * tile, tile)
            ids = ids_of(pos, starts)
            linked = lambda keys: keys[:, ID_K : ID_K + 1].astype(F32) == ids
            dq = back_tile(plan, branch, queries, grads, begin, kall, vall, k_fm, linked, dk_acc, dv_acc)
            dqf_ref[own : own + tile, :] = dq.T
        own = slice(branch["own"], branch["own"] + count)
        dkf_ref[own, :] = dk_acc[extra : extra + count, :]
        dvf_ref[own, :] = dv_acc[extra : extra + count, :]
        for side, ref in enumerate(halo_outs):
            at = side * (extra + count)
            if plan.paired:
                at = pl.multiple_of((1 - meta[2]) * (extra + count), 128)
            to = slice(branch["sel"], branch["sel"] + extra)
            dk = (dk_acc[pl.ds(at, extra), :] * size**-0.5).astype(BF)
            ref[:size, to] = dot_nt(eye[:size], dk).astype(BF)
            ref[size:, to] = dot_nt(eye[:size], dv_acc[pl.ds(at, extra), :].astype(BF)).astype(BF)


def near_back_kernel(
    plan, meta, lens, offsets, x_ref, st_ref, do_tm, dqf_ref, dkf_ref, dvf_ref, *rest,
):
    backs, (dx_ref, q_tm, k_tm, v_tm, dq_tm, dk_tm, dv_tm, kall, vall, k_fm, qid, dk_acc, dv_acc) = rest[:-13], rest[-13:]
    base, head = meta[0], meta[1]
    starts = slide_starts(lens)
    offs = [offsets[b["level"], head] for b in plan.branches]
    size, tq = plan.size, plan.tq
    lane = iota((tq, LANES), 1)
    to_rows(
        plan, base, offs, starts, x_ref, q_tm, k_tm, v_tm,
        lambda n, at: split3(-st_ref[at, :][:, ONE_LANE : ONE_LANE + 1], lane),
    )
    gather_near(plan, offs, k_tm, v_tm, kall, vall, plan.near)
    eye = jnp.where(iota((LANES, LANES), 0) == iota((LANES, LANES), 1), 1.0, 0.0).astype(BF)
    for branch in plan.near:
        off, first, wide, tile = offs[branch["level"]], branch["first"], branch["seg_k"], branch["tile"]
        count = branch["segs"] * branch["seg_q"]
        per = branch["seg_q"] // tile
        pos, _ = branch_pos(plan, branch, base, off, 0, count)
        qid[:, :count] = ids_of(pos, starts)

        def segment(seg, carry, branch=branch, off=off, first=first, wide=wide, tile=tile, per=per):
            key_seg = seg ^ branch["flip"]
            keys_at = pl.multiple_of(first + key_seg * wide, 128)
            k_fm[:, :wide] = dot_nt(eye, kall[pl.ds(keys_at, wide), :]).astype(BF)
            dk_acc[:wide, :] = jnp.zeros((wide, LANES), F32)
            dv_acc[:wide, :] = jnp.zeros((wide, LANES), F32)

            def one(j, carry):
                i = seg * per + j
                rows = picked(branch, off, i)
                queries = q_tm[rows, :].astype(BF)
                grads = do_tm[rows, :].astype(BF)
                ids = qid[:, pl.ds(pl.multiple_of(i * tile, tile), tile)]
                linked = lambda keys: keys[:, ID_K : ID_K + 1].astype(F32) == ids
                dq = back_tile(plan, branch, queries, grads, keys_at, kall, vall, k_fm, linked, dk_acc, dv_acc).T
                if branch["level"]:
                    dq = dq_tm[rows, :] + dq
                dq_tm[rows, :] = dq
                return carry

            lax.fori_loop(0, per, one, 0)
            step = min(256, branch["seg_q"])
            for c in range(branch["seg_q"] // step):
                begin = c * step
                if branch["rate"] == 1:
                    to = pl.ds(pl.multiple_of(key_seg * branch["seg_q"] + begin, step), step)
                    dk_tm[to, :] = dk_acc[begin : begin + step, :]
                    dv_tm[to, :] = dv_acc[begin : begin + step, :]
                else:
                    to = pl.ds(off + (key_seg * branch["seg_q"] + begin) * branch["rate"], step, stride=branch["rate"])
                    dk_tm[to, :] += dk_acc[begin : begin + step, :]
                    dv_tm[to, :] += dv_acc[begin : begin + step, :]
            return carry

        lax.fori_loop(0, branch["segs"], segment, 0, unroll=2 if branch["segs"] > 1 else 1)
    row, col, hit = placement(size, 2)
    place = jnp.where(hit, 1.0, 0.0).astype(BF)[: 2 * size]
    for branch in plan.far:
        off, rate, extra, count = offs[branch["level"]], branch["rate"], branch["extra"], branch["seg_q"]
        rows = pl.ds(off, count, stride=rate)
        own = slice(branch["own"], branch["own"] + count)
        for total, part in ((dq_tm, dqf_ref), (dk_tm, dkf_ref), (dv_tm, dvf_ref)):
            total[rows, :] += part[own, :]
        begins = [plan.tokens - plan.halo, 0]
        if plan.paired:
            begins = [(1 - meta[2]) * (plan.tokens - plan.halo)]
        for begin, ref in zip(begins, backs):
            more = dot_tn(ref[:, branch["sel"] : branch["sel"] + extra], place)
            rows = pl.ds(begin + off, extra, stride=rate)
            dk_tm[rows, :] += more[:, :LANES] * size**0.5
            dv_tm[rows, :] += more[:, LANES:]
    small_eye = eye[:size]

    def finish(n, carry):
        at = pl.ds(pl.multiple_of(n * tq, tq), tq)
        slot = plan.slot(n)
        dx_ref[slot, :size, :] = dot_nt(small_eye, (dq_tm[at, :] * size**-0.5).astype(BF)).astype(BF)
        dx_ref[slot, size : 2 * size, :] = dot_nt(small_eye, (dk_tm[at, :] * size**-0.5).astype(BF)).astype(BF)
        dx_ref[slot, 2 * size :, :] = dot_nt(small_eye, dv_tm[at, :].astype(BF)).astype(BF)
        return carry

    lax.fori_loop(0, plan.blocks, finish, 0, unroll=4)


SMEM = pl.BlockSpec(memory_space=pltpu.SMEM)
VMEM = pl.BlockSpec(memory_space=pltpu.VMEM)
TINY = pl.CostEstimate(flops=1000, bytes_accessed=1000, transcendentals=0)
PARAMS = pltpu.CompilerParams(vmem_limit_bytes=60 << 20)
ROOMY = pltpu.CompilerParams(vmem_limit_bytes=40 << 20)


def struct(shape, kind):
    return jax.ShapeDtypeStruct(shape, kind)


def kernel_call(name, kernel, ins, outs, scratch, flops):
    return pl.pallas_call(
        kernel,
        out_shape=tuple(struct(*out) for out in outs),
        in_specs=[SMEM] * 3 + [VMEM] * (len(ins) - 3),
        out_specs=(VMEM,) * len(outs),
        scratch_shapes=[pltpu.VMEM(*s) for s in scratch],
        compiler_params=ROOMY,
        cost_estimate=pl.CostEstimate(flops=flops, bytes_accessed=1000, transcendentals=0),
        name=name,
    )(*ins)


def near_call(plan, meta, lens, offsets, x):
    rows, keys = ((plan.tokens, LANES), F32), ((plan.near_keys, LANES), BF)
    own = ((plan.own, LANES), BF)
    return kernel_call(
        "near", functools.partial(near_kernel, plan), (meta, lens, offsets, x), (rows, own, own, own),
        (rows, rows, rows, keys, keys, ((1, plan.near_keys), F32)), 20_000_000_000,
    )


def far_call(plan, meta, lens, offsets, state, own, halo):
    keys = ((plan.far_keys, LANES), BF)
    return kernel_call(
        "far", functools.partial(far_kernel, plan), (meta, lens, offsets, state, *own, *halo),
        (((plan.blocks, plan.size, plan.tq), BF), ((plan.tokens, LANES), F32)), (keys, keys), 4_000_000_000,
    )


def far_back_call(plan, meta, lens, offsets, state, do, own, halo):
    keys = ((plan.far_keys, LANES), BF)
    part, side = ((plan.own, LANES), F32), ((2 * plan.size, max(plan.sel, LANES)), BF)
    acc = ((plan.widest, LANES), F32)
    return kernel_call(
        "far_back", functools.partial(far_back_kernel, plan), (meta, lens, offsets, state, do, *own, *halo),
        (((plan.tokens, LANES), F32), part, part, part) + (side,) * (1 if plan.paired else 2),
        (keys, keys, ((LANES, plan.widest), BF), acc, acc), 4_000_000_000,
    )


def near_back_call(plan, meta, lens, offsets, x, state, do_rows, parts, back):
    rows, keys = ((plan.tokens, LANES), F32), ((plan.near_keys, LANES), BF)
    acc = ((plan.widest, LANES), F32)
    return kernel_call(
        "near_back", functools.partial(near_back_kernel, plan),
        (meta, lens, offsets, x, state, do_rows, *parts, *back),
        (((plan.blocks, 3 * plan.size, plan.tq), BF),),
        (rows,) * 6 + (keys, keys, ((LANES, plan.widest), BF), ((1, plan.tokens), F32), acc, acc), 8_000_000_000,
    )[0]


def near_rows(values, norm_gain, norm_shift):
    centred = values - jnp.mean(values, 1, keepdims=True)
    inverse = lax.rsqrt(jnp.mean(centred * centred, 1, keepdims=True) + EPS)
    normed = centred * inverse
    return normed * norm_gain + norm_shift, normed, inverse


def back_rows(grad_out, normed, inverse, norm_gain):
    grad_norm = grad_out * norm_gain
    return inverse * (
        grad_norm
        - jnp.mean(grad_norm, 1, keepdims=True)
        - normed * jnp.mean(grad_norm * normed, 1, keepdims=True)
    )


def own_columns(size, unit, core):
    row, col = iota((size, size), 0), iota((size, size), 1)
    half = size // 2
    other = row >= half
    place = jnp.where(other, row - half, row)
    whole = jnp.floor((place.astype(F32) + 0.5) * (1.0 / unit)).astype(jnp.int32)
    parity = jnp.where(other, 1 - core, core)
    return jnp.where(col == place + unit * (whole + parity), 1.0, 0.0).astype(BF)


def middle_kernel(
    unit_up, unit, core_ref, attn_ref, tiles_ref, out_w, out_b, gain, shift, up_w, up_b, down_w, down_b, g_ref,
    y_ref, res_ref, ag_ref, common_ref, mine_ref, theirs_ref, sums_ref, up_sum_ref,
    pick_up, normed_s, lifted_s, inverse_s, out_s, back_s,
):
    step, steps = pl.program_id(0), pl.num_programs(0)
    width = tiles_ref.shape[1]
    chunk = up_w.shape[1]
    half = chunk // 2
    core = core_ref[0]
    hidden_sel = steps * half

    @pl.when(step == 0)
    def _():
        pick_up[...] = own_columns(chunk, unit_up, core)
        residual = tiles_ref[...].astype(F32) + dot_tn(attn_ref[...], out_w[...]) + out_b[...]
        lifted, normed, inverse = near_rows(residual, gain[...], shift[...])
        low = lifted.astype(BF)
        lifted_s[...] = low
        normed_s[...] = normed
        inverse_s[...] = jnp.broadcast_to(inverse, inverse_s.shape)
        out_s[...] = residual + down_b[...]
        back_s[...] = jnp.zeros_like(back_s)
        common_ref[pl.ds(steps * chunk, width), :] = low.T
        common_ref[pl.ds(steps * chunk + width, width), :] = attn_ref[...]
        pick = own_columns(width, unit, core)
        picked_g = dot_nt(pick, g_ref[...]).astype(BF)
        mine_ref[pl.ds(hidden_sel, width // 2), :] = picked_g[: width // 2]
        theirs_ref[pl.ds(hidden_sel, width // 2), :] = picked_g[width // 2 :]

    lifted = lifted_s[...]
    gate_in = dot_nn(lifted, up_w[...]) + up_b[...]
    cdf = 0.5 + 0.5 * lax.erf(gate_in * (0.5**0.5))
    act = (gate_in * cdf).astype(BF)
    slope = cdf + gate_in * (jnp.exp(-0.5 * gate_in * gate_in) * (1.0 / math.sqrt(2.0 * math.pi)))
    gate_grad = (dot_nt(g_ref[...], down_w[...]) * slope).astype(BF)
    out_s[...] += dot_nn(act, down_w[...])
    back_s[...] += dot_nt(gate_grad, up_w[...])
    up_sum_ref[...] = jnp.sum(gate_grad.astype(F32), 0, keepdims=True)
    common_ref[pl.ds(pl.multiple_of(step * chunk, chunk), chunk), :] = act.T
    picked_gate = dot_nt(pick_up[...], gate_grad).astype(BF)
    at = pl.ds(pl.multiple_of(step * half, half), half)
    mine_ref[at, :] = picked_gate[:half]
    theirs_ref[at, :] = picked_gate[half:]

    @pl.when(step == steps - 1)
    def _():
        y_ref[...] = out_s[...].astype(BF)
        grads = g_ref[...].astype(F32)
        lifted_grad = back_s[...]
        normed = normed_s[...]
        residual_grad = grads + back_rows(lifted_grad, normed, inverse_s[:, :1], gain[...])
        res_ref[...] = residual_grad
        low = residual_grad.astype(BF)
        ag_ref[...] = dot_nt(out_w[...], low).astype(BF)
        pick = own_columns(width, unit, core)
        picked_p = dot_nt(pick, low).astype(BF)
        at = pl.ds(hidden_sel + width // 2, width // 2)
        mine_ref[at, :] = picked_p[: width // 2]
        theirs_ref[at, :] = picked_p[width // 2 :]
        sums_ref[0:1, :] = jnp.sum(grads, 0, keepdims=True)
        sums_ref[1:2, :] = jnp.sum(residual_grad, 0, keepdims=True)
        sums_ref[2:3, :] = jnp.sum(lifted_grad * normed, 0, keepdims=True)
        sums_ref[3:4, :] = jnp.sum(lifted_grad, 0, keepdims=True)
        sums_ref[4:8, :] = jnp.zeros((4, width), F32)


def middle_call(devices, core, attn_t, tiles, out_w, out_b, gain, shift, up_w, up_b, down_w, down_b, g):
    tq, width = tiles.shape
    hidden = up_w.shape[1]
    steps = hidden // width
    whole = lambda *shape: pl.BlockSpec(shape, lambda j: (0,) * len(shape))
    vec = whole(1, width)
    sel = hidden // 2 + width
    return pl.pallas_call(
        functools.partial(middle_kernel, hidden // devices, width // devices),
        grid=(steps,),
        in_specs=[
            SMEM, whole(width, tq), whole(tq, width), whole(width, width), vec, vec, vec,
            pl.BlockSpec((width, width), lambda j: (0, j)), pl.BlockSpec((1, width), lambda j: (0, j)),
            pl.BlockSpec((width, width), lambda j: (j, 0)), vec, whole(tq, width),
        ],
        out_specs=(
            whole(tq, width), whole(tq, width), whole(width, tq), whole(hidden + 2 * width, tq), whole(sel, tq),
            whole(sel, tq), whole(8, width), pl.BlockSpec((1, width), lambda j: (0, j)),
        ),
        out_shape=(
            jax.ShapeDtypeStruct((tq, width), BF),
            pltpu.HBM((tq, width), F32),
            jax.ShapeDtypeStruct((width, tq), BF),
            pltpu.HBM((hidden + 2 * width, tq), BF),
            pltpu.HBM((sel, tq), BF),
            pltpu.HBM((sel, tq), BF),
            pltpu.HBM((8, width), F32),
            pltpu.HBM((1, hidden), F32),
        ),
        scratch_shapes=[
            pltpu.VMEM((width, width), BF), pltpu.VMEM((tq, width), F32), pltpu.VMEM((tq, width), BF),
            pltpu.VMEM((tq, LANES), F32), pltpu.VMEM((tq, width), F32), pltpu.VMEM((tq, width), F32),
        ],
        compiler_params=ROOMY,
        cost_estimate=pl.CostEstimate(flops=14 * tq * width * hidden, bytes_accessed=20 << 20, transcendentals=0),
        name="middle",
    )(core, attn_t, tiles, out_w, out_b, gain, shift, up_w, up_b, down_w, down_b, g)


def weights_kernel(unit_up, unit, meta, common_a, common_b, sel_a, sel_b, *rest):
    first_ref, second_refs, (first_s, second_s, sems) = rest[0], rest[1:5], rest[5:]
    width = 2 * unit * 16
    hidden = common_a.shape[0] - 2 * width
    chips = width // (2 * unit)

    def spot(chip):
        return (chip // 8) * 2 + chip % 2, chip // 2 % 4

    lifted, attn = slice(hidden, hidden + width), slice(hidden + width, hidden + 2 * width)
    group = width // (2 * unit_up)
    for step in range(hidden // width):
        rows = slice(step * width // 2, (step + 1) * width // 2)
        part = dot_nt(sel_a[rows, :], common_a[lifted, :]) + dot_nt(sel_b[rows, :], common_b[lifted, :])
        for i in range(group):
            plane, line = spot(step * group + i)
            first_s[plane, line, :unit_up, :] = part[i * unit_up : (i + 1) * unit_up].astype(BF)
    rows_out = slice(hidden // 2 + width // 2, hidden // 2 + width)
    rows = slice(hidden // 2, hidden // 2 + width // 2)
    out = dot_nt(sel_a[rows_out, :], common_a[attn, :]) + dot_nt(sel_b[rows_out, :], common_b[attn, :])
    held = [out]

    def down_part(step):
        cols = slice(step * width, (step + 1) * width)
        return dot_nt(sel_a[rows, :], common_a[cols, :]) + dot_nt(sel_b[rows, :], common_b[cols, :])

    held += [down_part(step) for step in range(FIRST_DOWN)]
    for chip in range(chips):
        plane, line = spot(chip)
        at = slice(chip * unit, (chip + 1) * unit)
        first_s[plane, line, unit_up:, :] = jnp.concatenate([part[at] for part in held], 0).astype(BF)
    copies = [pltpu.make_async_copy(first_s, first_ref, sems.at[4])]
    copies[0].start()
    for step in range(FIRST_DOWN, hidden // width):
        part = down_part(step)
        at = (step - FIRST_DOWN) * width
        for chip in range(chips):
            plane, line = spot(chip)
            second_s[line, plane, :, at : at + width] = part[chip * unit : (chip + 1) * unit].astype(BF)
    for k in range(4):
        copies.append(pltpu.make_async_copy(second_s.at[meta[5] ^ k], second_refs[k], sems.at[k]))
        copies[-1].start()
    for copy in copies:
        copy.wait()


def weights_call(devices, meta, width, common_a, common_b, sel_a, sel_b):
    tq = common_a.shape[1]
    hidden = common_a.shape[0] - 2 * width
    unit_up, unit = hidden // devices, width // devices
    first = (4, 4, unit_up + (1 + FIRST_DOWN) * unit, width)
    second = (4, unit, hidden - FIRST_DOWN * width)
    outs = pl.pallas_call(
        functools.partial(weights_kernel, unit_up, unit),
        in_specs=[SMEM] + [VMEM] * 4,
        out_specs=(pl.BlockSpec(memory_space=pltpu.HBM),) * 5,
        out_shape=(jax.ShapeDtypeStruct(first, BF),) + (jax.ShapeDtypeStruct(second, BF),) * 4,
        scratch_shapes=[pltpu.VMEM(first, BF), pltpu.VMEM((4,) + second, BF), pltpu.SemaphoreType.DMA((5,))],
        compiler_params=PARAMS,
        cost_estimate=pl.CostEstimate(flops=4 * tq * width * hidden, bytes_accessed=14 << 20, transcendentals=0),
        name="weights",
    )(meta, common_a, common_b, sel_a, sel_b)
    return outs[0], outs[1:]


def fold_kernel(meta, first_ref, own, got1, got2, got3, *outs):
    plane, line = meta[4], meta[5]
    for k in range(4):
        at = line ^ k
        total = first_ref[0, at].astype(F32)
        for i in range(1, 4):
            total += first_ref[i, at].astype(F32)
        outs[k][...] = total.astype(BF)
        at = plane ^ k
        total = own[at].astype(F32) + got1[at].astype(F32) + got2[at].astype(F32) + got3[at].astype(F32)
        outs[4 + k][...] = total.astype(BF)


def fold_call(meta, first, second):
    shapes = [jax.ShapeDtypeStruct(first.shape[2:], BF)] * 4 + [jax.ShapeDtypeStruct(second[0].shape[1:], BF)] * 4
    outs = pl.pallas_call(
        fold_kernel,
        in_specs=[SMEM] + [VMEM] * 5,
        out_specs=(VMEM,) * 8,
        out_shape=tuple(shapes),
        compiler_params=ROOMY,
        cost_estimate=TINY,
        name="fold",
    )(meta, first, *second)
    return outs[:4], outs[4:]


def small_places(unit_up, unit):
    sums = [(2, i * unit, unit) for i in range(4)]
    return [(0, 0, unit), (1, 0, unit), (4, 0, unit), (5, 0, unit)] + sums[1:] + [(3, 0, unit_up), sums[0]]


def last_kernel(unit_up, unit, meta, small_ref, *refs):
    columns, first, second, outs = refs[:4], refs[4:8], refs[8:12], refs[12:]
    qkv_ref, up_ref, out_ref, down_ref = outs[:4]
    small_refs, held = outs[4:-1], outs[-1]
    small = jnp.sum(small_ref[...], 0)
    for ref, (row, at, count) in zip(small_refs, small_places(unit_up, unit)):
        ref[...] = small[row : row + 1, at : at + count]
    size = columns[0].shape[0]
    held[...] = jnp.zeros_like(held)
    for i, ref in enumerate(columns):
        at = pl.multiple_of(meta[10 + i] + size // 2, 8)
        held[pl.ds(at, size), :] += ref[...].astype(F32)
    qkv_ref[...] = held[size // 2 : size // 2 + qkv_ref.shape[0], :]
    total = first[0][...].astype(F32)
    for ref in first[1:]:
        total += ref[...].astype(F32)
    up_ref[...] = total[:unit_up]
    out_ref[...] = total[unit_up : unit_up + unit]
    width = total.shape[1]
    for i in range(FIRST_DOWN):
        at = unit_up + (1 + i) * unit
        down_ref[:, i * width : (i + 1) * width] = total[at : at + unit]
    width = FIRST_DOWN * width
    total = second[0][...].astype(F32)
    for ref in second[1:]:
        total += ref[...].astype(F32)
    down_ref[:, width:] = total


def last_call(meta, small, unit_qkv, unit_up, unit, columns, first, second):
    size, width = columns[0].shape
    hidden = FIRST_DOWN * width + second[0].shape[1]
    outs = [(unit_qkv, width), (unit_up, width), (unit, width), (unit, hidden)]
    outs += [(1, count) for _, _, count in small_places(unit_up, unit)]
    return pl.pallas_call(
        functools.partial(last_kernel, unit_up, unit),
        in_specs=[SMEM] + [VMEM] * 13,
        out_specs=(VMEM,) * len(outs),
        out_shape=tuple(jax.ShapeDtypeStruct(s, F32) for s in outs),
        scratch_shapes=[pltpu.VMEM((unit_qkv + size, width), F32)],
        compiler_params=ROOMY,
        cost_estimate=TINY,
        name="last",
    )(meta, small, *columns, *first, *second)


def enter_kernel(tiles_ref, gain, shift, w_ref, query_b, value_b, x_ref, npre_ref, low_s):
    part = pl.program_id(0)

    @pl.when(part == 0)
    def _():
        scaled, normed, _ = near_rows(tiles_ref[...].astype(F32), gain[...], shift[...])
        low_s[...] = scaled.astype(BF)
        npre_ref[...] = normed.astype(BF)

    bias = jnp.where(part == 0, query_b[...], jnp.where(part == 2, value_b[...], 0.0))
    joined = (dot_nn(low_s[...], w_ref[...]) + bias).T
    heads, _, size, tq = x_ref.shape
    x_ref[:, 0] = joined.astype(BF).reshape(heads, size, tq)


def enter_call(heads, tiles, gain, shift, weight, query_b, value_b):
    tq, width = tiles.shape
    size = width // heads
    whole = lambda *shape: pl.BlockSpec(shape, lambda i: (0,) * len(shape))
    vec = whole(1, width)
    return pl.pallas_call(
        enter_kernel,
        grid=(3,),
        in_specs=[whole(tq, width), vec, vec, pl.BlockSpec((width, width), lambda i: (0, i)), vec, vec],
        out_specs=(pl.BlockSpec((heads, 1, size, tq), lambda i: (0, i, 0, 0)), whole(tq, width)),
        out_shape=(jax.ShapeDtypeStruct((heads, 3, size, tq), BF), jax.ShapeDtypeStruct((tq, width), BF)),
        scratch_shapes=[pltpu.VMEM((tq, width), BF)],
        compiler_params=PARAMS,
        name="enter",
    )(tiles, gain, shift, weight, query_b, value_b)


def leave_kernel(tiles_ref, gain, w_ref, jg_ref, res_ref, out_ref, acc):
    part = pl.program_id(0)
    width, tq = acc.shape
    more = dot_nn(w_ref[...], jg_ref[:, 0].reshape(width, tq))

    @pl.when(part == 0)
    def _():
        acc[...] = more

    @pl.when(part == 1)
    def _():
        acc[...] += more

    @pl.when(part == 2)
    def _():
        _, normed, inverse = near_rows(tiles_ref[...].astype(F32), gain[...], gain[...])
        grads = (acc[...] + more).T
        out_ref[...] = (res_ref[...] + back_rows(grads, normed, inverse, gain[...])).astype(BF)


def leave_call(tiles, gain, weight, joined_grad, residual_grad):
    tq, width = tiles.shape
    heads, _, size, _ = joined_grad.shape
    whole = lambda *shape: pl.BlockSpec(shape, lambda i: (0,) * len(shape))
    return pl.pallas_call(
        leave_kernel,
        grid=(3,),
        in_specs=[
            whole(tq, width), whole(1, width), pl.BlockSpec((width, width), lambda i: (0, i)),
            pl.BlockSpec((heads, 1, size, tq), lambda i: (0, i, 0, 0)), whole(tq, width),
        ],
        out_specs=whole(tq, width),
        out_shape=jax.ShapeDtypeStruct((tq, width), BF),
        scratch_shapes=[pltpu.VMEM((width, tq), F32)],
        compiler_params=PARAMS,
        cost_estimate=TINY,
        name="leave",
    )(tiles, gain, weight, joined_grad, residual_grad)


def halo_hits(plan, offs, first, dims):
    wide = max(plan.sel, LANES)
    shape = (plan.tq, wide)
    token, col = iota(shape, 0) + first, iota(shape, 1)
    hit = col < 0
    for branch in plan.branches:
        if branch["extra"]:
            at = col - branch["sel"]
            inside = (at >= 0) & (at < branch["extra"])
            hit |= inside & (token == at * branch["rate"] + offs[branch["level"]])
    return jnp.where(hit, 1.0, 0.0).astype(BF)


def halo_blocks(plan):
    count = plan.halo // plan.tq
    for i in range(count):
        yield 0, plan.blocks - count + i, i * plan.tq
        yield 1, i, i * plan.tq


def static_slot(plan, block):
    return block % plan.groups * plan.members + block // plan.groups


def select_kernel(plan, meta, offsets, x_ref, *outs):
    offs = [offsets[b["level"], meta[1]] for b in plan.branches]
    if plan.paired:
        count = plan.halo // plan.tq
        total = jnp.zeros((2 * plan.size, max(plan.sel, LANES)), F32)
        for i in range(count):
            block = (1 - meta[2]) * (plan.blocks - count) + i
            total += dot_nn(x_ref[plan.slot(block), plan.size :, :], halo_hits(plan, offs, i * plan.tq, None))
        outs[0][...] = total.astype(BF)
        return
    last_ref, first_ref = outs
    total = [jnp.zeros((2 * plan.size, max(plan.sel, LANES)), F32) for _ in range(2)]
    for side, block, first in halo_blocks(plan):
        hits = halo_hits(plan, offs, first, None)
        total[side] += dot_nn(x_ref[static_slot(plan, block), plan.size :, :], hits)
    last_ref[...] = total[0].astype(BF)
    first_ref[...] = total[1].astype(BF)


def select_call(plan, meta, offsets, x):
    shape = jax.ShapeDtypeStruct((2 * plan.size, max(plan.sel, LANES)), BF)
    return pl.pallas_call(
        functools.partial(select_kernel, plan),
        in_specs=[SMEM, SMEM, VMEM],
        out_specs=(VMEM,) * (1 if plan.paired else 2),
        out_shape=(shape,) * (1 if plan.paired else 2),
        compiler_params=ROOMY,
        name="select",
    )(meta, offsets, x)


def to_owners(vector, owner, lane_of, devices):
    count = vector.shape[1]
    held = jnp.where(iota((devices, count), 0) == owner, vector, 0.0)
    hits = jnp.where(iota((count, LANES), 1) == lane_of, 1.0, 0.0)
    return lax.dot_general(
        held, hits, (((1,), (0,)), ((), ())), precision=lax.Precision.HIGHEST, preferred_element_type=F32
    )


def cut(index, unit):
    whole = jnp.floor((index.astype(F32) + 0.5) * (1.0 / unit)).astype(jnp.int32)
    return whole, index - whole * unit


def head_kernel(devices, meta, dx_ref, near_ref, w_ref, gain, shift, sums_ref, up_ref, *rest):
    column_refs, (small_ref, acc, col_s, row_s) = rest[:-4], rest[-4:]
    step, steps = pl.program_id(0), pl.num_programs(0)
    tq = dx_ref.shape[2]
    rows = dx_ref.shape[1]
    per = near_ref.shape[0] // tq
    size = rows // 3
    width = near_ref.shape[1]

    @pl.when(step == 0)
    def _():
        acc[...] = jnp.zeros_like(acc)
        col_s[...] = jnp.zeros_like(col_s)
        row_s[...] = jnp.zeros_like(row_s)

    for i in range(per):
        grads = dx_ref[i]
        acc[...] += dot_nn(grads, near_ref[i * tq : (i + 1) * tq, :])
        col_s[...] += jnp.broadcast_to(jnp.sum(grads.astype(F32), 1, keepdims=True), col_s.shape)
        row_s[...] += dot_nt(jnp.ones((8, tq), BF), grads)

    @pl.when(step == steps - 1)
    def _():
        head = meta[1]
        plain = acc[...]
        weight = plain * gain[...] + col_s[:, :1] * shift[...]
        acc[...] = weight
        for i, ref in enumerate(column_refs):
            at = pl.multiple_of(meta[6 + i] * size, 8)
            ref[...] = acc[pl.ds(at, size), :].astype(BF)
        own = w_ref[...].astype(F32)
        gain_part = jnp.sum(own * plain, 0, keepdims=True)
        shift_part = jnp.sum(own * col_s[:, :1], 0, keepdims=True)
        unit = width // devices
        owner = cut(iota((1, width), 1), unit)[0]
        lane = cut(iota((width, 1), 0), unit)[1]
        small_ref[:, 0, :] = to_owners(gain_part, owner, lane, devices)
        small_ref[:, 1, :] = to_owners(shift_part, owner, lane, devices)
        held = jnp.zeros((devices, LANES), F32)
        for i in range(4):
            held += to_owners(sums_ref[i : i + 1, :], owner, lane + i * unit, devices)
        small_ref[:, 2, :] = held
        hidden = up_ref.shape[1]
        unit_up = hidden // devices
        held = jnp.zeros((devices, LANES), F32)
        for i in range(hidden // width):
            owner_up = cut(iota((1, width), 1) + i * width, unit_up)[0]
            lane_up = cut(iota((width, 1), 0) + i * width, unit_up)[1]
            held += to_owners(up_ref[:, i * width : (i + 1) * width], owner_up, lane_up, devices)
        small_ref[:, 3, :] = held
        line = row_s[0:1, :]
        for i, part in enumerate((0, 2)):
            index = iota((1, rows), 1) - part * size
            inside = (index >= 0) & (index < size)
            owner_h = jnp.where(inside, 2 * head + cut(index, size // 2)[0], -1)
            lane_h = cut(iota((rows, 1), 0), size // 2)[1]
            small_ref[:, 4 + i, :] = to_owners(line, owner_h, lane_h, devices)
        small_ref[:, 6, :] = jnp.zeros((devices, LANES), F32)
        small_ref[:, 7, :] = jnp.zeros((devices, LANES), F32)


def head_call(devices, meta, dx, npre_all, own_w, gain, shift, sums, up_sums):
    blocks, rows, tq = dx.shape
    width = npre_all.shape[1]
    per = blocks // 4
    whole = lambda *shape: pl.BlockSpec(shape, lambda i: (0,) * len(shape))
    return pl.pallas_call(
        functools.partial(head_kernel, devices),
        grid=(4,),
        in_specs=[
            SMEM, pl.BlockSpec((per, rows, tq), lambda i: (i, 0, 0)), pl.BlockSpec((per * tq, width), lambda i: (i, 0)),
            whole(rows, width), whole(1, width), whole(1, width), whole(8, width), whole(1, up_sums.shape[1]),
        ],
        out_specs=(whole(rows // 3, width),) * 4 + (whole(devices, 8, LANES),),
        out_shape=(jax.ShapeDtypeStruct((rows // 3, width), BF),) * 4
        + (jax.ShapeDtypeStruct((devices, 8, LANES), F32),),
        scratch_shapes=[
            pltpu.VMEM((rows, width), F32), pltpu.VMEM((rows, LANES), F32), pltpu.VMEM((8, rows), F32),
        ],
        compiler_params=PARAMS,
        cost_estimate=TINY,
        name="head",
    )(meta, dx, npre_all, own_w, gain, shift, sums, up_sums)


def layer_norm_rows(values, norm_gain, norm_shift):
    row_mean = jnp.mean(values, -1, keepdims=True)
    centred = values - row_mean
    inverse = lax.rsqrt(jnp.mean(centred * centred, -1, keepdims=True) + EPS)
    normed = centred * inverse
    return (normed * norm_gain + norm_shift, normed, inverse)


def norm_back(grad_out, normed, inverse, norm_gain):
    grad_norm = grad_out * norm_gain
    grad_in = inverse * (
        grad_norm
        - jnp.mean(grad_norm, -1, keepdims=True)
        - normed * jnp.mean(grad_norm * normed, -1, keepdims=True)
    )
    return (grad_in, jnp.sum(grad_out * normed, 0), jnp.sum(grad_out, 0))


def swap(values, axes):
    return lax.all_to_all(values, axes, 0, 0, tiled=True)


def scatter_sum(values, orders):
    sizes = {name: lax.axis_size(name) for name in ALL}
    left = list(ALL)
    rows, cols = values.shape[1:]
    for stage, axes in enumerate(orders):
        values = values.reshape([sizes[name] for name in left] + [rows, cols])
        rest = [name for name in left if name not in axes]
        order = [left.index(name) for name in list(axes) + rest]
        values = values.transpose(order + [len(left), len(left) + 1])
        count = math.prod(sizes[name] for name in axes)
        values = values.reshape((count, -1, rows, cols))
        if count > 1:
            values = swap(values, axes)
            values = jnp.sum(values.astype(F32), 0)
            if stage < len(orders) - 1:
                values = values.astype(BF)
        left = rest
    return values.reshape(rows, cols).astype(F32)


def to_neighbours(pieces, count):
    if count == 2:
        return (lax.ppermute(pieces[0], "grp", [(0, 1), (1, 0)]),)
    return (
        lax.ppermute(pieces[0], "grp", [(i, i + 1) for i in range(count - 1)]),
        lax.ppermute(pieces[1], "grp", [(i + 1, i) for i in range(count - 1)]),
    )


def from_neighbours(pieces, count):
    return to_neighbours(pieces[::-1], count)[::-1]


def share_columns(weight_t, sums, width):
    members, size = lax.axis_size(GROUP), weight_t.shape[1]
    head = lax.axis_index(GROUP)
    full = jnp.zeros((3, members) + weight_t.shape[1:], F32)
    full = lax.dynamic_update_slice(full, weight_t[:, None], (0, head, 0, 0))
    full_sums = lax.dynamic_update_slice(jnp.zeros((3, members, size), F32), sums[:, None], (0, head, 0))
    weight = lax.psum_scatter(full.reshape(3 * members * size, width), ALL, scatter_dimension=0, tiled=True)
    sums = lax.psum_scatter(full_sums.reshape(3, members * size), ALL, scatter_dimension=1, tiled=True)
    return weight, sums[0], sums[2]


def body(
    tile_embed,
    slide_lengths,
    head_offsets,
    pre_gain,
    pre_shift,
    qkv_weight,
    query_bias,
    value_bias,
    out_weight,
    out_bias,
    post_gain,
    post_shift,
    up_weight,
    up_bias,
    down_weight,
    down_bias,
    out_grad,
):
    width = qkv_weight.shape[0]
    hidden = up_weight.shape[1]
    heads = head_offsets.shape[1]
    size = width // heads
    tq = tile_embed.shape[1]
    br, groups = lax.axis_size("br"), lax.axis_size("grp")
    members = heads // br
    devices = heads * groups
    plan = Plan(heads, size, head_offsets.shape[0], br, members, tq, devices * tq)
    head = lax.axis_index(GROUP)
    base = lax.axis_index("grp") * plan.tokens
    meta = jnp.stack([base, head, lax.axis_index("grp")]).astype(jnp.int32)

    tiles = tile_embed[0].astype(F32)
    pre_out, normed_pre, inverse_pre = layer_norm_rows(tiles, pre_gain, pre_shift)
    normed_low = pre_out.astype(BF)
    bias_col = jnp.concatenate([query_bias, jnp.zeros_like(query_bias), value_bias], 1).reshape(-1, 1)
    joined_t = (
        lax.dot_general(qkv_weight, normed_low, (((0,), (1,)), ((), ())), preferred_element_type=F32) + bias_col
    ).astype(BF)
    x = joined_t.reshape(3, heads, size, tq).transpose(1, 0, 2, 3).reshape(heads, 3 * size, tq)
    x = swap(x, GROUP)
    normed_all = lax.all_gather(normed_low, GROUP, axis=0, tiled=True)

    halo = to_neighbours(select_call(plan, meta, head_offsets, x), groups)
    state, *own = near_call(plan, meta, slide_lengths, head_offsets, x)
    mixed, state = far_call(plan, meta, slide_lengths, head_offsets, state, own, halo)
    attn_t = swap(mixed, GROUP).reshape(width, tq)

    projected = lax.dot_general(attn_t, out_weight, (((0,), (0,)), ((), ())), preferred_element_type=F32)
    residual = tiles + projected + out_bias
    post_out, normed_post, inverse_post = layer_norm_rows(residual, post_gain, post_shift)
    lifted = post_out.astype(BF)
    gate_in = jnp.dot(lifted, up_weight, preferred_element_type=F32) + up_bias
    act_float, gelu_pull = jax.vjp(lambda v: jax.nn.gelu(v, approximate=False), gate_in)
    act_low = act_float.astype(BF)
    layer_out = (residual + jnp.dot(act_low, down_weight, preferred_element_type=F32) + down_bias).astype(BF)[None]
    grad_low = out_grad[0]
    grad_float = grad_low.astype(F32)
    act_grad = lax.dot_general(grad_low, down_weight, (((1,), (1,)), ((), ())), preferred_element_type=F32)
    gate_grad = gelu_pull(act_grad)[0].astype(BF)
    lifted_grad = lax.dot_general(gate_grad, up_weight, (((1,), (1,)), ((), ())), preferred_element_type=F32)
    norm_part, post_gain_sum, post_shift_sum = norm_back(lifted_grad, normed_post, inverse_post, post_gain)
    residual_grad = grad_float + norm_part
    proj_grad = residual_grad.astype(BF)
    attn_grad_t = lax.dot_general(
        out_weight, proj_grad, (((1,), (1,)), ((), ())), preferred_element_type=F32
    ).astype(BF)
    do = swap(attn_grad_t.reshape(heads, size, tq), GROUP)

    tokens = (((0,), (0,)), ((), ()))
    up_part = lax.dot_general(gate_grad, lifted, tokens, preferred_element_type=F32).astype(BF)
    down_part = lax.dot_general(grad_low, act_low, tokens, preferred_element_type=F32).astype(BF)
    out_part = lax.dot_general(proj_grad, attn_t, (((0,), (1,)), ((), ())), preferred_element_type=F32).astype(BF)
    vectors = [
        jnp.sum(gate_grad.astype(F32), 0).reshape(devices, -1),
        jnp.sum(grad_float, 0).reshape(devices, -1),
        jnp.sum(residual_grad, 0).reshape(devices, -1),
        post_gain_sum.reshape(devices, -1),
        post_shift_sum.reshape(devices, -1),
    ]
    ends = [0]
    for vector in vectors:
        ends.append(ends[-1] + vector.shape[1])
    small = jnp.concatenate(vectors, 1)
    small = jnp.pad(small[:, None, :], ((0, 0), (0, 7), (0, width - small.shape[1]))).astype(BF)
    misc = jnp.concatenate([out_part.reshape(devices, -1, width), small], 1)
    first, second = (("s0",), ("br", "s1"), ("grp", "s2")), (("s0",), ("grp", "s2"), ("br", "s1"))
    up_own = scatter_sum(up_part.reshape(devices, -1, width), first)
    down_own = scatter_sum(down_part.reshape(devices, -1, hidden), second)
    misc_own = scatter_sum(misc, first)
    unit = width // devices
    small_own = misc_own[unit]
    small_own = [small_own[None, ends[i] : ends[i + 1]] for i in range(len(vectors))]

    rows, dq, dk, dv, *sides = far_back_call(plan, meta, slide_lengths, head_offsets, state, do, own, halo)
    back = from_neighbours(sides, groups)
    dx = near_back_call(plan, meta, slide_lengths, head_offsets, x, state, rows, (dq, dk, dv), back)
    joined_grad_t = swap(dx, GROUP).reshape(heads, 3, size, tq).transpose(1, 0, 2, 3).reshape(3 * width, tq)
    weight_t = jnp.einsum(
        "nct,ntd->cd", dx, normed_all.reshape(heads, tq, width), preferred_element_type=F32
    ).reshape(3, size, width)
    head_sums = jnp.sum(dx.astype(F32), (0, 2)).reshape(3, size)
    qkv_own, query_own, value_own = share_columns(weight_t, head_sums, width)
    normed_grad = lax.dot_general(joined_grad_t, qkv_weight, (((0,), (1,)), ((), ())), preferred_element_type=F32)
    tile_part, pre_gain_sum, pre_shift_sum = norm_back(normed_grad, normed_pre, inverse_pre, pre_gain)
    tile_grad = (residual_grad + tile_part).astype(BF)[None]
    last = jnp.stack([pre_gain_sum, pre_shift_sum]).reshape(2, devices, unit).transpose(1, 0, 2)
    last = jnp.pad(last, ((0, 0), (0, 6), (0, LANES - unit)))
    last = jnp.sum(swap(last, ALL).reshape(devices, 8, LANES), 0)
    return (
        layer_out,
        tile_grad,
        last[0:1, :unit],
        last[1:2, :unit],
        qkv_own.T,
        query_own[None],
        value_own[None],
        misc_own[:unit].T,
        small_own[2],
        small_own[3],
        small_own[4],
        up_own.T,
        small_own[0],
        down_own.T,
        small_own[1],
    )


def across(piece, axes, k):
    return lax.ppermute(piece, axes, [(i, i ^ k) for i in range(4)])


def matchings(edges, count):
    edges, found = list(edges), []
    while edges:
        by_source = {}
        for edge in edges:
            by_source.setdefault(edge[0], []).append(edge)
        taken = {}

        def place(source, seen):
            for edge in by_source[source]:
                if edge[1] not in seen:
                    seen.add(edge[1])
                    if edge[1] not in taken or place(taken[edge[1]][0], seen):
                        taken[edge[1]] = edge
                        return True
            return False

        for source in range(count):
            place(source, set())
        found.append(sorted(taken.values()))
        for edge in taken.values():
            edges.remove(edge)
    return found


def column_routes(heads, size, unit):
    sizes = [lax.axis_size(name) for name in ALL]
    inner = sizes[2] * sizes[3] * sizes[4]
    edges = []
    for head in range(heads):
        for grp in range(sizes[1]):
            source = (head // inner * sizes[1] + grp) * inner + head % inner
            for part in range(3):
                start = (part * heads + head) * size
                for owner in sorted({start // unit, (start + size - 1) // unit}):
                    edges.append((source, owner, (part, start - owner * unit)))
    devices = heads * sizes[1]
    for matching in matchings(edges, devices):
        route = [edge[:2] for edge in matching]
        part_of, begin_of = [0] * devices, [0] * devices
        for source, owner, (part, begin) in matching:
            part_of[source], begin_of[owner] = part, begin
        yield route, part_of, begin_of


def fast_body(
    tile_embed, slide_lengths, head_offsets, pre_gain, pre_shift, qkv_weight, query_bias, value_bias, out_weight,
    out_bias, post_gain, post_shift, up_weight, up_bias, down_weight, down_bias, out_grad,
):
    width = qkv_weight.shape[0]
    heads = head_offsets.shape[1]
    size = width // heads
    tq = tile_embed.shape[1]
    br, groups = lax.axis_size("br"), lax.axis_size("grp")
    members = heads // br
    devices = heads * groups
    plan = Plan(heads, size, head_offsets.shape[0], br, members, tq, devices * tq)
    head = lax.axis_index(GROUP)
    group = lax.axis_index("grp")
    core = lax.axis_index("s0")
    meta = [group * plan.tokens, head, group, core, lax.axis_index(("br", "s1")), lax.axis_index(("grp", "s2"))]
    routes = list(column_routes(heads, size, 3 * width // devices))[::-1]
    table = jnp.array([parts for _, parts, _ in routes] + [begins for _, _, begins in routes], jnp.int32)
    meta.extend(lax.dynamic_index_in_dim(table, lax.axis_index(ALL), 1, False))
    meta = jnp.stack(meta).astype(jnp.int32)
    tiles = tile_embed[0]
    own_w = jnp.concatenate(
        [lax.dynamic_slice_in_dim(qkv_weight, part * width + head * size, size, 1) for part in range(3)], 1
    ).T
    pair = [(0, 1), (1, 0)]
    plane, line = ("br", "s1"), ("grp", "s2")

    x, npre = enter_call(heads, tiles, pre_gain, pre_shift, qkv_weight, query_bias, value_bias)
    x = swap(x.reshape(heads, 3 * size, tq), GROUP)
    x, npre, own_w, meta = lax.optimization_barrier((x, npre, own_w, meta))
    halo = to_neighbours(select_call(plan, meta, head_offsets, x), groups)
    state, *own = near_call(plan, meta, slide_lengths, head_offsets, x)
    mixed, state = far_call(plan, meta, slide_lengths, head_offsets, state, own, halo)
    attn_t = swap(mixed, GROUP).reshape(width, tq)
    npre_all = lax.all_gather(npre, GROUP, axis=0, tiled=True)
    layer_out, residual_grad, attn_grad_t, common, sel, sel_give, sums, up_sums = middle_call(
        devices, core[None].astype(jnp.int32), attn_t, tiles, out_weight, out_bias, post_gain, post_shift,
        up_weight, up_bias, down_weight, down_bias, out_grad[0],
    )
    do = swap(attn_grad_t.reshape(heads, size, tq), GROUP)
    common_b = lax.ppermute(common, "s0", pair)
    sel_b = lax.ppermute(sel_give, "s0", pair)
    first, second = weights_call(devices, meta, width, common, common_b, sel, sel_b)
    do, first, second, npre_all = lax.optimization_barrier((do, first, second, npre_all))
    first = swap(first, plane)
    second = [second[0]] + [across(second[k], line, k) for k in (1, 2, 3)]
    rows, dq, dk, dv, *sides = far_back_call(plan, meta, slide_lengths, head_offsets, state, do, own, halo)
    back = from_neighbours(sides, groups)
    dx = near_back_call(plan, meta, slide_lengths, head_offsets, x, state, rows, (dq, dk, dv), back)
    dx, first, second = lax.optimization_barrier((dx, first, second))
    first, second = fold_call(meta, first, second)
    dx, first, second = lax.optimization_barrier((dx, first, second))
    first = [first[0]] + [across(first[k], line, k) for k in (1, 2, 3)]
    joined_grad = swap(dx, GROUP).reshape(heads, 3, size, tq)
    *columns, small = head_call(devices, meta, dx, npre_all, own_w, pre_gain, pre_shift, sums, up_sums)
    *columns, third = lax.optimization_barrier((*columns, second[3]))
    columns = [lax.ppermute(piece, ALL, route) for piece, (route, _, _) in zip(columns, routes)]
    second = [second[0], across(second[1], plane, 1), across(second[2], plane, 2), across(third, plane, 3)]
    joined_grad, small, second = lax.optimization_barrier((joined_grad, small, second))
    small = swap(small, ALL)
    joined_grad, first = lax.optimization_barrier((joined_grad, first))
    tile_grad = leave_call(tiles, pre_gain, qkv_weight, joined_grad, residual_grad)
    unit_up, unit = up_weight.shape[1] // devices, width // devices
    qkv_own, up_own, out_own, down_own, *vectors = last_call(
        meta, small, 3 * unit, unit_up, unit, columns, first, second
    )
    gain_own, shift_own, query_own, value_own, out_b, post_gain_own, post_shift_own, up_b, down_b = vectors
    return (
        layer_out[None], tile_grad[None], gain_own, shift_own, qkv_own.T, query_own, value_own, out_own.T, out_b,
        post_gain_own, post_shift_own, up_own.T, up_b, down_own.T, down_b,
    )


def solution(mesh):
    br, rows = mesh.shape["br"], mesh.shape["rows"]

    def run(*args):
        members = args[2].shape[1] // br
        shape = (br, rows // members, members // 4, 2, 2)
        split = jax.sharding.Mesh(mesh.devices.reshape(shape), ALL)
        tokens = P(("grp", "s2", "s1", "s0"), "br", None)
        owned = P(None, ALL)
        return jax.shard_map(
            fast_body if shape == (2, 2, 2, 2, 2) else body,
            mesh=split,
            in_specs=(tokens,) + (P(),) * 15 + (tokens,),
            out_specs=(tokens, tokens) + (owned,) * 13,
            check_vma=False,
        )(*args)

    return run
```

```python
import functools
import math

import jax
import jax.numpy as jnp
import ml_dtypes
import numpy as np
from jax import lax
from jax.experimental import pallas as pl
from jax.experimental.pallas import tpu as pltpu
from jax.sharding import PartitionSpec as P

SEG_BASE = 1024
DOC_MOST = 2048
LANES = 128
BF = jnp.bfloat16
F32 = jnp.float32
NEG = -1e30
EPS = 1e-05
ALL = ("br", "grp", "s2", "s1", "s0")
GROUP = ("br", "s2", "s1", "s0")
FIRST_DOWN = 2
ONE_LANE = 48
ID_Q = 51
ID_K = 52
TWICE = 53


class Plan:
    def __init__(self, heads, head_size, branches, groups, members, tq, total):
        self.heads, self.size, self.groups, self.members, self.tq = heads, head_size, groups, members, tq
        self.blocks = groups * members
        self.paired = groups * members * tq * 2 == total
        self.tokens = self.blocks * tq
        self.total = total
        self.halo = min(DOC_MOST, self.tokens)
        self.factor = math.log2(math.e) * head_size**-0.5
        self.branches = []
        keys, sel = 0, 0
        for level in range(branches):
            rate = 2**level
            span = min(SEG_BASE * rate, total)
            near = span <= self.tokens
            extra = 0 if near else self.halo // rate
            segs = self.tokens // span if near else 1
            seg_q = self.tokens // rate // segs
            seg_k = seg_q + 2 * extra
            flip = 0
            if level == 1 and near and span == 2 * self.branches[0]["span"]:
                segs, seg_q, seg_k, flip = segs * 2, seg_q // 2, seg_k // 2, 1
            self.branches.append(
                dict(
                    level=level, rate=rate, span=span, near=near, extra=extra, segs=segs,
                    seg_q=seg_q, seg_k=seg_k, tile=min(1024, seg_q), first=keys, sel=sel, flip=flip,
                )
            )
            keys += segs * seg_k
            sel += extra
        self.sel = sel
        self.twice = any(b["flip"] for b in self.branches)
        self.near = [b for b in self.branches if b["near"]]
        self.far = [b for b in self.branches if not b["near"]]
        self.near_keys = sum(b["segs"] * b["seg_k"] for b in self.near)
        self.far_keys, self.own = 0, 0
        for b in self.far:
            b["begin"], b["own"] = self.far_keys, self.own
            self.far_keys += b["seg_k"]
            self.own += b["seg_q"]
        self.widest = max(b["seg_k"] for b in self.branches)

    def slot(self, block):
        return lax.rem(block, self.groups) * self.members + lax.div(block, self.groups)


def dot_nt(a, b):
    return lax.dot_general(a, b, (((1,), (1,)), ((), ())), preferred_element_type=F32)


def dot_tn(a, b):
    return lax.dot_general(a, b, (((0,), (0,)), ((), ())), preferred_element_type=F32)


def dot_nn(a, b):
    return lax.dot_general(a, b, (((1,), (0,)), ((), ())), preferred_element_type=F32)


def iota(shape, dim):
    return lax.broadcasted_iota(jnp.int32, shape, dim)


def placement(size, parts):
    shape = (parts * size + 16, parts * LANES)
    row, col = iota(shape, 0), iota(shape, 1)
    hit = col < 0
    for part in range(parts):
        hit |= (row >= part * size) & (row < (part + 1) * size) & (col == row - part * size + part * LANES)
    return row, col, hit


def ids_of(pos, starts, gate=None):
    found = jnp.zeros(pos.shape, jnp.int32)
    for start in starts:
        found += jnp.where(pos >= start, 1, 0)
    if gate is not None:
        found = jnp.where(gate, found, -1)
    return found.astype(F32)


def slide_starts(lens_ref):
    starts, at = [], jnp.int32(0)
    for i in range(lens_ref.shape[0]):
        starts.append(at)
        at = at + lens_ref[i]
    return starts


def branch_pos(plan, branch, base, off, first, count):
    start = base - branch["extra"] * branch["rate"] + off
    pos = start + branch["rate"] * (first + iota((1, count), 1))
    if branch["near"]:
        return pos, None
    shift = int(math.log2(branch["span"]))
    return pos, lax.shift_right_arithmetic(pos, shift) == lax.shift_right_arithmetic(base, shift)


def plain_keys(rows):
    lane = iota(rows.shape, 1)
    return jnp.where((lane >= TWICE) & (lane < TWICE + 3), 0.0, rows)


def to_rows(plan, base, offs, starts, x_ref, q_tm, k_tm, v_tm, extra_q=None):
    size, tq = plan.size, plan.tq
    row, col, hit = placement(size, 3)
    hit |= (row == 3 * size) & ((col == ID_Q) | (col == LANES + ID_K))
    place = jnp.where(hit, 1.0, 0.0).astype(BF)
    lane = iota((1, 3 * LANES), 1)
    in_k, in_v = lane - LANES, lane - 2 * LANES
    ones = jnp.where(
        ((in_k >= ONE_LANE) & (in_k < ONE_LANE + 3)) | ((in_v >= ONE_LANE) & (in_v < ONE_LANE + 3)), 1.0, 0.0
    )

    more = jnp.zeros((1, LANES), F32)
    rest = 1.0 / plan.factor
    for i in range(3 if plan.twice else 0):
        term = float(np.float32(rest).astype(ml_dtypes.bfloat16))
        more = jnp.where(lane[:, :LANES] == TWICE + i, term, more)
        rest -= term
    own = iota((1, LANES), 1)
    both = jnp.where((own >= TWICE) & (own < TWICE + 3), 1.0, 0.0)

    def block(n, carry):
        pos = base + n * tq + iota((1, tq), 1)
        ids = jnp.where(iota((16, tq), 0) == 0, ids_of(pos, starts), 0.0).astype(BF)
        full = jnp.concatenate([x_ref[plan.slot(n)], ids], 0)
        rows = dot_tn(full, place) + ones
        at = pl.ds(pl.multiple_of(n * tq, tq), tq)
        queries = rows[:, :LANES]
        if extra_q is not None:
            queries = queries + extra_q(n, at)
        keys = rows[:, LANES : 2 * LANES]
        if plan.twice:
            member = (iota((tq, 1), 0) & 1) == offs[1]
            queries = jnp.where(member, queries + more, queries)
            keys = jnp.where(member, keys + both, keys)
        q_tm[at, :] = queries
        k_tm[at, :] = keys
        v_tm[at, :] = rows[:, 2 * LANES :]
        if extra_q is not None:
            return carry
        squares = [jnp.square(full[i * size : (i + 1) * size].astype(F32)) for i in range(2)]
        return tuple(jnp.maximum(a, jnp.sum(b, 0, keepdims=True)) for a, b in zip(carry, squares))

    start = (jnp.zeros((1, tq), F32),) * 2 if extra_q is None else 0
    most = lax.fori_loop(0, plan.blocks, block, start, unroll=4)
    if extra_q is None:
        return jnp.sqrt(jnp.max(most[0], 1, keepdims=True) * jnp.max(most[1], 1, keepdims=True)) * 1.0001
    return None


def gather_near(plan, offs, k_tm, v_tm, kall, vall, branches):
    for branch in branches:
        rate, first, off = branch["rate"], branch["first"], offs[branch["level"]]
        count = plan.tokens // rate
        step = min(256, count)

        def chunk(i, carry, rate=rate, first=first, off=off, step=step):
            keys = k_tm[pl.ds(off + i * step * rate, step, stride=rate) if rate > 1 else pl.ds(i * step, step), :]
            rows = pl.ds(off + i * step * rate, step, stride=rate) if rate > 1 else pl.ds(i * step, step)
            to = pl.ds(pl.multiple_of(first + i * step, step), step)
            kall[to, :] = (plain_keys(keys) if rate > 1 else keys).astype(BF)
            vall[to, :] = v_tm[rows, :].astype(BF)
            return carry

        lax.fori_loop(0, count // step, chunk, 0, unroll=min(4, count // step))


def far_keys(plan, base, offs, starts, halos, k_far, v_far, kall, vall):
    size = plan.size
    row, col, hit = placement(size, 2)
    hit |= (row == 2 * size) & (col == ID_K)
    place = jnp.where(hit, 1.0, 0.0).astype(BF)
    lane = iota((1, 2 * LANES), 1)
    in_v = lane - LANES
    ones = jnp.where(
        ((lane >= ONE_LANE) & (lane < ONE_LANE + 3)) | ((in_v >= ONE_LANE) & (in_v < ONE_LANE + 3)), 1.0, 0.0
    )
    for branch in plan.far:
        extra, first, own, count = branch["extra"], branch["begin"], branch["own"], branch["seg_q"]
        kall[first + extra : first + extra + count, :] = k_far[own : own + count, :]
        vall[first + extra : first + extra + count, :] = v_far[own : own + count, :]
        for side, ref in enumerate((halos[0], halos[-1])):
            begin = side * (extra + count)
            pos, gate = branch_pos(plan, branch, base, offs[branch["level"]], begin, extra)
            ids = jnp.where(iota((16, extra), 0) == 0, ids_of(pos, starts, gate), 0.0).astype(BF)
            piece = ref[:, branch["sel"] : branch["sel"] + extra]
            rows = dot_tn(jnp.concatenate([piece, ids], 0), place) + ones
            kall[first + begin : first + begin + extra, :] = rows[:, :LANES].astype(BF)
            vall[first + begin : first + begin + extra, :] = rows[:, LANES:].astype(BF)


def picked(branch, off, i):
    tile, rate = branch["tile"], branch["rate"]
    if rate == 1:
        return pl.ds(pl.multiple_of(i * tile, tile), tile)
    return pl.ds(off + i * tile * rate, tile, stride=rate)


def pieces_of(wide, most):
    step = next(n for n in (most, 512, 256, 128) if wide % n == 0)
    return [(at, step) for at in range(0, wide, step)]


def split3(column, lane):
    high = column.astype(BF).astype(F32)
    rest = column - high
    mid = rest.astype(BF).astype(F32)
    low = rest - mid
    return jnp.where(
        lane == ONE_LANE, high, jnp.where(lane == ONE_LANE + 1, mid, jnp.where(lane == ONE_LANE + 2, low, 0.0))
    )


def near_kernel(plan, meta, lens, offsets, x_ref, st_ref, qf_ref, kf_ref, vf_ref, q_tm, k_tm, v_tm, kall, vall, kid):
    base, head = meta[0], meta[1]
    starts = slide_starts(lens)
    offs = [offsets[b["level"], head] for b in plan.branches]
    top = to_rows(plan, base, offs, starts, x_ref, q_tm, k_tm, v_tm)
    gather_near(plan, offs, k_tm, v_tm, kall, vall, plan.near)
    for branch in plan.far:
        rows = pl.ds(offs[branch["level"]], branch["seg_q"], stride=branch["rate"])
        own = slice(branch["own"], branch["own"] + branch["seg_q"])
        qf_ref[own, :] = q_tm[rows, :].astype(BF)
        kf_ref[own, :] = plain_keys(k_tm[rows, :]).astype(BF)
        vf_ref[own, :] = v_tm[rows, :].astype(BF)
    for branch in plan.near:
        first, total = branch["first"], branch["segs"] * branch["seg_k"]
        pos, gate = branch_pos(plan, branch, base, offs[branch["level"]], 0, total)
        kid[:, first : first + total] = ids_of(pos, starts, gate)
    factor = plan.factor
    lane = iota((1, LANES), 1)

    def scan(visit):
        for branch in plan.near:
            per = branch["seg_q"] // branch["tile"]

            def tile(i, carry, branch=branch, per=per):
                rows = picked(branch, offs[branch["level"]], i)
                at = pl.multiple_of(branch["first"] + (lax.div(i, per) ^ branch["flip"]) * branch["seg_k"], 128)
                visit(branch, rows, q_tm[rows, :], at)
                return carry

            lax.fori_loop(0, branch["segs"] * per, tile, 0, unroll=4 if branch["flip"] else min(2, branch["segs"] * per))

    def attend(top_lanes):
        def visit(branch, rows, queries, at):
            ids = queries[:, ID_Q : ID_Q + 1]
            low = (queries + top_lanes).astype(BF)
            mixed = None
            for begin, step in pieces_of(branch["seg_k"], 1024):
                to = pl.ds(at + begin, step)
                weights = jnp.exp2(dot_nt(low, kall[to, :]) * factor)
                weights = jnp.where(ids == kid[:, to], weights, 0.0).astype(BF)
                more = dot_nn(weights, vall[to, :])
                mixed = more if mixed is None else mixed + more
            if branch["level"]:
                mixed = st_ref[rows, :] + mixed
            st_ref[rows, :] = mixed

        scan(visit)

    attend(split3(-top, lane))
    step = min(512, plan.tokens)

    def least(n, low):
        at = pl.ds(pl.multiple_of(n * step, step), step)
        state = st_ref[at, :]
        st_ref[at, :] = jnp.where(iota((step, LANES), 1) == ID_Q, top, state)
        return jnp.minimum(low, jnp.min(state, 0, keepdims=True))

    weight = lax.fori_loop(0, plan.tokens // step, least, jnp.full((1, LANES), jnp.inf, F32), unroll=2)
    weight = jnp.min(jnp.where(lane == ONE_LANE, weight, jnp.inf))

    @pl.when(jnp.logical_not(weight > 2.0**-60))
    def _():
        def clear(n, carry):
            st_ref[pl.ds(pl.multiple_of(n * step, step), step), :] = jnp.full((step, LANES), NEG, F32)
            return carry

        def largest(branch, rows, queries, at):
            low = queries.astype(BF)
            best = st_ref[rows, :]
            for begin, step in pieces_of(branch["seg_k"], 256):
                to = pl.ds(at + begin, step)
                scores = jnp.where(queries[:, ID_Q : ID_Q + 1] == kid[:, to], dot_nt(low, kall[to, :]), NEG)
                best = jnp.maximum(best, jnp.max(scores, 1, keepdims=True))
            st_ref[rows, :] = best

        def settle(n, carry):
            at = pl.ds(pl.multiple_of(n * step, step), step)
            own = st_ref[at, :]
            tops[at, :] = own
            wide = iota((step, LANES), 1)
            q_tm[at, :] = q_tm[at, :] + split3(-own, wide)
            return carry

        def restore(n, carry):
            at = pl.ds(pl.multiple_of(n * step, step), step)
            st_ref[at, :] = jnp.where(iota((step, LANES), 1) == ID_Q, tops[at, :], st_ref[at, :])
            return carry

        tops = k_tm
        lax.fori_loop(0, plan.tokens // step, clear, 0)
        scan(largest)
        lax.fori_loop(0, plan.tokens // step, settle, 0)
        attend(jnp.zeros((1, LANES), F32))
        lax.fori_loop(0, plan.tokens // step, restore, 0)


def far_kernel(plan, meta, lens, offsets, st_in, qf_ref, kf_ref, vf_ref, *rest):
    halos, (o_ref, st_ref, kall, vall) = rest[:-4], rest[-4:]
    base, head = meta[0], meta[1]
    starts = slide_starts(lens)
    offs = [offsets[b["level"], head] for b in plan.branches]
    factor = plan.factor
    step = min(512, plan.tokens)

    def carry_over(n, carry):
        at = pl.ds(pl.multiple_of(n * step, step), step)
        st_ref[at, :] = st_in[at, :]
        return carry

    lax.fori_loop(0, plan.tokens // step, carry_over, 0, unroll=2)
    if plan.far:
        far_keys(plan, base, offs, starts, halos, kf_ref, vf_ref, kall, vall)
    for branch in plan.far:
        off, tile, wide = offs[branch["level"]], branch["tile"], branch["seg_k"]
        pos, gate = branch_pos(plan, branch, base, off, 0, wide)
        ids = ids_of(pos, starts, gate)
        keys = kall[branch["begin"] : branch["begin"] + wide, :]
        values = vall[branch["begin"] : branch["begin"] + wide, :]
        for i in range(branch["seg_q"] // tile):
            own = branch["own"] + i * tile
            queries = qf_ref[own : own + tile, :]
            rows = picked(branch, off, i)
            scores = dot_nt(queries, keys)
            scores = jnp.where(queries[:, ID_Q : ID_Q + 1].astype(F32) == ids, scores, NEG)
            top = jnp.max(scores, 1, keepdims=True)
            mixed = dot_nn(jnp.exp2((scores - top) * factor).astype(BF), values)
            old = st_ref[rows, :]
            old_top = old[:, ID_Q : ID_Q + 1]
            new_top = jnp.maximum(old_top, top)
            mixed = old * jnp.exp2((old_top - new_top) * factor) + mixed * jnp.exp2((top - new_top) * factor)
            st_ref[rows, :] = jnp.where(iota((tile, LANES), 1) == ID_Q, new_top, mixed)
    eye = jnp.where(iota((plan.size, LANES), 0) == iota((plan.size, LANES), 1), 1.0, 0.0).astype(BF)

    def finish(n, carry):
        at = pl.ds(pl.multiple_of(n * plan.tq, plan.tq), plan.tq)
        state = st_ref[at, :]
        weight = state[:, ONE_LANE : ONE_LANE + 1]
        top = state[:, ID_Q : ID_Q + 1]
        attn = state * (1.0 / weight)
        merged = top + jnp.log2(weight) * (1.0 / factor)
        lane = iota((plan.tq, LANES), 1)
        st_ref[at, :] = jnp.where(lane < plan.size, attn, jnp.where(lane == ONE_LANE, merged, 0.0))
        o_ref[plan.slot(n)] = dot_nt(eye, attn.astype(BF)).astype(BF)
        return carry

    lax.fori_loop(0, plan.blocks, finish, 0, unroll=4)


def back_tile(plan, branch, queries, grads, keys_at, kall, vall, k_fm, linked, dk_acc, dv_acc):
    dq = None
    for begin, step in pieces_of(branch["seg_k"], 256):
        to = pl.ds(keys_at + begin, step)
        part = slice(begin, begin + step)
        keys = kall[to, :]
        probs = jnp.where(linked(keys), jnp.exp2(dot_nt(keys, queries) * plan.factor), 0.0)
        dv_acc[part, :] += dot_nn(probs.astype(BF), grads)
        moved = (probs * dot_nt(vall[to, :], grads)).astype(BF)
        dk_acc[part, :] += dot_nn(moved, queries)
        more = dot_nn(k_fm[:, part], moved)
        dq = more if dq is None else dq + more
    return dq


def far_back_kernel(
    plan, meta, lens, offsets, st_ref, do_ref, qf_ref, kf_ref, vf_ref, *rest,
):
    sides = 1 if plan.paired else 2
    halos, (do_tm, dqf_ref, dkf_ref, dvf_ref), rest = rest[:sides], rest[sides : sides + 4], rest[sides + 4 :]
    halo_outs, (kall, vall, k_fm, dk_acc, dv_acc) = rest[:sides], rest[sides:]
    base, head = meta[0], meta[1]
    starts = slide_starts(lens)
    offs = [offsets[b["level"], head] for b in plan.branches]
    size, tq = plan.size, plan.tq
    row, col, hit = placement(size, 1)
    place = jnp.where(hit, 1.0, 0.0).astype(BF)
    lane = iota((tq, LANES), 1)

    def block(n, carry):
        at = pl.ds(pl.multiple_of(n * tq, tq), tq)
        grads = dot_tn(jnp.concatenate([do_ref[plan.slot(n)], jnp.zeros((16, tq), BF)], 0), place)
        dots = jnp.sum(jnp.where(lane < size, grads * st_ref[at, :], 0.0), 1, keepdims=True)
        do_tm[at, :] = grads + split3(-dots, lane)
        return carry

    lax.fori_loop(0, plan.blocks, block, 0, unroll=4)
    if plan.far:
        far_keys(plan, base, offs, starts, halos, kf_ref, vf_ref, kall, vall)
    eye = jnp.where(iota((LANES, LANES), 0) == iota((LANES, LANES), 1), 1.0, 0.0).astype(BF)
    for branch in plan.far:
        off, tile, wide, begin = offs[branch["level"]], branch["tile"], branch["seg_k"], branch["begin"]
        k_fm[:, :wide] = dot_nt(eye, kall[begin : begin + wide, :]).astype(BF)
        dk_acc[:wide, :] = jnp.zeros((wide, LANES), F32)
        dv_acc[:wide, :] = jnp.zeros((wide, LANES), F32)
        extra, count = branch["extra"], branch["seg_q"]
        for i in range(count // tile):
            own = branch["own"] + i * tile
            rows = picked(branch, off, i)
            wide_lane = iota((tile, LANES), 1)
            merged = st_ref[rows, :][:, ONE_LANE : ONE_LANE + 1]
            queries = jnp.where(wide_lane == ID_Q, 0.0, qf_ref[own : own + tile, :].astype(F32))
            queries = (queries + split3(-merged, wide_lane)).astype(BF)
            grads = do_tm[rows, :].astype(BF)
            pos, _ = branch_pos(plan, branch, base, off, extra + i * tile, tile)
            ids = ids_of(pos, starts)
            linked = lambda keys: keys[:, ID_K : ID_K + 1].astype(F32) == ids
            dq = back_tile(plan, branch, queries, grads, begin, kall, vall, k_fm, linked, dk_acc, dv_acc)
            dqf_ref[own : own + tile, :] = dq.T
        own = slice(branch["own"], branch["own"] + count)
        dkf_ref[own, :] = dk_acc[extra : extra + count, :]
        dvf_ref[own, :] = dv_acc[extra : extra + count, :]
        for side, ref in enumerate(halo_outs):
            at = side * (extra + count)
            if plan.paired:
                at = pl.multiple_of((1 - meta[2]) * (extra + count), 128)
            to = slice(branch["sel"], branch["sel"] + extra)
            dk = (dk_acc[pl.ds(at, extra), :] * size**-0.5).astype(BF)
            ref[:size, to] = dot_nt(eye[:size], dk).astype(BF)
            ref[size:, to] = dot_nt(eye[:size], dv_acc[pl.ds(at, extra), :].astype(BF)).astype(BF)


def near_back_kernel(
    plan, meta, lens, offsets, x_ref, st_ref, do_tm, dqf_ref, dkf_ref, dvf_ref, *rest,
):
    backs, (dx_ref, q_tm, k_tm, v_tm, dq_tm, dk_tm, dv_tm, kall, vall, k_fm, qid, dk_acc, dv_acc) = rest[:-13], rest[-13:]
    base, head = meta[0], meta[1]
    starts = slide_starts(lens)
    offs = [offsets[b["level"], head] for b in plan.branches]
    size, tq = plan.size, plan.tq
    lane = iota((tq, LANES), 1)
    to_rows(
        plan, base, offs, starts, x_ref, q_tm, k_tm, v_tm,
        lambda n, at: split3(-st_ref[at, :][:, ONE_LANE : ONE_LANE + 1], lane),
    )
    gather_near(plan, offs, k_tm, v_tm, kall, vall, plan.near)
    eye = jnp.where(iota((LANES, LANES), 0) == iota((LANES, LANES), 1), 1.0, 0.0).astype(BF)
    for branch in plan.near:
        off, first, wide, tile = offs[branch["level"]], branch["first"], branch["seg_k"], branch["tile"]
        count = branch["segs"] * branch["seg_q"]
        per = branch["seg_q"] // tile
        pos, _ = branch_pos(plan, branch, base, off, 0, count)
        qid[:, :count] = ids_of(pos, starts)

        def segment(seg, carry, branch=branch, off=off, first=first, wide=wide, tile=tile, per=per):
            key_seg = seg ^ branch["flip"]
            keys_at = pl.multiple_of(first + key_seg * wide, 128)
            k_fm[:, :wide] = dot_nt(eye, kall[pl.ds(keys_at, wide), :]).astype(BF)
            dk_acc[:wide, :] = jnp.zeros((wide, LANES), F32)
            dv_acc[:wide, :] = jnp.zeros((wide, LANES), F32)

            def one(j, carry):
                i = seg * per + j
                rows = picked(branch, off, i)
                queries = q_tm[rows, :].astype(BF)
                grads = do_tm[rows, :].astype(BF)
                ids = qid[:, pl.ds(pl.multiple_of(i * tile, tile), tile)]
                linked = lambda keys: keys[:, ID_K : ID_K + 1].astype(F32) == ids
                dq = back_tile(plan, branch, queries, grads, keys_at, kall, vall, k_fm, linked, dk_acc, dv_acc).T
                if branch["level"]:
                    dq = dq_tm[rows, :] + dq
                dq_tm[rows, :] = dq
                return carry

            lax.fori_loop(0, per, one, 0)
            step = min(256, branch["seg_q"])
            for c in range(branch["seg_q"] // step):
                begin = c * step
                if branch["rate"] == 1:
                    to = pl.ds(pl.multiple_of(key_seg * branch["seg_q"] + begin, step), step)
                    dk_tm[to, :] = dk_acc[begin : begin + step, :]
                    dv_tm[to, :] = dv_acc[begin : begin + step, :]
                else:
                    to = pl.ds(off + (key_seg * branch["seg_q"] + begin) * branch["rate"], step, stride=branch["rate"])
                    dk_tm[to, :] += dk_acc[begin : begin + step, :]
                    dv_tm[to, :] += dv_acc[begin : begin + step, :]
            return carry

        lax.fori_loop(0, branch["segs"], segment, 0, unroll=2 if branch["segs"] > 1 else 1)
    row, col, hit = placement(size, 2)
    place = jnp.where(hit, 1.0, 0.0).astype(BF)[: 2 * size]
    for branch in plan.far:
        off, rate, extra, count = offs[branch["level"]], branch["rate"], branch["extra"], branch["seg_q"]
        rows = pl.ds(off, count, stride=rate)
        own = slice(branch["own"], branch["own"] + count)
        for total, part in ((dq_tm, dqf_ref), (dk_tm, dkf_ref), (dv_tm, dvf_ref)):
            total[rows, :] += part[own, :]
        begins = [plan.tokens - plan.halo, 0]
        if plan.paired:
            begins = [(1 - meta[2]) * (plan.tokens - plan.halo)]
        for begin, ref in zip(begins, backs):
            more = dot_tn(ref[:, branch["sel"] : branch["sel"] + extra], place)
            rows = pl.ds(begin + off, extra, stride=rate)
            dk_tm[rows, :] += more[:, :LANES] * size**0.5
            dv_tm[rows, :] += more[:, LANES:]
    small_eye = eye[:size]

    def finish(n, carry):
        at = pl.ds(pl.multiple_of(n * tq, tq), tq)
        slot = plan.slot(n)
        dx_ref[slot, :size, :] = dot_nt(small_eye, (dq_tm[at, :] * size**-0.5).astype(BF)).astype(BF)
        dx_ref[slot, size : 2 * size, :] = dot_nt(small_eye, (dk_tm[at, :] * size**-0.5).astype(BF)).astype(BF)
        dx_ref[slot, 2 * size :, :] = dot_nt(small_eye, dv_tm[at, :].astype(BF)).astype(BF)
        return carry

    lax.fori_loop(0, plan.blocks, finish, 0, unroll=4)


SMEM = pl.BlockSpec(memory_space=pltpu.SMEM)
VMEM = pl.BlockSpec(memory_space=pltpu.VMEM)
TINY = pl.CostEstimate(flops=1000, bytes_accessed=1000, transcendentals=0)
PARAMS = pltpu.CompilerParams(vmem_limit_bytes=60 << 20)
ROOMY = pltpu.CompilerParams(vmem_limit_bytes=40 << 20)


def struct(shape, kind):
    return jax.ShapeDtypeStruct(shape, kind)


def kernel_call(name, kernel, ins, outs, scratch, flops):
    return pl.pallas_call(
        kernel,
        out_shape=tuple(struct(*out) for out in outs),
        in_specs=[SMEM] * 3 + [VMEM] * (len(ins) - 3),
        out_specs=(VMEM,) * len(outs),
        scratch_shapes=[pltpu.VMEM(*s) for s in scratch],
        compiler_params=ROOMY,
        cost_estimate=pl.CostEstimate(flops=flops, bytes_accessed=1000, transcendentals=0),
        name=name,
    )(*ins)


def near_call(plan, meta, lens, offsets, x):
    rows, keys = ((plan.tokens, LANES), F32), ((plan.near_keys, LANES), BF)
    own = ((plan.own, LANES), BF)
    return kernel_call(
        "near", functools.partial(near_kernel, plan), (meta, lens, offsets, x), (rows, own, own, own),
        (rows, rows, rows, keys, keys, ((1, plan.near_keys), F32)), 20_000_000_000,
    )


def far_call(plan, meta, lens, offsets, state, own, halo):
    keys = ((plan.far_keys, LANES), BF)
    return kernel_call(
        "far", functools.partial(far_kernel, plan), (meta, lens, offsets, state, *own, *halo),
        (((plan.blocks, plan.size, plan.tq), BF), ((plan.tokens, LANES), F32)), (keys, keys), 4_000_000_000,
    )


def far_back_call(plan, meta, lens, offsets, state, do, own, halo):
    keys = ((plan.far_keys, LANES), BF)
    part, side = ((plan.own, LANES), F32), ((2 * plan.size, max(plan.sel, LANES)), BF)
    acc = ((plan.widest, LANES), F32)
    return kernel_call(
        "far_back", functools.partial(far_back_kernel, plan), (meta, lens, offsets, state, do, *own, *halo),
        (((plan.tokens, LANES), F32), part, part, part) + (side,) * (1 if plan.paired else 2),
        (keys, keys, ((LANES, plan.widest), BF), acc, acc), 4_000_000_000,
    )


def near_back_call(plan, meta, lens, offsets, x, state, do_rows, parts, back):
    rows, keys = ((plan.tokens, LANES), F32), ((plan.near_keys, LANES), BF)
    acc = ((plan.widest, LANES), F32)
    return kernel_call(
        "near_back", functools.partial(near_back_kernel, plan),
        (meta, lens, offsets, x, state, do_rows, *parts, *back),
        (((plan.blocks, 3 * plan.size, plan.tq), BF),),
        (rows,) * 6 + (keys, keys, ((LANES, plan.widest), BF), ((1, plan.tokens), F32), acc, acc), 8_000_000_000,
    )[0]


def near_rows(values, norm_gain, norm_shift):
    centred = values - jnp.mean(values, 1, keepdims=True)
    inverse = lax.rsqrt(jnp.mean(centred * centred, 1, keepdims=True) + EPS)
    normed = centred * inverse
    return normed * norm_gain + norm_shift, normed, inverse


def back_rows(grad_out, normed, inverse, norm_gain):
    grad_norm = grad_out * norm_gain
    return inverse * (
        grad_norm
        - jnp.mean(grad_norm, 1, keepdims=True)
        - normed * jnp.mean(grad_norm * normed, 1, keepdims=True)
    )


def own_columns(size, unit, core):
    row, col = iota((size, size), 0), iota((size, size), 1)
    half = size // 2
    other = row >= half
    place = jnp.where(other, row - half, row)
    whole = jnp.floor((place.astype(F32) + 0.5) * (1.0 / unit)).astype(jnp.int32)
    parity = jnp.where(other, 1 - core, core)
    return jnp.where(col == place + unit * (whole + parity), 1.0, 0.0).astype(BF)


def middle_kernel(
    unit_up, unit, core_ref, attn_ref, tiles_ref, out_w, out_b, gain, shift, up_w, up_b, down_w, down_b, g_ref,
    y_ref, res_ref, ag_ref, common_ref, mine_ref, theirs_ref, sums_ref, up_sum_ref,
    pick_up, normed_s, lifted_s, inverse_s, out_s, back_s,
):
    step, steps = pl.program_id(0), pl.num_programs(0)
    width = tiles_ref.shape[1]
    chunk = up_w.shape[1]
    half = chunk // 2
    core = core_ref[0]
    hidden_sel = steps * half

    @pl.when(step == 0)
    def _():
        pick_up[...] = own_columns(chunk, unit_up, core)
        residual = tiles_ref[...].astype(F32) + dot_tn(attn_ref[...], out_w[...]) + out_b[...]
        lifted, normed, inverse = near_rows(residual, gain[...], shift[...])
        low = lifted.astype(BF)
        lifted_s[...] = low
        normed_s[...] = normed
        inverse_s[...] = jnp.broadcast_to(inverse, inverse_s.shape)
        out_s[...] = residual + down_b[...]
        back_s[...] = jnp.zeros_like(back_s)
        common_ref[pl.ds(steps * chunk, width), :] = low.T
        common_ref[pl.ds(steps * chunk + width, width), :] = attn_ref[...]
        pick = own_columns(width, unit, core)
        picked_g = dot_nt(pick, g_ref[...]).astype(BF)
        mine_ref[pl.ds(hidden_sel, width // 2), :] = picked_g[: width // 2]
        theirs_ref[pl.ds(hidden_sel, width // 2), :] = picked_g[width // 2 :]

    lifted = lifted_s[...]
    gate_in = dot_nn(lifted, up_w[...]) + up_b[...]
    cdf = 0.5 + 0.5 * lax.erf(gate_in * (0.5**0.5))
    act = (gate_in * cdf).astype(BF)
    slope = cdf + gate_in * (jnp.exp(-0.5 * gate_in * gate_in) * (1.0 / math.sqrt(2.0 * math.pi)))
    gate_grad = (dot_nt(g_ref[...], down_w[...]) * slope).astype(BF)
    out_s[...] += dot_nn(act, down_w[...])
    back_s[...] += dot_nt(gate_grad, up_w[...])
    up_sum_ref[...] = jnp.sum(gate_grad.astype(F32), 0, keepdims=True)
    common_ref[pl.ds(pl.multiple_of(step * chunk, chunk), chunk), :] = act.T
    picked_gate = dot_nt(pick_up[...], gate_grad).astype(BF)
    at = pl.ds(pl.multiple_of(step * half, half), half)
    mine_ref[at, :] = picked_gate[:half]
    theirs_ref[at, :] = picked_gate[half:]

    @pl.when(step == steps - 1)
    def _():
        y_ref[...] = out_s[...].astype(BF)
        grads = g_ref[...].astype(F32)
        lifted_grad = back_s[...]
        normed = normed_s[...]
        residual_grad = grads + back_rows(lifted_grad, normed, inverse_s[:, :1], gain[...])
        res_ref[...] = residual_grad
        low = residual_grad.astype(BF)
        ag_ref[...] = dot_nt(out_w[...], low).astype(BF)
        pick = own_columns(width, unit, core)
        picked_p = dot_nt(pick, low).astype(BF)
        at = pl.ds(hidden_sel + width // 2, width // 2)
        mine_ref[at, :] = picked_p[: width // 2]
        theirs_ref[at, :] = picked_p[width // 2 :]
        sums_ref[0:1, :] = jnp.sum(grads, 0, keepdims=True)
        sums_ref[1:2, :] = jnp.sum(residual_grad, 0, keepdims=True)
        sums_ref[2:3, :] = jnp.sum(lifted_grad * normed, 0, keepdims=True)
        sums_ref[3:4, :] = jnp.sum(lifted_grad, 0, keepdims=True)
        sums_ref[4:8, :] = jnp.zeros((4, width), F32)


def middle_call(devices, core, attn_t, tiles, out_w, out_b, gain, shift, up_w, up_b, down_w, down_b, g):
    tq, width = tiles.shape
    hidden = up_w.shape[1]
    steps = hidden // width
    whole = lambda *shape: pl.BlockSpec(shape, lambda j: (0,) * len(shape))
    vec = whole(1, width)
    sel = hidden // 2 + width
    return pl.pallas_call(
        functools.partial(middle_kernel, hidden // devices, width // devices),
        grid=(steps,),
        in_specs=[
            SMEM, whole(width, tq), whole(tq, width), whole(width, width), vec, vec, vec,
            pl.BlockSpec((width, width), lambda j: (0, j)), pl.BlockSpec((1, width), lambda j: (0, j)),
            pl.BlockSpec((width, width), lambda j: (j, 0)), vec, whole(tq, width),
        ],
        out_specs=(
            whole(tq, width), whole(tq, width), whole(width, tq), whole(hidden + 2 * width, tq), whole(sel, tq),
            whole(sel, tq), whole(8, width), pl.BlockSpec((1, width), lambda j: (0, j)),
        ),
        out_shape=(
            jax.ShapeDtypeStruct((tq, width), BF),
            pltpu.HBM((tq, width), F32),
            jax.ShapeDtypeStruct((width, tq), BF),
            pltpu.HBM((hidden + 2 * width, tq), BF),
            pltpu.HBM((sel, tq), BF),
            pltpu.HBM((sel, tq), BF),
            pltpu.HBM((8, width), F32),
            pltpu.HBM((1, hidden), F32),
        ),
        scratch_shapes=[
            pltpu.VMEM((width, width), BF), pltpu.VMEM((tq, width), F32), pltpu.VMEM((tq, width), BF),
            pltpu.VMEM((tq, LANES), F32), pltpu.VMEM((tq, width), F32), pltpu.VMEM((tq, width), F32),
        ],
        compiler_params=ROOMY,
        cost_estimate=pl.CostEstimate(flops=14 * tq * width * hidden, bytes_accessed=20 << 20, transcendentals=0),
        name="middle",
    )(core, attn_t, tiles, out_w, out_b, gain, shift, up_w, up_b, down_w, down_b, g)


def weights_kernel(unit_up, unit, meta, common_a, common_b, sel_a, sel_b, *rest):
    first_ref, second_refs, (first_s, second_s, sems) = rest[0], rest[1:5], rest[5:]
    width = 2 * unit * 16
    hidden = common_a.shape[0] - 2 * width
    chips = width // (2 * unit)

    def spot(chip):
        return (chip // 8) * 2 + chip % 2, chip // 2 % 4

    lifted, attn = slice(hidden, hidden + width), slice(hidden + width, hidden + 2 * width)
    group = width // (2 * unit_up)
    for step in range(hidden // width):
        rows = slice(step * width // 2, (step + 1) * width // 2)
        part = dot_nt(sel_a[rows, :], common_a[lifted, :]) + dot_nt(sel_b[rows, :], common_b[lifted, :])
        for i in range(group):
            plane, line = spot(step * group + i)
            first_s[plane, line, :unit_up, :] = part[i * unit_up : (i + 1) * unit_up].astype(BF)
    rows_out = slice(hidden // 2 + width // 2, hidden // 2 + width)
    rows = slice(hidden // 2, hidden // 2 + width // 2)
    out = dot_nt(sel_a[rows_out, :], common_a[attn, :]) + dot_nt(sel_b[rows_out, :], common_b[attn, :])
    held = [out]

    def down_part(step):
        cols = slice(step * width, (step + 1) * width)
        return dot_nt(sel_a[rows, :], common_a[cols, :]) + dot_nt(sel_b[rows, :], common_b[cols, :])

    held += [down_part(step) for step in range(FIRST_DOWN)]
    for chip in range(chips):
        plane, line = spot(chip)
        at = slice(chip * unit, (chip + 1) * unit)
        first_s[plane, line, unit_up:, :] = jnp.concatenate([part[at] for part in held], 0).astype(BF)
    copies = [pltpu.make_async_copy(first_s, first_ref, sems.at[4])]
    copies[0].start()
    for step in range(FIRST_DOWN, hidden // width):
        part = down_part(step)
        at = (step - FIRST_DOWN) * width
        for chip in range(chips):
            plane, line = spot(chip)
            second_s[line, plane, :, at : at + width] = part[chip * unit : (chip + 1) * unit].astype(BF)
    for k in range(4):
        copies.append(pltpu.make_async_copy(second_s.at[meta[5] ^ k], second_refs[k], sems.at[k]))
        copies[-1].start()
    for copy in copies:
        copy.wait()


def weights_call(devices, meta, width, common_a, common_b, sel_a, sel_b):
    tq = common_a.shape[1]
    hidden = common_a.shape[0] - 2 * width
    unit_up, unit = hidden // devices, width // devices
    first = (4, 4, unit_up + (1 + FIRST_DOWN) * unit, width)
    second = (4, unit, hidden - FIRST_DOWN * width)
    outs = pl.pallas_call(
        functools.partial(weights_kernel, unit_up, unit),
        in_specs=[SMEM] + [VMEM] * 4,
        out_specs=(pl.BlockSpec(memory_space=pltpu.HBM),) * 5,
        out_shape=(jax.ShapeDtypeStruct(first, BF),) + (jax.ShapeDtypeStruct(second, BF),) * 4,
        scratch_shapes=[pltpu.VMEM(first, BF), pltpu.VMEM((4,) + second, BF), pltpu.SemaphoreType.DMA((5,))],
        compiler_params=PARAMS,
        cost_estimate=pl.CostEstimate(flops=4 * tq * width * hidden, bytes_accessed=14 << 20, transcendentals=0),
        name="weights",
    )(meta, common_a, common_b, sel_a, sel_b)
    return outs[0], outs[1:]


def fold_kernel(meta, first_ref, own, got1, got2, got3, *outs):
    plane, line = meta[4], meta[5]
    for k in range(4):
        at = line ^ k
        total = first_ref[0, at].astype(F32)
        for i in range(1, 4):
            total += first_ref[i, at].astype(F32)
        outs[k][...] = total.astype(BF)
        at = plane ^ k
        total = own[at].astype(F32) + got1[at].astype(F32) + got2[at].astype(F32) + got3[at].astype(F32)
        outs[4 + k][...] = total.astype(BF)


def fold_call(meta, first, second):
    shapes = [jax.ShapeDtypeStruct(first.shape[2:], BF)] * 4 + [jax.ShapeDtypeStruct(second[0].shape[1:], BF)] * 4
    outs = pl.pallas_call(
        fold_kernel,
        in_specs=[SMEM] + [VMEM] * 5,
        out_specs=(VMEM,) * 8,
        out_shape=tuple(shapes),
        compiler_params=ROOMY,
        cost_estimate=TINY,
        name="fold",
    )(meta, first, *second)
    return outs[:4], outs[4:]


def small_places(unit_up, unit):
    sums = [(2, i * unit, unit) for i in range(4)]
    return [(0, 0, unit), (1, 0, unit), (4, 0, unit), (5, 0, unit)] + sums[1:] + [(3, 0, unit_up), sums[0]]


def last_kernel(unit_up, unit, meta, small_ref, *refs):
    columns, first, second, outs = refs[:4], refs[4:8], refs[8:12], refs[12:]
    qkv_ref, up_ref, out_ref, down_ref = outs[:4]
    small_refs, held = outs[4:-1], outs[-1]
    small = jnp.sum(small_ref[...], 0)
    for ref, (row, at, count) in zip(small_refs, small_places(unit_up, unit)):
        ref[...] = small[row : row + 1, at : at + count]
    size = columns[0].shape[0]
    held[...] = jnp.zeros_like(held)
    for i, ref in enumerate(columns):
        at = pl.multiple_of(meta[10 + i] + size // 2, 8)
        held[pl.ds(at, size), :] += ref[...].astype(F32)
    qkv_ref[...] = held[size // 2 : size // 2 + qkv_ref.shape[0], :]
    total = first[0][...].astype(F32)
    for ref in first[1:]:
        total += ref[...].astype(F32)
    up_ref[...] = total[:unit_up]
    out_ref[...] = total[unit_up : unit_up + unit]
    width = total.shape[1]
    for i in range(FIRST_DOWN):
        at = unit_up + (1 + i) * unit
        down_ref[:, i * width : (i + 1) * width] = total[at : at + unit]
    width = FIRST_DOWN * width
    total = second[0][...].astype(F32)
    for ref in second[1:]:
        total += ref[...].astype(F32)
    down_ref[:, width:] = total


def last_call(meta, small, unit_qkv, unit_up, unit, columns, first, second):
    size, width = columns[0].shape
    hidden = FIRST_DOWN * width + second[0].shape[1]
    outs = [(unit_qkv, width), (unit_up, width), (unit, width), (unit, hidden)]
    outs += [(1, count) for _, _, count in small_places(unit_up, unit)]
    return pl.pallas_call(
        functools.partial(last_kernel, unit_up, unit),
        in_specs=[SMEM] + [VMEM] * 13,
        out_specs=(VMEM,) * len(outs),
        out_shape=tuple(jax.ShapeDtypeStruct(s, F32) for s in outs),
        scratch_shapes=[pltpu.VMEM((unit_qkv + size, width), F32)],
        compiler_params=ROOMY,
        cost_estimate=TINY,
        name="last",
    )(meta, small, *columns, *first, *second)


def enter_kernel(tiles_ref, gain, shift, w_ref, query_b, value_b, x_ref, npre_ref, low_s):
    part = pl.program_id(0)

    @pl.when(part == 0)
    def _():
        scaled, normed, _ = near_rows(tiles_ref[...].astype(F32), gain[...], shift[...])
        low_s[...] = scaled.astype(BF)
        npre_ref[...] = normed.astype(BF)

    bias = jnp.where(part == 0, query_b[...], jnp.where(part == 2, value_b[...], 0.0))
    joined = (dot_nn(low_s[...], w_ref[...]) + bias).T
    heads, _, size, tq = x_ref.shape
    x_ref[:, 0] = joined.astype(BF).reshape(heads, size, tq)


def enter_call(heads, tiles, gain, shift, weight, query_b, value_b):
    tq, width = tiles.shape
    size = width // heads
    whole = lambda *shape: pl.BlockSpec(shape, lambda i: (0,) * len(shape))
    vec = whole(1, width)
    return pl.pallas_call(
        enter_kernel,
        grid=(3,),
        in_specs=[whole(tq, width), vec, vec, pl.BlockSpec((width, width), lambda i: (0, i)), vec, vec],
        out_specs=(pl.BlockSpec((heads, 1, size, tq), lambda i: (0, i, 0, 0)), whole(tq, width)),
        out_shape=(jax.ShapeDtypeStruct((heads, 3, size, tq), BF), jax.ShapeDtypeStruct((tq, width), BF)),
        scratch_shapes=[pltpu.VMEM((tq, width), BF)],
        compiler_params=PARAMS,
        name="enter",
    )(tiles, gain, shift, weight, query_b, value_b)


def leave_kernel(tiles_ref, gain, w_ref, jg_ref, res_ref, out_ref, acc):
    part = pl.program_id(0)
    width, tq = acc.shape
    more = dot_nn(w_ref[...], jg_ref[:, 0].reshape(width, tq))

    @pl.when(part == 0)
    def _():
        acc[...] = more

    @pl.when(part == 1)
    def _():
        acc[...] += more

    @pl.when(part == 2)
    def _():
        _, normed, inverse = near_rows(tiles_ref[...].astype(F32), gain[...], gain[...])
        grads = (acc[...] + more).T
        out_ref[...] = (res_ref[...] + back_rows(grads, normed, inverse, gain[...])).astype(BF)


def leave_call(tiles, gain, weight, joined_grad, residual_grad):
    tq, width = tiles.shape
    heads, _, size, _ = joined_grad.shape
    whole = lambda *shape: pl.BlockSpec(shape, lambda i: (0,) * len(shape))
    return pl.pallas_call(
        leave_kernel,
        grid=(3,),
        in_specs=[
            whole(tq, width), whole(1, width), pl.BlockSpec((width, width), lambda i: (0, i)),
            pl.BlockSpec((heads, 1, size, tq), lambda i: (0, i, 0, 0)), whole(tq, width),
        ],
        out_specs=whole(tq, width),
        out_shape=jax.ShapeDtypeStruct((tq, width), BF),
        scratch_shapes=[pltpu.VMEM((width, tq), F32)],
        compiler_params=PARAMS,
        cost_estimate=TINY,
        name="leave",
    )(tiles, gain, weight, joined_grad, residual_grad)


def halo_hits(plan, offs, first, dims):
    wide = max(plan.sel, LANES)
    shape = (plan.tq, wide)
    token, col = iota(shape, 0) + first, iota(shape, 1)
    hit = col < 0
    for branch in plan.branches:
        if branch["extra"]:
            at = col - branch["sel"]
            inside = (at >= 0) & (at < branch["extra"])
            hit |= inside & (token == at * branch["rate"] + offs[branch["level"]])
    return jnp.where(hit, 1.0, 0.0).astype(BF)


def halo_blocks(plan):
    count = plan.halo // plan.tq
    for i in range(count):
        yield 0, plan.blocks - count + i, i * plan.tq
        yield 1, i, i * plan.tq


def static_slot(plan, block):
    return block % plan.groups * plan.members + block // plan.groups


def select_kernel(plan, meta, offsets, x_ref, *outs):
    offs = [offsets[b["level"], meta[1]] for b in plan.branches]
    if plan.paired:
        count = plan.halo // plan.tq
        total = jnp.zeros((2 * plan.size, max(plan.sel, LANES)), F32)
        for i in range(count):
            block = (1 - meta[2]) * (plan.blocks - count) + i
            total += dot_nn(x_ref[plan.slot(block), plan.size :, :], halo_hits(plan, offs, i * plan.tq, None))
        outs[0][...] = total.astype(BF)
        return
    last_ref, first_ref = outs
    total = [jnp.zeros((2 * plan.size, max(plan.sel, LANES)), F32) for _ in range(2)]
    for side, block, first in halo_blocks(plan):
        hits = halo_hits(plan, offs, first, None)
        total[side] += dot_nn(x_ref[static_slot(plan, block), plan.size :, :], hits)
    last_ref[...] = total[0].astype(BF)
    first_ref[...] = total[1].astype(BF)


def select_call(plan, meta, offsets, x):
    shape = jax.ShapeDtypeStruct((2 * plan.size, max(plan.sel, LANES)), BF)
    return pl.pallas_call(
        functools.partial(select_kernel, plan),
        in_specs=[SMEM, SMEM, VMEM],
        out_specs=(VMEM,) * (1 if plan.paired else 2),
        out_shape=(shape,) * (1 if plan.paired else 2),
        compiler_params=ROOMY,
        name="select",
    )(meta, offsets, x)


def to_owners(vector, owner, lane_of, devices):
    count = vector.shape[1]
    held = jnp.where(iota((devices, count), 0) == owner, vector, 0.0)
    hits = jnp.where(iota((count, LANES), 1) == lane_of, 1.0, 0.0)
    return lax.dot_general(
        held, hits, (((1,), (0,)), ((), ())), precision=lax.Precision.HIGHEST, preferred_element_type=F32
    )


def cut(index, unit):
    whole = jnp.floor((index.astype(F32) + 0.5) * (1.0 / unit)).astype(jnp.int32)
    return whole, index - whole * unit


def head_kernel(devices, meta, dx_ref, near_ref, w_ref, gain, shift, sums_ref, up_ref, *rest):
    column_refs, (small_ref, acc, col_s, row_s) = rest[:-4], rest[-4:]
    step, steps = pl.program_id(0), pl.num_programs(0)
    tq = dx_ref.shape[2]
    rows = dx_ref.shape[1]
    per = near_ref.shape[0] // tq
    size = rows // 3
    width = near_ref.shape[1]

    @pl.when(step == 0)
    def _():
        acc[...] = jnp.zeros_like(acc)
        col_s[...] = jnp.zeros_like(col_s)
        row_s[...] = jnp.zeros_like(row_s)

    for i in range(per):
        grads = dx_ref[i]
        acc[...] += dot_nn(grads, near_ref[i * tq : (i + 1) * tq, :])
        col_s[...] += jnp.broadcast_to(jnp.sum(grads.astype(F32), 1, keepdims=True), col_s.shape)
        row_s[...] += dot_nt(jnp.ones((8, tq), BF), grads)

    @pl.when(step == steps - 1)
    def _():
        head = meta[1]
        plain = acc[...]
        weight = plain * gain[...] + col_s[:, :1] * shift[...]
        acc[...] = weight
        for i, ref in enumerate(column_refs):
            at = pl.multiple_of(meta[6 + i] * size, 8)
            ref[...] = acc[pl.ds(at, size), :].astype(BF)
        own = w_ref[...].astype(F32)
        gain_part = jnp.sum(own * plain, 0, keepdims=True)
        shift_part = jnp.sum(own * col_s[:, :1], 0, keepdims=True)
        unit = width // devices
        owner = cut(iota((1, width), 1), unit)[0]
        lane = cut(iota((width, 1), 0), unit)[1]
        small_ref[:, 0, :] = to_owners(gain_part, owner, lane, devices)
        small_ref[:, 1, :] = to_owners(shift_part, owner, lane, devices)
        held = jnp.zeros((devices, LANES), F32)
        for i in range(4):
            held += to_owners(sums_ref[i : i + 1, :], owner, lane + i * unit, devices)
        small_ref[:, 2, :] = held
        hidden = up_ref.shape[1]
        unit_up = hidden // devices
        held = jnp.zeros((devices, LANES), F32)
        for i in range(hidden // width):
            owner_up = cut(iota((1, width), 1) + i * width, unit_up)[0]
            lane_up = cut(iota((width, 1), 0) + i * width, unit_up)[1]
            held += to_owners(up_ref[:, i * width : (i + 1) * width], owner_up, lane_up, devices)
        small_ref[:, 3, :] = held
        line = row_s[0:1, :]
        for i, part in enumerate((0, 2)):
            index = iota((1, rows), 1) - part * size
            inside = (index >= 0) & (index < size)
            owner_h = jnp.where(inside, 2 * head + cut(index, size // 2)[0], -1)
            lane_h = cut(iota((rows, 1), 0), size // 2)[1]
            small_ref[:, 4 + i, :] = to_owners(line, owner_h, lane_h, devices)
        small_ref[:, 6, :] = jnp.zeros((devices, LANES), F32)
        small_ref[:, 7, :] = jnp.zeros((devices, LANES), F32)


def head_call(devices, meta, dx, npre_all, own_w, gain, shift, sums, up_sums):
    blocks, rows, tq = dx.shape
    width = npre_all.shape[1]
    per = blocks // 4
    whole = lambda *shape: pl.BlockSpec(shape, lambda i: (0,) * len(shape))
    return pl.pallas_call(
        functools.partial(head_kernel, devices),
        grid=(4,),
        in_specs=[
            SMEM, pl.BlockSpec((per, rows, tq), lambda i: (i, 0, 0)), pl.BlockSpec((per * tq, width), lambda i: (i, 0)),
            whole(rows, width), whole(1, width), whole(1, width), whole(8, width), whole(1, up_sums.shape[1]),
        ],
        out_specs=(whole(rows // 3, width),) * 4 + (whole(devices, 8, LANES),),
        out_shape=(jax.ShapeDtypeStruct((rows // 3, width), BF),) * 4
        + (jax.ShapeDtypeStruct((devices, 8, LANES), F32),),
        scratch_shapes=[
            pltpu.VMEM((rows, width), F32), pltpu.VMEM((rows, LANES), F32), pltpu.VMEM((8, rows), F32),
        ],
        compiler_params=PARAMS,
        cost_estimate=TINY,
        name="head",
    )(meta, dx, npre_all, own_w, gain, shift, sums, up_sums)


def layer_norm_rows(values, norm_gain, norm_shift):
    row_mean = jnp.mean(values, -1, keepdims=True)
    centred = values - row_mean
    inverse = lax.rsqrt(jnp.mean(centred * centred, -1, keepdims=True) + EPS)
    normed = centred * inverse
    return (normed * norm_gain + norm_shift, normed, inverse)


def norm_back(grad_out, normed, inverse, norm_gain):
    grad_norm = grad_out * norm_gain
    grad_in = inverse * (
        grad_norm
        - jnp.mean(grad_norm, -1, keepdims=True)
        - normed * jnp.mean(grad_norm * normed, -1, keepdims=True)
    )
    return (grad_in, jnp.sum(grad_out * normed, 0), jnp.sum(grad_out, 0))


def swap(values, axes):
    return lax.all_to_all(values, axes, 0, 0, tiled=True)


def scatter_sum(values, orders):
    sizes = {name: lax.axis_size(name) for name in ALL}
    left = list(ALL)
    rows, cols = values.shape[1:]
    for stage, axes in enumerate(orders):
        values = values.reshape([sizes[name] for name in left] + [rows, cols])
        rest = [name for name in left if name not in axes]
        order = [left.index(name) for name in list(axes) + rest]
        values = values.transpose(order + [len(left), len(left) + 1])
        count = math.prod(sizes[name] for name in axes)
        values = values.reshape((count, -1, rows, cols))
        if count > 1:
            values = swap(values, axes)
            values = jnp.sum(values.astype(F32), 0)
            if stage < len(orders) - 1:
                values = values.astype(BF)
        left = rest
    return values.reshape(rows, cols).astype(F32)


def to_neighbours(pieces, count):
    if count == 2:
        return (lax.ppermute(pieces[0], "grp", [(0, 1), (1, 0)]),)
    return (
        lax.ppermute(pieces[0], "grp", [(i, i + 1) for i in range(count - 1)]),
        lax.ppermute(pieces[1], "grp", [(i + 1, i) for i in range(count - 1)]),
    )


def from_neighbours(pieces, count):
    return to_neighbours(pieces[::-1], count)[::-1]


def share_columns(weight_t, sums, width):
    members, size = lax.axis_size(GROUP), weight_t.shape[1]
    head = lax.axis_index(GROUP)
    full = jnp.zeros((3, members) + weight_t.shape[1:], F32)
    full = lax.dynamic_update_slice(full, weight_t[:, None], (0, head, 0, 0))
    full_sums = lax.dynamic_update_slice(jnp.zeros((3, members, size), F32), sums[:, None], (0, head, 0))
    weight = lax.psum_scatter(full.reshape(3 * members * size, width), ALL, scatter_dimension=0, tiled=True)
    sums = lax.psum_scatter(full_sums.reshape(3, members * size), ALL, scatter_dimension=1, tiled=True)
    return weight, sums[0], sums[2]


def body(
    tile_embed,
    slide_lengths,
    head_offsets,
    pre_gain,
    pre_shift,
    qkv_weight,
    query_bias,
    value_bias,
    out_weight,
    out_bias,
    post_gain,
    post_shift,
    up_weight,
    up_bias,
    down_weight,
    down_bias,
    out_grad,
):
    width = qkv_weight.shape[0]
    hidden = up_weight.shape[1]
    heads = head_offsets.shape[1]
    size = width // heads
    tq = tile_embed.shape[1]
    br, groups = lax.axis_size("br"), lax.axis_size("grp")
    members = heads // br
    devices = heads * groups
    plan = Plan(heads, size, head_offsets.shape[0], br, members, tq, devices * tq)
    head = lax.axis_index(GROUP)
    base = lax.axis_index("grp") * plan.tokens
    meta = jnp.stack([base, head, lax.axis_index("grp")]).astype(jnp.int32)

    tiles = tile_embed[0].astype(F32)
    pre_out, normed_pre, inverse_pre = layer_norm_rows(tiles, pre_gain, pre_shift)
    normed_low = pre_out.astype(BF)
    bias_col = jnp.concatenate([query_bias, jnp.zeros_like(query_bias), value_bias], 1).reshape(-1, 1)
    joined_t = (
        lax.dot_general(qkv_weight, normed_low, (((0,), (1,)), ((), ())), preferred_element_type=F32) + bias_col
    ).astype(BF)
    x = joined_t.reshape(3, heads, size, tq).transpose(1, 0, 2, 3).reshape(heads, 3 * size, tq)
    x = swap(x, GROUP)
    normed_all = lax.all_gather(normed_low, GROUP, axis=0, tiled=True)

    halo = to_neighbours(select_call(plan, meta, head_offsets, x), groups)
    state, *own = near_call(plan, meta, slide_lengths, head_offsets, x)
    mixed, state = far_call(plan, meta, slide_lengths, head_offsets, state, own, halo)
    attn_t = swap(mixed, GROUP).reshape(width, tq)

    projected = lax.dot_general(attn_t, out_weight, (((0,), (0,)), ((), ())), preferred_element_type=F32)
    residual = tiles + projected + out_bias
    post_out, normed_post, inverse_post = layer_norm_rows(residual, post_gain, post_shift)
    lifted = post_out.astype(BF)
    gate_in = jnp.dot(lifted, up_weight, preferred_element_type=F32) + up_bias
    act_float, gelu_pull = jax.vjp(lambda v: jax.nn.gelu(v, approximate=False), gate_in)
    act_low = act_float.astype(BF)
    layer_out = (residual + jnp.dot(act_low, down_weight, preferred_element_type=F32) + down_bias).astype(BF)[None]
    grad_low = out_grad[0]
    grad_float = grad_low.astype(F32)
    act_grad = lax.dot_general(grad_low, down_weight, (((1,), (1,)), ((), ())), preferred_element_type=F32)
    gate_grad = gelu_pull(act_grad)[0].astype(BF)
    lifted_grad = lax.dot_general(gate_grad, up_weight, (((1,), (1,)), ((), ())), preferred_element_type=F32)
    norm_part, post_gain_sum, post_shift_sum = norm_back(lifted_grad, normed_post, inverse_post, post_gain)
    residual_grad = grad_float + norm_part
    proj_grad = residual_grad.astype(BF)
    attn_grad_t = lax.dot_general(
        out_weight, proj_grad, (((1,), (1,)), ((), ())), preferred_element_type=F32
    ).astype(BF)
    do = swap(attn_grad_t.reshape(heads, size, tq), GROUP)

    tokens = (((0,), (0,)), ((), ()))
    up_part = lax.dot_general(gate_grad, lifted, tokens, preferred_element_type=F32).astype(BF)
    down_part = lax.dot_general(grad_low, act_low, tokens, preferred_element_type=F32).astype(BF)
    out_part = lax.dot_general(proj_grad, attn_t, (((0,), (1,)), ((), ())), preferred_element_type=F32).astype(BF)
    vectors = [
        jnp.sum(gate_grad.astype(F32), 0).reshape(devices, -1),
        jnp.sum(grad_float, 0).reshape(devices, -1),
        jnp.sum(residual_grad, 0).reshape(devices, -1),
        post_gain_sum.reshape(devices, -1),
        post_shift_sum.reshape(devices, -1),
    ]
    ends = [0]
    for vector in vectors:
        ends.append(ends[-1] + vector.shape[1])
    small = jnp.concatenate(vectors, 1)
    small = jnp.pad(small[:, None, :], ((0, 0), (0, 7), (0, width - small.shape[1]))).astype(BF)
    misc = jnp.concatenate([out_part.reshape(devices, -1, width), small], 1)
    first, second = (("s0",), ("br", "s1"), ("grp", "s2")), (("s0",), ("grp", "s2"), ("br", "s1"))
    up_own = scatter_sum(up_part.reshape(devices, -1, width), first)
    down_own = scatter_sum(down_part.reshape(devices, -1, hidden), second)
    misc_own = scatter_sum(misc, first)
    unit = width // devices
    small_own = misc_own[unit]
    small_own = [small_own[None, ends[i] : ends[i + 1]] for i in range(len(vectors))]

    rows, dq, dk, dv, *sides = far_back_call(plan, meta, slide_lengths, head_offsets, state, do, own, halo)
    back = from_neighbours(sides, groups)
    dx = near_back_call(plan, meta, slide_lengths, head_offsets, x, state, rows, (dq, dk, dv), back)
    joined_grad_t = swap(dx, GROUP).reshape(heads, 3, size, tq).transpose(1, 0, 2, 3).reshape(3 * width, tq)
    weight_t = jnp.einsum(
        "nct,ntd->cd", dx, normed_all.reshape(heads, tq, width), preferred_element_type=F32
    ).reshape(3, size, width)
    head_sums = jnp.sum(dx.astype(F32), (0, 2)).reshape(3, size)
    qkv_own, query_own, value_own = share_columns(weight_t, head_sums, width)
    normed_grad = lax.dot_general(joined_grad_t, qkv_weight, (((0,), (1,)), ((), ())), preferred_element_type=F32)
    tile_part, pre_gain_sum, pre_shift_sum = norm_back(normed_grad, normed_pre, inverse_pre, pre_gain)
    tile_grad = (residual_grad + tile_part).astype(BF)[None]
    last = jnp.stack([pre_gain_sum, pre_shift_sum]).reshape(2, devices, unit).transpose(1, 0, 2)
    last = jnp.pad(last, ((0, 0), (0, 6), (0, LANES - unit)))
    last = jnp.sum(swap(last, ALL).reshape(devices, 8, LANES), 0)
    return (
        layer_out,
        tile_grad,
        last[0:1, :unit],
        last[1:2, :unit],
        qkv_own.T,
        query_own[None],
        value_own[None],
        misc_own[:unit].T,
        small_own[2],
        small_own[3],
        small_own[4],
        up_own.T,
        small_own[0],
        down_own.T,
        small_own[1],
    )


def across(piece, axes, k):
    return lax.ppermute(piece, axes, [(i, i ^ k) for i in range(4)])


def matchings(edges, count):
    edges, found = list(edges), []
    while edges:
        by_source = {}
        for edge in edges:
            by_source.setdefault(edge[0], []).append(edge)
        taken = {}

        def place(source, seen):
            for edge in by_source[source]:
                if edge[1] not in seen:
                    seen.add(edge[1])
                    if edge[1] not in taken or place(taken[edge[1]][0], seen):
                        taken[edge[1]] = edge
                        return True
            return False

        for source in range(count):
            place(source, set())
        found.append(sorted(taken.values()))
        for edge in taken.values():
            edges.remove(edge)
    return found


def column_routes(heads, size, unit):
    sizes = [lax.axis_size(name) for name in ALL]
    inner = sizes[2] * sizes[3] * sizes[4]
    edges = []
    for head in range(heads):
        for grp in range(sizes[1]):
            source = (head // inner * sizes[1] + grp) * inner + head % inner
            for part in range(3):
                start = (part * heads + head) * size
                for owner in sorted({start // unit, (start + size - 1) // unit}):
                    edges.append((source, owner, (part, start - owner * unit)))
    devices = heads * sizes[1]
    for matching in matchings(edges, devices):
        route = [edge[:2] for edge in matching]
        part_of, begin_of = [0] * devices, [0] * devices
        for source, owner, (part, begin) in matching:
            part_of[source], begin_of[owner] = part, begin
        yield route, part_of, begin_of


def fast_body(
    tile_embed, slide_lengths, head_offsets, pre_gain, pre_shift, qkv_weight, query_bias, value_bias, out_weight,
    out_bias, post_gain, post_shift, up_weight, up_bias, down_weight, down_bias, out_grad,
):
    width = qkv_weight.shape[0]
    heads = head_offsets.shape[1]
    size = width // heads
    tq = tile_embed.shape[1]
    br, groups = lax.axis_size("br"), lax.axis_size("grp")
    members = heads // br
    devices = heads * groups
    plan = Plan(heads, size, head_offsets.shape[0], br, members, tq, devices * tq)
    head = lax.axis_index(GROUP)
    group = lax.axis_index("grp")
    core = lax.axis_index("s0")
    meta = [group * plan.tokens, head, group, core, lax.axis_index(("br", "s1")), lax.axis_index(("grp", "s2"))]
    routes = list(column_routes(heads, size, 3 * width // devices))[::-1]
    table = jnp.array([parts for _, parts, _ in routes] + [begins for _, _, begins in routes], jnp.int32)
    meta.extend(lax.dynamic_index_in_dim(table, lax.axis_index(ALL), 1, False))
    meta = jnp.stack(meta).astype(jnp.int32)
    tiles = tile_embed[0]
    own_w = jnp.concatenate(
        [lax.dynamic_slice_in_dim(qkv_weight, part * width + head * size, size, 1) for part in range(3)], 1
    ).T
    pair = [(0, 1), (1, 0)]
    plane, line = ("br", "s1"), ("grp", "s2")

    x, npre = enter_call(heads, tiles, pre_gain, pre_shift, qkv_weight, query_bias, value_bias)
    x = swap(x.reshape(heads, 3 * size, tq), GROUP)
    x, npre, own_w, meta = lax.optimization_barrier((x, npre, own_w, meta))
    halo = to_neighbours(select_call(plan, meta, head_offsets, x), groups)
    state, *own = near_call(plan, meta, slide_lengths, head_offsets, x)
    mixed, state = far_call(plan, meta, slide_lengths, head_offsets, state, own, halo)
    attn_t = swap(mixed, GROUP).reshape(width, tq)
    npre_all = lax.all_gather(npre, GROUP, axis=0, tiled=True)
    layer_out, residual_grad, attn_grad_t, common, sel, sel_give, sums, up_sums = middle_call(
        devices, core[None].astype(jnp.int32), attn_t, tiles, out_weight, out_bias, post_gain, post_shift,
        up_weight, up_bias, down_weight, down_bias, out_grad[0],
    )
    do = swap(attn_grad_t.reshape(heads, size, tq), GROUP)
    common_b = lax.ppermute(common, "s0", pair)
    sel_b = lax.ppermute(sel_give, "s0", pair)
    first, second = weights_call(devices, meta, width, common, common_b, sel, sel_b)
    do, first, second, npre_all = lax.optimization_barrier((do, first, second, npre_all))
    first = swap(first, plane)
    second = [second[0]] + [across(second[k], line, k) for k in (1, 2, 3)]
    rows, dq, dk, dv, *sides = far_back_call(plan, meta, slide_lengths, head_offsets, state, do, own, halo)
    back = from_neighbours(sides, groups)
    dx = near_back_call(plan, meta, slide_lengths, head_offsets, x, state, rows, (dq, dk, dv), back)
    *columns, small = head_call(devices, meta, dx, npre_all, own_w, pre_gain, pre_shift, sums, up_sums)
    dx, columns, small, first, second = lax.optimization_barrier((dx, columns, small, first, second))
    joined_grad = swap(dx, GROUP).reshape(heads, 3, size, tq)
    first, second = fold_call(meta, first, second)
    first = [first[0]] + [across(first[k], line, k) for k in (1, 2, 3)]
    second = [second[0]] + [across(second[k], plane, k) for k in (1, 2, 3)]
    joined_grad, small, second = lax.optimization_barrier((joined_grad, small, second))
    small = swap(small, ALL)
    columns = [lax.ppermute(piece, ALL, route) for piece, (route, _, _) in zip(columns, routes)]
    joined_grad, first = lax.optimization_barrier((joined_grad, first))
    tile_grad = leave_call(tiles, pre_gain, qkv_weight, joined_grad, residual_grad)
    unit_up, unit = up_weight.shape[1] // devices, width // devices
    qkv_own, up_own, out_own, down_own, *vectors = last_call(
        meta, small, 3 * unit, unit_up, unit, columns, first, second
    )
    gain_own, shift_own, query_own, value_own, out_b, post_gain_own, post_shift_own, up_b, down_b = vectors
    return (
        layer_out[None], tile_grad[None], gain_own, shift_own, qkv_own.T, query_own, value_own, out_own.T, out_b,
        post_gain_own, post_shift_own, up_own.T, up_b, down_own.T, down_b,
    )


def solution(mesh):
    br, rows = mesh.shape["br"], mesh.shape["rows"]

    def run(*args):
        members = args[2].shape[1] // br
        shape = (br, rows // members, members // 4, 2, 2)
        split = jax.sharding.Mesh(mesh.devices.reshape(shape), ALL)
        tokens = P(("grp", "s2", "s1", "s0"), "br", None)
        owned = P(None, ALL)
        return jax.shard_map(
            fast_body if shape == (2, 2, 2, 2, 2) else body,
            mesh=split,
            in_specs=(tokens,) + (P(),) * 15 + (tokens,),
            out_specs=(tokens, tokens) + (owned,) * 13,
            check_vma=False,
        )(*args)

    return run
```

```python
import functools
import math

import jax
import jax.numpy as jnp
import ml_dtypes
import numpy as np
from jax import lax
from jax.experimental import pallas as pl
from jax.experimental.pallas import tpu as pltpu
from jax.sharding import PartitionSpec as P

SEG_BASE = 1024
DOC_MOST = 2048
LANES = 128
BF = jnp.bfloat16
F32 = jnp.float32
NEG = -1e30
EPS = 1e-05
ALL = ("br", "grp", "s2", "s1", "s0")
GROUP = ("br", "s2", "s1", "s0")
FIRST_DOWN = 2
ONE_LANE = 48
ID_Q = 51
ID_K = 52
TWICE = 53


class Plan:
    def __init__(self, heads, head_size, branches, groups, members, tq, total):
        self.heads, self.size, self.groups, self.members, self.tq = heads, head_size, groups, members, tq
        self.blocks = groups * members
        self.paired = groups * members * tq * 2 == total
        self.tokens = self.blocks * tq
        self.total = total
        self.halo = min(DOC_MOST, self.tokens)
        self.factor = math.log2(math.e) * head_size**-0.5
        self.branches = []
        keys, sel = 0, 0
        for level in range(branches):
            rate = 2**level
            span = min(SEG_BASE * rate, total)
            near = span <= self.tokens
            extra = 0 if near else self.halo // rate
            segs = self.tokens // span if near else 1
            seg_q = self.tokens // rate // segs
            seg_k = seg_q + 2 * extra
            flip = 0
            if level == 1 and near and span == 2 * self.branches[0]["span"]:
                segs, seg_q, seg_k, flip = segs * 2, seg_q // 2, seg_k // 2, 1
            self.branches.append(
                dict(
                    level=level, rate=rate, span=span, near=near, extra=extra, segs=segs,
                    seg_q=seg_q, seg_k=seg_k, tile=min(1024, seg_q), first=keys, sel=sel, flip=flip,
                )
            )
            keys += segs * seg_k
            sel += extra
        self.sel = sel
        self.twice = any(b["flip"] for b in self.branches)
        self.near = [b for b in self.branches if b["near"]]
        self.far = [b for b in self.branches if not b["near"]]
        self.near_keys = sum(b["segs"] * b["seg_k"] for b in self.near)
        self.far_keys, self.own = 0, 0
        for b in self.far:
            b["begin"], b["own"] = self.far_keys, self.own
            self.far_keys += b["seg_k"]
            self.own += b["seg_q"]
        self.widest = max(b["seg_k"] for b in self.branches)

    def slot(self, block):
        return lax.rem(block, self.groups) * self.members + lax.div(block, self.groups)


def dot_nt(a, b):
    return lax.dot_general(a, b, (((1,), (1,)), ((), ())), preferred_element_type=F32)


def dot_tn(a, b):
    return lax.dot_general(a, b, (((0,), (0,)), ((), ())), preferred_element_type=F32)


def dot_nn(a, b):
    return lax.dot_general(a, b, (((1,), (0,)), ((), ())), preferred_element_type=F32)


def iota(shape, dim):
    return lax.broadcasted_iota(jnp.int32, shape, dim)


def placement(size, parts):
    shape = (parts * size + 16, parts * LANES)
    row, col = iota(shape, 0), iota(shape, 1)
    hit = col < 0
    for part in range(parts):
        hit |= (row >= part * size) & (row < (part + 1) * size) & (col == row - part * size + part * LANES)
    return row, col, hit


def ids_of(pos, starts, gate=None):
    found = jnp.zeros(pos.shape, jnp.int32)
    for start in starts:
        found += jnp.where(pos >= start, 1, 0)
    if gate is not None:
        found = jnp.where(gate, found, -1)
    return found.astype(F32)


def slide_starts(lens_ref):
    starts, at = [], jnp.int32(0)
    for i in range(lens_ref.shape[0]):
        starts.append(at)
        at = at + lens_ref[i]
    return starts


def branch_pos(plan, branch, base, off, first, count):
    start = base - branch["extra"] * branch["rate"] + off
    pos = start + branch["rate"] * (first + iota((1, count), 1))
    if branch["near"]:
        return pos, None
    shift = int(math.log2(branch["span"]))
    return pos, lax.shift_right_arithmetic(pos, shift) == lax.shift_right_arithmetic(base, shift)


def plain_keys(rows):
    lane = iota(rows.shape, 1)
    return jnp.where((lane >= TWICE) & (lane < TWICE + 3), 0.0, rows)


def to_rows(plan, base, offs, starts, x_ref, q_tm, k_tm, v_tm, extra_q=None):
    size, tq = plan.size, plan.tq
    row, col, hit = placement(size, 3)
    hit |= (row == 3 * size) & ((col == ID_Q) | (col == LANES + ID_K))
    place = jnp.where(hit, 1.0, 0.0).astype(BF)
    lane = iota((1, 3 * LANES), 1)
    in_k, in_v = lane - LANES, lane - 2 * LANES
    ones = jnp.where(
        ((in_k >= ONE_LANE) & (in_k < ONE_LANE + 3)) | ((in_v >= ONE_LANE) & (in_v < ONE_LANE + 3)), 1.0, 0.0
    )

    more = jnp.zeros((1, LANES), F32)
    rest = 1.0 / plan.factor
    for i in range(3 if plan.twice else 0):
        term = float(np.float32(rest).astype(ml_dtypes.bfloat16))
        more = jnp.where(lane[:, :LANES] == TWICE + i, term, more)
        rest -= term
    own = iota((1, LANES), 1)
    both = jnp.where((own >= TWICE) & (own < TWICE + 3), 1.0, 0.0)

    def block(n, carry):
        pos = base + n * tq + iota((1, tq), 1)
        ids = jnp.where(iota((16, tq), 0) == 0, ids_of(pos, starts), 0.0).astype(BF)
        full = jnp.concatenate([x_ref[plan.slot(n)], ids], 0)
        rows = dot_tn(full, place) + ones
        at = pl.ds(pl.multiple_of(n * tq, tq), tq)
        queries = rows[:, :LANES]
        if extra_q is not None:
            queries = queries + extra_q(n, at)
        keys = rows[:, LANES : 2 * LANES]
        if plan.twice:
            member = (iota((tq, 1), 0) & 1) == offs[1]
            queries = jnp.where(member, queries + more, queries)
            keys = jnp.where(member, keys + both, keys)
        q_tm[at, :] = queries
        k_tm[at, :] = keys
        v_tm[at, :] = rows[:, 2 * LANES :]
        if extra_q is not None:
            return carry
        squares = [jnp.square(full[i * size : (i + 1) * size].astype(F32)) for i in range(2)]
        return tuple(jnp.maximum(a, jnp.sum(b, 0, keepdims=True)) for a, b in zip(carry, squares))

    start = (jnp.zeros((1, tq), F32),) * 2 if extra_q is None else 0
    most = lax.fori_loop(0, plan.blocks, block, start, unroll=4)
    if extra_q is None:
        return jnp.sqrt(jnp.max(most[0], 1, keepdims=True) * jnp.max(most[1], 1, keepdims=True)) * 1.0001
    return None


def gather_near(plan, offs, k_tm, v_tm, kall, vall, branches):
    for branch in branches:
        rate, first, off = branch["rate"], branch["first"], offs[branch["level"]]
        count = plan.tokens // rate
        step = min(256, count)

        def chunk(i, carry, rate=rate, first=first, off=off, step=step):
            keys = k_tm[pl.ds(off + i * step * rate, step, stride=rate) if rate > 1 else pl.ds(i * step, step), :]
            rows = pl.ds(off + i * step * rate, step, stride=rate) if rate > 1 else pl.ds(i * step, step)
            to = pl.ds(pl.multiple_of(first + i * step, step), step)
            kall[to, :] = (plain_keys(keys) if rate > 1 else keys).astype(BF)
            vall[to, :] = v_tm[rows, :].astype(BF)
            return carry

        lax.fori_loop(0, count // step, chunk, 0, unroll=min(4, count // step))


def far_keys(plan, base, offs, starts, halos, k_far, v_far, kall, vall):
    size = plan.size
    row, col, hit = placement(size, 2)
    hit |= (row == 2 * size) & (col == ID_K)
    place = jnp.where(hit, 1.0, 0.0).astype(BF)
    lane = iota((1, 2 * LANES), 1)
    in_v = lane - LANES
    ones = jnp.where(
        ((lane >= ONE_LANE) & (lane < ONE_LANE + 3)) | ((in_v >= ONE_LANE) & (in_v < ONE_LANE + 3)), 1.0, 0.0
    )
    for branch in plan.far:
        extra, first, own, count = branch["extra"], branch["begin"], branch["own"], branch["seg_q"]
        kall[first + extra : first + extra + count, :] = k_far[own : own + count, :]
        vall[first + extra : first + extra + count, :] = v_far[own : own + count, :]
        for side, ref in enumerate((halos[0], halos[-1])):
            begin = side * (extra + count)
            pos, gate = branch_pos(plan, branch, base, offs[branch["level"]], begin, extra)
            ids = jnp.where(iota((16, extra), 0) == 0, ids_of(pos, starts, gate), 0.0).astype(BF)
            piece = ref[:, branch["sel"] : branch["sel"] + extra]
            rows = dot_tn(jnp.concatenate([piece, ids], 0), place) + ones
            kall[first + begin : first + begin + extra, :] = rows[:, :LANES].astype(BF)
            vall[first + begin : first + begin + extra, :] = rows[:, LANES:].astype(BF)


def picked(branch, off, i):
    tile, rate = branch["tile"], branch["rate"]
    if rate == 1:
        return pl.ds(pl.multiple_of(i * tile, tile), tile)
    return pl.ds(off + i * tile * rate, tile, stride=rate)


def pieces_of(wide, most):
    step = next(n for n in (most, 512, 256, 128) if wide % n == 0)
    return [(at, step) for at in range(0, wide, step)]


def split3(column, lane):
    high = column.astype(BF).astype(F32)
    rest = column - high
    mid = rest.astype(BF).astype(F32)
    low = rest - mid
    return jnp.where(
        lane == ONE_LANE, high, jnp.where(lane == ONE_LANE + 1, mid, jnp.where(lane == ONE_LANE + 2, low, 0.0))
    )


def near_kernel(plan, meta, lens, offsets, x_ref, st_ref, qf_ref, kf_ref, vf_ref, q_tm, k_tm, v_tm, kall, vall, kid):
    base, head = meta[0], meta[1]
    starts = slide_starts(lens)
    offs = [offsets[b["level"], head] for b in plan.branches]
    top = to_rows(plan, base, offs, starts, x_ref, q_tm, k_tm, v_tm)
    gather_near(plan, offs, k_tm, v_tm, kall, vall, plan.near)
    for branch in plan.far:
        rows = pl.ds(offs[branch["level"]], branch["seg_q"], stride=branch["rate"])
        own = slice(branch["own"], branch["own"] + branch["seg_q"])
        qf_ref[own, :] = q_tm[rows, :].astype(BF)
        kf_ref[own, :] = plain_keys(k_tm[rows, :]).astype(BF)
        vf_ref[own, :] = v_tm[rows, :].astype(BF)
    for branch in plan.near:
        first, total = branch["first"], branch["segs"] * branch["seg_k"]
        pos, gate = branch_pos(plan, branch, base, offs[branch["level"]], 0, total)
        kid[:, first : first + total] = ids_of(pos, starts, gate)
    factor = plan.factor
    lane = iota((1, LANES), 1)

    def scan(visit):
        for branch in plan.near:
            per = branch["seg_q"] // branch["tile"]

            def tile(i, carry, branch=branch, per=per):
                rows = picked(branch, offs[branch["level"]], i)
                at = pl.multiple_of(branch["first"] + (lax.div(i, per) ^ branch["flip"]) * branch["seg_k"], 128)
                visit(branch, rows, q_tm[rows, :], at)
                return carry

            lax.fori_loop(0, branch["segs"] * per, tile, 0, unroll=4 if branch["flip"] else min(2, branch["segs"] * per))

    def attend(top_lanes):
        def visit(branch, rows, queries, at):
            ids = queries[:, ID_Q : ID_Q + 1]
            low = (queries + top_lanes).astype(BF)
            mixed = None
            for begin, step in pieces_of(branch["seg_k"], 1024):
                to = pl.ds(at + begin, step)
                weights = jnp.exp2(dot_nt(low, kall[to, :]) * factor)
                weights = jnp.where(ids == kid[:, to], weights, 0.0).astype(BF)
                more = dot_nn(weights, vall[to, :])
                mixed = more if mixed is None else mixed + more
            if branch["level"]:
                mixed = st_ref[rows, :] + mixed
            st_ref[rows, :] = mixed

        scan(visit)

    attend(split3(-top, lane))
    step = min(512, plan.tokens)

    def least(n, low):
        at = pl.ds(pl.multiple_of(n * step, step), step)
        state = st_ref[at, :]
        st_ref[at, :] = jnp.where(iota((step, LANES), 1) == ID_Q, top, state)
        return jnp.minimum(low, jnp.min(state, 0, keepdims=True))

    weight = lax.fori_loop(0, plan.tokens // step, least, jnp.full((1, LANES), jnp.inf, F32), unroll=2)
    weight = jnp.min(jnp.where(lane == ONE_LANE, weight, jnp.inf))

    @pl.when(jnp.logical_not(weight > 2.0**-60))
    def _():
        def clear(n, carry):
            st_ref[pl.ds(pl.multiple_of(n * step, step), step), :] = jnp.full((step, LANES), NEG, F32)
            return carry

        def largest(branch, rows, queries, at):
            low = queries.astype(BF)
            best = st_ref[rows, :]
            for begin, step in pieces_of(branch["seg_k"], 256):
                to = pl.ds(at + begin, step)
                scores = jnp.where(queries[:, ID_Q : ID_Q + 1] == kid[:, to], dot_nt(low, kall[to, :]), NEG)
                best = jnp.maximum(best, jnp.max(scores, 1, keepdims=True))
            st_ref[rows, :] = best

        def settle(n, carry):
            at = pl.ds(pl.multiple_of(n * step, step), step)
            own = st_ref[at, :]
            tops[at, :] = own
            wide = iota((step, LANES), 1)
            q_tm[at, :] = q_tm[at, :] + split3(-own, wide)
            return carry

        def restore(n, carry):
            at = pl.ds(pl.multiple_of(n * step, step), step)
            st_ref[at, :] = jnp.where(iota((step, LANES), 1) == ID_Q, tops[at, :], st_ref[at, :])
            return carry

        tops = k_tm
        lax.fori_loop(0, plan.tokens // step, clear, 0)
        scan(largest)
        lax.fori_loop(0, plan.tokens // step, settle, 0)
        attend(jnp.zeros((1, LANES), F32))
        lax.fori_loop(0, plan.tokens // step, restore, 0)


def far_kernel(plan, meta, lens, offsets, st_in, qf_ref, kf_ref, vf_ref, *rest):
    halos, (o_ref, st_ref, kall, vall) = rest[:-4], rest[-4:]
    base, head = meta[0], meta[1]
    starts = slide_starts(lens)
    offs = [offsets[b["level"], head] for b in plan.branches]
    factor = plan.factor
    step = min(512, plan.tokens)

    def carry_over(n, carry):
        at = pl.ds(pl.multiple_of(n * step, step), step)
        st_ref[at, :] = st_in[at, :]
        return carry

    lax.fori_loop(0, plan.tokens // step, carry_over, 0, unroll=4)
    if plan.far:
        far_keys(plan, base, offs, starts, halos, kf_ref, vf_ref, kall, vall)
    for branch in plan.far:
        off, tile, wide = offs[branch["level"]], branch["tile"], branch["seg_k"]
        pos, gate = branch_pos(plan, branch, base, off, 0, wide)
        ids = ids_of(pos, starts, gate)
        keys = kall[branch["begin"] : branch["begin"] + wide, :]
        values = vall[branch["begin"] : branch["begin"] + wide, :]
        for i in range(branch["seg_q"] // tile):
            own = branch["own"] + i * tile
            queries = qf_ref[own : own + tile, :]
            rows = picked(branch, off, i)
            scores = dot_nt(queries, keys)
            scores = jnp.where(queries[:, ID_Q : ID_Q + 1].astype(F32) == ids, scores, NEG)
            top = jnp.max(scores, 1, keepdims=True)
            mixed = dot_nn(jnp.exp2((scores - top) * factor).astype(BF), values)
            old = st_ref[rows, :]
            old_top = old[:, ID_Q : ID_Q + 1]
            new_top = jnp.maximum(old_top, top)
            mixed = old * jnp.exp2((old_top - new_top) * factor) + mixed * jnp.exp2((top - new_top) * factor)
            st_ref[rows, :] = jnp.where(iota((tile, LANES), 1) == ID_Q, new_top, mixed)
    eye = jnp.where(iota((plan.size, LANES), 0) == iota((plan.size, LANES), 1), 1.0, 0.0).astype(BF)

    def finish(n, carry):
        at = pl.ds(pl.multiple_of(n * plan.tq, plan.tq), plan.tq)
        state = st_ref[at, :]
        weight = state[:, ONE_LANE : ONE_LANE + 1]
        top = state[:, ID_Q : ID_Q + 1]
        attn = state * (1.0 / weight)
        merged = top + jnp.log2(weight) * (1.0 / factor)
        lane = iota((plan.tq, LANES), 1)
        st_ref[at, :] = jnp.where(lane < plan.size, attn, jnp.where(lane == ONE_LANE, merged, 0.0))
        o_ref[plan.slot(n)] = dot_nt(eye, attn.astype(BF)).astype(BF)
        return carry

    lax.fori_loop(0, plan.blocks, finish, 0, unroll=8)


def back_tile(plan, branch, queries, grads, keys_at, kall, vall, k_fm, linked, dk_acc, dv_acc):
    dq = None
    for begin, step in pieces_of(branch["seg_k"], 256):
        to = pl.ds(keys_at + begin, step)
        part = slice(begin, begin + step)
        keys = kall[to, :]
        probs = jnp.where(linked(keys), jnp.exp2(dot_nt(keys, queries) * plan.factor), 0.0)
        dv_acc[part, :] += dot_nn(probs.astype(BF), grads)
        moved = (probs * dot_nt(vall[to, :], grads)).astype(BF)
        dk_acc[part, :] += dot_nn(moved, queries)
        more = dot_nn(k_fm[:, part], moved)
        dq = more if dq is None else dq + more
    return dq


def far_back_kernel(
    plan, meta, lens, offsets, st_ref, do_ref, qf_ref, kf_ref, vf_ref, *rest,
):
    sides = 1 if plan.paired else 2
    halos, (do_tm, dqf_ref, dkf_ref, dvf_ref), rest = rest[:sides], rest[sides : sides + 4], rest[sides + 4 :]
    halo_outs, (kall, vall, k_fm, dk_acc, dv_acc) = rest[:sides], rest[sides:]
    base, head = meta[0], meta[1]
    starts = slide_starts(lens)
    offs = [offsets[b["level"], head] for b in plan.branches]
    size, tq = plan.size, plan.tq
    row, col, hit = placement(size, 1)
    place = jnp.where(hit, 1.0, 0.0).astype(BF)
    lane = iota((tq, LANES), 1)

    def block(n, carry):
        at = pl.ds(pl.multiple_of(n * tq, tq), tq)
        grads = dot_tn(jnp.concatenate([do_ref[plan.slot(n)], jnp.zeros((16, tq), BF)], 0), place)
        dots = jnp.sum(jnp.where(lane < size, grads * st_ref[at, :], 0.0), 1, keepdims=True)
        do_tm[at, :] = grads + split3(-dots, lane)
        return carry

    lax.fori_loop(0, plan.blocks, block, 0, unroll=4)
    if plan.far:
        far_keys(plan, base, offs, starts, halos, kf_ref, vf_ref, kall, vall)
    eye = jnp.where(iota((LANES, LANES), 0) == iota((LANES, LANES), 1), 1.0, 0.0).astype(BF)
    for branch in plan.far:
        off, tile, wide, begin = offs[branch["level"]], branch["tile"], branch["seg_k"], branch["begin"]
        k_fm[:, :wide] = dot_nt(eye, kall[begin : begin + wide, :]).astype(BF)
        dk_acc[:wide, :] = jnp.zeros((wide, LANES), F32)
        dv_acc[:wide, :] = jnp.zeros((wide, LANES), F32)
        extra, count = branch["extra"], branch["seg_q"]
        for i in range(count // tile):
            own = branch["own"] + i * tile
            rows = picked(branch, off, i)
            wide_lane = iota((tile, LANES), 1)
            merged = st_ref[rows, :][:, ONE_LANE : ONE_LANE + 1]
            queries = jnp.where(wide_lane == ID_Q, 0.0, qf_ref[own : own + tile, :].astype(F32))
            queries = (queries + split3(-merged, wide_lane)).astype(BF)
            grads = do_tm[rows, :].astype(BF)
            pos, _ = branch_pos(plan, branch, base, off, extra + i * tile, tile)
            ids = ids_of(pos, starts)
            linked = lambda keys: keys[:, ID_K : ID_K + 1].astype(F32) == ids
            dq = back_tile(plan, branch, queries, grads, begin, kall, vall, k_fm, linked, dk_acc, dv_acc)
            dqf_ref[own : own + tile, :] = dq.T
        own = slice(branch["own"], branch["own"] + count)
        dkf_ref[own, :] = dk_acc[extra : extra + count, :]
        dvf_ref[own, :] = dv_acc[extra : extra + count, :]
        for side, ref in enumerate(halo_outs):
            at = side * (extra + count)
            if plan.paired:
                at = pl.multiple_of((1 - meta[2]) * (extra + count), 128)
            to = slice(branch["sel"], branch["sel"] + extra)
            dk = (dk_acc[pl.ds(at, extra), :] * size**-0.5).astype(BF)
            ref[:size, to] = dot_nt(eye[:size], dk).astype(BF)
            ref[size:, to] = dot_nt(eye[:size], dv_acc[pl.ds(at, extra), :].astype(BF)).astype(BF)


def near_back_kernel(
    plan, meta, lens, offsets, x_ref, st_ref, do_tm, dqf_ref, dkf_ref, dvf_ref, *rest,
):
    backs, (dx_ref, q_tm, k_tm, v_tm, dq_tm, dk_tm, dv_tm, kall, vall, k_fm, qid, dk_acc, dv_acc) = rest[:-13], rest[-13:]
    base, head = meta[0], meta[1]
    starts = slide_starts(lens)
    offs = [offsets[b["level"], head] for b in plan.branches]
    size, tq = plan.size, plan.tq
    lane = iota((tq, LANES), 1)
    to_rows(
        plan, base, offs, starts, x_ref, q_tm, k_tm, v_tm,
        lambda n, at: split3(-st_ref[at, :][:, ONE_LANE : ONE_LANE + 1], lane),
    )
    gather_near(plan, offs, k_tm, v_tm, kall, vall, plan.near)
    eye = jnp.where(iota((LANES, LANES), 0) == iota((LANES, LANES), 1), 1.0, 0.0).astype(BF)
    for branch in plan.near:
        off, first, wide, tile = offs[branch["level"]], branch["first"], branch["seg_k"], branch["tile"]
        count = branch["segs"] * branch["seg_q"]
        per = branch["seg_q"] // tile
        pos, _ = branch_pos(plan, branch, base, off, 0, count)
        qid[:, :count] = ids_of(pos, starts)

        def segment(seg, carry, branch=branch, off=off, first=first, wide=wide, tile=tile, per=per):
            key_seg = seg ^ branch["flip"]
            keys_at = pl.multiple_of(first + key_seg * wide, 128)
            k_fm[:, :wide] = dot_nt(eye, kall[pl.ds(keys_at, wide), :]).astype(BF)
            dk_acc[:wide, :] = jnp.zeros((wide, LANES), F32)
            dv_acc[:wide, :] = jnp.zeros((wide, LANES), F32)

            def one(j, carry):
                i = seg * per + j
                rows = picked(branch, off, i)
                queries = q_tm[rows, :].astype(BF)
                grads = do_tm[rows, :].astype(BF)
                ids = qid[:, pl.ds(pl.multiple_of(i * tile, tile), tile)]
                linked = lambda keys: keys[:, ID_K : ID_K + 1].astype(F32) == ids
                dq = back_tile(plan, branch, queries, grads, keys_at, kall, vall, k_fm, linked, dk_acc, dv_acc).T
                if branch["level"]:
                    dq = dq_tm[rows, :] + dq
                dq_tm[rows, :] = dq
                return carry

            lax.fori_loop(0, per, one, 0)
            step = min(256, branch["seg_q"])
            for c in range(branch["seg_q"] // step):
                begin = c * step
                if branch["rate"] == 1:
                    to = pl.ds(pl.multiple_of(key_seg * branch["seg_q"] + begin, step), step)
                    dk_tm[to, :] = dk_acc[begin : begin + step, :]
                    dv_tm[to, :] = dv_acc[begin : begin + step, :]
                else:
                    to = pl.ds(off + (key_seg * branch["seg_q"] + begin) * branch["rate"], step, stride=branch["rate"])
                    dk_tm[to, :] += dk_acc[begin : begin + step, :]
                    dv_tm[to, :] += dv_acc[begin : begin + step, :]
            return carry

        lax.fori_loop(0, branch["segs"], segment, 0, unroll=2 if branch["segs"] > 1 else 1)
    row, col, hit = placement(size, 2)
    place = jnp.where(hit, 1.0, 0.0).astype(BF)[: 2 * size]
    for branch in plan.far:
        off, rate, extra, count = offs[branch["level"]], branch["rate"], branch["extra"], branch["seg_q"]
        rows = pl.ds(off, count, stride=rate)
        own = slice(branch["own"], branch["own"] + count)
        for total, part in ((dq_tm, dqf_ref), (dk_tm, dkf_ref), (dv_tm, dvf_ref)):
            total[rows, :] += part[own, :]
        begins = [plan.tokens - plan.halo, 0]
        if plan.paired:
            begins = [(1 - meta[2]) * (plan.tokens - plan.halo)]
        for begin, ref in zip(begins, backs):
            more = dot_tn(ref[:, branch["sel"] : branch["sel"] + extra], place)
            rows = pl.ds(begin + off, extra, stride=rate)
            dk_tm[rows, :] += more[:, :LANES] * size**0.5
            dv_tm[rows, :] += more[:, LANES:]
    small_eye = eye[:size]

    def finish(n, carry):
        at = pl.ds(pl.multiple_of(n * tq, tq), tq)
        slot = plan.slot(n)
        dx_ref[slot, :size, :] = dot_nt(small_eye, (dq_tm[at, :] * size**-0.5).astype(BF)).astype(BF)
        dx_ref[slot, size : 2 * size, :] = dot_nt(small_eye, (dk_tm[at, :] * size**-0.5).astype(BF)).astype(BF)
        dx_ref[slot, 2 * size :, :] = dot_nt(small_eye, dv_tm[at, :].astype(BF)).astype(BF)
        return carry

    lax.fori_loop(0, plan.blocks, finish, 0, unroll=4)


SMEM = pl.BlockSpec(memory_space=pltpu.SMEM)
VMEM = pl.BlockSpec(memory_space=pltpu.VMEM)
TINY = pl.CostEstimate(flops=1000, bytes_accessed=1000, transcendentals=0)
PARAMS = pltpu.CompilerParams(vmem_limit_bytes=60 << 20)
ROOMY = pltpu.CompilerParams(vmem_limit_bytes=40 << 20)


def struct(shape, kind):
    return jax.ShapeDtypeStruct(shape, kind)


def kernel_call(name, kernel, ins, outs, scratch, flops):
    return pl.pallas_call(
        kernel,
        out_shape=tuple(struct(*out) for out in outs),
        in_specs=[SMEM] * 3 + [VMEM] * (len(ins) - 3),
        out_specs=(VMEM,) * len(outs),
        scratch_shapes=[pltpu.VMEM(*s) for s in scratch],
        compiler_params=ROOMY,
        cost_estimate=pl.CostEstimate(flops=flops, bytes_accessed=1000, transcendentals=0),
        name=name,
    )(*ins)


def near_call(plan, meta, lens, offsets, x):
    rows, keys = ((plan.tokens, LANES), F32), ((plan.near_keys, LANES), BF)
    own = ((plan.own, LANES), BF)
    return kernel_call(
        "near", functools.partial(near_kernel, plan), (meta, lens, offsets, x), (rows, own, own, own),
        (rows, rows, rows, keys, keys, ((1, plan.near_keys), F32)), 20_000_000_000,
    )


def far_call(plan, meta, lens, offsets, state, own, halo):
    keys = ((plan.far_keys, LANES), BF)
    return kernel_call(
        "far", functools.partial(far_kernel, plan), (meta, lens, offsets, state, *own, *halo),
        (((plan.blocks, plan.size, plan.tq), BF), ((plan.tokens, LANES), F32)), (keys, keys), 4_000_000_000,
    )


def far_back_call(plan, meta, lens, offsets, state, do, own, halo):
    keys = ((plan.far_keys, LANES), BF)
    part, side = ((plan.own, LANES), F32), ((2 * plan.size, max(plan.sel, LANES)), BF)
    acc = ((plan.widest, LANES), F32)
    return kernel_call(
        "far_back", functools.partial(far_back_kernel, plan), (meta, lens, offsets, state, do, *own, *halo),
        (((plan.tokens, LANES), F32), part, part, part) + (side,) * (1 if plan.paired else 2),
        (keys, keys, ((LANES, plan.widest), BF), acc, acc), 4_000_000_000,
    )


def near_back_call(plan, meta, lens, offsets, x, state, do_rows, parts, back):
    rows, keys = ((plan.tokens, LANES), F32), ((plan.near_keys, LANES), BF)
    acc = ((plan.widest, LANES), F32)
    return kernel_call(
        "near_back", functools.partial(near_back_kernel, plan),
        (meta, lens, offsets, x, state, do_rows, *parts, *back),
        (((plan.blocks, 3 * plan.size, plan.tq), BF),),
        (rows,) * 6 + (keys, keys, ((LANES, plan.widest), BF), ((1, plan.tokens), F32), acc, acc), 8_000_000_000,
    )[0]


def near_rows(values, norm_gain, norm_shift):
    centred = values - jnp.mean(values, 1, keepdims=True)
    inverse = lax.rsqrt(jnp.mean(centred * centred, 1, keepdims=True) + EPS)
    normed = centred * inverse
    return normed * norm_gain + norm_shift, normed, inverse


def back_rows(grad_out, normed, inverse, norm_gain):
    grad_norm = grad_out * norm_gain
    return inverse * (
        grad_norm
        - jnp.mean(grad_norm, 1, keepdims=True)
        - normed * jnp.mean(grad_norm * normed, 1, keepdims=True)
    )


def own_columns(size, unit, core):
    row, col = iota((size, size), 0), iota((size, size), 1)
    half = size // 2
    other = row >= half
    place = jnp.where(other, row - half, row)
    whole = jnp.floor((place.astype(F32) + 0.5) * (1.0 / unit)).astype(jnp.int32)
    parity = jnp.where(other, 1 - core, core)
    return jnp.where(col == place + unit * (whole + parity), 1.0, 0.0).astype(BF)


def middle_kernel(
    unit_up, unit, core_ref, attn_ref, tiles_ref, out_w, out_b, gain, shift, up_w, up_b, down_w, down_b, g_ref,
    y_ref, res_ref, ag_ref, common_ref, mine_ref, theirs_ref, sums_ref, up_sum_ref,
    pick_up, normed_s, lifted_s, inverse_s, out_s, back_s,
):
    step, steps = pl.program_id(0), pl.num_programs(0)
    width = tiles_ref.shape[1]
    chunk = up_w.shape[1]
    half = chunk // 2
    core = core_ref[0]
    hidden_sel = steps * half

    @pl.when(step == 0)
    def _():
        pick_up[...] = own_columns(chunk, unit_up, core)
        residual = tiles_ref[...].astype(F32) + dot_tn(attn_ref[...], out_w[...]) + out_b[...]
        lifted, normed, inverse = near_rows(residual, gain[...], shift[...])
        low = lifted.astype(BF)
        lifted_s[...] = low
        normed_s[...] = normed
        inverse_s[...] = jnp.broadcast_to(inverse, inverse_s.shape)
        out_s[...] = residual + down_b[...]
        back_s[...] = jnp.zeros_like(back_s)
        common_ref[pl.ds(steps * chunk, width), :] = low.T
        common_ref[pl.ds(steps * chunk + width, width), :] = attn_ref[...]
        pick = own_columns(width, unit, core)
        picked_g = dot_nt(pick, g_ref[...]).astype(BF)
        mine_ref[pl.ds(hidden_sel, width // 2), :] = picked_g[: width // 2]
        theirs_ref[pl.ds(hidden_sel, width // 2), :] = picked_g[width // 2 :]

    lifted = lifted_s[...]
    gate_in = dot_nn(lifted, up_w[...]) + up_b[...]
    cdf = 0.5 + 0.5 * lax.erf(gate_in * (0.5**0.5))
    act = (gate_in * cdf).astype(BF)
    slope = cdf + gate_in * (jnp.exp(-0.5 * gate_in * gate_in) * (1.0 / math.sqrt(2.0 * math.pi)))
    gate_grad = (dot_nt(g_ref[...], down_w[...]) * slope).astype(BF)
    out_s[...] += dot_nn(act, down_w[...])
    back_s[...] += dot_nt(gate_grad, up_w[...])
    up_sum_ref[...] = jnp.sum(gate_grad.astype(F32), 0, keepdims=True)
    common_ref[pl.ds(pl.multiple_of(step * chunk, chunk), chunk), :] = act.T
    picked_gate = dot_nt(pick_up[...], gate_grad).astype(BF)
    at = pl.ds(pl.multiple_of(step * half, half), half)
    mine_ref[at, :] = picked_gate[:half]
    theirs_ref[at, :] = picked_gate[half:]

    @pl.when(step == steps - 1)
    def _():
        y_ref[...] = out_s[...].astype(BF)
        grads = g_ref[...].astype(F32)
        lifted_grad = back_s[...]
        normed = normed_s[...]
        residual_grad = grads + back_rows(lifted_grad, normed, inverse_s[:, :1], gain[...])
        res_ref[...] = residual_grad
        low = residual_grad.astype(BF)
        ag_ref[...] = dot_nt(out_w[...], low).astype(BF)
        pick = own_columns(width, unit, core)
        picked_p = dot_nt(pick, low).astype(BF)
        at = pl.ds(hidden_sel + width // 2, width // 2)
        mine_ref[at, :] = picked_p[: width // 2]
        theirs_ref[at, :] = picked_p[width // 2 :]
        sums_ref[0:1, :] = jnp.sum(grads, 0, keepdims=True)
        sums_ref[1:2, :] = jnp.sum(residual_grad, 0, keepdims=True)
        sums_ref[2:3, :] = jnp.sum(lifted_grad * normed, 0, keepdims=True)
        sums_ref[3:4, :] = jnp.sum(lifted_grad, 0, keepdims=True)
        sums_ref[4:8, :] = jnp.zeros((4, width), F32)


def middle_call(devices, core, attn_t, tiles, out_w, out_b, gain, shift, up_w, up_b, down_w, down_b, g):
    tq, width = tiles.shape
    hidden = up_w.shape[1]
    steps = hidden // width
    whole = lambda *shape: pl.BlockSpec(shape, lambda j: (0,) * len(shape))
    vec = whole(1, width)
    sel = hidden // 2 + width
    return pl.pallas_call(
        functools.partial(middle_kernel, hidden // devices, width // devices),
        grid=(steps,),
        in_specs=[
            SMEM, whole(width, tq), whole(tq, width), whole(width, width), vec, vec, vec,
            pl.BlockSpec((width, width), lambda j: (0, j)), pl.BlockSpec((1, width), lambda j: (0, j)),
            pl.BlockSpec((width, width), lambda j: (j, 0)), vec, whole(tq, width),
        ],
        out_specs=(
            whole(tq, width), whole(tq, width), whole(width, tq), whole(hidden + 2 * width, tq), whole(sel, tq),
            whole(sel, tq), whole(8, width), pl.BlockSpec((1, width), lambda j: (0, j)),
        ),
        out_shape=(
            jax.ShapeDtypeStruct((tq, width), BF),
            pltpu.HBM((tq, width), F32),
            jax.ShapeDtypeStruct((width, tq), BF),
            pltpu.HBM((hidden + 2 * width, tq), BF),
            pltpu.HBM((sel, tq), BF),
            pltpu.HBM((sel, tq), BF),
            pltpu.HBM((8, width), F32),
            pltpu.HBM((1, hidden), F32),
        ),
        scratch_shapes=[
            pltpu.VMEM((width, width), BF), pltpu.VMEM((tq, width), F32), pltpu.VMEM((tq, width), BF),
            pltpu.VMEM((tq, LANES), F32), pltpu.VMEM((tq, width), F32), pltpu.VMEM((tq, width), F32),
        ],
        compiler_params=ROOMY,
        cost_estimate=pl.CostEstimate(flops=14 * tq * width * hidden, bytes_accessed=20 << 20, transcendentals=0),
        name="middle",
    )(core, attn_t, tiles, out_w, out_b, gain, shift, up_w, up_b, down_w, down_b, g)


def weights_kernel(unit_up, unit, meta, common_a, common_b, sel_a, sel_b, *rest):
    first_ref, second_refs, (first_s, second_s, sems) = rest[0], rest[1:5], rest[5:]
    width = 2 * unit * 16
    hidden = common_a.shape[0] - 2 * width
    chips = width // (2 * unit)

    def spot(chip):
        return (chip // 8) * 2 + chip % 2, chip // 2 % 4

    lifted, attn = slice(hidden, hidden + width), slice(hidden + width, hidden + 2 * width)
    group = width // (2 * unit_up)
    for step in range(hidden // width):
        rows = slice(step * width // 2, (step + 1) * width // 2)
        part = dot_nt(sel_a[rows, :], common_a[lifted, :]) + dot_nt(sel_b[rows, :], common_b[lifted, :])
        for i in range(group):
            plane, line = spot(step * group + i)
            first_s[plane, line, :unit_up, :] = part[i * unit_up : (i + 1) * unit_up].astype(BF)
    rows_out = slice(hidden // 2 + width // 2, hidden // 2 + width)
    rows = slice(hidden // 2, hidden // 2 + width // 2)
    out = dot_nt(sel_a[rows_out, :], common_a[attn, :]) + dot_nt(sel_b[rows_out, :], common_b[attn, :])
    held = [out]

    def down_part(step):
        cols = slice(step * width, (step + 1) * width)
        return dot_nt(sel_a[rows, :], common_a[cols, :]) + dot_nt(sel_b[rows, :], common_b[cols, :])

    held += [down_part(step) for step in range(FIRST_DOWN)]
    for chip in range(chips):
        plane, line = spot(chip)
        at = slice(chip * unit, (chip + 1) * unit)
        first_s[plane, line, unit_up:, :] = jnp.concatenate([part[at] for part in held], 0).astype(BF)
    copies = [pltpu.make_async_copy(first_s, first_ref, sems.at[4])]
    copies[0].start()
    for step in range(FIRST_DOWN, hidden // width):
        part = down_part(step)
        at = (step - FIRST_DOWN) * width
        for chip in range(chips):
            plane, line = spot(chip)
            second_s[line, plane, :, at : at + width] = part[chip * unit : (chip + 1) * unit].astype(BF)
    for k in range(4):
        copies.append(pltpu.make_async_copy(second_s.at[meta[5] ^ k], second_refs[k], sems.at[k]))
        copies[-1].start()
    for copy in copies:
        copy.wait()


def weights_call(devices, meta, width, common_a, common_b, sel_a, sel_b):
    tq = common_a.shape[1]
    hidden = common_a.shape[0] - 2 * width
    unit_up, unit = hidden // devices, width // devices
    first = (4, 4, unit_up + (1 + FIRST_DOWN) * unit, width)
    second = (4, unit, hidden - FIRST_DOWN * width)
    outs = pl.pallas_call(
        functools.partial(weights_kernel, unit_up, unit),
        in_specs=[SMEM] + [VMEM] * 4,
        out_specs=(pl.BlockSpec(memory_space=pltpu.HBM),) * 5,
        out_shape=(jax.ShapeDtypeStruct(first, BF),) + (jax.ShapeDtypeStruct(second, BF),) * 4,
        scratch_shapes=[pltpu.VMEM(first, BF), pltpu.VMEM((4,) + second, BF), pltpu.SemaphoreType.DMA((5,))],
        compiler_params=PARAMS,
        cost_estimate=pl.CostEstimate(flops=4 * tq * width * hidden, bytes_accessed=14 << 20, transcendentals=0),
        name="weights",
    )(meta, common_a, common_b, sel_a, sel_b)
    return outs[0], outs[1:]


def fold_kernel(meta, first_ref, own, got1, got2, got3, *outs):
    plane, line = meta[4], meta[5]
    for k in range(4):
        at = line ^ k
        total = first_ref[0, at].astype(F32)
        for i in range(1, 4):
            total += first_ref[i, at].astype(F32)
        outs[k][...] = total.astype(BF)
        at = plane ^ k
        total = own[at].astype(F32) + got1[at].astype(F32) + got2[at].astype(F32) + got3[at].astype(F32)
        outs[4 + k][...] = total.astype(BF)


def fold_call(meta, first, second):
    shapes = [jax.ShapeDtypeStruct(first.shape[2:], BF)] * 4 + [jax.ShapeDtypeStruct(second[0].shape[1:], BF)] * 4
    outs = pl.pallas_call(
        fold_kernel,
        in_specs=[SMEM] + [VMEM] * 5,
        out_specs=(VMEM,) * 8,
        out_shape=tuple(shapes),
        compiler_params=ROOMY,
        cost_estimate=TINY,
        name="fold",
    )(meta, first, *second)
    return outs[:4], outs[4:]


def small_places(unit_up, unit):
    sums = [(2, i * unit, unit) for i in range(4)]
    return [(0, 0, unit), (1, 0, unit), (4, 0, unit), (5, 0, unit)] + sums[1:] + [(3, 0, unit_up), sums[0]]


def last_kernel(unit_up, unit, meta, small_ref, *refs):
    columns, first, second, outs = refs[:4], refs[4:8], refs[8:12], refs[12:]
    qkv_ref, up_ref, out_ref, down_ref = outs[:4]
    small_refs, held = outs[4:-1], outs[-1]
    small = jnp.sum(small_ref[...], 0)
    for ref, (row, at, count) in zip(small_refs, small_places(unit_up, unit)):
        ref[...] = small[row : row + 1, at : at + count]
    size = columns[0].shape[0]
    held[...] = jnp.zeros_like(held)
    for i, ref in enumerate(columns):
        at = pl.multiple_of(meta[10 + i] + size // 2, 8)
        held[pl.ds(at, size), :] += ref[...].astype(F32)
    qkv_ref[...] = held[size // 2 : size // 2 + qkv_ref.shape[0], :]
    total = first[0][...].astype(F32)
    for ref in first[1:]:
        total += ref[...].astype(F32)
    up_ref[...] = total[:unit_up]
    out_ref[...] = total[unit_up : unit_up + unit]
    width = total.shape[1]
    for i in range(FIRST_DOWN):
        at = unit_up + (1 + i) * unit
        down_ref[:, i * width : (i + 1) * width] = total[at : at + unit]
    width = FIRST_DOWN * width
    total = second[0][...].astype(F32)
    for ref in second[1:]:
        total += ref[...].astype(F32)
    down_ref[:, width:] = total


def last_call(meta, small, unit_qkv, unit_up, unit, columns, first, second):
    size, width = columns[0].shape
    hidden = FIRST_DOWN * width + second[0].shape[1]
    outs = [(unit_qkv, width), (unit_up, width), (unit, width), (unit, hidden)]
    outs += [(1, count) for _, _, count in small_places(unit_up, unit)]
    return pl.pallas_call(
        functools.partial(last_kernel, unit_up, unit),
        in_specs=[SMEM] + [VMEM] * 13,
        out_specs=(VMEM,) * len(outs),
        out_shape=tuple(jax.ShapeDtypeStruct(s, F32) for s in outs),
        scratch_shapes=[pltpu.VMEM((unit_qkv + size, width), F32)],
        compiler_params=ROOMY,
        cost_estimate=TINY,
        name="last",
    )(meta, small, *columns, *first, *second)


def enter_kernel(tiles_ref, gain, shift, w_ref, query_b, value_b, x_ref, npre_ref, low_s):
    part = pl.program_id(0)

    @pl.when(part == 0)
    def _():
        scaled, normed, _ = near_rows(tiles_ref[...].astype(F32), gain[...], shift[...])
        low_s[...] = scaled.astype(BF)
        npre_ref[...] = normed.astype(BF)

    bias = jnp.where(part == 0, query_b[...], jnp.where(part == 2, value_b[...], 0.0))
    joined = (dot_nn(low_s[...], w_ref[...]) + bias).T
    heads, _, size, tq = x_ref.shape
    x_ref[:, 0] = joined.astype(BF).reshape(heads, size, tq)


def enter_call(heads, tiles, gain, shift, weight, query_b, value_b):
    tq, width = tiles.shape
    size = width // heads
    whole = lambda *shape: pl.BlockSpec(shape, lambda i: (0,) * len(shape))
    vec = whole(1, width)
    return pl.pallas_call(
        enter_kernel,
        grid=(3,),
        in_specs=[whole(tq, width), vec, vec, pl.BlockSpec((width, width), lambda i: (0, i)), vec, vec],
        out_specs=(pl.BlockSpec((heads, 1, size, tq), lambda i: (0, i, 0, 0)), whole(tq, width)),
        out_shape=(jax.ShapeDtypeStruct((heads, 3, size, tq), BF), jax.ShapeDtypeStruct((tq, width), BF)),
        scratch_shapes=[pltpu.VMEM((tq, width), BF)],
        compiler_params=PARAMS,
        name="enter",
    )(tiles, gain, shift, weight, query_b, value_b)


def leave_kernel(tiles_ref, gain, w_ref, jg_ref, res_ref, out_ref, acc):
    part = pl.program_id(0)
    width, tq = acc.shape
    more = dot_nn(w_ref[...], jg_ref[:, 0].reshape(width, tq))

    @pl.when(part == 0)
    def _():
        acc[...] = more

    @pl.when(part == 1)
    def _():
        acc[...] += more

    @pl.when(part == 2)
    def _():
        _, normed, inverse = near_rows(tiles_ref[...].astype(F32), gain[...], gain[...])
        grads = (acc[...] + more).T
        out_ref[...] = (res_ref[...] + back_rows(grads, normed, inverse, gain[...])).astype(BF)


def leave_call(tiles, gain, weight, joined_grad, residual_grad):
    tq, width = tiles.shape
    heads, _, size, _ = joined_grad.shape
    whole = lambda *shape: pl.BlockSpec(shape, lambda i: (0,) * len(shape))
    return pl.pallas_call(
        leave_kernel,
        grid=(3,),
        in_specs=[
            whole(tq, width), whole(1, width), pl.BlockSpec((width, width), lambda i: (0, i)),
            pl.BlockSpec((heads, 1, size, tq), lambda i: (0, i, 0, 0)), whole(tq, width),
        ],
        out_specs=whole(tq, width),
        out_shape=jax.ShapeDtypeStruct((tq, width), BF),
        scratch_shapes=[pltpu.VMEM((width, tq), F32)],
        compiler_params=PARAMS,
        cost_estimate=TINY,
        name="leave",
    )(tiles, gain, weight, joined_grad, residual_grad)


def halo_hits(plan, offs, first, dims):
    wide = max(plan.sel, LANES)
    shape = (plan.tq, wide)
    token, col = iota(shape, 0) + first, iota(shape, 1)
    hit = col < 0
    for branch in plan.branches:
        if branch["extra"]:
            at = col - branch["sel"]
            inside = (at >= 0) & (at < branch["extra"])
            hit |= inside & (token == at * branch["rate"] + offs[branch["level"]])
    return jnp.where(hit, 1.0, 0.0).astype(BF)


def halo_blocks(plan):
    count = plan.halo // plan.tq
    for i in range(count):
        yield 0, plan.blocks - count + i, i * plan.tq
        yield 1, i, i * plan.tq


def static_slot(plan, block):
    return block % plan.groups * plan.members + block // plan.groups


def select_kernel(plan, meta, offsets, x_ref, *outs):
    offs = [offsets[b["level"], meta[1]] for b in plan.branches]
    if plan.paired:
        count = plan.halo // plan.tq
        total = jnp.zeros((2 * plan.size, max(plan.sel, LANES)), F32)
        for i in range(count):
            block = (1 - meta[2]) * (plan.blocks - count) + i
            total += dot_nn(x_ref[plan.slot(block), plan.size :, :], halo_hits(plan, offs, i * plan.tq, None))
        outs[0][...] = total.astype(BF)
        return
    last_ref, first_ref = outs
    total = [jnp.zeros((2 * plan.size, max(plan.sel, LANES)), F32) for _ in range(2)]
    for side, block, first in halo_blocks(plan):
        hits = halo_hits(plan, offs, first, None)
        total[side] += dot_nn(x_ref[static_slot(plan, block), plan.size :, :], hits)
    last_ref[...] = total[0].astype(BF)
    first_ref[...] = total[1].astype(BF)


def select_call(plan, meta, offsets, x):
    shape = jax.ShapeDtypeStruct((2 * plan.size, max(plan.sel, LANES)), BF)
    return pl.pallas_call(
        functools.partial(select_kernel, plan),
        in_specs=[SMEM, SMEM, VMEM],
        out_specs=(VMEM,) * (1 if plan.paired else 2),
        out_shape=(shape,) * (1 if plan.paired else 2),
        compiler_params=ROOMY,
        name="select",
    )(meta, offsets, x)


def to_owners(vector, owner, lane_of, devices):
    count = vector.shape[1]
    held = jnp.where(iota((devices, count), 0) == owner, vector, 0.0)
    hits = jnp.where(iota((count, LANES), 1) == lane_of, 1.0, 0.0)
    return lax.dot_general(
        held, hits, (((1,), (0,)), ((), ())), precision=lax.Precision.HIGHEST, preferred_element_type=F32
    )


def cut(index, unit):
    whole = jnp.floor((index.astype(F32) + 0.5) * (1.0 / unit)).astype(jnp.int32)
    return whole, index - whole * unit


def head_kernel(devices, meta, dx_ref, near_ref, w_ref, gain, shift, sums_ref, up_ref, *rest):
    column_refs, (small_ref, acc, col_s, row_s) = rest[:-4], rest[-4:]
    step, steps = pl.program_id(0), pl.num_programs(0)
    tq = dx_ref.shape[2]
    rows = dx_ref.shape[1]
    per = near_ref.shape[0] // tq
    size = rows // 3
    width = near_ref.shape[1]

    @pl.when(step == 0)
    def _():
        acc[...] = jnp.zeros_like(acc)
        col_s[...] = jnp.zeros_like(col_s)
        row_s[...] = jnp.zeros_like(row_s)

    for i in range(per):
        grads = dx_ref[i]
        acc[...] += dot_nn(grads, near_ref[i * tq : (i + 1) * tq, :])
        col_s[...] += jnp.broadcast_to(jnp.sum(grads.astype(F32), 1, keepdims=True), col_s.shape)
        row_s[...] += dot_nt(jnp.ones((8, tq), BF), grads)

    @pl.when(step == steps - 1)
    def _():
        head = meta[1]
        plain = acc[...]
        weight = plain * gain[...] + col_s[:, :1] * shift[...]
        acc[...] = weight
        for i, ref in enumerate(column_refs):
            at = pl.multiple_of(meta[6 + i] * size, 8)
            ref[...] = acc[pl.ds(at, size), :].astype(BF)
        own = w_ref[...].astype(F32)
        gain_part = jnp.sum(own * plain, 0, keepdims=True)
        shift_part = jnp.sum(own * col_s[:, :1], 0, keepdims=True)
        unit = width // devices
        owner = cut(iota((1, width), 1), unit)[0]
        lane = cut(iota((width, 1), 0), unit)[1]
        small_ref[:, 0, :] = to_owners(gain_part, owner, lane, devices)
        small_ref[:, 1, :] = to_owners(shift_part, owner, lane, devices)
        held = jnp.zeros((devices, LANES), F32)
        for i in range(4):
            held += to_owners(sums_ref[i : i + 1, :], owner, lane + i * unit, devices)
        small_ref[:, 2, :] = held
        hidden = up_ref.shape[1]
        unit_up = hidden // devices
        held = jnp.zeros((devices, LANES), F32)
        for i in range(hidden // width):
            owner_up = cut(iota((1, width), 1) + i * width, unit_up)[0]
            lane_up = cut(iota((width, 1), 0) + i * width, unit_up)[1]
            held += to_owners(up_ref[:, i * width : (i + 1) * width], owner_up, lane_up, devices)
        small_ref[:, 3, :] = held
        line = row_s[0:1, :]
        for i, part in enumerate((0, 2)):
            index = iota((1, rows), 1) - part * size
            inside = (index >= 0) & (index < size)
            owner_h = jnp.where(inside, 2 * head + cut(index, size // 2)[0], -1)
            lane_h = cut(iota((rows, 1), 0), size // 2)[1]
            small_ref[:, 4 + i, :] = to_owners(line, owner_h, lane_h, devices)
        small_ref[:, 6, :] = jnp.zeros((devices, LANES), F32)
        small_ref[:, 7, :] = jnp.zeros((devices, LANES), F32)


def head_call(devices, meta, dx, npre_all, own_w, gain, shift, sums, up_sums):
    blocks, rows, tq = dx.shape
    width = npre_all.shape[1]
    per = blocks // 4
    whole = lambda *shape: pl.BlockSpec(shape, lambda i: (0,) * len(shape))
    return pl.pallas_call(
        functools.partial(head_kernel, devices),
        grid=(4,),
        in_specs=[
            SMEM, pl.BlockSpec((per, rows, tq), lambda i: (i, 0, 0)), pl.BlockSpec((per * tq, width), lambda i: (i, 0)),
            whole(rows, width), whole(1, width), whole(1, width), whole(8, width), whole(1, up_sums.shape[1]),
        ],
        out_specs=(whole(rows // 3, width),) * 4 + (whole(devices, 8, LANES),),
        out_shape=(jax.ShapeDtypeStruct((rows // 3, width), BF),) * 4
        + (jax.ShapeDtypeStruct((devices, 8, LANES), F32),),
        scratch_shapes=[
            pltpu.VMEM((rows, width), F32), pltpu.VMEM((rows, LANES), F32), pltpu.VMEM((8, rows), F32),
        ],
        compiler_params=PARAMS,
        cost_estimate=TINY,
        name="head",
    )(meta, dx, npre_all, own_w, gain, shift, sums, up_sums)


def layer_norm_rows(values, norm_gain, norm_shift):
    row_mean = jnp.mean(values, -1, keepdims=True)
    centred = values - row_mean
    inverse = lax.rsqrt(jnp.mean(centred * centred, -1, keepdims=True) + EPS)
    normed = centred * inverse
    return (normed * norm_gain + norm_shift, normed, inverse)


def norm_back(grad_out, normed, inverse, norm_gain):
    grad_norm = grad_out * norm_gain
    grad_in = inverse * (
        grad_norm
        - jnp.mean(grad_norm, -1, keepdims=True)
        - normed * jnp.mean(grad_norm * normed, -1, keepdims=True)
    )
    return (grad_in, jnp.sum(grad_out * normed, 0), jnp.sum(grad_out, 0))


def swap(values, axes):
    return lax.all_to_all(values, axes, 0, 0, tiled=True)


def scatter_sum(values, orders):
    sizes = {name: lax.axis_size(name) for name in ALL}
    left = list(ALL)
    rows, cols = values.shape[1:]
    for stage, axes in enumerate(orders):
        values = values.reshape([sizes[name] for name in left] + [rows, cols])
        rest = [name for name in left if name not in axes]
        order = [left.index(name) for name in list(axes) + rest]
        values = values.transpose(order + [len(left), len(left) + 1])
        count = math.prod(sizes[name] for name in axes)
        values = values.reshape((count, -1, rows, cols))
        if count > 1:
            values = swap(values, axes)
            values = jnp.sum(values.astype(F32), 0)
            if stage < len(orders) - 1:
                values = values.astype(BF)
        left = rest
    return values.reshape(rows, cols).astype(F32)


def to_neighbours(pieces, count):
    if count == 2:
        return (lax.ppermute(pieces[0], "grp", [(0, 1), (1, 0)]),)
    return (
        lax.ppermute(pieces[0], "grp", [(i, i + 1) for i in range(count - 1)]),
        lax.ppermute(pieces[1], "grp", [(i + 1, i) for i in range(count - 1)]),
    )


def from_neighbours(pieces, count):
    return to_neighbours(pieces[::-1], count)[::-1]


def share_columns(weight_t, sums, width):
    members, size = lax.axis_size(GROUP), weight_t.shape[1]
    head = lax.axis_index(GROUP)
    full = jnp.zeros((3, members) + weight_t.shape[1:], F32)
    full = lax.dynamic_update_slice(full, weight_t[:, None], (0, head, 0, 0))
    full_sums = lax.dynamic_update_slice(jnp.zeros((3, members, size), F32), sums[:, None], (0, head, 0))
    weight = lax.psum_scatter(full.reshape(3 * members * size, width), ALL, scatter_dimension=0, tiled=True)
    sums = lax.psum_scatter(full_sums.reshape(3, members * size), ALL, scatter_dimension=1, tiled=True)
    return weight, sums[0], sums[2]


def body(
    tile_embed,
    slide_lengths,
    head_offsets,
    pre_gain,
    pre_shift,
    qkv_weight,
    query_bias,
    value_bias,
    out_weight,
    out_bias,
    post_gain,
    post_shift,
    up_weight,
    up_bias,
    down_weight,
    down_bias,
    out_grad,
):
    width = qkv_weight.shape[0]
    hidden = up_weight.shape[1]
    heads = head_offsets.shape[1]
    size = width // heads
    tq = tile_embed.shape[1]
    br, groups = lax.axis_size("br"), lax.axis_size("grp")
    members = heads // br
    devices = heads * groups
    plan = Plan(heads, size, head_offsets.shape[0], br, members, tq, devices * tq)
    head = lax.axis_index(GROUP)
    base = lax.axis_index("grp") * plan.tokens
    meta = jnp.stack([base, head, lax.axis_index("grp")]).astype(jnp.int32)

    tiles = tile_embed[0].astype(F32)
    pre_out, normed_pre, inverse_pre = layer_norm_rows(tiles, pre_gain, pre_shift)
    normed_low = pre_out.astype(BF)
    bias_col = jnp.concatenate([query_bias, jnp.zeros_like(query_bias), value_bias], 1).reshape(-1, 1)
    joined_t = (
        lax.dot_general(qkv_weight, normed_low, (((0,), (1,)), ((), ())), preferred_element_type=F32) + bias_col
    ).astype(BF)
    x = joined_t.reshape(3, heads, size, tq).transpose(1, 0, 2, 3).reshape(heads, 3 * size, tq)
    x = swap(x, GROUP)
    normed_all = lax.all_gather(normed_low, GROUP, axis=0, tiled=True)

    halo = to_neighbours(select_call(plan, meta, head_offsets, x), groups)
    state, *own = near_call(plan, meta, slide_lengths, head_offsets, x)
    mixed, state = far_call(plan, meta, slide_lengths, head_offsets, state, own, halo)
    attn_t = swap(mixed, GROUP).reshape(width, tq)

    projected = lax.dot_general(attn_t, out_weight, (((0,), (0,)), ((), ())), preferred_element_type=F32)
    residual = tiles + projected + out_bias
    post_out, normed_post, inverse_post = layer_norm_rows(residual, post_gain, post_shift)
    lifted = post_out.astype(BF)
    gate_in = jnp.dot(lifted, up_weight, preferred_element_type=F32) + up_bias
    act_float, gelu_pull = jax.vjp(lambda v: jax.nn.gelu(v, approximate=False), gate_in)
    act_low = act_float.astype(BF)
    layer_out = (residual + jnp.dot(act_low, down_weight, preferred_element_type=F32) + down_bias).astype(BF)[None]
    grad_low = out_grad[0]
    grad_float = grad_low.astype(F32)
    act_grad = lax.dot_general(grad_low, down_weight, (((1,), (1,)), ((), ())), preferred_element_type=F32)
    gate_grad = gelu_pull(act_grad)[0].astype(BF)
    lifted_grad = lax.dot_general(gate_grad, up_weight, (((1,), (1,)), ((), ())), preferred_element_type=F32)
    norm_part, post_gain_sum, post_shift_sum = norm_back(lifted_grad, normed_post, inverse_post, post_gain)
    residual_grad = grad_float + norm_part
    proj_grad = residual_grad.astype(BF)
    attn_grad_t = lax.dot_general(
        out_weight, proj_grad, (((1,), (1,)), ((), ())), preferred_element_type=F32
    ).astype(BF)
    do = swap(attn_grad_t.reshape(heads, size, tq), GROUP)

    tokens = (((0,), (0,)), ((), ()))
    up_part = lax.dot_general(gate_grad, lifted, tokens, preferred_element_type=F32).astype(BF)
    down_part = lax.dot_general(grad_low, act_low, tokens, preferred_element_type=F32).astype(BF)
    out_part = lax.dot_general(proj_grad, attn_t, (((0,), (1,)), ((), ())), preferred_element_type=F32).astype(BF)
    vectors = [
        jnp.sum(gate_grad.astype(F32), 0).reshape(devices, -1),
        jnp.sum(grad_float, 0).reshape(devices, -1),
        jnp.sum(residual_grad, 0).reshape(devices, -1),
        post_gain_sum.reshape(devices, -1),
        post_shift_sum.reshape(devices, -1),
    ]
    ends = [0]
    for vector in vectors:
        ends.append(ends[-1] + vector.shape[1])
    small = jnp.concatenate(vectors, 1)
    small = jnp.pad(small[:, None, :], ((0, 0), (0, 7), (0, width - small.shape[1]))).astype(BF)
    misc = jnp.concatenate([out_part.reshape(devices, -1, width), small], 1)
    first, second = (("s0",), ("br", "s1"), ("grp", "s2")), (("s0",), ("grp", "s2"), ("br", "s1"))
    up_own = scatter_sum(up_part.reshape(devices, -1, width), first)
    down_own = scatter_sum(down_part.reshape(devices, -1, hidden), second)
    misc_own = scatter_sum(misc, first)
    unit = width // devices
    small_own = misc_own[unit]
    small_own = [small_own[None, ends[i] : ends[i + 1]] for i in range(len(vectors))]

    rows, dq, dk, dv, *sides = far_back_call(plan, meta, slide_lengths, head_offsets, state, do, own, halo)
    back = from_neighbours(sides, groups)
    dx = near_back_call(plan, meta, slide_lengths, head_offsets, x, state, rows, (dq, dk, dv), back)
    joined_grad_t = swap(dx, GROUP).reshape(heads, 3, size, tq).transpose(1, 0, 2, 3).reshape(3 * width, tq)
    weight_t = jnp.einsum(
        "nct,ntd->cd", dx, normed_all.reshape(heads, tq, width), preferred_element_type=F32
    ).reshape(3, size, width)
    head_sums = jnp.sum(dx.astype(F32), (0, 2)).reshape(3, size)
    qkv_own, query_own, value_own = share_columns(weight_t, head_sums, width)
    normed_grad = lax.dot_general(joined_grad_t, qkv_weight, (((0,), (1,)), ((), ())), preferred_element_type=F32)
    tile_part, pre_gain_sum, pre_shift_sum = norm_back(normed_grad, normed_pre, inverse_pre, pre_gain)
    tile_grad = (residual_grad + tile_part).astype(BF)[None]
    last = jnp.stack([pre_gain_sum, pre_shift_sum]).reshape(2, devices, unit).transpose(1, 0, 2)
    last = jnp.pad(last, ((0, 0), (0, 6), (0, LANES - unit)))
    last = jnp.sum(swap(last, ALL).reshape(devices, 8, LANES), 0)
    return (
        layer_out,
        tile_grad,
        last[0:1, :unit],
        last[1:2, :unit],
        qkv_own.T,
        query_own[None],
        value_own[None],
        misc_own[:unit].T,
        small_own[2],
        small_own[3],
        small_own[4],
        up_own.T,
        small_own[0],
        down_own.T,
        small_own[1],
    )


def across(piece, axes, k):
    return lax.ppermute(piece, axes, [(i, i ^ k) for i in range(4)])


def matchings(edges, count):
    edges, found = list(edges), []
    while edges:
        by_source = {}
        for edge in edges:
            by_source.setdefault(edge[0], []).append(edge)
        taken = {}

        def place(source, seen):
            for edge in by_source[source]:
                if edge[1] not in seen:
                    seen.add(edge[1])
                    if edge[1] not in taken or place(taken[edge[1]][0], seen):
                        taken[edge[1]] = edge
                        return True
            return False

        for source in range(count):
            place(source, set())
        found.append(sorted(taken.values()))
        for edge in taken.values():
            edges.remove(edge)
    return found


def column_routes(heads, size, unit):
    sizes = [lax.axis_size(name) for name in ALL]
    inner = sizes[2] * sizes[3] * sizes[4]
    edges = []
    for head in range(heads):
        for grp in range(sizes[1]):
            source = (head // inner * sizes[1] + grp) * inner + head % inner
            for part in range(3):
                start = (part * heads + head) * size
                for owner in sorted({start // unit, (start + size - 1) // unit}):
                    edges.append((source, owner, (part, start - owner * unit)))
    devices = heads * sizes[1]
    for matching in matchings(edges, devices):
        route = [edge[:2] for edge in matching]
        part_of, begin_of = [0] * devices, [0] * devices
        for source, owner, (part, begin) in matching:
            part_of[source], begin_of[owner] = part, begin
        yield route, part_of, begin_of


def fast_body(
    tile_embed, slide_lengths, head_offsets, pre_gain, pre_shift, qkv_weight, query_bias, value_bias, out_weight,
    out_bias, post_gain, post_shift, up_weight, up_bias, down_weight, down_bias, out_grad,
):
    width = qkv_weight.shape[0]
    heads = head_offsets.shape[1]
    size = width // heads
    tq = tile_embed.shape[1]
    br, groups = lax.axis_size("br"), lax.axis_size("grp")
    members = heads // br
    devices = heads * groups
    plan = Plan(heads, size, head_offsets.shape[0], br, members, tq, devices * tq)
    head = lax.axis_index(GROUP)
    group = lax.axis_index("grp")
    core = lax.axis_index("s0")
    meta = [group * plan.tokens, head, group, core, lax.axis_index(("br", "s1")), lax.axis_index(("grp", "s2"))]
    routes = list(column_routes(heads, size, 3 * width // devices))[::-1]
    table = jnp.array([parts for _, parts, _ in routes] + [begins for _, _, begins in routes], jnp.int32)
    meta.extend(lax.dynamic_index_in_dim(table, lax.axis_index(ALL), 1, False))
    meta = jnp.stack(meta).astype(jnp.int32)
    tiles = tile_embed[0]
    own_w = jnp.concatenate(
        [lax.dynamic_slice_in_dim(qkv_weight, part * width + head * size, size, 1) for part in range(3)], 1
    ).T
    pair = [(0, 1), (1, 0)]
    plane, line = ("br", "s1"), ("grp", "s2")

    x, npre = enter_call(heads, tiles, pre_gain, pre_shift, qkv_weight, query_bias, value_bias)
    x = swap(x.reshape(heads, 3 * size, tq), GROUP)
    x, npre, own_w, meta = lax.optimization_barrier((x, npre, own_w, meta))
    halo = to_neighbours(select_call(plan, meta, head_offsets, x), groups)
    state, *own = near_call(plan, meta, slide_lengths, head_offsets, x)
    mixed, state = far_call(plan, meta, slide_lengths, head_offsets, state, own, halo)
    attn_t = swap(mixed, GROUP).reshape(width, tq)
    npre_all = lax.all_gather(npre, GROUP, axis=0, tiled=True)
    layer_out, residual_grad, attn_grad_t, common, sel, sel_give, sums, up_sums = middle_call(
        devices, core[None].astype(jnp.int32), attn_t, tiles, out_weight, out_bias, post_gain, post_shift,
        up_weight, up_bias, down_weight, down_bias, out_grad[0],
    )
    do = swap(attn_grad_t.reshape(heads, size, tq), GROUP)
    common_b = lax.ppermute(common, "s0", pair)
    sel_b = lax.ppermute(sel_give, "s0", pair)
    first, second = weights_call(devices, meta, width, common, common_b, sel, sel_b)
    do, first, second, npre_all = lax.optimization_barrier((do, first, second, npre_all))
    first = swap(first, plane)
    second = [second[0]] + [across(second[k], line, k) for k in (1, 2, 3)]
    rows, dq, dk, dv, *sides = far_back_call(plan, meta, slide_lengths, head_offsets, state, do, own, halo)
    back = from_neighbours(sides, groups)
    dx = near_back_call(plan, meta, slide_lengths, head_offsets, x, state, rows, (dq, dk, dv), back)
    *columns, small = head_call(devices, meta, dx, npre_all, own_w, pre_gain, pre_shift, sums, up_sums)
    dx, columns, small, first, second = lax.optimization_barrier((dx, columns, small, first, second))
    joined_grad = swap(dx, GROUP).reshape(heads, 3, size, tq)
    first, second = fold_call(meta, first, second)
    first = [first[0]] + [across(first[k], line, k) for k in (1, 2, 3)]
    second = [second[0]] + [across(second[k], plane, k) for k in (1, 2, 3)]
    joined_grad, small, second = lax.optimization_barrier((joined_grad, small, second))
    small = swap(small, ALL)
    columns = [lax.ppermute(piece, ALL, route) for piece, (route, _, _) in zip(columns, routes)]
    joined_grad, first = lax.optimization_barrier((joined_grad, first))
    tile_grad = leave_call(tiles, pre_gain, qkv_weight, joined_grad, residual_grad)
    unit_up, unit = up_weight.shape[1] // devices, width // devices
    qkv_own, up_own, out_own, down_own, *vectors = last_call(
        meta, small, 3 * unit, unit_up, unit, columns, first, second
    )
    gain_own, shift_own, query_own, value_own, out_b, post_gain_own, post_shift_own, up_b, down_b = vectors
    return (
        layer_out[None], tile_grad[None], gain_own, shift_own, qkv_own.T, query_own, value_own, out_own.T, out_b,
        post_gain_own, post_shift_own, up_own.T, up_b, down_own.T, down_b,
    )


def solution(mesh):
    br, rows = mesh.shape["br"], mesh.shape["rows"]

    def run(*args):
        members = args[2].shape[1] // br
        shape = (br, rows // members, members // 4, 2, 2)
        split = jax.sharding.Mesh(mesh.devices.reshape(shape), ALL)
        tokens = P(("grp", "s2", "s1", "s0"), "br", None)
        owned = P(None, ALL)
        return jax.shard_map(
            fast_body if shape == (2, 2, 2, 2, 2) else body,
            mesh=split,
            in_specs=(tokens,) + (P(),) * 15 + (tokens,),
            out_specs=(tokens, tokens) + (owned,) * 13,
            check_vma=False,
        )(*args)

    return run
```
